32 devices in a mesh: rows: 8 (over z, x), tp: 4 (over y, core).
Axes of the slice: x: 2, y: 2, z: 4, core: 2. Of those that a mesh axis runs over, the one named last changes fastest.
Arguments:
- tokens: bfloat16 [1024, 8, 1024], P('tp', 'rows'), may hold values from -6 to 6
- memory: bfloat16 [1024, 8, 1024], P('tp', 'rows'), may hold values from -6 to 6
- out_grad: bfloat16 [1024, 8, 1024], P('tp', 'rows'), may hold values from -6 to 6
- dec_segments: int32 [8, 1024], P('rows'), may hold values from 0 to 2, as said below
- src_segments: int32 [8, 1024], P('rows'), may hold values from 0 to 2, as said below
- self_query: bfloat16 [1024, 1024], P(None, 'tp'), may hold values from -0.1875 to 0.1875
- self_key: bfloat16 [1024, 1024], P(None, 'tp'), may hold values from -0.1875 to 0.1875
- self_value: bfloat16 [1024, 1024], P(None, 'tp'), may hold values from -0.1875 to 0.1875
- self_out: bfloat16 [1024, 1024], P('tp'), may hold values from -1.5 to 1.5
- cross_query: bfloat16 [1024, 1024], P(None, 'tp'), may hold values from -0.1875 to 0.1875
- cross_key: bfloat16 [1024, 1024], P(None, 'tp'), may hold values from -0.1875 to 0.1875
- cross_value: bfloat16 [1024, 1024], P(None, 'tp'), may hold values from -0.1875 to 0.1875
- cross_out: bfloat16 [1024, 1024], P('tp'), may hold values from -1.5 to 1.5
- ffn_in: bfloat16 [1024, 4096], P(None, 'tp'), may hold values from -0.1875 to 0.1875
- ffn_out: bfloat16 [4096, 1024], P('tp'), may hold values from -0.09375 to 0.09375
- adapt_down: bfloat16 [1024, 512], replicated, may hold values from -0.1875 to 0.1875
- adapt_down_bias: float32 [512], replicated, may hold values from -3 to 3
- adapt_up: bfloat16 [512, 1024], replicated, may hold values from -0.0625 to 0.0625
- adapt_up_bias: float32 [1024], replicated, may hold values from -0.6 to 0.6
- self_prefix: bfloat16 [2, 30, 1024], P(None, None, 'tp'), may hold values from -6 to 6
- cross_prefix: bfloat16 [2, 30, 1024], P(None, None, 'tp'), may hold values from -6 to 6
- norm_gain: float32 [3, 1024], replicated, may hold values from 0.5 to 1.5
- norm_shift: float32 [3, 1024], replicated, may hold values from -1.8 to 1.8
Outputs:
- output: bfloat16 [1024, 8, 1024], P('tp', 'rows')
- tokens_grad: bfloat16 [1024, 8, 1024], P('tp', 'rows')
- memory_grad: bfloat16 [1024, 8, 1024], P('tp', 'rows')
- self_prefix_grad: float32 [2, 30, 1024], P(None, None, 'tp')
- cross_prefix_grad: float32 [2, 30, 1024], P(None, None, 'tp')
- gain_grad: float32 [3, 1024], replicated
- shift_grad: float32 [3, 1024], replicated
- adapt_down_grad: float32 [1024, 512], replicated
- adapt_down_bias_grad: float32 [512], replicated
- adapt_up_grad: float32 [512, 1024], replicated
- adapt_up_bias_grad: float32 [1024], replicated
The draws below stay inside these ranges and needn't reach their ends.
Inputs may be any that keep to these rules, and one draw needn't show every extreme that they name: `dec_segments`: each row holds documents 0, 1 and 2 in this order; document 1 begins at a position from 1 to 127 and ends among the last 128 positions, before the row's last position. `src_segments`: each row holds documents 0, 1 and 2 in this order; document 1 begins at a position from 1 to 127 and ends among the last 128 positions, before the row's last position.
All inputs are finite; a program needn't handle non-finite values.
Results may differ from the reference program's by a relative error of at most 0.025.
Values may be sent and summed in bfloat16 or wider, within the bound.
A program may use at most 192 MiB of HBM per device.

```python
import jax
import jax.numpy as jnp
from jax import lax

D = 1024
HEAD = 64
FF = 4096
ADAPT = 512
PREFIX = 30
SEQ = 1024
ROWS = 8


def document_layout(key):
    start_key, finish_key = jax.random.split(key, 2)
    position = jnp.arange(SEQ)[None, :]
    start = jax.random.randint(start_key, (ROWS, 1), 1, max(2, SEQ // 8))
    finish = jax.random.randint(finish_key, (ROWS, 1), 7 * SEQ // 8 + 1, SEQ)
    boundary = (position == start) | (position == finish)
    boundary = boundary & (position > 0)
    doc_ids = jnp.cumsum(boundary.astype(jnp.int32), axis=1)
    return (doc_ids.astype(jnp.int32), start.astype(jnp.int32))


def draw_dec_segments(key, part):
    doc_ids, start = document_layout(key)
    return doc_ids


def draw_src_segments(key, part):
    dec_ids, dec_start = document_layout(key)
    largest = dec_ids[:, -1:]
    long_id = jnp.take_along_axis(dec_ids, dec_start, axis=1)
    key = jax.random.fold_in(key, 7)
    src_ids, src_start = document_layout(key)
    src_long = jnp.take_along_axis(src_ids, src_start, axis=1)
    position = jnp.arange(SEQ)[None, :]
    head_ids = jnp.minimum(src_ids, long_id - 1)
    rest_ids = jnp.minimum(src_ids - src_long + long_id, largest)
    return jnp.where(position < src_start, head_ids, rest_ids).astype(jnp.int32)


def shard_levels(own_key, dims, cuts, smallest, top_value):
    def one(axis_at, blocks):
        heights = jax.random.uniform(jax.random.fold_in(jax.random.fold_in(own_key, 6), axis_at), (blocks,), jnp.float32, smallest / len(cuts), top_value / len(cuts))
        return jnp.repeat(jnp.exp(heights), dims[axis_at] // blocks).reshape((-1,) + (1,) * (len(dims) - axis_at - 1))

    factor_of = one(*cuts[0])
    for cut in cuts[1:]:
        factor_of = factor_of * one(*cut)
    return factor_of


def noise(key, extent, deviation, bound, cuts=(), kind=jnp.bfloat16):
    values = jax.random.normal(key, extent, jnp.float32) * deviation
    if len(cuts) > 0:
        values = shard_levels(key, extent, cuts, -0.22, 0.18) * values
    return jnp.clip(values, min=-bound, max=bound).astype(kind)


def setup_inputs(seed: int = 0) -> dict:
    streams_of = jax.random.split(jax.random.key(seed), 24)
    return {
        "tokens": noise(streams_of[0], (SEQ, ROWS, D), 1.0, 6.0, ((0, 4), (1, 8))),
        "memory": noise(streams_of[1], (SEQ, ROWS, D), 1.0, 6.0, ((0, 4), (1, 8))),
        "out_grad": noise(streams_of[2], (SEQ, ROWS, D), 1.0, 6.0, ((0, 4), (1, 8))),
        "dec_segments": draw_dec_segments(jax.random.fold_in(streams_of[23], 71), 0),
        "src_segments": draw_src_segments(jax.random.fold_in(streams_of[23], 71), 0),
        "self_query": noise(streams_of[5], (D, D), D ** -0.5, 0.1875, ((1, 4),)),
        "self_key": noise(streams_of[6], (D, D), D ** -0.5, 0.1875, ((1, 4),)),
        "self_value": noise(streams_of[7], (D, D), D ** -0.5, 0.1875, ((1, 4),)),
        "self_out": noise(streams_of[8], (D, D), 16 ** -0.5, 1.5, ((0, 4),)),
        "cross_query": noise(streams_of[9], (D, D), D ** -0.5, 0.1875, ((1, 4),)),
        "cross_key": noise(streams_of[10], (D, D), D ** -0.5, 0.1875, ((1, 4),)),
        "cross_value": noise(streams_of[11], (D, D), D ** -0.5, 0.1875, ((1, 4),)),
        "cross_out": noise(streams_of[12], (D, D), 16 ** -0.5, 1.5, ((0, 4),)),
        "ffn_in": noise(streams_of[13], (D, FF), D ** -0.5, 0.1875, ((1, 4),)),
        "ffn_out": noise(streams_of[14], (FF, D), FF ** -0.5, 0.09375, ((0, 4),)),
        "adapt_down": noise(streams_of[15], (D, ADAPT), D ** -0.5, 0.1875),
        "adapt_down_bias": noise(streams_of[16], (ADAPT,), 0.5, 3.0, (), jnp.float32),
        "adapt_up": noise(streams_of[17], (ADAPT, D), (16 * ADAPT) ** -0.5, 0.0625),
        "adapt_up_bias": noise(streams_of[18], (D,), 0.1, 0.6, (), jnp.float32),
        "self_prefix": noise(streams_of[19], (2, PREFIX, D), 1.0, 6.0, ((2, 4),)),
        "cross_prefix": noise(streams_of[20], (2, PREFIX, D), 1.0, 6.0, ((2, 4),)),
        "norm_gain": jnp.clip(1.0 + 0.1 * jax.random.normal(streams_of[21], (3, D), jnp.float32), 0.5, 1.5),
        "norm_shift": noise(streams_of[22], (3, D), 0.3, 1.8, (), jnp.float32),
    }


@jax.custom_vjp
def low(v):
    return lax.optimization_barrier(v.astype(jnp.bfloat16)).astype(jnp.float32)

@jax.custom_vjp
def low_back(v):
    return v

def low_keep(v):
    return (low(v), None)

def low_pass(kept, grad):
    return (grad,)

def back_keep(v):
    return (v, None)

def back_low(kept, grad):
    return (low(grad),)
low.defvjp(low_keep, low_pass)
low_back.defvjp(back_keep, back_low)
HIGHEST = lax.Precision.HIGHEST
MASKED = -1000000000.0
EPSILON = 1e-05

def matmul(left_side, right_side):
    return jnp.dot(left_side, right_side, precision=HIGHEST, preferred_element_type=jnp.float32)

def gelu_exact(value):
    return jax.nn.gelu(value, approximate=False)

def layer_norm(value, gain, shift):
    centered = value - lax.optimization_barrier(jnp.mean(value, axis=-1, keepdims=True))
    spread = lax.rsqrt(lax.optimization_barrier(jnp.mean(centered * centered, axis=-1, keepdims=True)) + EPSILON)
    return centered * spread * gain + shift

def self_allowed(segments):
    position = jnp.arange(segments.shape[0])
    same_doc = (segments[:, None] == segments[None, :]) & (position[None, :] <= position[:, None])
    return jnp.concatenate([jnp.ones((segments.shape[0], PREFIX), dtype=bool), same_doc], axis=1)

def cross_allowed(dec_row, src_row):
    same_doc = dec_row[:, None] == src_row[None, :]
    return jnp.concatenate([jnp.ones((dec_row.shape[0], PREFIX), dtype=bool), same_doc], axis=1)

def attend(queries, key_rows, value_rows, allowed):
    head_count = queries.shape[1] // HEAD
    query_heads = queries.reshape(queries.shape[0], head_count, HEAD)
    key_heads = key_rows.reshape(key_rows.shape[0], head_count, HEAD)
    value_heads = value_rows.reshape(value_rows.shape[0], head_count, HEAD)
    scores = low_back(jnp.einsum('qhd,khd->hqk', query_heads, key_heads, precision=HIGHEST))
    scores = jnp.where(allowed[None], scores, MASKED)
    row_max = lax.optimization_barrier(jnp.max(scores, axis=2, keepdims=True))
    exponent = jnp.exp(scores - row_max)
    weights_low = low(exponent / lax.optimization_barrier(jnp.sum(exponent, axis=2, keepdims=True)))
    mixture = jnp.einsum('hqk,khd->qhd', weights_low, value_heads, precision=HIGHEST)
    return mixture.reshape(queries.shape[0], -1)

def forward(tokens, memory, self_prefix, cross_prefix, norm_gain, norm_shift, adapt_down, adapt_down_bias, adapt_up, adapt_up_bias, frozen, dec_segments, src_segments):
    self_query, self_key, self_value, self_out, cross_query, cross_key, cross_value, cross_out, ffn_in, ffn_out = frozen
    seq_len, row_count, width = tokens.shape
    score_scale = HEAD ** (-0.5)
    flat_tokens = tokens.reshape(seq_len * row_count, width)
    flat_memory = memory.reshape(seq_len * row_count, width)

    def to_rows(array):
        return jnp.moveaxis(array.reshape(seq_len, row_count, -1), 1, 0)

    def to_positions(array):
        return jnp.moveaxis(array, 0, 1).reshape(seq_len * row_count, -1)
    queries = low(low_back(score_scale * matmul(flat_tokens, self_query)))
    key_rows = low(low_back(matmul(flat_tokens, self_key)))
    value_rows = low(low_back(matmul(flat_tokens, self_value)))

    def self_row(packed):
        row_queries, row_keys, row_values, segments = packed
        return attend(row_queries, jnp.concatenate([self_prefix[0], row_keys]), jnp.concatenate([self_prefix[1], row_values]), self_allowed(segments))
    mixture = lax.map(jax.checkpoint(self_row), (to_rows(queries), to_rows(key_rows), to_rows(value_rows), dec_segments))
    mixture = low(low_back(to_positions(mixture)))
    normed_one = layer_norm(flat_tokens + low_back(matmul(mixture, self_out)), norm_gain[0], norm_shift[0])
    normed_one_low = low(normed_one)
    cross_queries = low(low_back(score_scale * matmul(normed_one_low, cross_query)))
    cross_keys = low(low_back(matmul(flat_memory, cross_key)))
    cross_values = low(low_back(matmul(flat_memory, cross_value)))

    def cross_row(packed):
        row_queries, row_keys, row_values, dec_row, src_row = packed
        return attend(row_queries, jnp.concatenate([cross_prefix[0], row_keys]), jnp.concatenate([cross_prefix[1], row_values]), cross_allowed(dec_row, src_row))
    cross_mix = lax.map(jax.checkpoint(cross_row), (to_rows(cross_queries), to_rows(cross_keys), to_rows(cross_values), dec_segments, src_segments))
    cross_mix = low(low_back(to_positions(cross_mix)))
    normed_two = layer_norm(normed_one + low_back(matmul(cross_mix, cross_out)), norm_gain[1], norm_shift[1])
    normed_two_low = low(normed_two)
    hidden = low(gelu_exact(low_back(matmul(normed_two_low, ffn_in))))
    ffn_result = low_back(matmul(hidden, ffn_out))
    adapt_hidden = low(gelu_exact(low_back(matmul(normed_two_low, adapt_down) + adapt_down_bias)))
    adapt_result = low_back(matmul(adapt_hidden, adapt_up) + adapt_up_bias)
    mixed_out = layer_norm(normed_two + ffn_result + 4.0 * adapt_result, norm_gain[2], norm_shift[2])
    return mixed_out.reshape(seq_len, row_count, width)

def reference(tokens, memory, out_grad, dec_segments, src_segments, self_query, self_key, self_value, self_out, cross_query, cross_key, cross_value, cross_out, ffn_in, ffn_out, adapt_down, adapt_down_bias, adapt_up, adapt_up_bias, self_prefix, cross_prefix, norm_gain, norm_shift):

    def widen(array):
        return array.astype(jnp.float32)
    frozen = tuple((widen(array) for array in (self_query, self_key, self_value, self_out, cross_query, cross_key, cross_value, cross_out, ffn_in, ffn_out)))

    def layer_run(tok_in, mem_in, self_pre, cross_pre, gain, shift, down, down_bias, upward, up_bias):
        return forward(tok_in, mem_in, self_pre, cross_pre, gain, shift, down, down_bias, upward, up_bias, frozen, dec_segments, src_segments)
    mixed, backward = jax.vjp(layer_run, widen(tokens), widen(memory), widen(self_prefix), widen(cross_prefix), widen(norm_gain), widen(norm_shift), widen(adapt_down), widen(adapt_down_bias), widen(adapt_up), widen(adapt_up_bias))
    grads = backward(widen(out_grad))
    return (mixed.astype(jnp.bfloat16), grads[0].astype(jnp.bfloat16), grads[1].astype(jnp.bfloat16), grads[2], grads[3], grads[4], grads[5], grads[6], grads[7], grads[8], grads[9])
```

```python
import functools

import jax
import jax.numpy as jnp
from jax import lax
from jax.experimental import pallas as pl
from jax.experimental.pallas import tpu as pltpu
from jax.sharding import PartitionSpec as P

HEAD = 64
PAIR = 2 * HEAD
PRE = 128
PRE_PACK = 32
GROUP = 8
LINE = 4
MASKED = -1000000000.0
EPSILON = 1e-05
SCALE = HEAD**-0.5
f32 = jnp.float32
bf16 = jnp.bfloat16
MESH = pl.DeviceIdType.MESH
VMEM = pltpu.VMEM
ANY = pl.ANY


def nn(a, b):
    return lax.dot_general(a, b, (((1,), (0,)), ((), ())), preferred_element_type=f32)


def nt(a, b):
    return lax.dot_general(a, b, (((1,), (1,)), ((), ())), preferred_element_type=f32)


def tn(a, b):
    return lax.dot_general(a, b, (((0,), (0,)), ((), ())), preferred_element_type=f32)


def gelu_parts(v):
    phi = 0.5 + 0.5 * lax.erf(v * (0.5**0.5))
    slope = phi + v * (jnp.exp(-0.5 * v * v) * 0.3989422804014327)
    return v * phi, slope


def norm_parts(v):
    centered = v - jnp.mean(v, axis=-1, keepdims=True)
    spread = lax.rsqrt(jnp.mean(centered * centered, axis=-1, keepdims=True) + EPSILON)
    return centered * spread, spread


def norm_back(dy, gain, n, spread):
    dn = dy * gain
    dv = spread * (
        dn - jnp.mean(dn, axis=-1, keepdims=True) - n * jnp.mean(dn * n, axis=-1, keepdims=True)
    )
    return dv, jnp.sum(dy * n, axis=0, keepdims=True), jnp.sum(dy, axis=0, keepdims=True)


def lane_half(shape, h):
    return (lax.broadcasted_iota(jnp.int32, shape, 1) // HEAD) == h


def mask_bias(seg_q, seg_k, q_index, k_index, prefix_len):
    keep = seg_q == seg_k
    if q_index is not None:
        keep = keep & (k_index - PRE <= q_index)
    keep = keep | (k_index < prefix_len)
    return jnp.where(keep, 0.0, MASKED)


def pair_forward(q_pair, k_pair, v_pair, bias):
    outs = []
    for h in range(2):
        half = lane_half(q_pair.shape, h)
        scores = nt(jnp.where(half, q_pair, jnp.zeros_like(q_pair)), k_pair) + bias
        top = jnp.max(scores, axis=1, keepdims=True)
        e = jnp.exp(scores - top)
        total = jnp.sum(e, axis=1, keepdims=True)
        outs.append(nn(e.astype(bf16), v_pair) * (1.0 / total))
    return jnp.where(lane_half(outs[0].shape, 0), outs[0], outs[1]).astype(bf16)


def pair_backward(q_pair, k_pair, v_pair, da_pair, bias_t):
    k_turned = k_pair.T
    dk = dv = None
    dq = []
    for h in range(2):
        half = lane_half(q_pair.shape, h)
        q = jnp.where(half, q_pair, jnp.zeros_like(q_pair))
        da = jnp.where(half, da_pair, jnp.zeros_like(da_pair))
        scores = nt(k_pair, q) + bias_t
        top = jnp.max(scores, axis=0, keepdims=True)
        e = jnp.exp(scores - top)
        p = e * (1.0 / jnp.sum(e, axis=0, keepdims=True))
        weighted = p * nt(v_pair, da)
        ds = (weighted - p * jnp.sum(weighted, axis=0, keepdims=True)).astype(bf16)
        dv_h = nn(p.astype(bf16), da)
        dk_h = nn(ds, q)
        dk = dk_h if dk is None else dk + dk_h
        dv = dv_h if dv is None else dv + dv_h
        dq.append(nn(k_turned[h * HEAD : (h + 1) * HEAD], ds))
    return jnp.concatenate(dq, axis=0).T.astype(bf16), dk, dv


def self_forward_kernel(
    prefix_len, x, wq, wk, wv, wo, pre, seg_col, seg_row, q_out, k_out, v_out, part, mixed, bias
):
    block = q_out.shape[0] // 4
    lanes = q_out.shape[1]
    for target, at in ((k_out, 0), (v_out, PRE_PACK)):
        target[0:PRE_PACK] = pre[at : at + PRE_PACK]
        target[PRE_PACK:PRE] = jnp.zeros((PRE - PRE_PACK, lanes), bf16)

    @pl.loop(0, 4)
    def _(i):
        at = pl.multiple_of(i * block, block)
        rows = x[pl.ds(at, block)]
        q_out[pl.ds(at, block)] = (SCALE * nn(rows, wq[...])).astype(bf16)
        k_out[pl.ds(PRE + at, block)] = nn(rows, wk[...]).astype(bf16)
        v_out[pl.ds(PRE + at, block)] = nn(rows, wv[...]).astype(bf16)

    for i in range(4):
        keys = PRE + (i + 1) * block
        shape = (block, keys)
        bias[:, 0:keys] = mask_bias(
            seg_col[i * block : (i + 1) * block],
            seg_row[:, 0:keys],
            i * block + lax.broadcasted_iota(jnp.int32, shape, 0),
            lax.broadcasted_iota(jnp.int32, shape, 1),
            prefix_len,
        )

        @pl.loop(0, lanes // PAIR)
        def _(j):
            cols = pl.ds(pl.multiple_of(j * PAIR, PAIR), PAIR)
            mixed[:, cols] = pair_forward(
                q_out[i * block : (i + 1) * block, cols],
                k_out[0:keys, cols],
                v_out[0:keys, cols],
                bias[:, 0:keys],
            )

        part[i] = nn(mixed[...], wo[...]).astype(bf16)


def self_forward(prefix_len, x_full, wq, wk, wv, wo, pre, seg_col, seg_row):
    n, seq_local, width = x_full.shape
    seq, lanes = n * seq_local, wq.shape[1]
    out = jax.ShapeDtypeStruct
    return pl.pallas_call(
        functools.partial(self_forward_kernel, prefix_len),
        out_shape=(
            out((seq, lanes), bf16),
            out((PRE + seq, lanes), bf16),
            out((PRE + seq, lanes), bf16),
            out((n, seq_local, width), bf16),
        ),
        in_specs=[pl.BlockSpec(memory_space=VMEM)] * 8,
        out_specs=[pl.BlockSpec(memory_space=VMEM)] * 4,
        scratch_shapes=[
            VMEM((seq_local, lanes), bf16),
            VMEM((seq_local, PRE + seq), f32),
        ],
        compiler_params=pltpu.CompilerParams(vmem_limit_bytes=48 << 20),
        name="self_forward",
    )(x_full.reshape(seq, width), wq, wk, wv, wo, pre, seg_col, seg_row)


def cross_forward_kernel(
    prefix_len, v1, memory, wq, wk, wv, wo, pre, seg_col, seg_row, gain, shift,
    q_out, k_out, v_out, v2, n1_low, bias, mixed,
):
    step = pl.program_id(0)
    block, lanes = q_out.shape[1:]
    keys = k_out.shape[1]

    @pl.when(step == 0)
    def _():
        n, _ = norm_parts(v1[...])
        normed = n * gain[0:1] + shift[0:1]
        v2[...] = normed
        n1_low[...] = normed.astype(bf16)
        bias[...] = mask_bias(
            seg_col[...],
            seg_row[...],
            None,
            lax.broadcasted_iota(jnp.int32, (block, keys), 1),
            prefix_len,
        )

    q_out[0] = (SCALE * nn(n1_low[...], wq[0])).astype(bf16)
    for target, at in ((k_out, 0), (v_out, PRE_PACK)):
        target[0, 0:PRE_PACK] = pre[0, at : at + PRE_PACK]
        target[0, PRE_PACK:PRE] = jnp.zeros((PRE - PRE_PACK, lanes), bf16)

    @pl.loop(0, (keys - PRE) // block)
    def _(i):
        at = pl.multiple_of(i * block, block)
        rows = memory[pl.ds(at, block)]
        k_out[0, pl.ds(PRE + at, block)] = nn(rows, wk[0]).astype(bf16)
        v_out[0, pl.ds(PRE + at, block)] = nn(rows, wv[0]).astype(bf16)

    @pl.loop(0, lanes // PAIR)
    def _(j):
        cols = pl.ds(pl.multiple_of(j * PAIR, PAIR), PAIR)
        mixed[:, cols] = pair_forward(
            q_out[0, :, cols], k_out[0, :, cols], v_out[0, :, cols], bias[...]
        )

    v2[...] += nn(mixed[...], wo[0])


def whole_spec(shape):
    return pl.BlockSpec(shape, lambda i: (0,) * len(shape))


def shard_spec(shape, index=lambda i: i):
    return pl.BlockSpec((1,) + shape[1:], lambda i: (index(i), 0, 0))


def cross_forward(prefix_len, v1, memory, weights, pre, seg_col, seg_row, gain, shift):
    wq, wk, wv, wo = weights
    n, width, lanes = wq.shape
    block = v1.shape[0]
    seq = memory.shape[0]
    out = jax.ShapeDtypeStruct
    outs = (
        out((n, block, lanes), bf16),
        out((n, PRE + seq, lanes), bf16),
        out((n, PRE + seq, lanes), bf16),
    )
    return pl.pallas_call(
        functools.partial(cross_forward_kernel, prefix_len),
        grid=(n,),
        out_shape=outs + (out((block, width), f32),),
        in_specs=[whole_spec(v1.shape), whole_spec(memory.shape)]
        + [shard_spec(a.shape) for a in (wq, wk, wv, wo, pre)]
        + [whole_spec(a.shape) for a in (seg_col, seg_row, gain, shift)],
        out_specs=[shard_spec(a.shape) for a in outs] + [whole_spec((block, width))],
        scratch_shapes=[
            VMEM((block, width), bf16),
            VMEM((block, PRE + seq), f32),
            VMEM((block, lanes), bf16),
        ],
        compiler_params=pltpu.CompilerParams(vmem_limit_bytes=48 << 20),
        name="cross_forward",
    )(v1, memory, wq, wk, wv, wo, pre, seg_col, seg_row, gain, shift)


def feed_forward_kernel(
    v2, out_grad, w_in, w_out, down, down_bias, up, up_bias, gain, shift,
    output, dr2, up_grad, down_grad, vecs,
    n2_low, n2_hat, total, e_low, slope, grad,
):
    step = pl.program_id(0)
    half = pl.num_programs(0) // 2
    width = v2.shape[1]

    @pl.when(step == 0)
    def _():
        n, _ = norm_parts(v2[...])
        n2_hat[...] = n
        normed = n * gain[1:2] + shift[1:2]
        total[...] = normed
        n2_low[...] = normed.astype(bf16)

    @pl.when(step < half)
    def _():
        act, bend = gelu_parts(nn(n2_low[...], w_in[0]))
        slope[step] = bend
        total[...] += nn(act.astype(bf16), w_out[0])

    @pl.when(step == half - 1)
    def _():
        act, bend = gelu_parts(nn(n2_low[...], down[...]) + down_bias[...])
        act = act.astype(bf16)
        resid = total[...] + 4.0 * (nn(act, up[...]) + up_bias[...])
        n, spread = norm_parts(resid)
        output[...] = (n * gain[2:3] + shift[2:3]).astype(bf16)
        dz, gain_part, shift_part = norm_back(out_grad[...].astype(f32), gain[2:3], n, spread)
        e_low[...] = dz.astype(bf16)
        four = (4.0 * dz).astype(bf16)
        up_grad[...] = tn(act, four).astype(bf16)
        da = (nt(four, up[...]) * bend).astype(bf16)
        down_grad[...] = tn(da, n2_low[...]).astype(bf16)
        grad[...] = dz + nt(da, down[...])
        vecs[...] = jnp.zeros_like(vecs)
        vecs[2:3] = gain_part
        vecs[5:6] = shift_part
        vecs[6:7] = jnp.sum(four.astype(f32), axis=0, keepdims=True)
        vecs[7:8, 0 : down.shape[1]] = jnp.sum(da.astype(f32), axis=0, keepdims=True)

    @pl.when(step >= half)
    def _():
        du = (nt(e_low[...], w_out[0]) * slope[2 * half - 1 - step]).astype(bf16)
        grad[...] += nt(du, w_in[0])

    @pl.when(step == 2 * half - 1)
    def _():
        _, spread = norm_parts(v2[...])
        dv, gain_part, shift_part = norm_back(grad[...], gain[1:2], n2_hat[...], spread)
        dr2[...] = dv
        vecs[1:2] = gain_part
        vecs[4:5] = shift_part


def feed_forward(v2, out_grad, w_in, w_out, down, down_bias, up, up_bias, gain, shift):
    n, width, inner = w_in.shape
    block = v2.shape[0]
    adapt = down.shape[1]
    out = jax.ShapeDtypeStruct
    outs = (
        out((block, width), bf16),
        out((block, width), f32),
        out((adapt, width), bf16),
        out((adapt, width), bf16),
        out((8, width), f32),
    )
    turn = lambda i: jnp.minimum(i, 2 * n - 1 - i)
    return pl.pallas_call(
        feed_forward_kernel,
        grid=(2 * n,),
        out_shape=outs,
        in_specs=[whole_spec(v2.shape), whole_spec(out_grad.shape)]
        + [shard_spec(w_in.shape, turn), shard_spec(w_out.shape, turn)]
        + [whole_spec(a.shape) for a in (down, down_bias, up, up_bias, gain, shift)],
        out_specs=[whole_spec(a.shape) for a in outs],
        scratch_shapes=[
            VMEM((block, width), bf16),
            VMEM((block, width), f32),
            VMEM((block, width), f32),
            VMEM((block, width), bf16),
            VMEM((n, block, inner), f32),
            VMEM((block, width), f32),
        ],
        compiler_params=pltpu.CompilerParams(vmem_limit_bytes=56 << 20),
        name="feed_forward",
    )(v2, out_grad, w_in, w_out, down, down_bias, up, up_bias, gain, shift)


def cross_backward_kernel(
    prefix_len, dr2, v1, q, k, v, wq, wk, wv, wo, seg_row, seg_col, gain,
    dr1, dr1_low, dm_out, pre_grad, vecs,
    dr2_low, bias, da, dq, dk, dv, total, dm,
):
    step = pl.program_id(0)
    steps = pl.num_programs(0)
    block, lanes = q.shape[1:]
    keys = k.shape[1]

    @pl.when(step == 0)
    def _():
        dr2_low[...] = dr2[...].astype(bf16)
        total[...] = jnp.zeros_like(total)
        dm[...] = jnp.zeros_like(dm)
        bias[...] = mask_bias(
            seg_row[...],
            seg_col[...],
            None,
            lax.broadcasted_iota(jnp.int32, (keys, block), 0),
            prefix_len,
        )

    da[...] = nt(dr2_low[...], wo[0]).astype(bf16)

    @pl.loop(0, lanes // PAIR)
    def _(j):
        cols = pl.ds(pl.multiple_of(j * PAIR, PAIR), PAIR)
        dq_pair, dk_pair, dv_pair = pair_backward(
            q[0, :, cols], k[0, :, cols], v[0, :, cols], da[:, cols], bias[...]
        )
        dq[:, cols] = dq_pair
        pre_grad[0, 0:PRE_PACK, cols] = dk_pair[0:PRE_PACK]
        pre_grad[0, PRE_PACK : 2 * PRE_PACK, cols] = dv_pair[0:PRE_PACK]
        dk[:, cols] = dk_pair[PRE:].astype(bf16)
        dv[:, cols] = dv_pair[PRE:].astype(bf16)

    total[...] += nt(dq[...], wq[0])

    @pl.loop(0, (keys - PRE) // block)
    def _(i):
        rows = pl.ds(pl.multiple_of(i * block, block), block)
        dm[rows] += nt(dk[rows], wk[0]) + nt(dv[rows], wv[0])

    @pl.when(step == steps - 1)
    def _():
        n, spread = norm_parts(v1[...])
        grad, gain_part, shift_part = norm_back(
            dr2[...] + SCALE * total[...], gain[0:1], n, spread
        )
        dr1[...] = grad
        dr1_low[...] = grad.astype(bf16)
        vecs[...] = jnp.zeros_like(vecs)
        vecs[0:1] = gain_part
        vecs[3:4] = shift_part

        @pl.loop(0, (keys - PRE) // block)
        def _(i):
            rows = pl.ds(pl.multiple_of(i * block, block), block)
            dm_out[rows] = dm[rows].astype(bf16)


def cross_backward(prefix_len, dr2, v1, q, k, v, weights, seg_row, seg_col, gain):
    wq, wk, wv, wo = weights
    n, block, lanes = q.shape
    keys = k.shape[1]
    width = dr2.shape[1]
    out = jax.ShapeDtypeStruct
    outs = (
        out((block, width), f32),
        out((block, width), bf16),
        out((keys - PRE, width), bf16),
        out((n, 2 * PRE_PACK, lanes), f32),
        out((8, width), f32),
    )
    out_specs = [whole_spec(a.shape) for a in outs]
    out_specs[3] = shard_spec(outs[3].shape)
    return pl.pallas_call(
        functools.partial(cross_backward_kernel, prefix_len),
        grid=(n,),
        out_shape=outs,
        in_specs=[whole_spec(dr2.shape), whole_spec(v1.shape)]
        + [shard_spec(a.shape) for a in (q, k, v, wq, wk, wv, wo)]
        + [whole_spec(a.shape) for a in (seg_row, seg_col, gain)],
        out_specs=out_specs,
        scratch_shapes=[
            VMEM((block, width), bf16),
            VMEM((keys, block), f32),
            VMEM((block, lanes), bf16),
            VMEM((block, lanes), bf16),
            VMEM((keys - PRE, lanes), bf16),
            VMEM((keys - PRE, lanes), bf16),
            VMEM((block, width), f32),
            VMEM((keys - PRE, width), f32),
        ],
        compiler_params=pltpu.CompilerParams(vmem_limit_bytes=56 << 20),
        name="cross_backward",
    )(dr2, v1, q, k, v, wq, wk, wv, wo, seg_row, seg_col, gain)


def self_backward_kernel(
    prefix_len, dr1, q, k, v, wq, wk, wv, wo, seg_row, seg_col,
    part, pre_grad, bias, da, dq, dk, dv,
):
    seq, lanes = q.shape
    block = seq // 4
    dk[...] = jnp.zeros_like(dk)
    dv[...] = jnp.zeros_like(dv)

    for i in reversed(range(4)):
        rows = slice(i * block, (i + 1) * block)
        keys = PRE + (i + 1) * block
        shape = (keys, block)
        bias[0:keys] = mask_bias(
            seg_row[:, rows],
            seg_col[0:keys],
            i * block + lax.broadcasted_iota(jnp.int32, shape, 1),
            lax.broadcasted_iota(jnp.int32, shape, 0),
            prefix_len,
        )
        da[...] = nt(dr1[i], wo[...]).astype(bf16)

        @pl.loop(0, lanes // PAIR)
        def _(j):
            cols = pl.ds(pl.multiple_of(j * PAIR, PAIR), PAIR)
            dq_pair, dk_pair, dv_pair = pair_backward(
                q[rows, cols], k[0:keys, cols], v[0:keys, cols], da[:, cols], bias[0:keys]
            )
            dq[:, cols] = dq_pair
            dk[0:keys, cols] += dk_pair
            dv[0:keys, cols] += dv_pair

        done = slice(PRE + i * block, PRE + (i + 1) * block)
        part[i] = (
            SCALE * nt(dq[...], wq[...])
            + nt(dk[done].astype(bf16), wk[...])
            + nt(dv[done].astype(bf16), wv[...])
        ).astype(bf16)

    pre_grad[0:PRE_PACK] = dk[0:PRE_PACK]
    pre_grad[PRE_PACK : 2 * PRE_PACK] = dv[0:PRE_PACK]


def self_backward(prefix_len, dr1_full, q, k, v, wq, wk, wv, wo, seg_row, seg_col):
    n, block, width = dr1_full.shape
    seq, lanes = q.shape
    out = jax.ShapeDtypeStruct
    return pl.pallas_call(
        functools.partial(self_backward_kernel, prefix_len),
        out_shape=(out((n, block, width), bf16), out((2 * PRE_PACK, lanes), f32)),
        in_specs=[pl.BlockSpec(memory_space=VMEM)] * 10,
        out_specs=[pl.BlockSpec(memory_space=VMEM)] * 2,
        scratch_shapes=[
            VMEM((PRE + seq, block), f32),
            VMEM((block, lanes), bf16),
            VMEM((block, lanes), bf16),
            VMEM((PRE + seq, lanes), f32),
            VMEM((PRE + seq, lanes), f32),
        ],
        compiler_params=pltpu.CompilerParams(vmem_limit_bytes=48 << 20),
        name="self_backward",
    )(dr1_full, q, k, v, wq, wk, wv, wo, seg_row, seg_col)


class Links:
    def __init__(self, send, recv):
        self.send, self.recv = send, recv
        self.row = lax.axis_index("rows")
        self.t = lax.axis_index("tp")
        self.flows = 0
        place = lax.rem(self.row, GROUP)
        self.base = self.row - place
        self.a = place // 2
        self.b = lax.rem(place, 2)
        self.place = place

    def flow(self):
        self.flows += 1
        return self.flows - 1

    def tp_peer(self, mask):
        return (self.row, self.t ^ mask)

    def line_peer(self, d):
        return (self.base + lax.rem(self.a + d, LINE) * 2 + self.b, self.t)

    def side_peer(self):
        return (self.base + self.a * 2 + (1 - self.b), self.t)

    def copy(self, src, dst, flow, peer):
        return pltpu.make_async_remote_copy(
            src_ref=src,
            dst_ref=dst,
            send_sem=self.send.at[flow],
            recv_sem=self.recv.at[flow],
            device_id=peer,
            device_id_type=MESH,
        )

    def start(self, src, dst, flow, peer):
        made = self.copy(src, dst, flow, peer)
        made.start()
        return made

    def arrived(self, dst, flow, peer):
        self.copy(dst, dst, flow, peer).wait_recv()


def greet(peers):
    barrier = pltpu.get_barrier_semaphore()
    for peer in peers:
        pl.semaphore_signal(barrier, inc=1, device_id=peer, device_id_type=MESH)
    pl.semaphore_wait(barrier, len(peers))


CHUNKS = 4


def gather_rows_start(links, own, full):
    rows = own.shape[0] // CHUNKS
    t = links.t
    flow = links.flow()
    sends = [links.start(own, full.at[t], flow, links.tp_peer(1))]
    chunk_flows = []
    for c in range(CHUNKS):
        at = pl.ds(c * rows, rows)
        f = links.flow()
        chunk_flows.append(f)
        sends.append(links.start(own.at[at], full.at[t, at], f, links.tp_peer(2)))
    return flow, chunk_flows, sends


def gather_rows_pass(links, full, state):
    flow, chunk_flows, sends = state
    rows = full.shape[1] // CHUNKS
    far, beside, last = links.t ^ 2, links.t ^ 1, links.t ^ 3
    passed = []
    for c in range(CHUNKS):
        at = pl.ds(c * rows, rows)
        links.arrived(full.at[far, at], chunk_flows[c], links.tp_peer(2))
        f = links.flow()
        passed.append(f)
        sends.append(links.start(full.at[far, at], full.at[far, at], f, links.tp_peer(1)))
    links.arrived(full.at[beside], flow, links.tp_peer(1))
    for c in range(CHUNKS):
        at = pl.ds(c * rows, rows)
        links.arrived(full.at[last, at], passed[c], links.tp_peer(1))
    return sends


def gather_kernel(count, *refs):
    own, full = refs[:count], refs[count : 2 * count]
    send, recv, local = refs[2 * count :]
    links = Links(send, recv)
    greet([links.tp_peer(1), links.tp_peer(2)])
    kept = [pltpu.make_async_copy(own[i], full[i].at[links.t], local.at[i]) for i in range(count)]
    for one in kept:
        one.start()
    states = [gather_rows_start(links, own[i], full[i]) for i in range(count)]
    for i in range(count):
        for one in gather_rows_pass(links, full[i], states[i]):
            one.wait_send()
    for one in kept:
        one.wait()


def gather_rows(collective_id, *own):
    n = 4
    flows = (1 + 2 * CHUNKS) * len(own)
    return pl.pallas_call(
        functools.partial(gather_kernel, len(own)),
        out_shape=tuple(jax.ShapeDtypeStruct((n,) + a.shape, a.dtype) for a in own),
        in_specs=[pl.BlockSpec(memory_space=ANY)] * len(own),
        out_specs=[pl.BlockSpec(memory_space=ANY)] * len(own),
        scratch_shapes=[
            pltpu.SemaphoreType.DMA((flows,)),
            pltpu.SemaphoreType.DMA((flows,)),
            pltpu.SemaphoreType.DMA((len(own),)),
        ],
        compiler_params=pltpu.CompilerParams(
            collective_id=collective_id, has_side_effects=True
        ),
        name="gather_rows",
    )(*own)


def gather_all_kernel(count, *refs):
    x, memory, pre = refs[0:3]
    own = refs[3 : 3 + count]
    x_full, m_full, pre_full = refs[3 + count : 6 + count]
    full = refs[6 + count : 6 + 2 * count]
    send, recv, local = refs[6 + 2 * count :]
    links = Links(send, recv)
    t, far, last = links.t, links.t ^ 2, links.t ^ 3
    greet(
        [links.tp_peer(m) for m in (1, 2, 3)]
        + [links.line_peer(d) for d in range(1, LINE)]
        + [links.side_peer()]
    )
    kept = []
    for i, (src, dst) in enumerate(
        [(x, x_full), (memory, m_full), (pre, pre_full)] + list(zip(own, full))
    ):
        kept.append(pltpu.make_async_copy(src, dst.at[t], local.at[i]))
        kept[-1].start()
    sends = []
    state = gather_rows_start(links, x, x_full)
    pre_flows = []
    for m in (1, 2, 3):
        pre_flows.append(links.flow())
        sends.append(links.start(pre, pre_full.at[t], pre_flows[-1], links.tp_peer(m)))
    beside = []
    across = []
    for i in range(count):
        rows = own[i].shape[0] // GROUP
        at = pl.ds(pl.multiple_of(links.place * rows, rows), rows)
        across.append(links.flow())
        sends.append(links.start(own[i].at[at], full[i].at[t, at], across[-1], links.tp_peer(2)))
        beside.append(links.flow())
        sends.append(links.start(own[i], full[i].at[t], beside[-1], links.tp_peer(1)))
    state_m = gather_rows_start(links, memory, m_full)
    line_flows, side_flows = [], []
    for i in range(count):
        rows = own[i].shape[0] // GROUP
        mine = full[i].at[far, pl.ds(pl.multiple_of(links.place * rows, rows), rows)]
        links.arrived(mine, across[i], links.tp_peer(2))
        flows = []
        for d in range(1, LINE):
            flows.append(links.flow())
            sends.append(links.start(mine, mine, flows[-1], links.line_peer(d)))
        line_flows.append(flows)
        side_flows.append([links.flow()])
        sends.append(links.start(mine, mine, side_flows[i][0], links.side_peer()))
    sends += gather_rows_pass(links, x_full, state)
    for i in range(count):
        rows = own[i].shape[0] // GROUP
        for d in range(1, LINE):
            piece = lax.rem(links.a - d + LINE, LINE) * 2 + links.b
            here = full[i].at[far, pl.ds(pl.multiple_of(piece * rows, rows), rows)]
            links.arrived(here, line_flows[i][d - 1], links.line_peer(d))
            side_flows[i].append(links.flow())
            sends.append(links.start(here, here, side_flows[i][d], links.side_peer()))
    sends += gather_rows_pass(links, m_full, state_m)
    passed = []
    for i in range(count):
        rows = own[i].shape[0] // GROUP
        for d in range(LINE):
            piece = lax.rem(links.a - d + LINE, LINE) * 2 + (1 - links.b)
            here = full[i].at[far, pl.ds(pl.multiple_of(piece * rows, rows), rows)]
            links.arrived(here, side_flows[i][d], links.side_peer())
        passed.append(links.flow())
        sends.append(links.start(full[i].at[far], full[i].at[far], passed[i], links.tp_peer(1)))
    for m in (1, 2, 3):
        links.arrived(pre_full.at[t ^ m], pre_flows[m - 1], links.tp_peer(m))
    for i in range(count):
        links.arrived(full[i].at[t ^ 1], beside[i], links.tp_peer(1))
        links.arrived(full[i].at[last], passed[i], links.tp_peer(1))
    for one in sends:
        one.wait_send()
    for one in kept:
        one.wait()


def gather_all(collective_id, x, memory, pre, weights):
    n = 4
    count = len(weights)
    given = (x, memory, pre) + tuple(weights)
    flows = 2 * (1 + 2 * CHUNKS) + 3 + count * (3 + 2 * LINE - 1)
    return pl.pallas_call(
        functools.partial(gather_all_kernel, count),
        out_shape=tuple(jax.ShapeDtypeStruct((n,) + a.shape, a.dtype) for a in given),
        in_specs=[pl.BlockSpec(memory_space=ANY)] * len(given),
        out_specs=[pl.BlockSpec(memory_space=ANY)] * len(given),
        scratch_shapes=[
            pltpu.SemaphoreType.DMA((flows,)),
            pltpu.SemaphoreType.DMA((flows,)),
            pltpu.SemaphoreType.DMA((len(given),)),
        ],
        compiler_params=pltpu.CompilerParams(
            collective_id=collective_id, has_side_effects=True
        ),
        name="gather_all",
    )(*given)


def scatter_kernel(count, bases, *refs):
    parts = refs[:count]
    base = refs[count : count + bases]
    outs = refs[count + bases : 2 * count + bases]
    near, near_far, mid, far = refs[2 * count + bases : 2 * count + bases + 4]
    send, recv = refs[2 * count + bases + 4 :]
    links = Links(send, recv)
    t = links.t
    greet([links.tp_peer(1), links.tp_peer(2)])
    rows = parts[0].shape[1] // CHUNKS
    sends, first, second, across = [], [], [], []
    for i in range(count):
        first.append(links.flow())
        sends.append(
            links.start(parts[i].at[t ^ 3], near_far.at[i], first[i], links.tp_peer(1))
        )
        second.append(links.flow())
        sends.append(links.start(parts[i].at[t ^ 1], near.at[i], second[i], links.tp_peer(1)))
    for i in range(count):
        links.arrived(near_far.at[i], first[i], links.tp_peer(1))
        across.append([])
        for c in range(CHUNKS):
            at = pl.ds(c * rows, rows)
            mid[i, at] = (
                parts[i][t ^ 2, at].astype(f32) + near_far[i, at].astype(f32)
            ).astype(bf16)
            across[i].append(links.flow())
            sends.append(
                links.start(mid.at[i, at], far.at[i, at], across[i][c], links.tp_peer(2))
            )
    for i in range(count):
        links.arrived(near.at[i], second[i], links.tp_peer(1))
        for c in range(CHUNKS):
            at = pl.ds(c * rows, rows)
            links.arrived(far.at[i, at], across[i][c], links.tp_peer(2))
            value = (
                parts[i][t, at].astype(f32)
                + near[i, at].astype(f32)
                + far[i, at].astype(f32)
            )
            if i < bases:
                value = value + base[i][at].astype(f32)
            outs[i][at] = value.astype(outs[i].dtype)
    for one in sends:
        one.wait_send()


def scatter_sum(collective_id, parts, base, kinds):
    count = len(parts)
    _, block, width = parts[0].shape
    flows = count * (2 + CHUNKS)
    slots = VMEM((count, block, width), bf16)
    return pl.pallas_call(
        functools.partial(scatter_kernel, count, len(base)),
        out_shape=tuple(jax.ShapeDtypeStruct((block, width), kind) for kind in kinds),
        in_specs=[pl.BlockSpec(memory_space=VMEM)] * (count + len(base)),
        out_specs=[pl.BlockSpec(memory_space=VMEM)] * count,
        scratch_shapes=[
            slots,
            slots,
            slots,
            slots,
            pltpu.SemaphoreType.DMA((flows,)),
            pltpu.SemaphoreType.DMA((flows,)),
        ],
        compiler_params=pltpu.CompilerParams(
            collective_id=collective_id, has_side_effects=True, vmem_limit_bytes=40 << 20
        ),
        name="scatter_sum",
    )(*parts, *base)


def adapter_sum_kernel(levels, g, out, s1, h, xb, h2, zb, p3, yb, hb, send, recv):
    links = Links(send, recv)
    t, a, b = links.t, links.a, links.b
    c = lax.rem(t, 2)
    far_groups = []
    for level in range(levels):
        bit = GROUP << level
        far_groups.append((links.row ^ bit, t))
    greet(
        [links.tp_peer(1), links.tp_peer(2)]
        + [links.line_peer(d) for d in range(1, LINE)]
        + [links.side_peer()]
        + far_groups
    )
    sends = []

    def send_to(src, dst, peer):
        flow = links.flow()
        sends.append(links.start(src, dst, flow, peer))
        return flow

    flow = send_to(g.at[1 - c], s1, links.tp_peer(1))
    links.arrived(s1, flow, links.tp_peer(1))
    h[...] = (g[c].astype(f32) + s1[...].astype(f32)).astype(bf16)
    flow = send_to(h.at[1 - b], xb, links.side_peer())
    links.arrived(xb, flow, links.side_peer())
    h2[...] = (h[b].astype(f32) + xb[...].astype(f32)).astype(bf16)
    line = []
    for d in range(1, LINE):
        line.append(send_to(h2.at[lax.rem(a + d, LINE)], zb.at[d - 1], links.line_peer(d)))
    for d in range(1, LINE):
        links.arrived(zb.at[d - 1], line[d - 1], links.line_peer(d))
    total = h2[a].astype(f32)
    for d in range(1, LINE):
        total = total + zb[d - 1].astype(f32)
    p3[...] = total.astype(bf16)
    flow = send_to(p3, yb, links.tp_peer(2))
    links.arrived(yb, flow, links.tp_peer(2))
    value = p3[...].astype(f32) + yb[...].astype(f32)
    for level in range(levels):
        hb[2 * level] = value.astype(bf16)
        flow = send_to(hb.at[2 * level], hb.at[2 * level + 1], far_groups[level])
        links.arrived(hb.at[2 * level + 1], flow, far_groups[level])
        value = hb[2 * level].astype(f32) + hb[2 * level + 1].astype(f32)
    out[c, b, a] = value.astype(bf16)
    mine = out.at[c, b, a]
    line = []
    for d in range(1, LINE):
        line.append(send_to(mine, mine, links.line_peer(d)))
    side = [send_to(mine, mine, links.side_peer())]
    for d in range(1, LINE):
        here = out.at[c, b, lax.rem(a - d + LINE, LINE)]
        links.arrived(here, line[d - 1], links.line_peer(d))
        side.append(send_to(here, here, links.side_peer()))
    for d in range(LINE):
        links.arrived(out.at[c, 1 - b, lax.rem(a - d + LINE, LINE)], side[d], links.side_peer())
    flow = send_to(out.at[c], out.at[c], links.tp_peer(1))
    links.arrived(out.at[1 - c], flow, links.tp_peer(1))
    for one in sends:
        one.wait_send()


def doublings(count):
    levels = 0
    while (1 << levels) < count:
        levels += 1
    return levels


def adapter_sum(collective_id, row_count, grads):
    levels = doublings(row_count // GROUP)
    height, width = grads.shape
    piece = height // (2 * GROUP)
    half = (2, LINE, piece, width)
    flows = 1 + 1 + 3 + 1 + levels + 3 + 4 + 1
    return pl.pallas_call(
        functools.partial(adapter_sum_kernel, levels),
        out_shape=jax.ShapeDtypeStruct((2,) + half, bf16),
        in_specs=[pl.BlockSpec(memory_space=VMEM)],
        out_specs=pl.BlockSpec(memory_space=VMEM),
        scratch_shapes=[
            VMEM(half, bf16),
            VMEM(half, bf16),
            VMEM(half[1:], bf16),
            VMEM(half[1:], bf16),
            VMEM((LINE - 1, piece, width), bf16),
            VMEM((piece, width), bf16),
            VMEM((piece, width), bf16),
            VMEM((max(1, 2 * levels), piece, width), bf16),
            pltpu.SemaphoreType.DMA((flows,)),
            pltpu.SemaphoreType.DMA((flows,)),
        ],
        compiler_params=pltpu.CompilerParams(
            collective_id=collective_id, has_side_effects=True, vmem_limit_bytes=40 << 20
        ),
        name="adapter_sum",
    )(grads.reshape((2,) + half)).reshape(height, width)


def small_sum_kernel(levels, cross, own, vecs, out, cross_in, vecs_in, outgo, income, send, recv):
    links = Links(send, recv)
    t = links.t
    row_peers = [(links.row ^ (1 << level), t) for level in range(levels)]
    greet([links.tp_peer(m) for m in (1, 2, 3)] + row_peers)
    sends = []
    flows = []
    for m in (1, 2, 3):
        peer = links.tp_peer(m)
        for src, dst in ((cross.at[t ^ m], cross_in.at[t]), (vecs, vecs_in.at[t])):
            flow = links.flow()
            flows.append(flow)
            sends.append(links.start(src, dst, flow, peer))
    cross_in[t] = cross[t]
    vecs_in[t] = vecs[...]
    for m in (1, 2, 3):
        links.arrived(cross_in.at[t ^ m], flows[2 * (m - 1)], links.tp_peer(m))
        links.arrived(vecs_in.at[t ^ m], flows[2 * (m - 1) + 1], links.tp_peer(m))
    kept = cross.shape[1]
    height = vecs.shape[0]
    lanes = cross.shape[2]
    value_cross = cross_in[0] + cross_in[1] + cross_in[2] + cross_in[3]
    value_vecs = vecs_in[0] + vecs_in[1] + vecs_in[2] + vecs_in[3]
    pieces = [value_cross, own[...]] + [
        value_vecs[:, i * lanes : (i + 1) * lanes] for i in range(vecs.shape[1] // lanes)
    ]
    value = jnp.concatenate(pieces, axis=0)
    for level in range(levels):
        outgo[level] = value
        flow = links.flow()
        sends.append(
            links.start(outgo.at[level], income.at[level], flow, row_peers[level])
        )
        links.arrived(income.at[level], flow, row_peers[level])
        value = outgo[level] + income[level]
    out[...] = value
    for one in sends:
        one.wait_send()


def small_sum(collective_id, row_count, cross, own, vecs):
    levels = doublings(row_count)
    n, kept, lanes = cross.shape
    height = 2 * kept + vecs.shape[0] * vecs.shape[1] // lanes
    flows = 6 + levels
    total = pl.pallas_call(
        functools.partial(small_sum_kernel, levels),
        out_shape=jax.ShapeDtypeStruct((height, lanes), f32),
        in_specs=[pl.BlockSpec(memory_space=VMEM)] * 3,
        out_specs=pl.BlockSpec(memory_space=VMEM),
        scratch_shapes=[
            VMEM((n, kept, lanes), f32),
            VMEM((n,) + vecs.shape, f32),
            VMEM((levels, height, lanes), f32),
            VMEM((levels, height, lanes), f32),
            pltpu.SemaphoreType.DMA((flows,)),
            pltpu.SemaphoreType.DMA((flows,)),
        ],
        compiler_params=pltpu.CompilerParams(
            collective_id=collective_id, has_side_effects=True
        ),
        name="small_sum",
    )(cross, own, vecs)
    parts = total[2 * kept :].reshape(-1, vecs.shape[0], lanes)
    return (
        total[:kept],
        total[kept : 2 * kept],
        jnp.moveaxis(parts, 0, 1).reshape(vecs.shape),
    )


def per_device(
    row_count,
    tokens, memory, out_grad, dec_segments, src_segments,
    self_query, self_key, self_value, self_out,
    cross_query, cross_key, cross_value, cross_out,
    ffn_in, ffn_out, adapt_down, adapt_down_bias, adapt_up, adapt_up_bias,
    self_prefix, cross_prefix, norm_gain, norm_shift,
):
    seq_local, _, width = tokens.shape
    prefix_len = self_prefix.shape[1]
    lanes = self_query.shape[1]
    adapt = adapt_down.shape[1]
    t = lax.axis_index("tp")
    x, mem, grad_in = (a.reshape(seq_local, width) for a in (tokens, memory, out_grad))

    def pack_prefix(prefix):
        return jnp.pad(prefix, ((0, 0), (0, PRE_PACK - prefix_len), (0, 0))).reshape(
            2 * PRE_PACK, lanes
        )

    def unpack_prefix(packed):
        return packed.reshape(2, PRE_PACK, lanes)[:, :prefix_len]

    seq = dec_segments.shape[1]
    never = jnp.full((1, PRE), -1, jnp.int32)
    dec_row = jnp.concatenate([never, dec_segments], axis=1)
    src_row = jnp.concatenate([never, src_segments], axis=1)
    dec_q = dec_segments
    own_q = lax.dynamic_slice(dec_segments, (0, t * seq_local), (1, seq_local))

    gathered = gather_all(
        0,
        x,
        mem,
        pack_prefix(cross_prefix),
        (cross_query, cross_key, cross_value, cross_out, ffn_in, ffn_out),
    )
    x_full, m_full, pre_full = gathered[:3]
    cross_weights = gathered[3:7]
    w_in, w_out = gathered[7:]
    m_full = m_full.reshape(seq, width)

    q1, k1, v1_heads, part = self_forward(
        prefix_len, x_full, self_query, self_key, self_value, self_out,
        pack_prefix(self_prefix), dec_q.reshape(seq, 1), dec_row,
    )
    (resid_one,) = scatter_sum(1, (part,), (x,), (f32,))
    q2, k2, v2_heads, resid_two = cross_forward(
        prefix_len, resid_one, m_full, cross_weights, pre_full,
        own_q.reshape(seq_local, 1), src_row, norm_gain, norm_shift,
    )
    output, dr2, up_part, down_part, vecs_ff = feed_forward(
        resid_two, grad_in, w_in, w_out,
        adapt_down, adapt_down_bias.reshape(1, adapt), adapt_up, adapt_up_bias.reshape(1, width),
        norm_gain, norm_shift,
    )
    adapter = adapter_sum(2, row_count, jnp.concatenate([up_part, down_part], axis=0))
    dr1, dr1_low, dm, cross_pre_part, vecs_cross = cross_backward(
        prefix_len, dr2, resid_one, q2, k2, v2_heads, cross_weights,
        own_q, src_row.reshape(PRE + seq, 1), norm_gain,
    )
    (dr1_full,) = gather_rows(3, dr1_low)
    part, self_pre_part = self_backward(
        prefix_len, dr1_full, q1, k1, v1_heads,
        self_query, self_key, self_value, self_out, dec_q, dec_row.reshape(PRE + seq, 1),
    )
    tokens_grad, memory_grad = scatter_sum(
        4, (part, dm.reshape(part.shape)), (dr1,), (bf16, bf16)
    )
    cross_pre, self_pre, vecs = small_sum(
        5, row_count, cross_pre_part, self_pre_part, vecs_ff + vecs_cross
    )
    local = tokens.shape
    return (
        output.reshape(local),
        tokens_grad.reshape(local),
        memory_grad.reshape(local),
        unpack_prefix(self_pre),
        unpack_prefix(cross_pre),
        vecs[0:3],
        vecs[3:6],
        adapter[adapt:].T.astype(f32),
        vecs[7, :adapt],
        adapter[:adapt].astype(f32),
        vecs[6],
    )


def solution(mesh):
    placed = (
        (P("tp", "rows", None),) * 3
        + (P("rows", None),) * 2
        + (P(None, "tp"),) * 3
        + (P("tp", None),)
        + (P(None, "tp"),) * 3
        + (P("tp", None),)
        + (P(None, "tp"), P("tp", None))
        + (P(),) * 4
        + (P(None, None, "tp"),) * 2
        + (P(),) * 2
    )
    return jax.shard_map(
        functools.partial(per_device, mesh.shape["rows"]),
        mesh=mesh,
        in_specs=placed,
        out_specs=(P("tp", "rows", None),) * 3 + (P(None, None, "tp"),) * 2 + (P(),) * 6,
        check_vma=False,
    )
```

```python
import functools

import jax
import jax.numpy as jnp
from jax import lax
from jax.experimental import pallas as pl
from jax.experimental.pallas import tpu as pltpu
from jax.sharding import PartitionSpec as P

HEAD = 64
PAIR = 2 * HEAD
PRE = 128
PRE_PACK = 32
GROUP = 8
LINE = 4
MASKED = -1000000000.0
EPSILON = 1e-05
SCALE = HEAD**-0.5
f32 = jnp.float32
bf16 = jnp.bfloat16
MESH = pl.DeviceIdType.MESH
VMEM = pltpu.VMEM
ANY = pl.ANY


def nn(a, b):
    return lax.dot_general(a, b, (((1,), (0,)), ((), ())), preferred_element_type=f32)


def nt(a, b):
    return lax.dot_general(a, b, (((1,), (1,)), ((), ())), preferred_element_type=f32)


def tn(a, b):
    return lax.dot_general(a, b, (((0,), (0,)), ((), ())), preferred_element_type=f32)


def gelu_parts(v):
    phi = 0.5 + 0.5 * lax.erf(v * (0.5**0.5))
    slope = phi + v * (jnp.exp(-0.5 * v * v) * 0.3989422804014327)
    return v * phi, slope


def norm_parts(v):
    centered = v - jnp.mean(v, axis=-1, keepdims=True)
    spread = lax.rsqrt(jnp.mean(centered * centered, axis=-1, keepdims=True) + EPSILON)
    return centered * spread, spread


def norm_back(dy, gain, n, spread):
    dn = dy * gain
    dv = spread * (
        dn - jnp.mean(dn, axis=-1, keepdims=True) - n * jnp.mean(dn * n, axis=-1, keepdims=True)
    )
    return dv, jnp.sum(dy * n, axis=0, keepdims=True), jnp.sum(dy, axis=0, keepdims=True)


def lane_half(shape, h):
    return (lax.broadcasted_iota(jnp.int32, shape, 1) // HEAD) == h


def mask_bias(seg_q, seg_k, q_index, k_index, prefix_len):
    keep = seg_q == seg_k
    if q_index is not None:
        keep = keep & (k_index - PRE <= q_index)
    keep = keep | (k_index < prefix_len)
    return jnp.where(keep, 0.0, MASKED)


def pair_forward(q_pair, k_pair, v_pair, bias):
    outs = []
    for h in range(2):
        half = lane_half(q_pair.shape, h)
        scores = nt(jnp.where(half, q_pair, jnp.zeros_like(q_pair)), k_pair) + bias
        top = jnp.max(scores, axis=1, keepdims=True)
        e = jnp.exp(scores - top)
        total = jnp.sum(e, axis=1, keepdims=True)
        outs.append(nn(e.astype(bf16), v_pair) * (1.0 / total))
    return jnp.where(lane_half(outs[0].shape, 0), outs[0], outs[1]).astype(bf16)


def pair_backward(q_pair, k_pair, v_pair, da_pair, bias_t):
    k_turned = k_pair.T
    dk = dv = None
    dq = []
    for h in range(2):
        half = lane_half(q_pair.shape, h)
        q = jnp.where(half, q_pair, jnp.zeros_like(q_pair))
        da = jnp.where(half, da_pair, jnp.zeros_like(da_pair))
        scores = nt(k_pair, q) + bias_t
        top = jnp.max(scores, axis=0, keepdims=True)
        e = jnp.exp(scores - top)
        p = e * (1.0 / jnp.sum(e, axis=0, keepdims=True))
        weighted = p * nt(v_pair, da)
        ds = (weighted - p * jnp.sum(weighted, axis=0, keepdims=True)).astype(bf16)
        dv_h = nn(p.astype(bf16), da)
        dk_h = nn(ds, q)
        dk = dk_h if dk is None else dk + dk_h
        dv = dv_h if dv is None else dv + dv_h
        dq.append(nn(k_turned[h * HEAD : (h + 1) * HEAD], ds))
    return jnp.concatenate(dq, axis=0).T.astype(bf16), dk, dv


def cross_forward_kernel(
    prefix_len, v1, memory, wq, wk, wv, wo, pre, seg_col, seg_row, gain, shift, own,
    q_out, k_out, v_out, v2, full, n1_low, bias, mixed, stage, send, recv, local,
):
    step = pl.program_id(0)
    block, lanes = q_out.shape[1:]
    keys = k_out.shape[1]
    links = Links(send, recv)
    weights = WeightGather(links, 0, 2, [own], [full], [stage], local)

    @pl.when(step == 0)
    def _():
        greet(
            [links.tp_peer(1), links.tp_peer(2)]
            + [links.line_peer(d) for d in range(1, LINE)]
            + [links.side_peer()]
        )
        weights.start_over(0)
        weights.start_beside(0)

    @pl.when(step == 0)
    def _():
        n, _ = norm_parts(v1[...])
        normed = n * gain[0:1] + shift[0:1]
        v2[...] = normed
        n1_low[...] = normed.astype(bf16)
        bias[...] = mask_bias(
            seg_col[...],
            seg_row[...],
            None,
            lax.broadcasted_iota(jnp.int32, (block, keys), 1),
            prefix_len,
        )

    q_out[0] = (SCALE * nn(n1_low[...], wq[0])).astype(bf16)
    for target, at in ((k_out, 0), (v_out, PRE_PACK)):
        target[0, 0:PRE_PACK] = pre[0, at : at + PRE_PACK]
        target[0, PRE_PACK:PRE] = jnp.zeros((PRE - PRE_PACK, lanes), bf16)

    @pl.loop(0, (keys - PRE) // block)
    def _(i):
        at = pl.multiple_of(i * block, block)
        rows = memory[pl.ds(at, block)]
        k_out[0, pl.ds(PRE + at, block)] = nn(rows, wk[0]).astype(bf16)
        v_out[0, pl.ds(PRE + at, block)] = nn(rows, wv[0]).astype(bf16)

    @pl.loop(0, lanes // PAIR)
    def _(j):
        cols = pl.ds(pl.multiple_of(j * PAIR, PAIR), PAIR)
        mixed[:, cols] = pair_forward(
            q_out[0, :, cols], k_out[0, :, cols], v_out[0, :, cols], bias[...]
        )

    v2[...] += nn(mixed[...], wo[0])

    @pl.when(step == 0)
    def _():
        weights.keep_own(0)
        weights.came_over(0)

    @pl.when(step == 1)
    def _():
        weights.along(0, 0)

    @pl.when(step == 2)
    def _():
        weights.along(0, 1)

    @pl.when(step == pl.num_programs(0) - 1)
    def _():
        weights.along(0, 2)
        weights.complete(0)
        weights.finish(0)


def whole_spec(shape):
    return pl.BlockSpec(shape, lambda i: (0,) * len(shape))


def shard_spec(shape, index=lambda i: i):
    return pl.BlockSpec((1,) + shape[1:], lambda i: (index(i), 0, 0))


def cross_forward(prefix_len, v1, memory, weights, pre, seg_col, seg_row, gain, shift, own):
    wq, wk, wv, wo = weights
    n, width, lanes = wq.shape
    block = v1.shape[0]
    seq = memory.shape[0]
    out = jax.ShapeDtypeStruct
    outs = (
        out((n, block, lanes), bf16),
        out((n, PRE + seq, lanes), bf16),
        out((n, PRE + seq, lanes), bf16),
    )
    return pl.pallas_call(
        functools.partial(cross_forward_kernel, prefix_len),
        grid=(n,),
        out_shape=outs + (out((block, width), f32), out((n,) + own.shape, own.dtype)),
        in_specs=[whole_spec(v1.shape), whole_spec(memory.shape)]
        + [shard_spec(a.shape) for a in (wq, wk, wv, wo, pre)]
        + [whole_spec(a.shape) for a in (seg_col, seg_row, gain, shift)]
        + [pl.BlockSpec(memory_space=pltpu.HBM)],
        out_specs=[shard_spec(a.shape) for a in outs]
        + [whole_spec((block, width)), pl.BlockSpec(memory_space=pltpu.HBM)],
        scratch_shapes=[
            VMEM((block, width), bf16),
            VMEM((block, PRE + seq), f32),
            VMEM((block, lanes), bf16),
            VMEM(own.shape, own.dtype),
            pltpu.SemaphoreType.DMA((FLOWS,)),
            pltpu.SemaphoreType.DMA((FLOWS,)),
            pltpu.SemaphoreType.DMA((2,)),
        ],
        compiler_params=pltpu.CompilerParams(
            collective_id=1, has_side_effects=True, vmem_limit_bytes=48 << 20
        ),
        name="cross_forward",
    )(v1, memory, wq, wk, wv, wo, pre, seg_col, seg_row, gain, shift, own)


def feed_forward_kernel(
    v2, out_grad, w_in, w_out, down, down_bias, up, up_bias, gain, shift,
    output, dr2, up_grad, down_grad, vecs,
    n2_low, n2_hat, total, e_low, slope, grad,
):
    step = pl.program_id(0)
    half = pl.num_programs(0) // 2
    width = v2.shape[1]

    @pl.when(step == 0)
    def _():
        n, _ = norm_parts(v2[...])
        n2_hat[...] = n
        normed = n * gain[1:2] + shift[1:2]
        total[...] = normed
        n2_low[...] = normed.astype(bf16)

    @pl.when(step < half)
    def _():
        act, bend = gelu_parts(nn(n2_low[...], w_in[0]))
        slope[step] = bend
        total[...] += nn(act.astype(bf16), w_out[0])

    @pl.when(step == half - 1)
    def _():
        act, bend = gelu_parts(nn(n2_low[...], down[...]) + down_bias[...])
        act = act.astype(bf16)
        resid = total[...] + 4.0 * (nn(act, up[...]) + up_bias[...])
        n, spread = norm_parts(resid)
        output[...] = (n * gain[2:3] + shift[2:3]).astype(bf16)
        dz, gain_part, shift_part = norm_back(out_grad[...].astype(f32), gain[2:3], n, spread)
        e_low[...] = dz.astype(bf16)
        four = (4.0 * dz).astype(bf16)
        up_grad[...] = tn(act, four).astype(bf16)
        da = (nt(four, up[...]) * bend).astype(bf16)
        down_grad[...] = tn(da, n2_low[...]).astype(bf16)
        grad[...] = dz + nt(da, down[...])
        vecs[...] = jnp.zeros_like(vecs)
        vecs[2:3] = gain_part
        vecs[5:6] = shift_part
        vecs[6:7] = jnp.sum(four.astype(f32), axis=0, keepdims=True)
        vecs[7:8, 0 : down.shape[1]] = jnp.sum(da.astype(f32), axis=0, keepdims=True)

    @pl.when(step >= half)
    def _():
        du = (nt(e_low[...], w_out[0]) * slope[2 * half - 1 - step]).astype(bf16)
        grad[...] += nt(du, w_in[0])

    @pl.when(step == 2 * half - 1)
    def _():
        _, spread = norm_parts(v2[...])
        dv, gain_part, shift_part = norm_back(grad[...], gain[1:2], n2_hat[...], spread)
        dr2[...] = dv
        vecs[1:2] = gain_part
        vecs[4:5] = shift_part


def feed_forward(v2, out_grad, w_in, w_out, down, down_bias, up, up_bias, gain, shift):
    n, width, inner = w_in.shape
    block = v2.shape[0]
    adapt = down.shape[1]
    out = jax.ShapeDtypeStruct
    outs = (
        out((block, width), bf16),
        out((block, width), f32),
        out((adapt, width), bf16),
        out((adapt, width), bf16),
        out((8, width), f32),
    )
    turn = lambda i: jnp.minimum(i, 2 * n - 1 - i)
    return pl.pallas_call(
        feed_forward_kernel,
        grid=(2 * n,),
        out_shape=outs,
        in_specs=[whole_spec(v2.shape), whole_spec(out_grad.shape)]
        + [shard_spec(w_in.shape, turn), shard_spec(w_out.shape, turn)]
        + [whole_spec(a.shape) for a in (down, down_bias, up, up_bias, gain, shift)],
        out_specs=[whole_spec(a.shape) for a in outs],
        scratch_shapes=[
            VMEM((block, width), bf16),
            VMEM((block, width), f32),
            VMEM((block, width), f32),
            VMEM((block, width), bf16),
            VMEM((n, block, inner), f32),
            VMEM((block, width), f32),
        ],
        compiler_params=pltpu.CompilerParams(vmem_limit_bytes=56 << 20),
        name="feed_forward",
    )(v2, out_grad, w_in, w_out, down, down_bias, up, up_bias, gain, shift)


def cross_backward_kernel(
    prefix_len, dr2, v1, q, k, v, wq, wk, wv, wo, seg_row, seg_col, gain,
    dr1, dr1_low, dm_out, pre_grad, vecs,
    dr2_low, bias, da, dq, dk, dv, total, dm,
):
    step = pl.program_id(0)
    steps = pl.num_programs(0)
    block, lanes = q.shape[1:]
    keys = k.shape[1]

    @pl.when(step == 0)
    def _():
        dr2_low[...] = dr2[...].astype(bf16)
        total[...] = jnp.zeros_like(total)
        dm[...] = jnp.zeros_like(dm)
        bias[...] = mask_bias(
            seg_row[...],
            seg_col[...],
            None,
            lax.broadcasted_iota(jnp.int32, (keys, block), 0),
            prefix_len,
        )

    da[...] = nt(dr2_low[...], wo[0]).astype(bf16)

    @pl.loop(0, lanes // PAIR)
    def _(j):
        cols = pl.ds(pl.multiple_of(j * PAIR, PAIR), PAIR)
        dq_pair, dk_pair, dv_pair = pair_backward(
            q[0, :, cols], k[0, :, cols], v[0, :, cols], da[:, cols], bias[...]
        )
        dq[:, cols] = dq_pair
        pre_grad[0, 0:PRE_PACK, cols] = dk_pair[0:PRE_PACK]
        pre_grad[0, PRE_PACK : 2 * PRE_PACK, cols] = dv_pair[0:PRE_PACK]
        dk[:, cols] = dk_pair[PRE:].astype(bf16)
        dv[:, cols] = dv_pair[PRE:].astype(bf16)

    total[...] += nt(dq[...], wq[0])

    @pl.loop(0, (keys - PRE) // block)
    def _(i):
        rows = pl.ds(pl.multiple_of(i * block, block), block)
        dm[rows] += nt(dk[rows], wk[0]) + nt(dv[rows], wv[0])

    @pl.when(step == steps - 1)
    def _():
        n, spread = norm_parts(v1[...])
        grad, gain_part, shift_part = norm_back(
            dr2[...] + SCALE * total[...], gain[0:1], n, spread
        )
        dr1[...] = grad
        dr1_low[...] = grad.astype(bf16)
        vecs[...] = jnp.zeros_like(vecs)
        vecs[0:1] = gain_part
        vecs[3:4] = shift_part

        @pl.loop(0, (keys - PRE) // block)
        def _(i):
            rows = pl.ds(pl.multiple_of(i * block, block), block)
            dm_out[rows] = dm[rows].astype(bf16)


def cross_backward(prefix_len, dr2, v1, q, k, v, weights, seg_row, seg_col, gain):
    wq, wk, wv, wo = weights
    n, block, lanes = q.shape
    keys = k.shape[1]
    width = dr2.shape[1]
    out = jax.ShapeDtypeStruct
    outs = (
        out((block, width), f32),
        out((block, width), bf16),
        out((keys - PRE, width), bf16),
        out((n, 2 * PRE_PACK, lanes), f32),
        out((8, width), f32),
    )
    out_specs = [whole_spec(a.shape) for a in outs]
    out_specs[3] = shard_spec(outs[3].shape)
    return pl.pallas_call(
        functools.partial(cross_backward_kernel, prefix_len),
        grid=(n,),
        out_shape=outs,
        in_specs=[whole_spec(dr2.shape), whole_spec(v1.shape)]
        + [shard_spec(a.shape) for a in (q, k, v, wq, wk, wv, wo)]
        + [whole_spec(a.shape) for a in (seg_row, seg_col, gain)],
        out_specs=out_specs,
        scratch_shapes=[
            VMEM((block, width), bf16),
            VMEM((keys, block), f32),
            VMEM((block, lanes), bf16),
            VMEM((block, lanes), bf16),
            VMEM((keys - PRE, lanes), bf16),
            VMEM((keys - PRE, lanes), bf16),
            VMEM((block, width), f32),
            VMEM((keys - PRE, width), f32),
        ],
        compiler_params=pltpu.CompilerParams(vmem_limit_bytes=56 << 20),
        name="cross_backward",
    )(dr2, v1, q, k, v, wq, wk, wv, wo, seg_row, seg_col, gain)


def self_backward_kernel(
    prefix_len, dr1, q, k, v, wq, wk, wv, wo, seg_row, seg_col,
    part, pre_grad, bias, da, dq, dk, dv,
):
    seq, lanes = q.shape
    block = seq // 4
    dk[...] = jnp.zeros_like(dk)
    dv[...] = jnp.zeros_like(dv)

    for i in reversed(range(4)):
        rows = slice(i * block, (i + 1) * block)
        keys = PRE + (i + 1) * block
        shape = (keys, block)
        bias[0:keys] = mask_bias(
            seg_row[:, rows],
            seg_col[0:keys],
            i * block + lax.broadcasted_iota(jnp.int32, shape, 1),
            lax.broadcasted_iota(jnp.int32, shape, 0),
            prefix_len,
        )
        da[...] = nt(dr1[i], wo[...]).astype(bf16)

        @pl.loop(0, lanes // PAIR)
        def _(j):
            cols = pl.ds(pl.multiple_of(j * PAIR, PAIR), PAIR)
            dq_pair, dk_pair, dv_pair = pair_backward(
                q[rows, cols], k[0:keys, cols], v[0:keys, cols], da[:, cols], bias[0:keys]
            )
            dq[:, cols] = dq_pair
            dk[0:keys, cols] += dk_pair
            dv[0:keys, cols] += dv_pair

        done = slice(PRE + i * block, PRE + (i + 1) * block)
        part[i] = (
            SCALE * nt(dq[...], wq[...])
            + nt(dk[done].astype(bf16), wk[...])
            + nt(dv[done].astype(bf16), wv[...])
        ).astype(bf16)

    pre_grad[0:PRE_PACK] = dk[0:PRE_PACK]
    pre_grad[PRE_PACK : 2 * PRE_PACK] = dv[0:PRE_PACK]


def self_backward(prefix_len, dr1_full, q, k, v, wq, wk, wv, wo, seg_row, seg_col):
    n, block, width = dr1_full.shape
    seq, lanes = q.shape
    out = jax.ShapeDtypeStruct
    return pl.pallas_call(
        functools.partial(self_backward_kernel, prefix_len),
        out_shape=(out((n, block, width), bf16), out((2 * PRE_PACK, lanes), f32)),
        in_specs=[pl.BlockSpec(memory_space=VMEM)] * 10,
        out_specs=[pl.BlockSpec(memory_space=VMEM)] * 2,
        scratch_shapes=[
            VMEM((PRE + seq, block), f32),
            VMEM((block, lanes), bf16),
            VMEM((block, lanes), bf16),
            VMEM((PRE + seq, lanes), f32),
            VMEM((PRE + seq, lanes), f32),
        ],
        compiler_params=pltpu.CompilerParams(vmem_limit_bytes=48 << 20),
        name="self_backward",
    )(dr1_full, q, k, v, wq, wk, wv, wo, seg_row, seg_col)


class Links:
    def __init__(self, send, recv):
        self.send, self.recv = send, recv
        self.row = lax.axis_index("rows")
        self.t = lax.axis_index("tp")
        self.flows = 0
        place = lax.rem(self.row, GROUP)
        self.base = self.row - place
        self.a = place // 2
        self.b = lax.rem(place, 2)
        self.place = place

    def flow(self):
        self.flows += 1
        return self.flows - 1

    def tp_peer(self, mask):
        return (self.row, self.t ^ mask)

    def line_peer(self, d):
        return (self.base + lax.rem(self.a + d, LINE) * 2 + self.b, self.t)

    def side_peer(self):
        return (self.base + self.a * 2 + (1 - self.b), self.t)

    def copy(self, src, dst, flow, peer):
        return pltpu.make_async_remote_copy(
            src_ref=src,
            dst_ref=dst,
            send_sem=self.send.at[flow],
            recv_sem=self.recv.at[flow],
            device_id=peer,
            device_id_type=MESH,
        )

    def start(self, src, dst, flow, peer):
        made = self.copy(src, dst, flow, peer)
        made.start()
        return made

    def arrived(self, dst, flow, peer):
        self.copy(dst, dst, flow, peer).wait_recv()


def greet(peers):
    barrier = pltpu.get_barrier_semaphore()
    for peer in peers:
        pl.semaphore_signal(barrier, inc=1, device_id=peer, device_id_type=MESH)
    pl.semaphore_wait(barrier, len(peers))


CHUNKS = 4


FLOWS = 14


class WeightGather:
    def __init__(self, links, base, across, own, full, stage, local):
        self.links, self.base, self.across = links, base, across
        self.own, self.full, self.stage, self.local = own, full, stage, local
        self.far, self.last = links.t ^ 2, links.t ^ 3
        a = links.a
        self.right = (links.base + jnp.minimum(a + 1, LINE - 1) * 2 + links.b, links.t)
        self.left = (links.base + jnp.maximum(a - 1, 0) * 2 + links.b, links.t)
        self.side = links.side_peer()
        self.sibling = links.tp_peer(1)
        self.over = links.tp_peer(2)

    def at(self, i, a, b):
        rows = self.own[i].shape[0] // GROUP
        return pl.ds(pl.multiple_of((a * 2 + b) * rows, rows), rows)

    def part(self, i, a, b):
        return self.full[i].at[self.far, self.at(i, a, b)]

    def flow(self, i, k):
        return self.base + i * FLOWS + k

    def over_copy(self, i, k):
        links = self.links
        b = links.b if k == 0 else 1 - links.b
        at = self.at(i, links.a, b)
        return links.copy(
            self.own[i].at[at], self.full[i].at[links.t, at], self.flow(i, k), self.over
        )

    def beside_copy(self, i):
        return self.links.copy(
            self.own[i], self.full[i].at[self.links.t], self.flow(i, 2), self.sibling
        )

    def pass_copy(self, i):
        whole = self.full[i].at[self.far]
        return self.links.copy(whole, whole, self.flow(i, 3), self.sibling)

    def moved(self, i, a, flow, peer):
        part = self.part(i, a, self.links.b)
        return self.links.copy(part, part, self.flow(i, flow), peer)

    def stage_in(self, i):
        return pltpu.make_async_copy(self.own[i], self.stage[i], self.local.at[2 * i])

    def stage_out(self, i):
        return pltpu.make_async_copy(
            self.stage[i], self.full[i].at[self.links.t], self.local.at[2 * i + 1]
        )

    def start_over(self, i):
        for k in range(self.across):
            self.over_copy(i, k).start()

    def start_beside(self, i):
        self.beside_copy(i).start()
        self.stage_in(i).start()

    def keep_own(self, i):
        self.stage_in(i).wait()
        self.stage_out(i).start()

    def came_over(self, i):
        links, a = self.links, self.links.a
        mine = self.part(i, a, links.b)
        links.arrived(mine, self.flow(i, 0), self.over)

        @pl.when(a < LINE - 1)
        def _():
            self.moved(i, a, 4, self.right).start()

        @pl.when(a > 0)
        def _():
            self.moved(i, a, 7, self.left).start()

        if self.across == 1:
            self.moved(i, a, 10, self.side).start()

    def along(self, i, k):
        links, a = self.links, self.links.a

        @pl.when(a - 1 - k >= 0)
        def _():
            links.arrived(self.part(i, a - 1 - k, links.b), self.flow(i, 4 + k), self.left)
            if k < LINE - 2:

                @pl.when(a < LINE - 1)
                def _():
                    self.moved(i, a - 1 - k, 5 + k, self.right).start()

            self.moved(i, a - 1 - k, 11 + k, self.side).start()

        @pl.when(a + 1 + k <= LINE - 1)
        def _():
            links.arrived(self.part(i, a + 1 + k, links.b), self.flow(i, 7 + k), self.right)
            if k < LINE - 2:

                @pl.when(a > 0)
                def _():
                    self.moved(i, a + 1 + k, 8 + k, self.left).start()

            self.moved(i, a + 1 + k, 13 - k, self.side).start()

    def side_part(self, i, k):
        links, a = self.links, self.links.a
        if k == 0:
            return self.part(i, a, 1 - links.b)
        piece = jnp.where(k <= a, a - k, a + LINE - k)
        return self.part(i, piece, 1 - links.b)

    def complete(self, i):
        links = self.links
        if self.across == 2:
            links.arrived(self.side_part(i, 0), self.flow(i, 1), self.over)
        for k in range(self.across - 1, LINE):
            links.arrived(self.side_part(i, k), self.flow(i, 10 + k), self.side)
        self.pass_copy(i).start()

    def finish(self, i):
        links, a = self.links, self.links.a
        links.arrived(self.full[i].at[links.t ^ 1], self.flow(i, 2), self.sibling)
        links.arrived(self.full[i].at[self.last], self.flow(i, 3), self.sibling)
        for k in range(self.across):
            self.over_copy(i, k).wait_send()
        self.beside_copy(i).wait_send()
        self.pass_copy(i).wait_send()
        self.stage_out(i).wait()
        for k in range(LINE - 1):

            @pl.when((a < LINE - 1) & (a - k >= 0))
            def _():
                self.moved(i, a - k, 4 + k, self.right).wait_send()

            @pl.when((a > 0) & (a + k <= LINE - 1))
            def _():
                self.moved(i, a + k, 7 + k, self.left).wait_send()

        for k in range(self.across - 1, LINE):
            piece = a if k == 0 else jnp.where(k <= a, a - k, a + LINE - k)
            self.moved(i, piece, 10 + k, self.side).wait_send()


class RowGather:
    FLOWS = 1 + 2 * 4

    def __init__(self, links, base, own, full):
        self.links, self.base, self.own, self.full = links, base, own, full
        self.far, self.last = links.t ^ 2, links.t ^ 3
        self.sibling, self.over = links.tp_peer(1), links.tp_peer(2)

    def at(self, c):
        rows = self.own.shape[0] // CHUNKS
        return pl.ds(c * rows, rows)

    def beside_copy(self):
        return self.links.copy(self.own, self.full.at[self.links.t], self.base, self.sibling)

    def over_copy(self, c):
        at = self.at(c)
        return self.links.copy(
            self.own.at[at], self.full.at[self.links.t, at], self.base + 1 + c, self.over
        )

    def pass_copy(self, c):
        part = self.full.at[self.far, self.at(c)]
        return self.links.copy(part, part, self.base + 1 + CHUNKS + c, self.sibling)

    def start_beside(self):
        self.beside_copy().start()

    def start_over(self):
        for c in range(CHUNKS):
            self.over_copy(c).start()

    def came_beside(self):
        self.links.arrived(self.full.at[self.links.t ^ 1], self.base, self.sibling)

    def came_over(self):
        for c in range(CHUNKS):
            self.links.arrived(
                self.full.at[self.far, self.at(c)], self.base + 1 + c, self.over
            )
            self.pass_copy(c).start()

    def came_last(self):
        for c in range(CHUNKS):
            self.links.arrived(
                self.full.at[self.last, self.at(c)], self.base + 1 + CHUNKS + c, self.sibling
            )

    def sent(self):
        self.beside_copy().wait_send()
        for c in range(CHUNKS):
            self.over_copy(c).wait_send()
            self.pass_copy(c).wait_send()


class RowScatter:
    FLOWS = 2 + 4

    def __init__(self, links, base, part, near, near_far, mid, far):
        self.links, self.base, self.part = links, base, part
        self.near, self.near_far, self.mid, self.far = near, near_far, mid, far
        self.sibling, self.over = links.tp_peer(1), links.tp_peer(2)

    def at(self, c):
        rows = self.near.shape[0] // CHUNKS
        return pl.ds(c * rows, rows)

    def first_copy(self):
        return self.links.copy(
            self.part.at[self.links.t ^ 3], self.near_far, self.base, self.sibling
        )

    def second_copy(self):
        return self.links.copy(
            self.part.at[self.links.t ^ 1], self.near, self.base + 1, self.sibling
        )

    def over_copy(self, c):
        at = self.at(c)
        return self.links.copy(
            self.mid.at[at], self.far.at[at], self.base + 2 + c, self.over
        )

    def send_over(self):
        self.links.arrived(self.near_far, self.base, self.sibling)
        for c in range(CHUNKS):
            at = self.at(c)
            self.mid[at] = (
                self.part[self.links.t ^ 2, at].astype(f32) + self.near_far[at].astype(f32)
            ).astype(bf16)
            self.over_copy(c).start()

    def came_beside(self):
        self.links.arrived(self.near, self.base + 1, self.sibling)

    def came_over(self, c):
        at = self.at(c)
        self.links.arrived(self.far.at[at], self.base + 2 + c, self.over)
        return (
            self.part[self.links.t, at].astype(f32)
            + self.near[at].astype(f32)
            + self.far[at].astype(f32)
        )

    def sent(self):
        self.first_copy().wait_send()
        self.second_copy().wait_send()
        for c in range(CHUNKS):
            self.over_copy(c).wait_send()


def cut(refs, *counts):
    out, at = [], 0
    for count in counts:
        out.append(refs[at : at + count])
        at += count
    return out


def self_forward_kernel(prefix_len, count, *refs):
    ins, own, outs, full, stage, scratch = cut(refs, 10, count, 6, count, count + 1, 13)
    x, memory, pre_cross, wq, wk, wv, wo, pre, seg_col, seg_row = ins
    q_out, k_out, v_out, resid, m_full, pre_full = outs
    x_full, part, mixed, bias, near, near_far, mid, far, send, recv, local, m_local, pre_local = scratch
    links = Links(send, recv)
    t = links.t
    block, lanes = x.shape[0], q_out.shape[1]
    weights = WeightGather(links, 0, 1, own, full, stage[:count], local)
    at = count * FLOWS
    x_rows = RowGather(links, at, x, x_full)
    m_rows = RowGather(links, at + RowGather.FLOWS, memory, m_full)
    at += 2 * RowGather.FLOWS
    sums = RowScatter(links, at, part, near, near_far, mid, far)
    at += RowScatter.FLOWS
    m_in = pltpu.make_async_copy(memory, stage[count], m_local.at[0])
    m_keep = pltpu.make_async_copy(stage[count], m_full.at[t], m_local.at[1])
    pre_keep = pltpu.make_async_copy(pre_cross, pre_full.at[t], pre_local.at[0])
    pre_sends = [
        links.copy(pre_cross, pre_full.at[t], at + m - 1, links.tp_peer(m)) for m in (1, 2, 3)
    ]

    greet(
        [links.tp_peer(m) for m in (1, 2, 3)]
        + [links.line_peer(d) for d in range(1, LINE)]
        + [links.side_peer()]
    )
    x_rows.start_over()
    x_rows.start_beside()
    m_rows.start_beside()
    m_in.start()
    pre_keep.start()
    for one in pre_sends:
        one.start()
    for i in range(count):
        weights.start_beside(i)

    for target, at in ((k_out, 0), (v_out, PRE_PACK)):
        target[0:PRE_PACK] = pre[at : at + PRE_PACK]
        target[PRE_PACK:PRE] = jnp.zeros((PRE - PRE_PACK, lanes), bf16)

    def project(rows, index):
        at = pl.multiple_of(index * block, block)
        q_out[pl.ds(at, block)] = (SCALE * nn(rows, wq[...])).astype(bf16)
        k_out[pl.ds(PRE + at, block)] = nn(rows, wk[...]).astype(bf16)
        v_out[pl.ds(PRE + at, block)] = nn(rows, wv[...]).astype(bf16)

    project(x[...], t)
    x_rows.came_beside()
    project(x_full[t ^ 1], t ^ 1)
    m_in.wait()
    m_keep.start()
    for i in range(count):
        weights.keep_own(i)
    x_rows.came_over()
    for i in range(count):
        weights.start_over(i)
    m_rows.start_over()
    project(x_full[t ^ 2], t ^ 2)
    x_rows.came_last()
    project(x_full[t ^ 3], t ^ 3)

    @pl.loop(0, 4)
    def _(order):
        here = t ^ (3 - order)
        for i in range(4):
            keys = PRE + (i + 1) * block
            shape = (block, keys)

            @pl.when(here == i)
            def _():
                bias[:, 0:keys] = mask_bias(
                    seg_col[i * block : (i + 1) * block],
                    seg_row[:, 0:keys],
                    i * block + lax.broadcasted_iota(jnp.int32, shape, 0),
                    lax.broadcasted_iota(jnp.int32, shape, 1),
                    prefix_len,
                )

                @pl.loop(0, lanes // PAIR)
                def _(j):
                    cols = pl.ds(pl.multiple_of(j * PAIR, PAIR), PAIR)
                    mixed[:, cols] = pair_forward(
                        q_out[i * block : (i + 1) * block, cols],
                        k_out[0:keys, cols],
                        v_out[0:keys, cols],
                        bias[:, 0:keys],
                    )

        part[here] = nn(mixed[...], wo[...]).astype(bf16)

        @pl.when(order == 0)
        def _():
            sums.first_copy().start()
            for i in range(count):
                weights.came_over(i)

        @pl.when(order == 1)
        def _():
            sums.send_over()

        @pl.when(order == 2)
        def _():
            sums.second_copy().start()
            for i in range(count):
                weights.along(i, 0)

    for i in range(count):
        weights.along(i, 1)
    m_rows.came_over()
    for i in range(count):
        weights.along(i, 2)
    sums.came_beside()
    for i in range(count - 1):
        weights.complete(i)
    for c in range(CHUNKS):
        rows = sums.at(c)
        resid[rows] = x[rows].astype(f32) + sums.came_over(c)
    weights.complete(count - 1)
    m_rows.came_beside()
    m_rows.came_last()
    for m, one in zip((1, 2, 3), pre_sends):
        links.copy(
            pre_full.at[t ^ m], pre_full.at[t ^ m], small_base(count) + m - 1, links.tp_peer(m)
        ).wait_recv()
        one.wait_send()
    for i in range(count):
        weights.finish(i)
    x_rows.sent()
    m_rows.sent()
    sums.sent()
    m_keep.wait()
    pre_keep.wait()


def small_base(count):
    return count * FLOWS + 2 * RowGather.FLOWS + RowScatter.FLOWS


def self_forward(prefix_len, x, memory, pre_cross, own_weights, pre, seg_col, seg_row, weights):
    n = 4
    count = len(weights)
    block, width = x.shape
    lanes = own_weights[0].shape[1]
    seq = n * block
    out = jax.ShapeDtypeStruct
    flows = small_base(count) + 3
    outs = (
        out((seq, lanes), bf16),
        out((PRE + seq, lanes), bf16),
        out((PRE + seq, lanes), bf16),
        out((block, width), f32),
        out((n, block, width), bf16),
        out((n,) + pre_cross.shape, bf16),
    ) + tuple(out((n,) + a.shape, a.dtype) for a in weights)
    v, a = pl.BlockSpec(memory_space=VMEM), pl.BlockSpec(memory_space=pltpu.HBM)
    rows = VMEM((block, width), bf16)
    return pl.pallas_call(
        functools.partial(self_forward_kernel, prefix_len, count),
        out_shape=outs,
        in_specs=[v, a] + [v] * 8 + [a] * count,
        out_specs=[v] * 4 + [a] * (2 + count),
        scratch_shapes=[VMEM(w.shape, w.dtype) for w in weights]
        + [rows]
        + [
            VMEM((n, block, width), bf16),
            VMEM((n, block, width), bf16),
            VMEM((block, lanes), bf16),
            VMEM((block, PRE + seq), f32),
            rows,
            rows,
            rows,
            rows,
            pltpu.SemaphoreType.DMA((flows,)),
            pltpu.SemaphoreType.DMA((flows,)),
            pltpu.SemaphoreType.DMA((2 * count,)),
            pltpu.SemaphoreType.DMA((2,)),
            pltpu.SemaphoreType.DMA((1,)),
        ],
        compiler_params=pltpu.CompilerParams(
            collective_id=0, has_side_effects=True, vmem_limit_bytes=48 << 20
        ),
        name="self_forward",
    )(x, memory, pre_cross, *own_weights, pre, seg_col, seg_row, *weights)


def gather_rows_start(links, own, full):
    rows = own.shape[0] // CHUNKS
    t = links.t
    flow = links.flow()
    sends = [links.start(own, full.at[t], flow, links.tp_peer(1))]
    chunk_flows = []
    for c in range(CHUNKS):
        at = pl.ds(c * rows, rows)
        f = links.flow()
        chunk_flows.append(f)
        sends.append(links.start(own.at[at], full.at[t, at], f, links.tp_peer(2)))
    return flow, chunk_flows, sends


def gather_rows_pass(links, full, state):
    flow, chunk_flows, sends = state
    rows = full.shape[1] // CHUNKS
    far, beside, last = links.t ^ 2, links.t ^ 1, links.t ^ 3
    passed = []
    for c in range(CHUNKS):
        at = pl.ds(c * rows, rows)
        links.arrived(full.at[far, at], chunk_flows[c], links.tp_peer(2))
        f = links.flow()
        passed.append(f)
        sends.append(links.start(full.at[far, at], full.at[far, at], f, links.tp_peer(1)))
    links.arrived(full.at[beside], flow, links.tp_peer(1))
    for c in range(CHUNKS):
        at = pl.ds(c * rows, rows)
        links.arrived(full.at[last, at], passed[c], links.tp_peer(1))
    return sends


def gather_kernel(count, *refs):
    own, full = refs[:count], refs[count : 2 * count]
    send, recv, local = refs[2 * count :]
    links = Links(send, recv)
    greet([links.tp_peer(1), links.tp_peer(2)])
    kept = [pltpu.make_async_copy(own[i], full[i].at[links.t], local.at[i]) for i in range(count)]
    for one in kept:
        one.start()
    states = [gather_rows_start(links, own[i], full[i]) for i in range(count)]
    for i in range(count):
        for one in gather_rows_pass(links, full[i], states[i]):
            one.wait_send()
    for one in kept:
        one.wait()


def gather_rows(collective_id, *own):
    n = 4
    flows = (1 + 2 * CHUNKS) * len(own)
    return pl.pallas_call(
        functools.partial(gather_kernel, len(own)),
        out_shape=tuple(jax.ShapeDtypeStruct((n,) + a.shape, a.dtype) for a in own),
        in_specs=[pl.BlockSpec(memory_space=VMEM)] * len(own),
        out_specs=[pl.BlockSpec(memory_space=VMEM)] * len(own),
        scratch_shapes=[
            pltpu.SemaphoreType.DMA((flows,)),
            pltpu.SemaphoreType.DMA((flows,)),
            pltpu.SemaphoreType.DMA((len(own),)),
        ],
        compiler_params=pltpu.CompilerParams(
            collective_id=collective_id, has_side_effects=True
        ),
        name="gather_rows",
    )(*own)


def scatter_kernel(count, bases, *refs):
    parts = refs[:count]
    base = refs[count : count + bases]
    outs = refs[count + bases : 2 * count + bases]
    near, near_far, mid, far = refs[2 * count + bases : 2 * count + bases + 4]
    send, recv = refs[2 * count + bases + 4 :]
    links = Links(send, recv)
    t = links.t
    greet([links.tp_peer(1), links.tp_peer(2)])
    rows = parts[0].shape[1] // CHUNKS
    sends, first, second, across = [], [], [], []
    for i in range(count):
        first.append(links.flow())
        sends.append(
            links.start(parts[i].at[t ^ 3], near_far.at[i], first[i], links.tp_peer(1))
        )
        second.append(links.flow())
        sends.append(links.start(parts[i].at[t ^ 1], near.at[i], second[i], links.tp_peer(1)))
    for i in range(count):
        links.arrived(near_far.at[i], first[i], links.tp_peer(1))
        across.append([])
        for c in range(CHUNKS):
            at = pl.ds(c * rows, rows)
            mid[i, at] = (
                parts[i][t ^ 2, at].astype(f32) + near_far[i, at].astype(f32)
            ).astype(bf16)
            across[i].append(links.flow())
            sends.append(
                links.start(mid.at[i, at], far.at[i, at], across[i][c], links.tp_peer(2))
            )
    for i in range(count):
        links.arrived(near.at[i], second[i], links.tp_peer(1))
        for c in range(CHUNKS):
            at = pl.ds(c * rows, rows)
            links.arrived(far.at[i, at], across[i][c], links.tp_peer(2))
            value = (
                parts[i][t, at].astype(f32)
                + near[i, at].astype(f32)
                + far[i, at].astype(f32)
            )
            if i < bases:
                value = value + base[i][at].astype(f32)
            outs[i][at] = value.astype(outs[i].dtype)
    for one in sends:
        one.wait_send()


def scatter_sum(collective_id, parts, base, kinds):
    count = len(parts)
    _, block, width = parts[0].shape
    flows = count * (2 + CHUNKS)
    slots = VMEM((count, block, width), bf16)
    return pl.pallas_call(
        functools.partial(scatter_kernel, count, len(base)),
        out_shape=tuple(jax.ShapeDtypeStruct((block, width), kind) for kind in kinds),
        in_specs=[pl.BlockSpec(memory_space=VMEM)] * (count + len(base)),
        out_specs=[pl.BlockSpec(memory_space=VMEM)] * count,
        scratch_shapes=[
            slots,
            slots,
            slots,
            slots,
            pltpu.SemaphoreType.DMA((flows,)),
            pltpu.SemaphoreType.DMA((flows,)),
        ],
        compiler_params=pltpu.CompilerParams(
            collective_id=collective_id, has_side_effects=True, vmem_limit_bytes=40 << 20
        ),
        name="scatter_sum",
    )(*parts, *base)


def adapter_sum_kernel(levels, g, out, s1, h, xb, h2, zb, p3, yb, hb, send, recv):
    links = Links(send, recv)
    t, a, b = links.t, links.a, links.b
    c = lax.rem(t, 2)
    far_groups = []
    for level in range(levels):
        bit = GROUP << level
        far_groups.append((links.row ^ bit, t))
    greet(
        [links.tp_peer(1), links.tp_peer(2)]
        + [links.line_peer(d) for d in range(1, LINE)]
        + [links.side_peer()]
        + far_groups
    )
    sends = []

    def send_to(src, dst, peer):
        flow = links.flow()
        sends.append(links.start(src, dst, flow, peer))
        return flow

    flow = send_to(g.at[1 - c], s1, links.tp_peer(1))
    links.arrived(s1, flow, links.tp_peer(1))
    h[...] = (g[c].astype(f32) + s1[...].astype(f32)).astype(bf16)
    flow = send_to(h.at[1 - b], xb, links.side_peer())
    links.arrived(xb, flow, links.side_peer())
    h2[...] = (h[b].astype(f32) + xb[...].astype(f32)).astype(bf16)
    line = []
    for d in range(1, LINE):
        line.append(send_to(h2.at[lax.rem(a + d, LINE)], zb.at[d - 1], links.line_peer(d)))
    for d in range(1, LINE):
        links.arrived(zb.at[d - 1], line[d - 1], links.line_peer(d))
    total = h2[a].astype(f32)
    for d in range(1, LINE):
        total = total + zb[d - 1].astype(f32)
    p3[...] = total.astype(bf16)
    flow = send_to(p3, yb, links.tp_peer(2))
    links.arrived(yb, flow, links.tp_peer(2))
    value = p3[...].astype(f32) + yb[...].astype(f32)
    for level in range(levels):
        hb[2 * level] = value.astype(bf16)
        flow = send_to(hb.at[2 * level], hb.at[2 * level + 1], far_groups[level])
        links.arrived(hb.at[2 * level + 1], flow, far_groups[level])
        value = hb[2 * level].astype(f32) + hb[2 * level + 1].astype(f32)
    out[c, b, a] = value.astype(bf16)
    mine = out.at[c, b, a]
    line = []
    for d in range(1, LINE):
        line.append(send_to(mine, mine, links.line_peer(d)))
    side = [send_to(mine, mine, links.side_peer())]
    for d in range(1, LINE):
        here = out.at[c, b, lax.rem(a - d + LINE, LINE)]
        links.arrived(here, line[d - 1], links.line_peer(d))
        side.append(send_to(here, here, links.side_peer()))
    for d in range(LINE):
        links.arrived(out.at[c, 1 - b, lax.rem(a - d + LINE, LINE)], side[d], links.side_peer())
    flow = send_to(out.at[c], out.at[c], links.tp_peer(1))
    links.arrived(out.at[1 - c], flow, links.tp_peer(1))
    for one in sends:
        one.wait_send()


def doublings(count):
    levels = 0
    while (1 << levels) < count:
        levels += 1
    return levels


def adapter_sum(collective_id, row_count, grads):
    levels = doublings(row_count // GROUP)
    height, width = grads.shape
    piece = height // (2 * GROUP)
    half = (2, LINE, piece, width)
    flows = 1 + 1 + 3 + 1 + levels + 3 + 4 + 1
    return pl.pallas_call(
        functools.partial(adapter_sum_kernel, levels),
        out_shape=jax.ShapeDtypeStruct((2,) + half, bf16),
        in_specs=[pl.BlockSpec(memory_space=VMEM)],
        out_specs=pl.BlockSpec(memory_space=VMEM),
        scratch_shapes=[
            VMEM(half, bf16),
            VMEM(half, bf16),
            VMEM(half[1:], bf16),
            VMEM(half[1:], bf16),
            VMEM((LINE - 1, piece, width), bf16),
            VMEM((piece, width), bf16),
            VMEM((piece, width), bf16),
            VMEM((max(1, 2 * levels), piece, width), bf16),
            pltpu.SemaphoreType.DMA((flows,)),
            pltpu.SemaphoreType.DMA((flows,)),
        ],
        compiler_params=pltpu.CompilerParams(
            collective_id=collective_id, has_side_effects=True, vmem_limit_bytes=40 << 20
        ),
        name="adapter_sum",
    )(grads.reshape((2,) + half)).reshape(height, width)


def small_sum_kernel(levels, cross, own, vecs, out, cross_in, vecs_in, outgo, income, send, recv):
    links = Links(send, recv)
    t = links.t
    row_peers = [(links.row ^ (1 << level), t) for level in range(levels)]
    greet([links.tp_peer(m) for m in (1, 2, 3)] + row_peers)
    sends = []
    flows = []
    for m in (1, 2, 3):
        peer = links.tp_peer(m)
        for src, dst in ((cross.at[t ^ m], cross_in.at[t]), (vecs, vecs_in.at[t])):
            flow = links.flow()
            flows.append(flow)
            sends.append(links.start(src, dst, flow, peer))
    cross_in[t] = cross[t]
    vecs_in[t] = vecs[...]
    for m in (1, 2, 3):
        links.arrived(cross_in.at[t ^ m], flows[2 * (m - 1)], links.tp_peer(m))
        links.arrived(vecs_in.at[t ^ m], flows[2 * (m - 1) + 1], links.tp_peer(m))
    kept = cross.shape[1]
    height = vecs.shape[0]
    lanes = cross.shape[2]
    value_cross = cross_in[0] + cross_in[1] + cross_in[2] + cross_in[3]
    value_vecs = vecs_in[0] + vecs_in[1] + vecs_in[2] + vecs_in[3]
    pieces = [value_cross, own[...]] + [
        value_vecs[:, i * lanes : (i + 1) * lanes] for i in range(vecs.shape[1] // lanes)
    ]
    value = jnp.concatenate(pieces, axis=0)
    for level in range(levels):
        outgo[level] = value
        flow = links.flow()
        sends.append(
            links.start(outgo.at[level], income.at[level], flow, row_peers[level])
        )
        links.arrived(income.at[level], flow, row_peers[level])
        value = outgo[level] + income[level]
    out[...] = value
    for one in sends:
        one.wait_send()


def small_sum(collective_id, row_count, cross, own, vecs):
    levels = doublings(row_count)
    n, kept, lanes = cross.shape
    height = 2 * kept + vecs.shape[0] * vecs.shape[1] // lanes
    flows = 6 + levels
    total = pl.pallas_call(
        functools.partial(small_sum_kernel, levels),
        out_shape=jax.ShapeDtypeStruct((height, lanes), f32),
        in_specs=[pl.BlockSpec(memory_space=VMEM)] * 3,
        out_specs=pl.BlockSpec(memory_space=VMEM),
        scratch_shapes=[
            VMEM((n, kept, lanes), f32),
            VMEM((n,) + vecs.shape, f32),
            VMEM((levels, height, lanes), f32),
            VMEM((levels, height, lanes), f32),
            pltpu.SemaphoreType.DMA((flows,)),
            pltpu.SemaphoreType.DMA((flows,)),
        ],
        compiler_params=pltpu.CompilerParams(
            collective_id=collective_id, has_side_effects=True
        ),
        name="small_sum",
    )(cross, own, vecs)
    parts = total[2 * kept :].reshape(-1, vecs.shape[0], lanes)
    return (
        total[:kept],
        total[kept : 2 * kept],
        jnp.moveaxis(parts, 0, 1).reshape(vecs.shape),
    )


def per_device(
    row_count,
    tokens, memory, out_grad, dec_segments, src_segments,
    self_query, self_key, self_value, self_out,
    cross_query, cross_key, cross_value, cross_out,
    ffn_in, ffn_out, adapt_down, adapt_down_bias, adapt_up, adapt_up_bias,
    self_prefix, cross_prefix, norm_gain, norm_shift,
):
    seq_local, _, width = tokens.shape
    prefix_len = self_prefix.shape[1]
    lanes = self_query.shape[1]
    adapt = adapt_down.shape[1]
    t = lax.axis_index("tp")
    x, mem, grad_in = (a.reshape(seq_local, width) for a in (tokens, memory, out_grad))

    def pack_prefix(prefix):
        return jnp.pad(prefix, ((0, 0), (0, PRE_PACK - prefix_len), (0, 0))).reshape(
            2 * PRE_PACK, lanes
        )

    def unpack_prefix(packed):
        return packed.reshape(2, PRE_PACK, lanes)[:, :prefix_len]

    seq = dec_segments.shape[1]
    never = jnp.full((1, PRE), -1, jnp.int32)
    dec_row = jnp.concatenate([never, dec_segments], axis=1)
    src_row = jnp.concatenate([never, src_segments], axis=1)
    dec_q = dec_segments
    own_q = lax.dynamic_slice(dec_segments, (0, t * seq_local), (1, seq_local))

    q1, k1, v1_heads, resid_one, m_full, pre_full, *gathered = self_forward(
        prefix_len, x, mem, pack_prefix(cross_prefix),
        (self_query, self_key, self_value, self_out),
        pack_prefix(self_prefix), dec_q.reshape(seq, 1), dec_row,
        (cross_query, cross_key, cross_value, cross_out, ffn_in),
    )
    cross_weights = gathered[:4]
    w_in = gathered[4]
    m_full = m_full.reshape(seq, width)
    q2, k2, v2_heads, resid_two, w_out = cross_forward(
        prefix_len, resid_one, m_full, cross_weights, pre_full,
        own_q.reshape(seq_local, 1), src_row, norm_gain, norm_shift, ffn_out,
    )
    output, dr2, up_part, down_part, vecs_ff = feed_forward(
        resid_two, grad_in, w_in, w_out,
        adapt_down, adapt_down_bias.reshape(1, adapt), adapt_up, adapt_up_bias.reshape(1, width),
        norm_gain, norm_shift,
    )
    adapter = adapter_sum(2, row_count, jnp.concatenate([up_part, down_part], axis=0))
    dr1, dr1_low, dm, cross_pre_part, vecs_cross = cross_backward(
        prefix_len, dr2, resid_one, q2, k2, v2_heads, cross_weights,
        own_q, src_row.reshape(PRE + seq, 1), norm_gain,
    )
    (dr1_full,) = gather_rows(3, dr1_low)
    part, self_pre_part = self_backward(
        prefix_len, dr1_full, q1, k1, v1_heads,
        self_query, self_key, self_value, self_out, dec_q, dec_row.reshape(PRE + seq, 1),
    )
    tokens_grad, memory_grad = scatter_sum(
        4, (part, dm.reshape(part.shape)), (dr1,), (bf16, bf16)
    )
    cross_pre, self_pre, vecs = small_sum(
        5, row_count, cross_pre_part, self_pre_part, vecs_ff + vecs_cross
    )
    local = tokens.shape
    return (
        output.reshape(local),
        tokens_grad.reshape(local),
        memory_grad.reshape(local),
        unpack_prefix(self_pre),
        unpack_prefix(cross_pre),
        vecs[0:3],
        vecs[3:6],
        adapter[adapt:].T.astype(f32),
        vecs[7, :adapt],
        adapter[:adapt].astype(f32),
        vecs[6],
    )


def solution(mesh):
    placed = (
        (P("tp", "rows", None),) * 3
        + (P("rows", None),) * 2
        + (P(None, "tp"),) * 3
        + (P("tp", None),)
        + (P(None, "tp"),) * 3
        + (P("tp", None),)
        + (P(None, "tp"), P("tp", None))
        + (P(),) * 4
        + (P(None, None, "tp"),) * 2
        + (P(),) * 2
    )
    return jax.shard_map(
        functools.partial(per_device, mesh.shape["rows"]),
        mesh=mesh,
        in_specs=placed,
        out_specs=(P("tp", "rows", None),) * 3 + (P(None, None, "tp"),) * 2 + (P(),) * 6,
        check_vma=False,
    )
```

```python
import functools

import jax
import jax.numpy as jnp
from jax import lax
from jax.experimental import pallas as pl
from jax.experimental.pallas import tpu as pltpu
from jax.sharding import PartitionSpec as P

HEAD = 64
PAIR = 2 * HEAD
PRE = 128
PRE_PACK = 32
GROUP = 8
LINE = 4
MASKED = -1000000000.0
EPSILON = 1e-05
SCALE = HEAD**-0.5
f32 = jnp.float32
bf16 = jnp.bfloat16
MESH = pl.DeviceIdType.MESH
VMEM = pltpu.VMEM
ANY = pl.ANY


def nn(a, b):
    return lax.dot_general(a, b, (((1,), (0,)), ((), ())), preferred_element_type=f32)


def nt(a, b):
    return lax.dot_general(a, b, (((1,), (1,)), ((), ())), preferred_element_type=f32)


def tn(a, b):
    return lax.dot_general(a, b, (((0,), (0,)), ((), ())), preferred_element_type=f32)


def gelu_parts(v):
    phi = 0.5 + 0.5 * lax.erf(v * (0.5**0.5))
    slope = phi + v * (jnp.exp(-0.5 * v * v) * 0.3989422804014327)
    return v * phi, slope


def norm_parts(v):
    centered = v - jnp.mean(v, axis=-1, keepdims=True)
    spread = lax.rsqrt(jnp.mean(centered * centered, axis=-1, keepdims=True) + EPSILON)
    return centered * spread, spread


def norm_back(dy, gain, n, spread):
    dn = dy * gain
    dv = spread * (
        dn - jnp.mean(dn, axis=-1, keepdims=True) - n * jnp.mean(dn * n, axis=-1, keepdims=True)
    )
    return dv, jnp.sum(dy * n, axis=0, keepdims=True), jnp.sum(dy, axis=0, keepdims=True)


def lane_half(shape, h):
    return (lax.broadcasted_iota(jnp.int32, shape, 1) // HEAD) == h


def mask_bias(seg_q, seg_k, q_index, k_index, prefix_len):
    keep = seg_q == seg_k
    if q_index is not None:
        keep = keep & (k_index - PRE <= q_index)
    keep = keep | (k_index < prefix_len)
    return jnp.where(keep, 0.0, MASKED)


def pair_forward(q_pair, k_pair, v_pair, bias):
    outs, logs = [], []
    for h in range(2):
        half = lane_half(q_pair.shape, h)
        scores = nt(jnp.where(half, q_pair, jnp.zeros_like(q_pair)), k_pair) + bias
        top = jnp.max(scores, axis=1, keepdims=True)
        e = jnp.exp(scores - top)
        total = jnp.sum(e, axis=1, keepdims=True)
        outs.append(nn(e.astype(bf16), v_pair) * (1.0 / total))
        logs.append(top + jnp.log(total))
    return jnp.where(lane_half(outs[0].shape, 0), outs[0], outs[1]).astype(bf16), logs


def keep_logs(kept, logs, j):
    lane = lax.broadcasted_iota(jnp.int32, kept.shape, 1)
    for h in range(2):
        kept[...] = jnp.where(lane == 2 * j + h, logs[h], kept[...])


def pair_backward(q_pair, k_pair, v_pair, a_pair, da_pair, logs, bias_t):
    k_turned = k_pair.T
    prod = da_pair.astype(f32) * a_pair.astype(f32)
    prod_high = prod.astype(bf16)
    prod_low = (prod - prod_high.astype(f32)).astype(bf16)
    pick = (
        lax.broadcasted_iota(jnp.int32, (8, PAIR), 1) // HEAD
        == lax.broadcasted_iota(jnp.int32, (8, PAIR), 0)
    ).astype(bf16)
    delta = nt(pick, prod_high) + nt(pick, prod_low)
    dk = dv = None
    dq = []
    for h in range(2):
        half = lane_half(q_pair.shape, h)
        q = jnp.where(half, q_pair, jnp.zeros_like(q_pair))
        da = jnp.where(half, da_pair, jnp.zeros_like(da_pair))
        p = jnp.exp(nt(k_pair, q) + (bias_t - logs[h]))
        ds = (p * (nt(v_pair, da) - delta[h : h + 1])).astype(bf16)
        dv_h = nn(p.astype(bf16), da)
        dk_h = nn(ds, q)
        dk = dk_h if dk is None else dk + dk_h
        dv = dv_h if dv is None else dv + dv_h
        dq.append(nn(k_turned[h * HEAD : (h + 1) * HEAD], ds))
    return jnp.concatenate(dq, axis=0).T.astype(bf16), dk, dv


def cross_forward_kernel(
    prefix_len, v1, memory, wq, wk, wv, wo, pre, seg_col, seg_row, gain, shift, own,
    q_out, k_out, v_out, a_out, l_out, v2, full, n1_low, bias, kept, stage, send, recv, local,
):
    step = pl.program_id(0)
    block, lanes = q_out.shape[1:]
    keys = k_out.shape[1]
    links = Links(send, recv)
    weights = WeightGather(links, 0, 2, [own], [full], [stage], local)

    @pl.when(step == 0)
    def _():
        greet(
            [links.tp_peer(1), links.tp_peer(2)]
            + [links.line_peer(d) for d in range(1, LINE)]
            + [links.side_peer()]
        )
        weights.start_over(0)
        weights.start_beside(0)

    @pl.when(step == 0)
    def _():
        n, _ = norm_parts(v1[...])
        normed = n * gain[0:1] + shift[0:1]
        v2[...] = normed
        n1_low[...] = normed.astype(bf16)
        kept[...] = jnp.zeros_like(kept)
        bias[...] = mask_bias(
            seg_col[...],
            seg_row[...],
            None,
            lax.broadcasted_iota(jnp.int32, (block, keys), 1),
            prefix_len,
        )

    q_out[0] = (SCALE * nn(n1_low[...], wq[0])).astype(bf16)
    for target, at in ((k_out, 0), (v_out, PRE_PACK)):
        target[0, 0:PRE_PACK] = pre[0, at : at + PRE_PACK]
        target[0, PRE_PACK:PRE] = jnp.zeros((PRE - PRE_PACK, lanes), bf16)

    @pl.loop(0, (keys - PRE) // block)
    def _(i):
        at = pl.multiple_of(i * block, block)
        rows = memory[pl.ds(at, block)]
        k_out[0, pl.ds(PRE + at, block)] = nn(rows, wk[0]).astype(bf16)
        v_out[0, pl.ds(PRE + at, block)] = nn(rows, wv[0]).astype(bf16)

    @pl.loop(0, lanes // PAIR)
    def _(j):
        cols = pl.ds(pl.multiple_of(j * PAIR, PAIR), PAIR)
        mixture, logs = pair_forward(
            q_out[0, :, cols], k_out[0, :, cols], v_out[0, :, cols], bias[...]
        )
        a_out[0, :, cols] = mixture
        keep_logs(kept, logs, j)

    l_out[0] = kept[...].T[0:8]
    v2[...] += nn(a_out[0], wo[0])

    @pl.when(step == 0)
    def _():
        weights.keep_own(0)
        weights.came_over(0)

    @pl.when(step == 1)
    def _():
        weights.along(0, 0)

    @pl.when(step == 2)
    def _():
        weights.along(0, 1)

    @pl.when(step == pl.num_programs(0) - 1)
    def _():
        weights.along(0, 2)
        weights.complete(0)
        weights.finish(0)


def whole_spec(shape):
    return pl.BlockSpec(shape, lambda i: (0,) * len(shape))


def shard_spec(shape, index=lambda i: i):
    return pl.BlockSpec((1,) + shape[1:], lambda i: (index(i), 0, 0))


def cross_forward(prefix_len, v1, memory, weights, pre, seg_col, seg_row, gain, shift, own):
    wq, wk, wv, wo = weights
    n, width, lanes = wq.shape
    block = v1.shape[0]
    seq = memory.shape[0]
    out = jax.ShapeDtypeStruct
    outs = (
        out((n, block, lanes), bf16),
        out((n, PRE + seq, lanes), bf16),
        out((n, PRE + seq, lanes), bf16),
        out((n, block, lanes), bf16),
        out((n, 8, block), f32),
    )
    return pl.pallas_call(
        functools.partial(cross_forward_kernel, prefix_len),
        grid=(n,),
        out_shape=outs + (out((block, width), f32), out((n,) + own.shape, own.dtype)),
        in_specs=[whole_spec(v1.shape), whole_spec(memory.shape)]
        + [shard_spec(a.shape) for a in (wq, wk, wv, wo, pre)]
        + [whole_spec(a.shape) for a in (seg_col, seg_row, gain, shift)]
        + [pl.BlockSpec(memory_space=pltpu.HBM)],
        out_specs=[shard_spec(a.shape) for a in outs]
        + [whole_spec((block, width)), pl.BlockSpec(memory_space=pltpu.HBM)],
        scratch_shapes=[
            VMEM((block, width), bf16),
            VMEM((block, PRE + seq), f32),
            VMEM((block, 128), f32),
            VMEM(own.shape, own.dtype),
            pltpu.SemaphoreType.DMA((FLOWS,)),
            pltpu.SemaphoreType.DMA((FLOWS,)),
            pltpu.SemaphoreType.DMA((2,)),
        ],
        compiler_params=pltpu.CompilerParams(
            collective_id=1, has_side_effects=True, vmem_limit_bytes=48 << 20
        ),
        name="cross_forward",
    )(v1, memory, wq, wk, wv, wo, pre, seg_col, seg_row, gain, shift, own)


def feed_forward_kernel(
    v2, out_grad, w_in, w_out, down, down_bias, up, up_bias, gain, shift,
    output, dr2, grads, vecs,
    n2_low, n2_hat, total, e_low, slope, grad,
):
    step = pl.program_id(0)
    half = pl.num_programs(0) // 2
    width = v2.shape[1]

    @pl.when(step == 0)
    def _():
        n, _ = norm_parts(v2[...])
        n2_hat[...] = n
        normed = n * gain[1:2] + shift[1:2]
        total[...] = normed
        n2_low[...] = normed.astype(bf16)

    @pl.when(step < half)
    def _():
        act, bend = gelu_parts(nn(n2_low[...], w_in[0]))
        slope[step] = bend
        total[...] += nn(act.astype(bf16), w_out[0])

    @pl.when(step == half - 1)
    def _():
        act, bend = gelu_parts(nn(n2_low[...], down[...]) + down_bias[...])
        act = act.astype(bf16)
        resid = total[...] + 4.0 * (nn(act, up[...]) + up_bias[...])
        n, spread = norm_parts(resid)
        output[...] = (n * gain[2:3] + shift[2:3]).astype(bf16)
        dz, gain_part, shift_part = norm_back(out_grad[...].astype(f32), gain[2:3], n, spread)
        e_low[...] = dz.astype(bf16)
        four = (4.0 * dz).astype(bf16)
        grads[0] = tn(act, four).astype(bf16)
        da = (nt(four, up[...]) * bend).astype(bf16)
        grads[1] = tn(da, n2_low[...]).astype(bf16)
        grad[...] = dz + nt(da, down[...])
        vecs[...] = jnp.zeros_like(vecs)
        vecs[2:3] = gain_part
        vecs[5:6] = shift_part
        vecs[6:7] = jnp.sum(four.astype(f32), axis=0, keepdims=True)
        vecs[7:8, 0 : down.shape[1]] = jnp.sum(da.astype(f32), axis=0, keepdims=True)

    @pl.when(step >= half)
    def _():
        du = (nt(e_low[...], w_out[0]) * slope[2 * half - 1 - step]).astype(bf16)
        grad[...] += nt(du, w_in[0])

    @pl.when(step == 2 * half - 1)
    def _():
        _, spread = norm_parts(v2[...])
        dv, gain_part, shift_part = norm_back(grad[...], gain[1:2], n2_hat[...], spread)
        dr2[...] = dv
        vecs[1:2] = gain_part
        vecs[4:5] = shift_part


def feed_forward(v2, out_grad, w_in, w_out, down, down_bias, up, up_bias, gain, shift):
    n, width, inner = w_in.shape
    block = v2.shape[0]
    adapt = down.shape[1]
    out = jax.ShapeDtypeStruct
    outs = (
        out((block, width), bf16),
        out((block, width), f32),
        out((2, adapt, width), bf16),
        out((8, width), f32),
    )
    turn = lambda i: jnp.minimum(i, 2 * n - 1 - i)
    return pl.pallas_call(
        feed_forward_kernel,
        grid=(2 * n,),
        out_shape=outs,
        in_specs=[whole_spec(v2.shape), whole_spec(out_grad.shape)]
        + [shard_spec(w_in.shape, turn), shard_spec(w_out.shape, turn)]
        + [whole_spec(a.shape) for a in (down, down_bias, up, up_bias, gain, shift)],
        out_specs=[whole_spec(a.shape) for a in outs],
        scratch_shapes=[
            VMEM((block, width), bf16),
            VMEM((block, width), f32),
            VMEM((block, width), f32),
            VMEM((block, width), bf16),
            VMEM((n, block, inner), f32),
            VMEM((block, width), f32),
        ],
        compiler_params=pltpu.CompilerParams(vmem_limit_bytes=56 << 20),
        name="feed_forward",
    )(v2, out_grad, w_in, w_out, down, down_bias, up, up_bias, gain, shift)


class Links:
    def __init__(self, send, recv):
        self.send, self.recv = send, recv
        self.row = lax.axis_index("rows")
        self.t = lax.axis_index("tp")
        self.flows = 0
        place = lax.rem(self.row, GROUP)
        self.base = self.row - place
        self.a = place // 2
        self.b = lax.rem(place, 2)
        self.place = place

    def flow(self):
        self.flows += 1
        return self.flows - 1

    def tp_peer(self, mask):
        return (self.row, self.t ^ mask)

    def line_peer(self, d):
        return (self.base + lax.rem(self.a + d, LINE) * 2 + self.b, self.t)

    def side_peer(self):
        return (self.base + self.a * 2 + (1 - self.b), self.t)

    def copy(self, src, dst, flow, peer):
        return pltpu.make_async_remote_copy(
            src_ref=src,
            dst_ref=dst,
            send_sem=self.send.at[flow],
            recv_sem=self.recv.at[flow],
            device_id=peer,
            device_id_type=MESH,
        )

    def start(self, src, dst, flow, peer):
        made = self.copy(src, dst, flow, peer)
        made.start()
        return made

    def arrived(self, dst, flow, peer):
        self.copy(dst, dst, flow, peer).wait_recv()


def greet(peers):
    barrier = pltpu.get_barrier_semaphore()
    for peer in peers:
        pl.semaphore_signal(barrier, inc=1, device_id=peer, device_id_type=MESH)
    pl.semaphore_wait(barrier, len(peers))


CHUNKS = 4


FLOWS = 14


class WeightGather:
    def __init__(self, links, base, across, own, full, stage, local):
        self.links, self.base, self.across = links, base, across
        self.own, self.full, self.stage, self.local = own, full, stage, local
        self.far, self.last = links.t ^ 2, links.t ^ 3
        a = links.a
        self.right = (links.base + jnp.minimum(a + 1, LINE - 1) * 2 + links.b, links.t)
        self.left = (links.base + jnp.maximum(a - 1, 0) * 2 + links.b, links.t)
        self.side = links.side_peer()
        self.sibling = links.tp_peer(1)
        self.over = links.tp_peer(2)

    def at(self, i, a, b):
        rows = self.own[i].shape[0] // GROUP
        return pl.ds(pl.multiple_of((a * 2 + b) * rows, rows), rows)

    def part(self, i, a, b):
        return self.full[i].at[self.far, self.at(i, a, b)]

    def flow(self, i, k):
        return self.base + i * FLOWS + k

    def over_copy(self, i, k):
        links = self.links
        b = links.b if k == 0 else 1 - links.b
        at = self.at(i, links.a, b)
        return links.copy(
            self.own[i].at[at], self.full[i].at[links.t, at], self.flow(i, k), self.over
        )

    def beside_copy(self, i):
        return self.links.copy(
            self.own[i], self.full[i].at[self.links.t], self.flow(i, 2), self.sibling
        )

    def pass_copy(self, i):
        whole = self.full[i].at[self.far]
        return self.links.copy(whole, whole, self.flow(i, 3), self.sibling)

    def moved(self, i, a, flow, peer):
        part = self.part(i, a, self.links.b)
        return self.links.copy(part, part, self.flow(i, flow), peer)

    def stage_in(self, i):
        return pltpu.make_async_copy(self.own[i], self.stage[i], self.local.at[2 * i])

    def stage_out(self, i):
        return pltpu.make_async_copy(
            self.stage[i], self.full[i].at[self.links.t], self.local.at[2 * i + 1]
        )

    def start_over(self, i):
        for k in range(self.across):
            self.over_copy(i, k).start()

    def start_beside(self, i):
        self.beside_copy(i).start()
        self.stage_in(i).start()

    def keep_own(self, i):
        self.stage_in(i).wait()
        self.stage_out(i).start()

    def came_over(self, i):
        mine = self.part(i, self.links.a, self.links.b)
        self.links.arrived(mine, self.flow(i, 0), self.over)
        self.spread(i)

    def spread(self, i):
        a = self.links.a

        @pl.when(a < LINE - 1)
        def _():
            self.moved(i, a, 4, self.right).start()

        @pl.when(a > 0)
        def _():
            self.moved(i, a, 7, self.left).start()

        if self.across == 1:
            self.moved(i, a, 10, self.side).start()

    def along(self, i, k):
        links, a = self.links, self.links.a

        @pl.when(a - 1 - k >= 0)
        def _():
            links.arrived(self.part(i, a - 1 - k, links.b), self.flow(i, 4 + k), self.left)
            if k < LINE - 2:

                @pl.when(a < LINE - 1)
                def _():
                    self.moved(i, a - 1 - k, 5 + k, self.right).start()

            self.moved(i, a - 1 - k, 11 + k, self.side).start()

        @pl.when(a + 1 + k <= LINE - 1)
        def _():
            links.arrived(self.part(i, a + 1 + k, links.b), self.flow(i, 7 + k), self.right)
            if k < LINE - 2:

                @pl.when(a > 0)
                def _():
                    self.moved(i, a + 1 + k, 8 + k, self.left).start()

            self.moved(i, a + 1 + k, 13 - k, self.side).start()

    def side_part(self, i, k):
        links, a = self.links, self.links.a
        if k == 0:
            return self.part(i, a, 1 - links.b)
        piece = jnp.where(k <= a, a - k, a + LINE - k)
        return self.part(i, piece, 1 - links.b)

    def complete(self, i):
        links = self.links
        if self.across == 2:
            links.arrived(self.side_part(i, 0), self.flow(i, 1), self.over)
        for k in range(self.across - 1, LINE):
            links.arrived(self.side_part(i, k), self.flow(i, 10 + k), self.side)
        self.pass_copy(i).start()

    def finish(self, i):
        links = self.links
        links.arrived(self.full[i].at[links.t ^ 1], self.flow(i, 2), self.sibling)
        links.arrived(self.full[i].at[self.last], self.flow(i, 3), self.sibling)
        for k in range(self.across):
            self.over_copy(i, k).wait_send()
        self.beside_copy(i).wait_send()
        self.stage_out(i).wait()
        self.spread_sent(i)

    def spread_sent(self, i):
        a = self.links.a
        self.pass_copy(i).wait_send()
        for k in range(LINE - 1):

            @pl.when((a < LINE - 1) & (a - k >= 0))
            def _():
                self.moved(i, a - k, 4 + k, self.right).wait_send()

            @pl.when((a > 0) & (a + k <= LINE - 1))
            def _():
                self.moved(i, a + k, 7 + k, self.left).wait_send()

        for k in range(self.across - 1, LINE):
            piece = a if k == 0 else jnp.where(k <= a, a - k, a + LINE - k)
            self.moved(i, piece, 10 + k, self.side).wait_send()


class AdapterSpread(WeightGather):
    def __init__(self, links, base, full):
        super().__init__(links, base, 1, None, full, None, None)
        self.half = lax.rem(links.t, 2)

    def part(self, i, a, b):
        return self.full.at[self.half, b, a]

    def pass_copy(self, i):
        whole = self.full.at[self.half]
        return self.links.copy(whole, whole, self.flow(i, 3), self.sibling)

    def finish(self, i):
        self.links.arrived(self.full.at[1 - self.half], self.flow(i, 3), self.sibling)
        self.spread_sent(i)


class AdapterReduce:
    def __init__(self, links, base, levels, g, s1, h, xb, h2, zb, p3, yb, hb):
        self.links, self.base, self.levels = links, base, levels
        self.g, self.s1, self.h, self.xb, self.h2 = g, s1, h, xb, h2
        self.zb, self.p3, self.yb, self.hb = zb, p3, yb, hb
        self.half = lax.rem(links.t, 2)
        self.groups = [(links.row ^ (GROUP << level), links.t) for level in range(levels)]

    def beside(self):
        return self.links.copy(
            self.g.at[1 - self.half], self.s1, self.base, self.links.tp_peer(1)
        )

    def side(self):
        links = self.links
        return links.copy(self.h.at[1 - links.b], self.xb, self.base + 1, links.side_peer())

    def line(self, d):
        links = self.links
        return links.copy(
            self.h2.at[lax.rem(links.a + d, LINE)],
            self.zb.at[d - 1],
            self.base + 1 + d,
            links.line_peer(d),
        )

    def over(self):
        return self.links.copy(self.p3, self.yb, self.base + 1 + LINE, self.links.tp_peer(2))

    def group(self, level):
        return self.links.copy(
            self.hb.at[2 * level],
            self.hb.at[2 * level + 1],
            self.base + 2 + LINE + level,
            self.groups[level],
        )

    def phase(self, number):
        if number == 0:
            self.beside().start()
        elif number == 1:
            self.beside().wait()
            self.h[...] = (self.g[self.half].astype(f32) + self.s1[...].astype(f32)).astype(bf16)
            self.side().start()
        elif number == 2:
            self.side().wait()
            self.h2[...] = (
                self.h[self.links.b].astype(f32) + self.xb[...].astype(f32)
            ).astype(bf16)
            for d in range(1, LINE):
                self.line(d).start()
        elif number == 3:
            for d in range(1, LINE):
                self.line(d).wait()
            total = self.h2[self.links.a].astype(f32)
            for d in range(1, LINE):
                total = total + self.zb[d - 1].astype(f32)
            self.p3[...] = total.astype(bf16)
            self.over().start()

    def result(self):
        self.over().wait()
        value = self.p3[...].astype(f32) + self.yb[...].astype(f32)
        for level in range(self.levels):
            self.hb[2 * level] = value.astype(bf16)
            self.group(level).start()
            self.group(level).wait()
            value = self.hb[2 * level].astype(f32) + self.hb[2 * level + 1].astype(f32)
        return value.astype(bf16)


class RowGather:
    FLOWS = 1 + 2 * 4

    def __init__(self, links, base, own, full):
        self.links, self.base, self.own, self.full = links, base, own, full
        self.far, self.last = links.t ^ 2, links.t ^ 3
        self.sibling, self.over = links.tp_peer(1), links.tp_peer(2)

    def at(self, c):
        rows = self.own.shape[0] // CHUNKS
        return pl.ds(c * rows, rows)

    def beside_copy(self):
        return self.links.copy(self.own, self.full.at[self.links.t], self.base, self.sibling)

    def over_copy(self, c):
        at = self.at(c)
        return self.links.copy(
            self.own.at[at], self.full.at[self.links.t, at], self.base + 1 + c, self.over
        )

    def pass_copy(self, c):
        part = self.full.at[self.far, self.at(c)]
        return self.links.copy(part, part, self.base + 1 + CHUNKS + c, self.sibling)

    def start_beside(self):
        self.beside_copy().start()

    def start_over(self):
        for c in range(CHUNKS):
            self.over_copy(c).start()

    def came_beside(self):
        self.links.arrived(self.full.at[self.links.t ^ 1], self.base, self.sibling)

    def came_over(self):
        for c in range(CHUNKS):
            self.links.arrived(
                self.full.at[self.far, self.at(c)], self.base + 1 + c, self.over
            )
            self.pass_copy(c).start()

    def came_last(self):
        for c in range(CHUNKS):
            self.links.arrived(
                self.full.at[self.last, self.at(c)], self.base + 1 + CHUNKS + c, self.sibling
            )

    def sent(self):
        self.beside_copy().wait_send()
        for c in range(CHUNKS):
            self.over_copy(c).wait_send()
            self.pass_copy(c).wait_send()


class RowScatter:
    FLOWS = 2 + 4

    def __init__(self, links, base, part, near, near_far, mid, far):
        self.links, self.base, self.part = links, base, part
        self.near, self.near_far, self.mid, self.far = near, near_far, mid, far
        self.sibling, self.over = links.tp_peer(1), links.tp_peer(2)

    def at(self, c):
        rows = self.near.shape[0] // CHUNKS
        return pl.ds(c * rows, rows)

    def first_copy(self):
        return self.links.copy(
            self.part.at[self.links.t ^ 3], self.near_far, self.base, self.sibling
        )

    def second_copy(self):
        return self.links.copy(
            self.part.at[self.links.t ^ 1], self.near, self.base + 1, self.sibling
        )

    def over_copy(self, c):
        at = self.at(c)
        return self.links.copy(
            self.mid.at[at], self.far.at[at], self.base + 2 + c, self.over
        )

    def send_over(self):
        self.links.arrived(self.near_far, self.base, self.sibling)
        for c in range(CHUNKS):
            at = self.at(c)
            self.mid[at] = (
                self.part[self.links.t ^ 2, at].astype(f32) + self.near_far[at].astype(f32)
            ).astype(bf16)
            self.over_copy(c).start()

    def came_beside(self):
        self.links.arrived(self.near, self.base + 1, self.sibling)

    def came_over(self, c):
        at = self.at(c)
        self.links.arrived(self.far.at[at], self.base + 2 + c, self.over)
        return (
            self.part[self.links.t, at].astype(f32)
            + self.near[at].astype(f32)
            + self.far[at].astype(f32)
        )

    def sent(self):
        self.first_copy().wait_send()
        self.second_copy().wait_send()
        for c in range(CHUNKS):
            self.over_copy(c).wait_send()


def cut(refs, *counts):
    out, at = [], 0
    for count in counts:
        out.append(refs[at : at + count])
        at += count
    return out


def self_forward_kernel(prefix_len, count, *refs):
    ins, own, outs, full, stage, scratch = cut(refs, 10, count, 8, count, count + 1, 13)
    x, memory, pre_cross, wq, wk, wv, wo, pre, seg_col, seg_row = ins
    q_out, k_out, v_out, a_out, l_out, resid, m_full, pre_full = outs
    x_full, part, kept, bias, near, near_far, mid, far, send, recv, local, m_local, pre_local = scratch
    links = Links(send, recv)
    t = links.t
    block, lanes = x.shape[0], q_out.shape[1]
    weights = WeightGather(links, 0, 1, own, full, stage[:count], local)
    at = count * FLOWS
    x_rows = RowGather(links, at, x, x_full)
    m_rows = RowGather(links, at + RowGather.FLOWS, memory, m_full)
    at += 2 * RowGather.FLOWS
    sums = RowScatter(links, at, part, near, near_far, mid, far)
    at += RowScatter.FLOWS
    m_in = pltpu.make_async_copy(memory, stage[count], m_local.at[0])
    m_keep = pltpu.make_async_copy(stage[count], m_full.at[t], m_local.at[1])
    pre_keep = pltpu.make_async_copy(pre_cross, pre_full.at[t], pre_local.at[0])
    pre_sends = [
        links.copy(pre_cross, pre_full.at[t], at + m - 1, links.tp_peer(m)) for m in (1, 2, 3)
    ]

    kept[...] = jnp.zeros_like(kept)
    greet(
        [links.tp_peer(m) for m in (1, 2, 3)]
        + [links.line_peer(d) for d in range(1, LINE)]
        + [links.side_peer()]
    )
    x_rows.start_over()
    x_rows.start_beside()
    m_rows.start_beside()
    m_in.start()
    pre_keep.start()
    for one in pre_sends:
        one.start()
    for i in range(count):
        weights.start_beside(i)

    for target, at in ((k_out, 0), (v_out, PRE_PACK)):
        target[0:PRE_PACK] = pre[at : at + PRE_PACK]
        target[PRE_PACK:PRE] = jnp.zeros((PRE - PRE_PACK, lanes), bf16)

    def project(rows, index):
        at = pl.multiple_of(index * block, block)
        q_out[pl.ds(at, block)] = (SCALE * nn(rows, wq[...])).astype(bf16)
        k_out[pl.ds(PRE + at, block)] = nn(rows, wk[...]).astype(bf16)
        v_out[pl.ds(PRE + at, block)] = nn(rows, wv[...]).astype(bf16)

    project(x[...], t)
    x_rows.came_beside()
    project(x_full[t ^ 1], t ^ 1)
    m_in.wait()
    m_keep.start()
    for i in range(count):
        weights.keep_own(i)
    x_rows.came_over()
    for i in range(count):
        weights.start_over(i)
    m_rows.start_over()
    project(x_full[t ^ 2], t ^ 2)
    x_rows.came_last()
    project(x_full[t ^ 3], t ^ 3)

    @pl.loop(0, 4)
    def _(order):
        here = t ^ (3 - order)
        for i in range(4):
            keys = PRE + (i + 1) * block
            shape = (block, keys)

            @pl.when(here == i)
            def _():
                bias[:, 0:keys] = mask_bias(
                    seg_col[i * block : (i + 1) * block],
                    seg_row[:, 0:keys],
                    i * block + lax.broadcasted_iota(jnp.int32, shape, 0),
                    lax.broadcasted_iota(jnp.int32, shape, 1),
                    prefix_len,
                )

                @pl.loop(0, lanes // PAIR)
                def _(j):
                    cols = pl.ds(pl.multiple_of(j * PAIR, PAIR), PAIR)
                    mixture, logs = pair_forward(
                        q_out[i * block : (i + 1) * block, cols],
                        k_out[0:keys, cols],
                        v_out[0:keys, cols],
                        bias[:, 0:keys],
                    )
                    a_out[i, :, cols] = mixture
                    keep_logs(kept, logs, j)

        l_out[here] = kept[...].T[0:8]
        part[here] = nn(a_out[here], wo[...]).astype(bf16)

        @pl.when(order == 0)
        def _():
            sums.first_copy().start()
            for i in range(count):
                weights.came_over(i)

        @pl.when(order == 1)
        def _():
            sums.send_over()

        @pl.when(order == 2)
        def _():
            sums.second_copy().start()
            for i in range(count):
                weights.along(i, 0)

    for i in range(count):
        weights.along(i, 1)
    m_rows.came_over()
    for i in range(count):
        weights.along(i, 2)
    sums.came_beside()
    for i in range(count - 1):
        weights.complete(i)
    for c in range(CHUNKS):
        rows = sums.at(c)
        resid[rows] = x[rows].astype(f32) + sums.came_over(c)
    weights.complete(count - 1)
    m_rows.came_beside()
    m_rows.came_last()
    for m, one in zip((1, 2, 3), pre_sends):
        links.copy(
            pre_full.at[t ^ m], pre_full.at[t ^ m], small_base(count) + m - 1, links.tp_peer(m)
        ).wait_recv()
        one.wait_send()
    for i in range(count):
        weights.finish(i)
    x_rows.sent()
    m_rows.sent()
    sums.sent()
    m_keep.wait()
    pre_keep.wait()


def small_base(count):
    return count * FLOWS + 2 * RowGather.FLOWS + RowScatter.FLOWS


def self_forward(prefix_len, x, memory, pre_cross, own_weights, pre, seg_col, seg_row, weights):
    n = 4
    count = len(weights)
    block, width = x.shape
    lanes = own_weights[0].shape[1]
    seq = n * block
    out = jax.ShapeDtypeStruct
    flows = small_base(count) + 3
    outs = (
        out((seq, lanes), bf16),
        out((PRE + seq, lanes), bf16),
        out((PRE + seq, lanes), bf16),
        out((n, block, lanes), bf16),
        out((n, 8, block), f32),
        out((block, width), f32),
        out((n, block, width), bf16),
        out((n,) + pre_cross.shape, bf16),
    ) + tuple(out((n,) + a.shape, a.dtype) for a in weights)
    a = pl.BlockSpec(memory_space=pltpu.HBM)
    rows = VMEM((block, width), bf16)
    given = (x, memory, pre_cross, *own_weights, pre, seg_col, seg_row)
    in_specs = [whole_spec(g.shape) for g in given]
    in_specs[1] = a
    return pl.pallas_call(
        functools.partial(self_forward_kernel, prefix_len, count),
        grid=(1,),
        out_shape=outs,
        in_specs=in_specs + [a] * count,
        out_specs=[whole_spec(o.shape) for o in outs[:6]] + [a] * (2 + count),
        scratch_shapes=[VMEM(w.shape, w.dtype) for w in weights]
        + [rows]
        + [
            VMEM((n, block, width), bf16),
            VMEM((n, block, width), bf16),
            VMEM((block, 128), f32),
            VMEM((block, PRE + seq), f32),
            rows,
            rows,
            rows,
            rows,
            pltpu.SemaphoreType.DMA((flows,)),
            pltpu.SemaphoreType.DMA((flows,)),
            pltpu.SemaphoreType.DMA((2 * count,)),
            pltpu.SemaphoreType.DMA((2,)),
            pltpu.SemaphoreType.DMA((1,)),
        ],
        compiler_params=pltpu.CompilerParams(
            collective_id=0, has_side_effects=True, vmem_limit_bytes=48 << 20
        ),
        name="self_forward",
    )(*given, *weights)


def doublings(count):
    levels = 0
    while (1 << levels) < count:
        levels += 1
    return levels


def cross_backward_kernel(
    prefix_len, levels, dr2, v1, q, k, v, a, logs, wq, wk, wv, wo, seg_row, seg_col, gain, vecs_in, g,
    dr1, dr1_full, dm, pre_grad, vecs, piece,
    dr1_low, dr2_low, bias, da, dq, dk, dv, total, s1, h, xb, h2, zb, p3, yb, hb, send, recv, local,
):
    step = pl.program_id(0)
    steps = pl.num_programs(0)
    block, lanes = q.shape[1:]
    keys = k.shape[1]
    links = Links(send, recv)
    t = links.t
    rows = RowGather(links, 0, dr1_low, dr1_full)
    keep = pltpu.make_async_copy(dr1_low, dr1_full.at[t], local.at[0])
    reduce = AdapterReduce(links, RowGather.FLOWS, levels, g, s1, h, xb, h2, zb, p3, yb, hb)

    @pl.when(step == 0)
    def _():
        greet(
            [links.tp_peer(1), links.tp_peer(2)]
            + [links.line_peer(d) for d in range(1, LINE)]
            + [links.side_peer()]
            + reduce.groups
        )
        reduce.phase(0)
        dr2_low[...] = dr2[...].astype(bf16)
        total[...] = jnp.zeros_like(total)
        bias[...] = mask_bias(
            seg_row[...],
            seg_col[...],
            None,
            lax.broadcasted_iota(jnp.int32, (keys, block), 0),
            prefix_len,
        )

    da[...] = nt(dr2_low[...], wo[0]).astype(bf16)

    @pl.loop(0, lanes // PAIR)
    def _(j):
        cols = pl.ds(pl.multiple_of(j * PAIR, PAIR), PAIR)
        dq_pair, dk_pair, dv_pair = pair_backward(
            q[0, :, cols],
            k[0, :, cols],
            v[0, :, cols],
            a[0, :, cols],
            da[:, cols],
            [logs[0, pl.ds(2 * j + i, 1)] for i in range(2)],
            bias[...],
        )
        dq[:, cols] = dq_pair
        pre_grad[0, 0:PRE_PACK, cols] = dk_pair[0:PRE_PACK]
        pre_grad[0, PRE_PACK : 2 * PRE_PACK, cols] = dv_pair[0:PRE_PACK]
        dk[step, :, cols] = dk_pair[PRE:].astype(bf16)
        dv[step, :, cols] = dv_pair[PRE:].astype(bf16)

    total[...] += nt(dq[...], wq[0])
    for number in range(3):

        @pl.when(step == number)
        def _():
            reduce.phase(number + 1)

    @pl.when(step == steps - 1)
    def _():
        n, spread = norm_parts(v1[...])
        grad, gain_part, shift_part = norm_back(
            dr2[...] + SCALE * total[...], gain[0:1], n, spread
        )
        dr1[...] = grad
        dr1_low[...] = grad.astype(bf16)
        rows.start_over()
        rows.start_beside()
        keep.start()
        vecs[...] = vecs_in[...]
        vecs[0:1] = gain_part
        vecs[3:4] = shift_part
        piece[...] = reduce.result()

        @pl.loop(0, 4)
        def _(i):
            at = pl.ds(pl.multiple_of(i * block, block), block)
            value = None
            for shard in range(dk.shape[0]):
                term = nt(dk[shard, at], wk[shard]) + nt(dv[shard, at], wv[shard])
                value = term if value is None else value + term
            dm[i] = value.astype(bf16)

        rows.came_over()
        rows.came_beside()
        rows.came_last()
        rows.sent()
        keep.wait()


def cross_backward(
    prefix_len, row_count, dr2, v1, q, k, v, a, logs, weights, seg_row, seg_col, gain, vecs, grads
):
    wq, wk, wv, wo = weights
    n, block, lanes = q.shape
    keys = k.shape[1]
    width = dr2.shape[1]
    levels = doublings(row_count // GROUP)
    part = grads.shape[1] // GROUP
    half = (2, LINE, part, width)
    g = grads.reshape((2,) + half)
    out = jax.ShapeDtypeStruct
    outs = (
        out((block, width), f32),
        out((n, block, width), bf16),
        out((n, block, width), bf16),
        out((n, 2 * PRE_PACK, lanes), f32),
        out((8, width), f32),
        out((part, width), bf16),
    )
    out_specs = [whole_spec(o.shape) for o in outs]
    out_specs[1] = pl.BlockSpec(memory_space=pltpu.HBM)
    out_specs[3] = shard_spec(outs[3].shape)
    flows = RowGather.FLOWS + 2 + LINE + levels
    return pl.pallas_call(
        functools.partial(cross_backward_kernel, prefix_len, levels),
        grid=(n,),
        out_shape=outs,
        in_specs=[whole_spec(dr2.shape), whole_spec(v1.shape)]
        + [shard_spec(x.shape) for x in (q, k, v, a, logs, wq)]
        + [whole_spec(wk.shape), whole_spec(wv.shape), shard_spec(wo.shape)]
        + [whole_spec(x.shape) for x in (seg_row, seg_col, gain, vecs, g)],
        out_specs=out_specs,
        scratch_shapes=[
            VMEM((block, width), bf16),
            VMEM((block, width), bf16),
            VMEM((keys, block), f32),
            VMEM((block, lanes), bf16),
            VMEM((block, lanes), bf16),
            VMEM((n, keys - PRE, lanes), bf16),
            VMEM((n, keys - PRE, lanes), bf16),
            VMEM((block, width), f32),
            VMEM(half, bf16),
            VMEM(half, bf16),
            VMEM(half[1:], bf16),
            VMEM(half[1:], bf16),
            VMEM((LINE - 1, part, width), bf16),
            VMEM((part, width), bf16),
            VMEM((part, width), bf16),
            VMEM((max(1, 2 * levels), part, width), bf16),
            pltpu.SemaphoreType.DMA((flows,)),
            pltpu.SemaphoreType.DMA((flows,)),
            pltpu.SemaphoreType.DMA((1,)),
        ],
        compiler_params=pltpu.CompilerParams(
            collective_id=2, has_side_effects=True, vmem_limit_bytes=58 << 20
        ),
        name="cross_backward",
    )(dr2, v1, q, k, v, a, logs, wq, wk, wv, wo, seg_row, seg_col, gain, vecs, g)


class Doubling:
    def __init__(self, links, base, levels, outgo, income):
        self.links, self.base, self.levels = links, base, levels
        self.outgo, self.income = outgo, income

    def move(self, level):
        return self.links.copy(
            self.outgo.at[level],
            self.income.at[level],
            self.base + level,
            (self.links.row ^ (1 << level), self.links.t),
        )

    def begin(self, value):
        self.outgo[0] = value
        self.move(0).start()

    def value(self, level):
        self.move(level).wait()
        return self.outgo[level] + self.income[level]

    def step(self, level):
        value = self.value(level)
        self.outgo[level + 1] = value
        self.move(level + 1).start()


def self_backward_kernel(
    prefix_len, levels, dr1_full, dr1, q, k, v, a, logs, wq, wk, wv, wo, seg_row, seg_col,
    dm, piece, cross, vecs,
    tokens_grad, memory_grad, adapter, self_pre, sums,
    part, bias, da, dq, dk, dv, near, near_far, mid, far, m_near, m_near_far, m_mid, m_far,
    cross_in, vecs_in, outgo, income, pre_outgo, pre_income, send, recv,
):
    seq, lanes = q.shape
    block = seq // 4
    links = Links(send, recv)
    t = links.t
    at = 0
    spread = AdapterSpread(links, at, adapter)
    at += FLOWS
    m_sums = RowScatter(links, at, dm, m_near, m_near_far, m_mid, m_far)
    at += RowScatter.FLOWS
    x_sums = RowScatter(links, at, part, near, near_far, mid, far)
    at += RowScatter.FLOWS
    total = Doubling(links, at, levels, outgo, income)
    at += levels
    pre_total = Doubling(links, at, levels, pre_outgo, pre_income)
    at += levels

    def exchange(m):
        peer = links.tp_peer(m)
        return (
            links.copy(cross.at[t ^ m], cross_in.at[t], at + 2 * (m - 1), peer),
            links.copy(vecs, vecs_in.at[t], at + 2 * (m - 1) + 1, peer),
        )

    greet(
        [links.tp_peer(m) for m in (1, 2, 3)]
        + [links.line_peer(d) for d in range(1, LINE)]
        + [links.side_peer()]
        + [(links.row ^ (1 << level), t) for level in range(doublings(GROUP), levels)]
    )
    m_sums.first_copy().start()
    m_sums.second_copy().start()
    for m in (1, 2, 3):
        for one in exchange(m):
            one.start()
    adapter[spread.half, links.b, links.a] = piece[...]
    spread.spread(0)
    cross_in[t] = cross[t]
    vecs_in[t] = vecs[...]
    dk[...] = jnp.zeros_like(dk)
    dv[...] = jnp.zeros_like(dv)

    for i in reversed(range(4)):
        rows = slice(i * block, (i + 1) * block)
        keys = PRE + (i + 1) * block
        shape = (keys, block)
        bias[0:keys] = mask_bias(
            seg_row[:, rows],
            seg_col[0:keys],
            i * block + lax.broadcasted_iota(jnp.int32, shape, 1),
            lax.broadcasted_iota(jnp.int32, shape, 0),
            prefix_len,
        )
        da[...] = nt(dr1_full[i], wo[...]).astype(bf16)

        @pl.loop(0, lanes // PAIR)
        def _(j):
            cols = pl.ds(pl.multiple_of(j * PAIR, PAIR), PAIR)
            dq_pair, dk_pair, dv_pair = pair_backward(
                q[rows, cols],
                k[0:keys, cols],
                v[0:keys, cols],
                a[i, :, cols],
                da[:, cols],
                [logs[i, pl.ds(2 * j + o, 1)] for o in range(2)],
                bias[0:keys],
            )
            dq[:, cols] = dq_pair
            dk[0:keys, cols] += dk_pair
            dv[0:keys, cols] += dv_pair

        done = slice(PRE + i * block, PRE + (i + 1) * block)
        part[i] = (
            SCALE * nt(dq[...], wq[...])
            + nt(dk[done].astype(bf16), wk[...])
            + nt(dv[done].astype(bf16), wv[...])
        ).astype(bf16)
        if i == 3:
            m_sums.send_over()
            for m in (1, 2, 3):
                peer = links.tp_peer(m)
                links.arrived(cross_in.at[t ^ m], at + 2 * (m - 1), peer)
                links.arrived(vecs_in.at[t ^ m], at + 2 * (m - 1) + 1, peer)
            value = vecs_in[0] + vecs_in[1] + vecs_in[2] + vecs_in[3]
            pieces = [cross_in[0] + cross_in[1] + cross_in[2] + cross_in[3]] + [
                value[:, o * lanes : (o + 1) * lanes] for o in range(vecs.shape[1] // lanes)
            ]
            total.begin(jnp.concatenate(pieces, axis=0))
        else:
            spread.along(0, 2 - i)
            if i > 0:
                total.step(2 - i)

    x_sums.first_copy().start()
    x_sums.second_copy().start()
    pre_total.begin(jnp.concatenate([dk[0:PRE_PACK], dv[0:PRE_PACK]], axis=0))
    spread.complete(0)
    x_sums.send_over()
    for level in range(2, levels - 1):
        total.step(level)
    sums[...] = total.value(levels - 1)
    for level in range(levels - 1):
        pre_total.step(level)
    m_sums.came_beside()
    for c in range(CHUNKS):
        memory_grad[m_sums.at(c)] = m_sums.came_over(c).astype(bf16)
    x_sums.came_beside()
    for c in range(CHUNKS):
        rows = x_sums.at(c)
        tokens_grad[rows] = (dr1[rows] + x_sums.came_over(c)).astype(bf16)
    self_pre[...] = pre_total.value(levels - 1)
    spread.finish(0)
    m_sums.sent()
    x_sums.sent()
    for m in (1, 2, 3):
        for one in exchange(m):
            one.wait_send()


def self_backward(
    prefix_len, row_count, dr1_full, dr1, q, k, v, a, logs, weights, seg_row, seg_col,
    dm, piece, cross, vecs,
):
    n, block, width = dr1_full.shape
    seq, lanes = q.shape
    levels = doublings(row_count)
    packed = 2 * PRE_PACK
    height = packed + vecs.shape[0] * vecs.shape[1] // lanes
    out = jax.ShapeDtypeStruct
    outs = (
        out((block, width), bf16),
        out((block, width), bf16),
        out((2, 2, LINE) + piece.shape, bf16),
        out((packed, lanes), f32),
        out((height, lanes), f32),
    )
    given = (
        (dr1_full, dr1, q, k, v, a, logs) + tuple(weights) + (seg_row, seg_col, dm, piece, cross, vecs)
    )
    rows = VMEM((block, width), bf16)
    flows = FLOWS + 2 * RowScatter.FLOWS + 2 * levels + 6
    return pl.pallas_call(
        functools.partial(self_backward_kernel, prefix_len, levels),
        grid=(1,),
        out_shape=outs,
        in_specs=[whole_spec(x.shape) for x in given],
        out_specs=[whole_spec(x.shape) for x in outs[:2]]
        + [pl.BlockSpec(memory_space=VMEM)]
        + [whole_spec(x.shape) for x in outs[3:]],
        scratch_shapes=[
            VMEM((n, block, width), bf16),
            VMEM((PRE + seq, block), f32),
            VMEM((block, lanes), bf16),
            VMEM((block, lanes), bf16),
            VMEM((PRE + seq, lanes), f32),
            VMEM((PRE + seq, lanes), f32),
        ]
        + [rows] * 8
        + [
            VMEM((n, packed, lanes), f32),
            VMEM((n,) + vecs.shape, f32),
            VMEM((levels, height, lanes), f32),
            VMEM((levels, height, lanes), f32),
            VMEM((levels, packed, lanes), f32),
            VMEM((levels, packed, lanes), f32),
            pltpu.SemaphoreType.DMA((flows,)),
            pltpu.SemaphoreType.DMA((flows,)),
        ],
        compiler_params=pltpu.CompilerParams(
            collective_id=3, has_side_effects=True, vmem_limit_bytes=58 << 20
        ),
        name="self_backward",
    )(*given)


def per_device(
    row_count,
    tokens, memory, out_grad, dec_segments, src_segments,
    self_query, self_key, self_value, self_out,
    cross_query, cross_key, cross_value, cross_out,
    ffn_in, ffn_out, adapt_down, adapt_down_bias, adapt_up, adapt_up_bias,
    self_prefix, cross_prefix, norm_gain, norm_shift,
):
    seq_local, _, width = tokens.shape
    prefix_len = self_prefix.shape[1]
    lanes = self_query.shape[1]
    adapt = adapt_down.shape[1]
    t = lax.axis_index("tp")
    x, mem, grad_in = (a.reshape(seq_local, width) for a in (tokens, memory, out_grad))

    def pack_prefix(prefix):
        return jnp.pad(prefix, ((0, 0), (0, PRE_PACK - prefix_len), (0, 0))).reshape(
            2 * PRE_PACK, lanes
        )

    def unpack_prefix(packed):
        return packed.reshape(2, PRE_PACK, lanes)[:, :prefix_len]

    seq = dec_segments.shape[1]
    never = jnp.full((1, PRE), -1, jnp.int32)
    dec_row = jnp.concatenate([never, dec_segments], axis=1)
    src_row = jnp.concatenate([never, src_segments], axis=1)
    dec_q = dec_segments
    own_q = lax.dynamic_slice(dec_segments, (0, t * seq_local), (1, seq_local))

    q1, k1, v1_heads, a1, logs1, resid_one, m_full, pre_full, *gathered = self_forward(
        prefix_len, x, mem, pack_prefix(cross_prefix),
        (self_query, self_key, self_value, self_out),
        pack_prefix(self_prefix), dec_q.reshape(seq, 1), dec_row,
        (cross_query, cross_key, cross_value, cross_out, ffn_in),
    )
    cross_weights = gathered[:4]
    w_in = gathered[4]
    m_full = m_full.reshape(seq, width)
    q2, k2, v2_heads, a2, logs2, resid_two, w_out = cross_forward(
        prefix_len, resid_one, m_full, cross_weights, pre_full,
        own_q.reshape(seq_local, 1), src_row, norm_gain, norm_shift, ffn_out,
    )
    output, dr2, grads, vecs = feed_forward(
        resid_two, grad_in, w_in, w_out,
        adapt_down, adapt_down_bias.reshape(1, adapt), adapt_up, adapt_up_bias.reshape(1, width),
        norm_gain, norm_shift,
    )
    dr1, dr1_full, dm, cross_pre_part, vecs, piece = cross_backward(
        prefix_len, row_count, dr2, resid_one, q2, k2, v2_heads, a2, logs2, cross_weights,
        own_q, src_row.reshape(PRE + seq, 1), norm_gain, vecs, grads,
    )
    tokens_grad, memory_grad, adapter, self_pre, sums = self_backward(
        prefix_len, row_count, dr1_full, dr1, q1, k1, v1_heads, a1, logs1,
        (self_query, self_key, self_value, self_out), dec_q, dec_row.reshape(PRE + seq, 1),
        dm, piece, cross_pre_part, vecs,
    )
    adapter = adapter.reshape(2 * adapt, width)
    cross_pre = sums[: 2 * PRE_PACK]
    vecs = jnp.moveaxis(sums[2 * PRE_PACK :].reshape(-1, 8, lanes), 0, 1).reshape(8, width)
    local = tokens.shape
    return (
        output.reshape(local),
        tokens_grad.reshape(local),
        memory_grad.reshape(local),
        unpack_prefix(self_pre),
        unpack_prefix(cross_pre),
        vecs[0:3],
        vecs[3:6],
        adapter[adapt:].T.astype(f32),
        vecs[7, :adapt],
        adapter[:adapt].astype(f32),
        vecs[6],
    )


def solution(mesh):
    placed = (
        (P("tp", "rows", None),) * 3
        + (P("rows", None),) * 2
        + (P(None, "tp"),) * 3
        + (P("tp", None),)
        + (P(None, "tp"),) * 3
        + (P("tp", None),)
        + (P(None, "tp"), P("tp", None))
        + (P(),) * 4
        + (P(None, None, "tp"),) * 2
        + (P(),) * 2
    )
    return jax.shard_map(
        functools.partial(per_device, mesh.shape["rows"]),
        mesh=mesh,
        in_specs=placed,
        out_specs=(P("tp", "rows", None),) * 3 + (P(None, None, "tp"),) * 2 + (P(),) * 6,
        check_vma=False,
    )
```

```python
import functools

import jax
import jax.numpy as jnp
from jax import lax
from jax.experimental import pallas as pl
from jax.experimental.pallas import tpu as pltpu
from jax.sharding import PartitionSpec as P

HEAD = 64
PAIR = 2 * HEAD
PRE = 128
PRE_PACK = 32
GROUP = 8
LINE = 4
MASKED = -1000000000.0
EPSILON = 1e-05
VMEM_BYTES = 62 << 20
SCALE = HEAD**-0.5
f32 = jnp.float32
bf16 = jnp.bfloat16
MESH = pl.DeviceIdType.MESH
VMEM = pltpu.VMEM
ANY = pl.ANY


def nn(a, b):
    return lax.dot_general(a, b, (((1,), (0,)), ((), ())), preferred_element_type=f32)


def nt(a, b):
    return lax.dot_general(a, b, (((1,), (1,)), ((), ())), preferred_element_type=f32)


def tn(a, b):
    return lax.dot_general(a, b, (((0,), (0,)), ((), ())), preferred_element_type=f32)


def gelu_parts(v):
    phi = 0.5 + 0.5 * lax.erf(v * (0.5**0.5))
    slope = phi + v * (jnp.exp(-0.5 * v * v) * 0.3989422804014327)
    return v * phi, slope


def norm_parts(v):
    centered = v - jnp.mean(v, axis=-1, keepdims=True)
    spread = lax.rsqrt(jnp.mean(centered * centered, axis=-1, keepdims=True) + EPSILON)
    return centered * spread, spread


def norm_back(dy, gain, n, spread):
    dn = dy * gain
    dv = spread * (
        dn - jnp.mean(dn, axis=-1, keepdims=True) - n * jnp.mean(dn * n, axis=-1, keepdims=True)
    )
    return dv, jnp.sum(dy * n, axis=0, keepdims=True), jnp.sum(dy, axis=0, keepdims=True)


def lane_half(shape, h):
    return (lax.broadcasted_iota(jnp.int32, shape, 1) // HEAD) == h


def column(row):
    return jnp.broadcast_to(row, (8, row.shape[1])).T[:, 0:1]


def prefix_bias(shape, axis, prefix_len):
    return jnp.where(lax.broadcasted_iota(jnp.int32, shape, axis) < prefix_len, 0.0, MASKED)


def mask_bias(seg_q, seg_k, shape, key_axis, first_query):
    keep = seg_q == seg_k
    if first_query is not None:
        query = first_query + lax.broadcasted_iota(jnp.int32, shape, 1 - key_axis)
        keep = keep & (lax.broadcasted_iota(jnp.int32, shape, key_axis) <= query)
    return jnp.where(keep, 0.0, MASKED)


def pair_forward(q_pair, k_pair, v_pair, bias):
    outs, logs = [], []
    for h in range(2):
        half = lane_half(q_pair.shape, h)
        scores = nt(jnp.where(half, q_pair, jnp.zeros_like(q_pair)), k_pair) + bias
        top = jnp.max(scores, axis=1, keepdims=True)
        e = jnp.exp(scores - top)
        total = jnp.sum(e, axis=1, keepdims=True)
        outs.append(nn(e.astype(bf16), v_pair) * (1.0 / total))
        logs.append(top + jnp.log(total))
    return jnp.where(lane_half(outs[0].shape, 0), outs[0], outs[1]).astype(bf16), logs


def keep_logs(kept, logs, j):
    lane = lax.broadcasted_iota(jnp.int32, kept.shape, 1)
    for h in range(2):
        kept[...] = jnp.where(lane == 2 * j + h, logs[h], kept[...])


def pair_backward(q_pair, k_pair, v_pair, a_pair, da_pair, logs, bias_t):
    k_turned = k_pair.T
    prod = da_pair.astype(f32) * a_pair.astype(f32)
    prod_high = prod.astype(bf16)
    prod_low = (prod - prod_high.astype(f32)).astype(bf16)
    pick = (
        lax.broadcasted_iota(jnp.int32, (8, PAIR), 1) // HEAD
        == lax.broadcasted_iota(jnp.int32, (8, PAIR), 0)
    ).astype(bf16)
    delta = nt(pick, prod_high) + nt(pick, prod_low)
    dk = dv = None
    dq = []
    for h in range(2):
        half = lane_half(q_pair.shape, h)
        q = jnp.where(half, q_pair, jnp.zeros_like(q_pair))
        da = jnp.where(half, da_pair, jnp.zeros_like(da_pair))
        p = jnp.exp(nt(k_pair, q) + (bias_t - logs[h]))
        ds = (p * (nt(v_pair, da) - delta[h : h + 1])).astype(bf16)
        dv_h = nn(p.astype(bf16), da)
        dk_h = nn(ds, q)
        dk = dk_h if dk is None else dk + dk_h
        dv = dv_h if dv is None else dv + dv_h
        dq.append(nn(k_turned[h * HEAD : (h + 1) * HEAD], ds))
    return jnp.concatenate(dq, axis=0).T.astype(bf16), dk, dv


def cross_forward_kernel(
    prefix_len, v1, memory, wq, wk, wv, wo, pre, dec, src, gain, shift, own,
    q_out, k_out, v_out, a_out, l_out, v2, full, n1_low, bias, kept, stage, send, recv, local,
):
    step = pl.program_id(0)
    block, lanes = q_out.shape[1:]
    keys = k_out.shape[1]
    links = Links(send, recv)
    weights = WeightGather(links, 0, [2, 2], *chunked([own], [full], [stage]), local)

    @pl.when(step == 0)
    def _():
        greet(
            [links.tp_peer(1), links.tp_peer(2)]
            + [links.line_peer(d) for d in range(1, LINE)]
            + [links.side_peer()]
        )
        for i in range(2):
            weights.start_over(i)
        for i in range(2):
            weights.start_beside(i)

    @pl.when(step == 0)
    def _():
        n, _ = norm_parts(v1[...])
        normed = n * gain[0:1] + shift[0:1]
        v2[...] = normed
        n1_low[...] = normed.astype(bf16)
        kept[...] = jnp.zeros_like(kept)
        own_queries = dec[:, pl.ds(pl.multiple_of(links.t * block, block), block)]
        bias[:, 0:PRE] = prefix_bias((block, PRE), 1, prefix_len)
        bias[:, PRE:] = mask_bias(
            column(own_queries), src[...], (block, keys - PRE), 1, None
        )

    q_out[0] = (SCALE * nn(n1_low[...], wq[0])).astype(bf16)
    for target, at in ((k_out, 0), (v_out, PRE_PACK)):
        target[0, 0:PRE_PACK] = pre[0, at : at + PRE_PACK]
        target[0, PRE_PACK:PRE] = jnp.zeros((PRE - PRE_PACK, lanes), bf16)

    @pl.loop(0, (keys - PRE) // block)
    def _(i):
        at = pl.multiple_of(i * block, block)
        rows = memory[pl.ds(at, block)]
        k_out[0, pl.ds(PRE + at, block)] = nn(rows, wk[0]).astype(bf16)
        v_out[0, pl.ds(PRE + at, block)] = nn(rows, wv[0]).astype(bf16)

    events = {
        0: [lambda: weights.keep_own(0), lambda: weights.keep_own(1), lambda: weights.came_over(0)],
        2: [lambda: weights.came_over(1)],
        3: [lambda: weights.along(0, 0)],
        4: [lambda: weights.along(1, 0), lambda: weights.along(0, 1)],
        5: [lambda: weights.along(1, 1)],
        6: [lambda: weights.along(0, 2)],
        7: [lambda: weights.along(1, 2)],
    }
    for j in range(lanes // PAIR):
        cols = slice(j * PAIR, (j + 1) * PAIR)
        mixture, logs = pair_forward(
            q_out[0, :, cols], k_out[0, :, cols], v_out[0, :, cols], bias[...]
        )
        a_out[0, :, cols] = mixture
        keep_logs(kept, logs, j)
        for shard in range(4):

            @pl.when(step == shard)
            def _():
                for event in events.get(2 * shard + j, []):
                    event()

    l_out[0] = kept[...].T[0:8]
    v2[...] += nn(a_out[0], wo[0])

    @pl.when(step == pl.num_programs(0) - 1)
    def _():
        for i in range(2):
            weights.complete(i)
        for i in range(2):
            weights.finish(i)


def whole_spec(shape):
    return pl.BlockSpec(shape, lambda i: (0,) * len(shape))


def shard_spec(shape, index=lambda i: i):
    return pl.BlockSpec((1,) + shape[1:], lambda i: (index(i), 0, 0))


def cross_forward(prefix_len, v1, memory, weights, pre, dec, src, gain, shift, own):
    wq, wk, wv, wo = weights
    n, width, lanes = wq.shape
    block = v1.shape[0]
    seq = memory.shape[0]
    out = jax.ShapeDtypeStruct
    outs = (
        out((n, block, lanes), bf16),
        out((n, PRE + seq, lanes), bf16),
        out((n, PRE + seq, lanes), bf16),
        out((n, block, lanes), bf16),
        out((n, 8, block), f32),
    )
    return pl.pallas_call(
        functools.partial(cross_forward_kernel, prefix_len),
        grid=(n,),
        out_shape=outs + (out((block, width), f32), out((n,) + own.shape, own.dtype)),
        in_specs=[whole_spec(v1.shape), whole_spec(memory.shape)]
        + [shard_spec(a.shape) for a in (wq, wk, wv, wo, pre)]
        + [whole_spec(a.shape) for a in (dec, src, gain, shift)]
        + [pl.BlockSpec(memory_space=pltpu.HBM)],
        out_specs=[shard_spec(a.shape) for a in outs]
        + [whole_spec((block, width)), pl.BlockSpec(memory_space=pltpu.HBM)],
        scratch_shapes=[
            VMEM((block, width), bf16),
            VMEM((block, PRE + seq), f32),
            VMEM((block, 128), f32),
            VMEM(own.shape, own.dtype),
            pltpu.SemaphoreType.DMA((2 * FLOWS,)),
            pltpu.SemaphoreType.DMA((2 * FLOWS,)),
            pltpu.SemaphoreType.DMA((4,)),
        ],
        compiler_params=pltpu.CompilerParams(
            collective_id=1, has_side_effects=True, vmem_limit_bytes=VMEM_BYTES
        ),
        name="cross_forward",
    )(v1, memory, wq, wk, wv, wo, pre, dec, src, gain, shift, own)


def feed_forward_kernel(
    v2, out_grad, w_in, w_out, down, down_bias, up, up_bias, gain, shift,
    output, dr2, grads, vecs,
    n2_low, n2_hat, total, e_low, slope, grad,
):
    step = pl.program_id(0)
    half = pl.num_programs(0) // 2
    width = v2.shape[1]

    @pl.when(step == 0)
    def _():
        n, _ = norm_parts(v2[...])
        n2_hat[...] = n
        normed = n * gain[1:2] + shift[1:2]
        total[...] = normed
        n2_low[...] = normed.astype(bf16)

    @pl.when(step < half)
    def _():
        act, bend = gelu_parts(nn(n2_low[...], w_in[0]))
        slope[step] = bend
        total[...] += nn(act.astype(bf16), w_out[0])

    @pl.when(step == half - 1)
    def _():
        act, bend = gelu_parts(nn(n2_low[...], down[...]) + down_bias[...])
        act = act.astype(bf16)
        resid = total[...] + 4.0 * (nn(act, up[...]) + up_bias[...])
        n, spread = norm_parts(resid)
        output[...] = (n * gain[2:3] + shift[2:3]).astype(bf16)
        dz, gain_part, shift_part = norm_back(out_grad[...].astype(f32), gain[2:3], n, spread)
        e_low[...] = dz.astype(bf16)
        four = (4.0 * dz).astype(bf16)
        grads[0] = tn(act, four).astype(bf16)
        da = (nt(four, up[...]) * bend).astype(bf16)
        grads[1] = tn(da, n2_low[...]).astype(bf16)
        grad[...] = dz + nt(da, down[...])
        vecs[...] = jnp.zeros_like(vecs)
        vecs[2:3] = gain_part
        vecs[5:6] = shift_part
        vecs[6:7] = jnp.sum(four.astype(f32), axis=0, keepdims=True)
        vecs[7:8, 0 : down.shape[1]] = jnp.sum(da.astype(f32), axis=0, keepdims=True)

    @pl.when(step >= half)
    def _():
        du = (nt(e_low[...], w_out[0]) * slope[2 * half - 1 - step]).astype(bf16)
        grad[...] += nt(du, w_in[0])

    @pl.when(step == 2 * half - 1)
    def _():
        _, spread = norm_parts(v2[...])
        dv, gain_part, shift_part = norm_back(grad[...], gain[1:2], n2_hat[...], spread)
        dr2[...] = dv
        vecs[1:2] = gain_part
        vecs[4:5] = shift_part


def feed_forward(v2, out_grad, w_in, w_out, down, down_bias, up, up_bias, gain, shift):
    n, width, inner = w_in.shape
    block = v2.shape[0]
    adapt = down.shape[1]
    out = jax.ShapeDtypeStruct
    outs = (
        out((block, width), bf16),
        out((block, width), f32),
        out((2, adapt, width), bf16),
        out((8, width), f32),
    )
    turn = lambda i: jnp.minimum(i, 2 * n - 1 - i)
    return pl.pallas_call(
        feed_forward_kernel,
        grid=(2 * n,),
        out_shape=outs,
        in_specs=[whole_spec(v2.shape), whole_spec(out_grad.shape)]
        + [shard_spec(w_in.shape, turn), shard_spec(w_out.shape, turn)]
        + [whole_spec(a.shape) for a in (down, down_bias, up, up_bias, gain, shift)],
        out_specs=[whole_spec(a.shape) for a in outs],
        scratch_shapes=[
            VMEM((block, width), bf16),
            VMEM((block, width), f32),
            VMEM((block, width), f32),
            VMEM((block, width), bf16),
            VMEM((n, block, inner), f32),
            VMEM((block, width), f32),
        ],
        compiler_params=pltpu.CompilerParams(vmem_limit_bytes=VMEM_BYTES),
        name="feed_forward",
    )(v2, out_grad, w_in, w_out, down, down_bias, up, up_bias, gain, shift)


class Links:
    def __init__(self, send, recv):
        self.send, self.recv = send, recv
        self.row = lax.axis_index("rows")
        self.t = lax.axis_index("tp")
        self.flows = 0
        place = lax.rem(self.row, GROUP)
        self.base = self.row - place
        self.a = place // 2
        self.b = lax.rem(place, 2)
        self.place = place

    def flow(self):
        self.flows += 1
        return self.flows - 1

    def tp_peer(self, mask):
        return (self.row, self.t ^ mask)

    def line_peer(self, d):
        return (self.base + lax.rem(self.a + d, LINE) * 2 + self.b, self.t)

    def side_peer(self):
        return (self.base + self.a * 2 + (1 - self.b), self.t)

    def copy(self, src, dst, flow, peer):
        return pltpu.make_async_remote_copy(
            src_ref=src,
            dst_ref=dst,
            send_sem=self.send.at[flow],
            recv_sem=self.recv.at[flow],
            device_id=peer,
            device_id_type=MESH,
        )

    def start(self, src, dst, flow, peer):
        made = self.copy(src, dst, flow, peer)
        made.start()
        return made

    def arrived(self, dst, flow, peer):
        self.copy(dst, dst, flow, peer).wait_recv()


def greet(peers):
    barrier = pltpu.get_barrier_semaphore()
    for peer in peers:
        pl.semaphore_signal(barrier, inc=1, device_id=peer, device_id_type=MESH)
    pl.semaphore_wait(barrier, len(peers))


CHUNKS = 4


FLOWS = 14


class WeightGather:
    def __init__(self, links, base, across, own, full, stage, local):
        self.links, self.base, self.across = links, base, across
        self.own, self.full, self.stage, self.local = own, full, stage, local
        self.far, self.last = links.t ^ 2, links.t ^ 3
        a = links.a
        self.right = (links.base + jnp.minimum(a + 1, LINE - 1) * 2 + links.b, links.t)
        self.left = (links.base + jnp.maximum(a - 1, 0) * 2 + links.b, links.t)
        self.side = links.side_peer()
        self.sibling = links.tp_peer(1)
        self.over = links.tp_peer(2)

    def at(self, i, a, b):
        rows = self.own[i].shape[0] // GROUP
        return pl.ds(pl.multiple_of((a * 2 + b) * rows, rows), rows)

    def part(self, i, a, b):
        return self.full[i].at[self.far, self.at(i, a, b)]

    def flow(self, i, k):
        return self.base + i * FLOWS + k

    def over_copy(self, i, k):
        links = self.links
        b = links.b if k == 0 else 1 - links.b
        at = self.at(i, links.a, b)
        return links.copy(
            self.own[i].at[at], self.full[i].at[links.t, at], self.flow(i, k), self.over
        )

    def beside_copy(self, i):
        return self.links.copy(
            self.own[i], self.full[i].at[self.links.t], self.flow(i, 2), self.sibling
        )

    def pass_copy(self, i):
        whole = self.full[i].at[self.far]
        return self.links.copy(whole, whole, self.flow(i, 3), self.sibling)

    def moved(self, i, a, flow, peer):
        part = self.part(i, a, self.links.b)
        return self.links.copy(part, part, self.flow(i, flow), peer)

    def stage_in(self, i):
        return pltpu.make_async_copy(self.own[i], self.stage[i], self.local.at[2 * i])

    def stage_out(self, i):
        return pltpu.make_async_copy(
            self.stage[i], self.full[i].at[self.links.t], self.local.at[2 * i + 1]
        )

    def start_over(self, i):
        for k in range(self.across[i]):
            self.over_copy(i, k).start()

    def start_beside(self, i):
        self.beside_copy(i).start()
        self.stage_in(i).start()

    def keep_own(self, i):
        self.stage_in(i).wait()
        self.stage_out(i).start()

    def came_over(self, i):
        mine = self.part(i, self.links.a, self.links.b)
        self.links.arrived(mine, self.flow(i, 0), self.over)
        self.spread(i)

    def spread(self, i):
        a = self.links.a

        @pl.when(a < LINE - 1)
        def _():
            self.moved(i, a, 4, self.right).start()

        @pl.when(a > 0)
        def _():
            self.moved(i, a, 7, self.left).start()

        if self.across[i] == 1:
            self.moved(i, a, 10, self.side).start()

    def along(self, i, k):
        links, a = self.links, self.links.a

        @pl.when(a - 1 - k >= 0)
        def _():
            links.arrived(self.part(i, a - 1 - k, links.b), self.flow(i, 4 + k), self.left)
            if k < LINE - 2:

                @pl.when(a < LINE - 1)
                def _():
                    self.moved(i, a - 1 - k, 5 + k, self.right).start()

            self.moved(i, a - 1 - k, 11 + k, self.side).start()

        @pl.when(a + 1 + k <= LINE - 1)
        def _():
            links.arrived(self.part(i, a + 1 + k, links.b), self.flow(i, 7 + k), self.right)
            if k < LINE - 2:

                @pl.when(a > 0)
                def _():
                    self.moved(i, a + 1 + k, 8 + k, self.left).start()

            self.moved(i, a + 1 + k, 13 - k, self.side).start()

    def side_part(self, i, k):
        links, a = self.links, self.links.a
        if k == 0:
            return self.part(i, a, 1 - links.b)
        piece = jnp.where(k <= a, a - k, a + LINE - k)
        return self.part(i, piece, 1 - links.b)

    def complete(self, i):
        links = self.links
        if self.across[i] == 2:
            links.arrived(self.side_part(i, 0), self.flow(i, 1), self.over)
        for k in range(self.across[i] - 1, LINE):
            links.arrived(self.side_part(i, k), self.flow(i, 10 + k), self.side)
        self.pass_copy(i).start()

    def finish(self, i):
        links = self.links
        links.arrived(self.full[i].at[links.t ^ 1], self.flow(i, 2), self.sibling)
        links.arrived(self.full[i].at[self.last], self.flow(i, 3), self.sibling)
        for k in range(self.across[i]):
            self.over_copy(i, k).wait_send()
        self.beside_copy(i).wait_send()
        self.stage_out(i).wait()
        self.spread_sent(i)

    def spread_sent(self, i):
        a = self.links.a
        self.pass_copy(i).wait_send()
        for k in range(LINE - 1):

            @pl.when((a < LINE - 1) & (a - k >= 0))
            def _():
                self.moved(i, a - k, 4 + k, self.right).wait_send()

            @pl.when((a > 0) & (a + k <= LINE - 1))
            def _():
                self.moved(i, a + k, 7 + k, self.left).wait_send()

        for k in range(self.across[i] - 1, LINE):
            piece = a if k == 0 else jnp.where(k <= a, a - k, a + LINE - k)
            self.moved(i, piece, 10 + k, self.side).wait_send()


class AdapterSpread(WeightGather):
    def __init__(self, links, base, full):
        super().__init__(links, base, [1], None, full, None, None)
        self.half = lax.rem(links.t, 2)

    def part(self, i, a, b):
        return self.full.at[self.half, b, a]

    def pass_copy(self, i):
        whole = self.full.at[self.half]
        return self.links.copy(whole, whole, self.flow(i, 3), self.sibling)

    def finish(self, i):
        self.links.arrived(self.full.at[1 - self.half], self.flow(i, 3), self.sibling)
        self.spread_sent(i)


class AdapterReduce:
    def __init__(self, links, base, levels, g, s1, h, xb, h2, zb, p3, yb, hb):
        self.links, self.base, self.levels = links, base, levels
        self.g, self.s1, self.h, self.xb, self.h2 = g, s1, h, xb, h2
        self.zb, self.p3, self.yb, self.hb = zb, p3, yb, hb
        self.half = lax.rem(links.t, 2)
        self.groups = [(links.row ^ (GROUP << level), links.t) for level in range(levels)]

    def beside(self):
        return self.links.copy(
            self.g.at[1 - self.half], self.s1, self.base, self.links.tp_peer(1)
        )

    def side(self):
        links = self.links
        return links.copy(self.h.at[1 - links.b], self.xb, self.base + 1, links.side_peer())

    def line(self, d):
        links = self.links
        return links.copy(
            self.h2.at[lax.rem(links.a + d, LINE)],
            self.zb.at[d - 1],
            self.base + 1 + d,
            links.line_peer(d),
        )

    def over(self):
        return self.links.copy(self.p3, self.yb, self.base + 1 + LINE, self.links.tp_peer(2))

    def group(self, level):
        return self.links.copy(
            self.hb.at[2 * level],
            self.hb.at[2 * level + 1],
            self.base + 2 + LINE + level,
            self.groups[level],
        )

    def phase(self, number):
        if number == 0:
            self.beside().start()
        elif number == 1:
            self.beside().wait()
            self.h[...] = (self.g[self.half].astype(f32) + self.s1[...].astype(f32)).astype(bf16)
            self.side().start()
        elif number == 2:
            self.side().wait()
            self.h2[...] = (
                self.h[self.links.b].astype(f32) + self.xb[...].astype(f32)
            ).astype(bf16)
            for d in range(1, LINE):
                self.line(d).start()
        elif number == 3:
            for d in range(1, LINE):
                self.line(d).wait()
            total = self.h2[self.links.a].astype(f32)
            for d in range(1, LINE):
                total = total + self.zb[d - 1].astype(f32)
            self.p3[...] = total.astype(bf16)
            self.over().start()

    def result(self):
        self.over().wait()
        value = self.p3[...].astype(f32) + self.yb[...].astype(f32)
        for level in range(self.levels):
            self.hb[2 * level] = value.astype(bf16)
            self.group(level).start()
            self.group(level).wait()
            value = self.hb[2 * level].astype(f32) + self.hb[2 * level + 1].astype(f32)
        return value.astype(bf16)


class RowGather:
    FLOWS = 1 + 2 * 4

    def __init__(self, links, base, own, full):
        self.links, self.base, self.own, self.full = links, base, own, full
        self.far, self.last = links.t ^ 2, links.t ^ 3
        self.sibling, self.over = links.tp_peer(1), links.tp_peer(2)

    def at(self, c):
        rows = self.own.shape[0] // CHUNKS
        return pl.ds(c * rows, rows)

    def beside_copy(self):
        return self.links.copy(self.own, self.full.at[self.links.t], self.base, self.sibling)

    def over_copy(self, c):
        at = self.at(c)
        return self.links.copy(
            self.own.at[at], self.full.at[self.links.t, at], self.base + 1 + c, self.over
        )

    def pass_copy(self, c):
        part = self.full.at[self.far, self.at(c)]
        return self.links.copy(part, part, self.base + 1 + CHUNKS + c, self.sibling)

    def start_beside(self):
        self.beside_copy().start()

    def start_over(self):
        for c in range(CHUNKS):
            self.over_copy(c).start()

    def came_beside(self):
        self.links.arrived(self.full.at[self.links.t ^ 1], self.base, self.sibling)

    def came_over(self):
        for c in range(CHUNKS):
            self.links.arrived(
                self.full.at[self.far, self.at(c)], self.base + 1 + c, self.over
            )
            self.pass_copy(c).start()

    def came_last(self):
        for c in range(CHUNKS):
            self.links.arrived(
                self.full.at[self.last, self.at(c)], self.base + 1 + CHUNKS + c, self.sibling
            )

    def sent(self):
        self.beside_copy().wait_send()
        for c in range(CHUNKS):
            self.over_copy(c).wait_send()
            self.pass_copy(c).wait_send()


class RowScatter:
    FLOWS = 2 + 4

    def __init__(self, links, base, part, near, near_far, mid, far):
        self.links, self.base, self.part = links, base, part
        self.near, self.near_far, self.mid, self.far = near, near_far, mid, far
        self.sibling, self.over = links.tp_peer(1), links.tp_peer(2)

    def at(self, c):
        rows = self.near.shape[0] // CHUNKS
        return pl.ds(c * rows, rows)

    def first_copy(self):
        return self.links.copy(
            self.part.at[self.links.t ^ 3], self.near_far, self.base, self.sibling
        )

    def second_copy(self):
        return self.links.copy(
            self.part.at[self.links.t ^ 1], self.near, self.base + 1, self.sibling
        )

    def over_copy(self, c):
        at = self.at(c)
        return self.links.copy(
            self.mid.at[at], self.far.at[at], self.base + 2 + c, self.over
        )

    def send_over(self):
        self.links.arrived(self.near_far, self.base, self.sibling)
        for c in range(CHUNKS):
            at = self.at(c)
            self.mid[at] = (
                self.part[self.links.t ^ 2, at].astype(f32) + self.near_far[at].astype(f32)
            ).astype(bf16)
            self.over_copy(c).start()

    def came_beside(self):
        self.links.arrived(self.near, self.base + 1, self.sibling)

    def came_over(self, c):
        at = self.at(c)
        self.links.arrived(self.far.at[at], self.base + 2 + c, self.over)
        return (
            self.part[self.links.t, at].astype(f32)
            + self.near[at].astype(f32)
            + self.far[at].astype(f32)
        )

    def sent(self):
        self.first_copy().wait_send()
        self.second_copy().wait_send()
        for c in range(CHUNKS):
            self.over_copy(c).wait_send()


def chunked(own, full, stage):
    rows = own[-1].shape[0] // 2
    halves = [pl.ds(o * rows, rows) for o in range(2)]
    return (
        list(own[:-1]) + [own[-1].at[at] for at in halves],
        list(full[:-1]) + [full[-1].at[:, at] for at in halves],
        list(stage[:-1]) + [stage[-1].at[at] for at in halves],
    )


def cut(refs, *counts):
    out, at = [], 0
    for count in counts:
        out.append(refs[at : at + count])
        at += count
    return out


def self_forward_kernel(prefix_len, arrays, *refs):
    ins, own, outs, full, stage, scratch = cut(refs, 9, arrays, 8, arrays, arrays + 1, 14)
    x, memory, pre_cross, wq, wk, wv, wo, pre, seg = ins
    q_out, k_out, v_out, a_out, l_out, resid, m_full, pre_full = outs
    x_full, part, kept, bias, near, near_far, mid, far, pre_stage, send, recv, local, m_local, pre_local = scratch
    links = Links(send, recv)
    t = links.t
    block, lanes = x.shape[0], q_out.shape[1]
    own, full, held = chunked(own, full, stage[:arrays])
    count = len(own)
    weights = WeightGather(links, 0, [1] * (count - 2) + [2] * 2, own, full, held, local)
    late = range(count - 2, count)
    early = range(count - 2)
    at = count * FLOWS
    x_rows = RowGather(links, at, x, x_full)
    m_rows = RowGather(links, at + RowGather.FLOWS, memory, m_full)
    at += 2 * RowGather.FLOWS
    sums = RowScatter(links, at, part, near, near_far, mid, far)
    at += RowScatter.FLOWS
    m_in = pltpu.make_async_copy(memory, stage[arrays], m_local.at[0])
    m_keep = pltpu.make_async_copy(stage[arrays], m_full.at[t], m_local.at[1])
    pre_keep = pltpu.make_async_copy(pre_stage, pre_full.at[t], pre_local.at[0])
    pre_sends = [
        links.copy(pre_stage, pre_full.at[t], at + m - 1, links.tp_peer(m)) for m in (1, 2, 3)
    ]

    greet(
        [links.tp_peer(m) for m in (1, 2, 3)]
        + [links.line_peer(d) for d in range(1, LINE)]
        + [links.side_peer()]
    )
    for i in early:
        weights.start_over(i)
    x_rows.start_beside()
    x_rows.start_over()
    kept[...] = jnp.zeros_like(kept)
    pre_stage[...] = jnp.zeros_like(pre_stage)
    for o in range(2):
        pre_stage[o * PRE_PACK : o * PRE_PACK + prefix_len] = pre_cross[o]
    m_rows.start_beside()
    m_in.start()
    pre_keep.start()
    for one in pre_sends:
        one.start()
    for i in range(count):
        weights.start_beside(i)

    for target, o in ((k_out, 0), (v_out, 1)):
        target[0:PRE] = jnp.zeros((PRE, lanes), bf16)
        target[0:prefix_len] = pre[o]

    def project(rows, index):
        at = pl.multiple_of(index * block, block)
        q_out[pl.ds(at, block)] = (SCALE * nn(rows, wq[...])).astype(bf16)
        k_out[pl.ds(PRE + at, block)] = nn(rows, wk[...]).astype(bf16)
        v_out[pl.ds(PRE + at, block)] = nn(rows, wv[...]).astype(bf16)

    project(x[...], t)
    x_rows.came_beside()
    project(x_full[t ^ 1], t ^ 1)
    m_in.wait()
    m_keep.start()
    for i in range(count):
        weights.keep_own(i)
    for i in early:
        weights.came_over(i)
    x_rows.came_over()
    for i in late:
        weights.start_over(i)
    for i in early:
        weights.along(i, 0)
    project(x_full[t ^ 2], t ^ 2)
    x_rows.came_last()
    project(x_full[t ^ 3], t ^ 3)

    @pl.loop(0, 4)
    def _(order):
        here = t ^ (3 - order)
        for i in range(4):
            keys = PRE + (i + 1) * block

            @pl.when(here == i)
            def _():
                bias[:, 0:PRE] = prefix_bias((block, PRE), 1, prefix_len)
                bias[:, PRE:keys] = mask_bias(
                    column(seg[:, i * block : (i + 1) * block]),
                    seg[:, 0 : keys - PRE],
                    (block, keys - PRE),
                    1,
                    i * block,
                )

                @pl.loop(0, lanes // PAIR)
                def _(j):
                    cols = pl.ds(pl.multiple_of(j * PAIR, PAIR), PAIR)
                    mixture, logs = pair_forward(
                        q_out[i * block : (i + 1) * block, cols],
                        k_out[0:keys, cols],
                        v_out[0:keys, cols],
                        bias[:, 0:keys],
                    )
                    a_out[i, :, cols] = mixture
                    keep_logs(kept, logs, j)

        l_out[here] = kept[...].T[0:8]
        part[here] = nn(a_out[here], wo[...]).astype(bf16)

        @pl.when(order == 0)
        def _():
            sums.first_copy().start()
            for i in early:
                weights.along(i, 1)

        @pl.when(order == 1)
        def _():
            sums.send_over()
            m_rows.start_over()
            for i in late:
                weights.came_over(i)

        @pl.when(order == 2)
        def _():
            sums.second_copy().start()
            for i in early:
                weights.along(i, 2)

    for i in late:
        weights.along(i, 0)
    for i in early:
        weights.complete(i)
    for i in late:
        weights.along(i, 1)
    sums.came_beside()
    for c in range(CHUNKS):
        rows = sums.at(c)
        resid[rows] = x[rows].astype(f32) + sums.came_over(c)
    for i in late:
        weights.along(i, 2)
    m_rows.came_over()
    for i in late:
        weights.complete(i)
    m_rows.came_beside()
    m_rows.came_last()
    for m, one in zip((1, 2, 3), pre_sends):
        links.copy(
            pre_full.at[t ^ m], pre_full.at[t ^ m], small_base(count) + m - 1, links.tp_peer(m)
        ).wait_recv()
        one.wait_send()
    for i in range(count):
        weights.finish(i)
    x_rows.sent()
    m_rows.sent()
    sums.sent()
    m_keep.wait()
    pre_keep.wait()


def small_base(count):
    return count * FLOWS + 2 * RowGather.FLOWS + RowScatter.FLOWS


def self_forward(prefix_len, x, memory, pre_cross, own_weights, pre, seg, weights):
    n = 4
    arrays = len(weights)
    count = arrays + 1
    block, width = x.shape
    lanes = own_weights[0].shape[1]
    seq = n * block
    out = jax.ShapeDtypeStruct
    flows = small_base(count) + 3
    outs = (
        out((seq, lanes), bf16),
        out((PRE + seq, lanes), bf16),
        out((PRE + seq, lanes), bf16),
        out((n, block, lanes), bf16),
        out((n, 8, block), f32),
        out((block, width), f32),
        out((n, block, width), bf16),
        out((n, 2 * PRE_PACK, lanes), bf16),
    ) + tuple(out((n,) + a.shape, a.dtype) for a in weights)
    a = pl.BlockSpec(memory_space=pltpu.HBM)
    rows = VMEM((block, width), bf16)
    given = (x, memory, pre_cross, *own_weights, pre, seg)
    in_specs = [whole_spec(g.shape) for g in given]
    in_specs[1] = a
    return pl.pallas_call(
        functools.partial(self_forward_kernel, prefix_len, arrays),
        grid=(1,),
        out_shape=outs,
        in_specs=in_specs + [a] * arrays,
        out_specs=[whole_spec(o.shape) for o in outs[:6]] + [a] * (2 + arrays),
        scratch_shapes=[VMEM(w.shape, w.dtype) for w in weights]
        + [rows]
        + [
            VMEM((n, block, width), bf16),
            VMEM((n, block, width), bf16),
            VMEM((block, 128), f32),
            VMEM((block, PRE + seq), f32),
            rows,
            rows,
            rows,
            rows,
            VMEM((2 * PRE_PACK, lanes), bf16),
            pltpu.SemaphoreType.DMA((flows,)),
            pltpu.SemaphoreType.DMA((flows,)),
            pltpu.SemaphoreType.DMA((2 * count,)),
            pltpu.SemaphoreType.DMA((2,)),
            pltpu.SemaphoreType.DMA((1,)),
        ],
        compiler_params=pltpu.CompilerParams(
            collective_id=0, has_side_effects=True, vmem_limit_bytes=VMEM_BYTES
        ),
        name="self_forward",
    )(*given, *weights)


def doublings(count):
    levels = 0
    while (1 << levels) < count:
        levels += 1
    return levels


def cross_backward_kernel(
    prefix_len, levels, dr2, v1, q, k, v, a, logs, wq, wk, wv, wo, dec, src, gain, vecs_in, g,
    dr1, dr1_full, dm, pre_grad, vecs, piece,
    dr1_low, dr2_low, bias, da, dq, dk, dv, total, s1, h, xb, h2, zb, p3, yb, hb, send, recv, local,
):
    step = pl.program_id(0)
    steps = pl.num_programs(0)
    block, lanes = q.shape[1:]
    keys = k.shape[1]
    links = Links(send, recv)
    t = links.t
    rows = RowGather(links, 0, dr1_low, dr1_full)
    keep = pltpu.make_async_copy(dr1_low, dr1_full.at[t], local.at[0])
    reduce = AdapterReduce(links, RowGather.FLOWS, levels, g, s1, h, xb, h2, zb, p3, yb, hb)

    @pl.when(step == 0)
    def _():
        greet(
            [links.tp_peer(1), links.tp_peer(2)]
            + [links.line_peer(d) for d in range(1, LINE)]
            + [links.side_peer()]
            + reduce.groups
        )
        reduce.phase(0)
        dr2_low[...] = dr2[...].astype(bf16)
        total[...] = jnp.zeros_like(total)
        own_queries = dec[:, pl.ds(pl.multiple_of(t * block, block), block)]
        bias[0:PRE] = prefix_bias((PRE, block), 0, prefix_len)
        bias[PRE:] = mask_bias(own_queries, column(src[...]), (keys - PRE, block), 0, None)

    da[...] = nt(dr2_low[...], wo[0]).astype(bf16)

    @pl.when(step == 0)
    def _():
        reduce.phase(1)

    @pl.loop(0, lanes // PAIR)
    def _(j):
        cols = pl.ds(pl.multiple_of(j * PAIR, PAIR), PAIR)
        dq_pair, dk_pair, dv_pair = pair_backward(
            q[0, :, cols],
            k[0, :, cols],
            v[0, :, cols],
            a[0, :, cols],
            da[:, cols],
            [logs[0, pl.ds(2 * j + i, 1)] for i in range(2)],
            bias[...],
        )
        dq[:, cols] = dq_pair
        pre_grad[0, 0:PRE_PACK, cols] = dk_pair[0:PRE_PACK]
        pre_grad[0, PRE_PACK : 2 * PRE_PACK, cols] = dv_pair[0:PRE_PACK]
        dk[step, :, cols] = dk_pair[PRE:].astype(bf16)
        dv[step, :, cols] = dv_pair[PRE:].astype(bf16)

    total[...] += nt(dq[...], wq[0])

    @pl.when(step == 1)
    def _():
        reduce.phase(2)

    @pl.when(step == steps - 1)
    def _():
        n, spread = norm_parts(v1[...])
        grad, gain_part, shift_part = norm_back(
            dr2[...] + SCALE * total[...], gain[0:1], n, spread
        )
        dr1[...] = grad
        dr1_low[...] = grad.astype(bf16)
        rows.start_over()
        rows.start_beside()
        keep.start()
        vecs[...] = vecs_in[...]
        vecs[0:1] = gain_part
        vecs[3:4] = shift_part
        reduce.phase(3)

        @pl.loop(0, 4)
        def _(i):
            at = pl.ds(pl.multiple_of(i * block, block), block)
            value = None
            for shard in range(dk.shape[0]):
                term = nt(dk[shard, at], wk[shard]) + nt(dv[shard, at], wv[shard])
                value = term if value is None else value + term
            dm[i] = value.astype(bf16)

        rows.came_over()
        rows.came_beside()
        rows.came_last()
        piece[...] = reduce.result()
        rows.sent()
        keep.wait()


def cross_backward(
    prefix_len, row_count, dr2, v1, q, k, v, a, logs, weights, dec, src, gain, vecs, grads
):
    wq, wk, wv, wo = weights
    n, block, lanes = q.shape
    keys = k.shape[1]
    width = dr2.shape[1]
    levels = doublings(row_count // GROUP)
    part = grads.shape[1] // GROUP
    half = (2, LINE, part, width)
    g = grads.reshape((2,) + half)
    out = jax.ShapeDtypeStruct
    outs = (
        out((block, width), f32),
        out((n, block, width), bf16),
        out((n, block, width), bf16),
        out((n, 2 * PRE_PACK, lanes), f32),
        out((8, width), f32),
        out((part, width), bf16),
    )
    out_specs = [whole_spec(o.shape) for o in outs]
    out_specs[1] = pl.BlockSpec(memory_space=pltpu.HBM)
    out_specs[3] = shard_spec(outs[3].shape)
    flows = RowGather.FLOWS + 2 + LINE + levels
    return pl.pallas_call(
        functools.partial(cross_backward_kernel, prefix_len, levels),
        grid=(n,),
        out_shape=outs,
        in_specs=[whole_spec(dr2.shape), whole_spec(v1.shape)]
        + [shard_spec(x.shape) for x in (q, k, v, a, logs, wq)]
        + [whole_spec(wk.shape), whole_spec(wv.shape), shard_spec(wo.shape)]
        + [whole_spec(x.shape) for x in (dec, src, gain, vecs, g)],
        out_specs=out_specs,
        scratch_shapes=[
            VMEM((block, width), bf16),
            VMEM((block, width), bf16),
            VMEM((keys, block), f32),
            VMEM((block, lanes), bf16),
            VMEM((block, lanes), bf16),
            VMEM((n, keys - PRE, lanes), bf16),
            VMEM((n, keys - PRE, lanes), bf16),
            VMEM((block, width), f32),
            VMEM(half, bf16),
            VMEM(half, bf16),
            VMEM(half[1:], bf16),
            VMEM(half[1:], bf16),
            VMEM((LINE - 1, part, width), bf16),
            VMEM((part, width), bf16),
            VMEM((part, width), bf16),
            VMEM((max(1, 2 * levels), part, width), bf16),
            pltpu.SemaphoreType.DMA((flows,)),
            pltpu.SemaphoreType.DMA((flows,)),
            pltpu.SemaphoreType.DMA((1,)),
        ],
        compiler_params=pltpu.CompilerParams(
            collective_id=2, has_side_effects=True, vmem_limit_bytes=VMEM_BYTES
        ),
        name="cross_backward",
    )(dr2, v1, q, k, v, a, logs, wq, wk, wv, wo, dec, src, gain, vecs, g)


class Doubling:
    def __init__(self, links, base, levels, outgo, income):
        self.links, self.base, self.levels = links, base, levels
        self.outgo, self.income = outgo, income

    def move(self, level):
        return self.links.copy(
            self.outgo.at[level],
            self.income.at[level],
            self.base + level,
            (self.links.row ^ (1 << level), self.links.t),
        )

    def begin(self, value):
        self.outgo[0] = value
        self.move(0).start()

    def value(self, level):
        self.move(level).wait()
        return self.outgo[level] + self.income[level]

    def step(self, level):
        value = self.value(level)
        self.outgo[level + 1] = value
        self.move(level + 1).start()


def self_backward_kernel(
    prefix_len, levels, dr1_full, dr1, q, k, v, a, logs, wq, wk, wv, wo, seg,
    dm, piece, cross, vecs,
    tokens_grad, memory_grad, adapter, self_pre, sums,
    part, bias, da, dq, dk, dv, near, near_far, mid, far, m_near, m_near_far, m_mid, m_far,
    cross_in, vecs_in, outgo, income, pre_outgo, pre_income, send, recv,
):
    seq, lanes = q.shape
    block = seq // 4
    links = Links(send, recv)
    t = links.t
    at = 0
    spread = AdapterSpread(links, at, adapter)
    at += FLOWS
    m_sums = RowScatter(links, at, dm, m_near, m_near_far, m_mid, m_far)
    at += RowScatter.FLOWS
    x_sums = RowScatter(links, at, part, near, near_far, mid, far)
    at += RowScatter.FLOWS
    total = Doubling(links, at, levels, outgo, income)
    at += levels
    pre_total = Doubling(links, at, levels, pre_outgo, pre_income)
    at += levels

    def exchange(m):
        peer = links.tp_peer(m)
        return (
            links.copy(cross.at[t ^ m], cross_in.at[t], at + 2 * (m - 1), peer),
            links.copy(vecs, vecs_in.at[t], at + 2 * (m - 1) + 1, peer),
        )

    greet(
        [links.tp_peer(m) for m in (1, 2, 3)]
        + [links.line_peer(d) for d in range(1, LINE)]
        + [links.side_peer()]
        + [(links.row ^ (1 << level), t) for level in range(doublings(GROUP), levels)]
    )
    m_sums.first_copy().start()
    m_sums.second_copy().start()
    for m in (1, 2, 3):
        for one in exchange(m):
            one.start()
    adapter[spread.half, links.b, links.a] = piece[...]
    spread.spread(0)
    cross_in[t] = cross[t]
    vecs_in[t] = vecs[...]
    dk[...] = jnp.zeros_like(dk)
    dv[...] = jnp.zeros_like(dv)

    for i in reversed(range(4)):
        rows = slice(i * block, (i + 1) * block)
        keys = PRE + (i + 1) * block
        bias[0:PRE] = prefix_bias((PRE, block), 0, prefix_len)
        bias[PRE:keys] = mask_bias(
            seg[:, rows], column(seg[:, 0 : keys - PRE]), (keys - PRE, block), 0, i * block
        )
        da[...] = nt(dr1_full[i], wo[...]).astype(bf16)

        @pl.loop(0, lanes // PAIR)
        def _(j):
            cols = pl.ds(pl.multiple_of(j * PAIR, PAIR), PAIR)
            dq_pair, dk_pair, dv_pair = pair_backward(
                q[rows, cols],
                k[0:keys, cols],
                v[0:keys, cols],
                a[i, :, cols],
                da[:, cols],
                [logs[i, pl.ds(2 * j + o, 1)] for o in range(2)],
                bias[0:keys],
            )
            dq[:, cols] = dq_pair
            dk[0:keys, cols] += dk_pair
            dv[0:keys, cols] += dv_pair

        done = slice(PRE + i * block, PRE + (i + 1) * block)
        part[i] = (
            SCALE * nt(dq[...], wq[...])
            + nt(dk[done].astype(bf16), wk[...])
            + nt(dv[done].astype(bf16), wv[...])
        ).astype(bf16)
        if i == 3:
            m_sums.send_over()
            for m in (1, 2, 3):
                peer = links.tp_peer(m)
                links.arrived(cross_in.at[t ^ m], at + 2 * (m - 1), peer)
                links.arrived(vecs_in.at[t ^ m], at + 2 * (m - 1) + 1, peer)
            value = vecs_in[0] + vecs_in[1] + vecs_in[2] + vecs_in[3]
            pieces = [cross_in[0] + cross_in[1] + cross_in[2] + cross_in[3]] + [
                value[:, o * lanes : (o + 1) * lanes] for o in range(vecs.shape[1] // lanes)
            ]
            total.begin(jnp.concatenate(pieces, axis=0))
        else:
            spread.along(0, 2 - i)
            if i > 0:
                total.step(2 - i)

    x_sums.first_copy().start()
    x_sums.second_copy().start()
    pre_total.begin(jnp.concatenate([dk[0:PRE_PACK], dv[0:PRE_PACK]], axis=0))
    spread.complete(0)
    x_sums.send_over()
    for level in range(2, levels - 1):
        total.step(level)
    sums[...] = total.value(levels - 1)
    for level in range(levels - 1):
        pre_total.step(level)
    m_sums.came_beside()
    for c in range(CHUNKS):
        memory_grad[m_sums.at(c)] = m_sums.came_over(c).astype(bf16)
    x_sums.came_beside()
    for c in range(CHUNKS):
        rows = x_sums.at(c)
        tokens_grad[rows] = (dr1[rows] + x_sums.came_over(c)).astype(bf16)
    self_pre[...] = pre_total.value(levels - 1)
    spread.finish(0)
    m_sums.sent()
    x_sums.sent()
    for m in (1, 2, 3):
        for one in exchange(m):
            one.wait_send()


def self_backward(
    prefix_len, row_count, dr1_full, dr1, q, k, v, a, logs, weights, seg,
    dm, piece, cross, vecs,
):
    n, block, width = dr1_full.shape
    seq, lanes = q.shape
    levels = doublings(row_count)
    packed = 2 * PRE_PACK
    height = packed + vecs.shape[0] * vecs.shape[1] // lanes
    out = jax.ShapeDtypeStruct
    outs = (
        out((block, width), bf16),
        out((block, width), bf16),
        out((2, 2, LINE) + piece.shape, bf16),
        out((packed, lanes), f32),
        out((height, lanes), f32),
    )
    given = (
        (dr1_full, dr1, q, k, v, a, logs) + tuple(weights) + (seg, dm, piece, cross, vecs)
    )
    rows = VMEM((block, width), bf16)
    flows = FLOWS + 2 * RowScatter.FLOWS + 2 * levels + 6
    return pl.pallas_call(
        functools.partial(self_backward_kernel, prefix_len, levels),
        grid=(1,),
        out_shape=outs,
        in_specs=[whole_spec(x.shape) for x in given],
        out_specs=[whole_spec(x.shape) for x in outs[:2]]
        + [pl.BlockSpec(memory_space=VMEM)]
        + [whole_spec(x.shape) for x in outs[3:]],
        scratch_shapes=[
            VMEM((n, block, width), bf16),
            VMEM((PRE + seq, block), f32),
            VMEM((block, lanes), bf16),
            VMEM((block, lanes), bf16),
            VMEM((PRE + seq, lanes), f32),
            VMEM((PRE + seq, lanes), f32),
        ]
        + [rows] * 8
        + [
            VMEM((n, packed, lanes), f32),
            VMEM((n,) + vecs.shape, f32),
            VMEM((levels, height, lanes), f32),
            VMEM((levels, height, lanes), f32),
            VMEM((levels, packed, lanes), f32),
            VMEM((levels, packed, lanes), f32),
            pltpu.SemaphoreType.DMA((flows,)),
            pltpu.SemaphoreType.DMA((flows,)),
        ],
        compiler_params=pltpu.CompilerParams(
            collective_id=3, has_side_effects=True, vmem_limit_bytes=VMEM_BYTES
        ),
        name="self_backward",
    )(*given)


def finish_kernel(
    prefix_len, lanes, tokens_low, memory_low, adapter, self_pre, sums,
    tokens_grad, memory_grad, self_out, cross_out, gains, shifts, down, down_bias, up, up_bias,
):
    tokens_grad[...] = tokens_low[...]
    memory_grad[...] = memory_low[...]
    up[...] = adapter[0].astype(f32)
    down[...] = adapter[1].astype(f32).T

    @pl.when(pl.program_id(0) == 0)
    def _():
        for o in range(2):
            rows = slice(o * PRE_PACK, o * PRE_PACK + prefix_len)
            self_out[o] = self_pre[rows]
            cross_out[o] = sums[rows]
        for i in range(gains.shape[1] // lanes):
            at = 2 * PRE_PACK + 8 * i
            cols = slice(i * lanes, (i + 1) * lanes)
            gains[:, cols] = sums[at : at + 3]
            shifts[:, cols] = sums[at + 3 : at + 6]
            up_bias[:, cols] = sums[at + 6 : at + 7]
            if (i + 1) * lanes <= down_bias.shape[1]:
                down_bias[:, cols] = sums[at + 7 : at + 8]


def finish(prefix_len, tokens_low, memory_low, adapter, self_pre, sums):
    steps = 4
    block, width = tokens_low.shape
    adapt = adapter.shape[1]
    lanes = sums.shape[1]
    out = jax.ShapeDtypeStruct
    outs = (
        out((block, width), bf16),
        out((block, width), bf16),
        out((2, prefix_len, lanes), f32),
        out((2, prefix_len, lanes), f32),
        out((3, width), f32),
        out((3, width), f32),
        out((width, adapt), f32),
        out((1, adapt), f32),
        out((adapt, width), f32),
        out((1, width), f32),
    )
    rows = pl.BlockSpec((block // steps, width), lambda i: (i, 0))
    specs = [whole_spec(o.shape) for o in outs]
    specs[0] = specs[1] = rows
    specs[6] = pl.BlockSpec((width, adapt // steps), lambda i: (0, i))
    specs[8] = pl.BlockSpec((adapt // steps, width), lambda i: (i, 0))
    return pl.pallas_call(
        functools.partial(finish_kernel, prefix_len, lanes),
        grid=(steps,),
        out_shape=outs,
        in_specs=[rows, rows, pl.BlockSpec((2, adapt // steps, width), lambda i: (0, i, 0))]
        + [whole_spec(self_pre.shape), whole_spec(sums.shape)],
        out_specs=specs,
        compiler_params=pltpu.CompilerParams(vmem_limit_bytes=VMEM_BYTES),
        name="finish",
    )(tokens_low, memory_low, adapter, self_pre, sums)


def per_device(
    row_count,
    tokens, memory, out_grad, dec_segments, src_segments,
    self_query, self_key, self_value, self_out,
    cross_query, cross_key, cross_value, cross_out,
    ffn_in, ffn_out, adapt_down, adapt_down_bias, adapt_up, adapt_up_bias,
    self_prefix, cross_prefix, norm_gain, norm_shift,
):
    seq_local, _, width = tokens.shape
    prefix_len = self_prefix.shape[1]
    adapt = adapt_down.shape[1]
    seq = dec_segments.shape[1]
    x, mem, grad_in = (a.reshape(seq_local, width) for a in (tokens, memory, out_grad))
    self_weights = (self_query, self_key, self_value, self_out)

    q1, k1, v1_heads, a1, logs1, resid_one, m_full, pre_full, *gathered = self_forward(
        prefix_len, x, mem, cross_prefix, self_weights, self_prefix, dec_segments,
        (cross_query, cross_key, cross_value, cross_out, ffn_in),
    )
    cross_weights = gathered[:4]
    w_in = gathered[4]
    q2, k2, v2_heads, a2, logs2, resid_two, w_out = cross_forward(
        prefix_len, resid_one, m_full.reshape(seq, width), cross_weights, pre_full,
        dec_segments, src_segments, norm_gain, norm_shift, ffn_out,
    )
    output, dr2, grads, vecs = feed_forward(
        resid_two, grad_in, w_in, w_out,
        adapt_down, adapt_down_bias.reshape(1, adapt), adapt_up, adapt_up_bias.reshape(1, width),
        norm_gain, norm_shift,
    )
    dr1, dr1_full, dm, cross_pre_part, vecs, piece = cross_backward(
        prefix_len, row_count, dr2, resid_one, q2, k2, v2_heads, a2, logs2, cross_weights,
        dec_segments, src_segments, norm_gain, vecs, grads,
    )
    tokens_low, memory_low, adapter, self_pre, sums = self_backward(
        prefix_len, row_count, dr1_full, dr1, q1, k1, v1_heads, a1, logs1,
        self_weights, dec_segments, dm, piece, cross_pre_part, vecs,
    )
    (
        tokens_grad, memory_grad, self_grad, cross_grad, gains, shifts,
        down, down_bias, up, up_bias,
    ) = finish(
        prefix_len, tokens_low, memory_low, adapter.reshape(2, adapt, width), self_pre, sums
    )
    local = tokens.shape
    return (
        output.reshape(local),
        tokens_grad.reshape(local),
        memory_grad.reshape(local),
        self_grad,
        cross_grad,
        gains,
        shifts,
        down,
        down_bias.reshape(adapt),
        up,
        up_bias.reshape(width),
    )


def solution(mesh):
    placed = (
        (P("tp", "rows", None),) * 3
        + (P("rows", None),) * 2
        + (P(None, "tp"),) * 3
        + (P("tp", None),)
        + (P(None, "tp"),) * 3
        + (P("tp", None),)
        + (P(None, "tp"), P("tp", None))
        + (P(),) * 4
        + (P(None, None, "tp"),) * 2
        + (P(),) * 2
    )
    return jax.shard_map(
        functools.partial(per_device, mesh.shape["rows"]),
        mesh=mesh,
        in_specs=placed,
        out_specs=(P("tp", "rows", None),) * 3 + (P(None, None, "tp"),) * 2 + (P(),) * 6,
        check_vma=False,
    )
```

```python
import functools

import jax
import jax.numpy as jnp
from jax import lax
from jax.experimental import pallas as pl
from jax.experimental.pallas import tpu as pltpu
from jax.sharding import PartitionSpec as P

HEAD = 64
PAIR = 2 * HEAD
PRE = 128
PRE_PACK = 32
GROUP = 8
LINE = 4
MASKED = -1000000000.0
EPSILON = 1e-05
VMEM_BYTES = 62 << 20
SCALE = HEAD**-0.5
f32 = jnp.float32
bf16 = jnp.bfloat16
MESH = pl.DeviceIdType.MESH
VMEM = pltpu.VMEM
ANY = pl.ANY


def nn(a, b):
    return lax.dot_general(a, b, (((1,), (0,)), ((), ())), preferred_element_type=f32)


def nt(a, b):
    return lax.dot_general(a, b, (((1,), (1,)), ((), ())), preferred_element_type=f32)


def tn(a, b):
    return lax.dot_general(a, b, (((0,), (0,)), ((), ())), preferred_element_type=f32)


def gelu_parts(v):
    phi = 0.5 + 0.5 * lax.erf(v * (0.5**0.5))
    slope = phi + v * (jnp.exp(-0.5 * v * v) * 0.3989422804014327)
    return v * phi, slope


def norm_parts(v):
    centered = v - jnp.mean(v, axis=-1, keepdims=True)
    spread = lax.rsqrt(jnp.mean(centered * centered, axis=-1, keepdims=True) + EPSILON)
    return centered * spread, spread


def norm_back(dy, gain, n, spread):
    dn = dy * gain
    dv = spread * (
        dn - jnp.mean(dn, axis=-1, keepdims=True) - n * jnp.mean(dn * n, axis=-1, keepdims=True)
    )
    return dv, jnp.sum(dy * n, axis=0, keepdims=True), jnp.sum(dy, axis=0, keepdims=True)


def lane_half(shape, h):
    return (lax.broadcasted_iota(jnp.int32, shape, 1) // HEAD) == h


def column(row):
    return jnp.broadcast_to(row, (8, row.shape[1])).T[:, 0:1]


def prefix_bias(shape, axis, prefix_len):
    return jnp.where(lax.broadcasted_iota(jnp.int32, shape, axis) < prefix_len, 0.0, MASKED)


def mask_bias(seg_q, seg_k, shape, key_axis, first_query):
    keep = seg_q == seg_k
    if first_query is not None:
        query = first_query + lax.broadcasted_iota(jnp.int32, shape, 1 - key_axis)
        keep = keep & (lax.broadcasted_iota(jnp.int32, shape, key_axis) <= query)
    return jnp.where(keep, 0.0, MASKED)


def pair_forward(q_pair, k_pair, v_pair, bias):
    outs, logs = [], []
    for h in range(2):
        half = lane_half(q_pair.shape, h)
        scores = nt(jnp.where(half, q_pair, jnp.zeros_like(q_pair)), k_pair) + bias
        top = jnp.max(scores, axis=1, keepdims=True)
        e = jnp.exp(scores - top)
        total = jnp.sum(e, axis=1, keepdims=True)
        outs.append(nn(e.astype(bf16), v_pair) * (1.0 / total))
        logs.append(top + jnp.log(total))
    return jnp.where(lane_half(outs[0].shape, 0), outs[0], outs[1]).astype(bf16), logs


def keep_logs(kept, logs, j):
    lane = lax.broadcasted_iota(jnp.int32, kept.shape, 1)
    for h in range(2):
        kept[...] = jnp.where(lane == 2 * j + h, logs[h], kept[...])


def pair_backward(q_pair, k_pair, v_pair, a_pair, da_pair, logs, bias_t):
    k_turned = k_pair.T
    prod = da_pair.astype(f32) * a_pair.astype(f32)
    prod_high = prod.astype(bf16)
    prod_low = (prod - prod_high.astype(f32)).astype(bf16)
    pick = (
        lax.broadcasted_iota(jnp.int32, (8, PAIR), 1) // HEAD
        == lax.broadcasted_iota(jnp.int32, (8, PAIR), 0)
    ).astype(bf16)
    delta = nt(pick, prod_high) + nt(pick, prod_low)
    dk = dv = None
    dq = []
    for h in range(2):
        half = lane_half(q_pair.shape, h)
        q = jnp.where(half, q_pair, jnp.zeros_like(q_pair))
        da = jnp.where(half, da_pair, jnp.zeros_like(da_pair))
        p = jnp.exp(nt(k_pair, q) + (bias_t - logs[h]))
        ds = (p * (nt(v_pair, da) - delta[h : h + 1])).astype(bf16)
        dv_h = nn(p.astype(bf16), da)
        dk_h = nn(ds, q)
        dk = dk_h if dk is None else dk + dk_h
        dv = dv_h if dv is None else dv + dv_h
        dq.append(nn(k_turned[h * HEAD : (h + 1) * HEAD], ds))
    return jnp.concatenate(dq, axis=0).T.astype(bf16), dk, dv


def whole_spec(shape):
    return pl.BlockSpec(shape, lambda i: (0,) * len(shape))


def shard_spec(shape, index=lambda i: i):
    return pl.BlockSpec((1,) + shape[1:], lambda i: (index(i), 0, 0))


def feed_forward_kernel(
    v2, out_grad, w_in, w_out, down, down_bias, up, up_bias, gain, shift,
    output, dr2, summed, vecs,
    n2_low, n2_hat, total, e_low, slope, grad, g, s1, h, xb, send, recv,
):
    step = pl.program_id(0)
    half = pl.num_programs(0) // 2
    links = Links(send, recv)
    reduce = AdapterReduce(links, 0, 0, g, s1, h, xb, summed, None, None, None, None)

    @pl.when(step == 0)
    def _():
        greet([links.tp_peer(1), links.side_peer()])
        n, _ = norm_parts(v2[...])
        n2_hat[...] = n
        normed = n * gain[1:2] + shift[1:2]
        total[...] = normed
        n2_low[...] = normed.astype(bf16)

    @pl.when(step < half)
    def _():
        act, bend = gelu_parts(nn(n2_low[...], w_in[0]))
        slope[step] = bend
        total[...] += nn(act.astype(bf16), w_out[0])

    @pl.when(step == half - 1)
    def _():
        act, bend = gelu_parts(nn(n2_low[...], down[...]) + down_bias[...])
        act = act.astype(bf16)
        resid = total[...] + 4.0 * (nn(act, up[...]) + up_bias[...])
        n, spread = norm_parts(resid)
        output[...] = (n * gain[2:3] + shift[2:3]).astype(bf16)
        dz, gain_part, shift_part = norm_back(out_grad[...].astype(f32), gain[2:3], n, spread)
        e_low[...] = dz.astype(bf16)
        four = (4.0 * dz).astype(bf16)
        g[0] = tn(act, four).astype(bf16).reshape(g.shape[1:])
        da = (nt(four, up[...]) * bend).astype(bf16)
        g[1] = tn(da, n2_low[...]).astype(bf16).reshape(g.shape[1:])
        reduce.start_beside()
        grad[...] = dz + nt(da, down[...])
        vecs[...] = jnp.zeros_like(vecs)
        vecs[2:3] = gain_part
        vecs[5:6] = shift_part
        vecs[6:7] = jnp.sum(four.astype(f32), axis=0, keepdims=True)
        vecs[7:8, 0 : down.shape[1]] = jnp.sum(da.astype(f32), axis=0, keepdims=True)

    @pl.when(step >= half)
    def _():
        du = (nt(e_low[...], w_out[0]) * slope[2 * half - 1 - step]).astype(bf16)
        grad[...] += nt(du, w_in[0])

    @pl.when(step == half)
    def _():
        reduce.start_side()

    @pl.when(step == 2 * half - 1)
    def _():
        _, spread = norm_parts(v2[...])
        dv, gain_part, shift_part = norm_back(grad[...], gain[1:2], n2_hat[...], spread)
        dr2[...] = dv
        vecs[1:2] = gain_part
        vecs[4:5] = shift_part
        reduce.sum_side()


def feed_forward(v2, out_grad, w_in, w_out, down, down_bias, up, up_bias, gain, shift):
    n, width, inner = w_in.shape
    block = v2.shape[0]
    adapt = down.shape[1]
    out = jax.ShapeDtypeStruct
    outs = (
        out((block, width), bf16),
        out((block, width), f32),
        out((LINE, adapt // GROUP, width), bf16),
        out((8, width), f32),
    )
    parts = (2, LINE, adapt // GROUP, width)
    turn = lambda i: jnp.minimum(i, 2 * n - 1 - i)
    return pl.pallas_call(
        feed_forward_kernel,
        grid=(2 * n,),
        out_shape=outs,
        in_specs=[whole_spec(v2.shape), whole_spec(out_grad.shape)]
        + [shard_spec(w_in.shape, turn), shard_spec(w_out.shape, turn)]
        + [whole_spec(a.shape) for a in (down, down_bias, up, up_bias, gain, shift)],
        out_specs=[whole_spec(a.shape) for a in outs],
        scratch_shapes=[
            VMEM((block, width), bf16),
            VMEM((block, width), f32),
            VMEM((block, width), f32),
            VMEM((block, width), bf16),
            VMEM((n, block, inner), f32),
            VMEM((block, width), f32),
            VMEM((2,) + parts, bf16),
            VMEM(parts, bf16),
            VMEM(parts, bf16),
            VMEM(parts[1:], bf16),
            pltpu.SemaphoreType.DMA((2,)),
            pltpu.SemaphoreType.DMA((2,)),
        ],
        compiler_params=pltpu.CompilerParams(
            collective_id=2, has_side_effects=True, vmem_limit_bytes=VMEM_BYTES
        ),
        name="feed_forward",
    )(v2, out_grad, w_in, w_out, down, down_bias, up, up_bias, gain, shift)


class Links:
    def __init__(self, send, recv):
        self.send, self.recv = send, recv
        self.row = lax.axis_index("rows")
        self.t = lax.axis_index("tp")
        self.flows = 0
        place = lax.rem(self.row, GROUP)
        self.base = self.row - place
        self.a = place // 2
        self.b = lax.rem(place, 2)
        self.place = place

    def flow(self):
        self.flows += 1
        return self.flows - 1

    def tp_peer(self, mask):
        return (self.row, self.t ^ mask)

    def line_peer(self, d):
        return (self.base + lax.rem(self.a + d, LINE) * 2 + self.b, self.t)

    def side_peer(self):
        return (self.base + self.a * 2 + (1 - self.b), self.t)

    def copy(self, src, dst, flow, peer):
        return pltpu.make_async_remote_copy(
            src_ref=src,
            dst_ref=dst,
            send_sem=self.send.at[flow],
            recv_sem=self.recv.at[flow],
            device_id=peer,
            device_id_type=MESH,
        )

    def start(self, src, dst, flow, peer):
        made = self.copy(src, dst, flow, peer)
        made.start()
        return made

    def arrived(self, dst, flow, peer):
        self.copy(dst, dst, flow, peer).wait_recv()


def greet(peers):
    barrier = pltpu.get_barrier_semaphore()
    for peer in peers:
        pl.semaphore_signal(barrier, inc=1, device_id=peer, device_id_type=MESH)
    pl.semaphore_wait(barrier, len(peers))


CHUNKS = 4


FLOWS = 14


class WeightGather:
    def __init__(self, links, base, across, own, full, stage, local):
        self.links, self.base, self.across = links, base, across
        self.own, self.full, self.stage, self.local = own, full, stage, local
        self.far, self.last = links.t ^ 2, links.t ^ 3
        a = links.a
        self.right = (links.base + jnp.minimum(a + 1, LINE - 1) * 2 + links.b, links.t)
        self.left = (links.base + jnp.maximum(a - 1, 0) * 2 + links.b, links.t)
        self.side = links.side_peer()
        self.sibling = links.tp_peer(1)
        self.over = links.tp_peer(2)

    def at(self, i, a, b):
        rows = self.own[i].shape[0] // GROUP
        return pl.ds(pl.multiple_of((a * 2 + b) * rows, rows), rows)

    def part(self, i, a, b):
        return self.full[i].at[self.far, self.at(i, a, b)]

    def flow(self, i, k):
        return self.base + i * FLOWS + k

    def over_copy(self, i, k):
        links = self.links
        b = links.b if k == 0 else 1 - links.b
        at = self.at(i, links.a, b)
        return links.copy(
            self.own[i].at[at], self.full[i].at[links.t, at], self.flow(i, k), self.over
        )

    def beside_copy(self, i):
        return self.links.copy(
            self.own[i], self.full[i].at[self.links.t], self.flow(i, 2), self.sibling
        )

    def pass_copy(self, i):
        whole = self.full[i].at[self.far]
        return self.links.copy(whole, whole, self.flow(i, 3), self.sibling)

    def moved(self, i, a, flow, peer):
        part = self.part(i, a, self.links.b)
        return self.links.copy(part, part, self.flow(i, flow), peer)

    def stage_in(self, i):
        stage = self.full[i].at[self.links.t] if self.stage is None else self.stage[i]
        return pltpu.make_async_copy(self.own[i], stage, self.local.at[2 * i])

    def stage_out(self, i):
        return pltpu.make_async_copy(
            self.stage[i], self.full[i].at[self.links.t], self.local.at[2 * i + 1]
        )

    def start_over(self, i, k):
        self.over_copy(i, k).start()

    def start_beside(self, i):
        self.beside_copy(i).start()
        self.stage_in(i).start()

    def own_ready(self, i):
        self.stage_in(i).wait()

    def beside_ready(self, i):
        self.links.arrived(self.full[i].at[self.links.t ^ 1], self.flow(i, 2), self.sibling)

    def far_ready(self, i):
        self.links.arrived(self.full[i].at[self.last], self.flow(i, 3), self.sibling)

    def keep_own(self, i):
        self.own_ready(i)
        self.stage_out(i).start()

    def came_over(self, i):
        mine = self.part(i, self.links.a, self.links.b)
        self.links.arrived(mine, self.flow(i, 0), self.over)
        self.spread(i)

    def spread(self, i):
        a = self.links.a

        @pl.when(a < LINE - 1)
        def _():
            self.moved(i, a, 4, self.right).start()

        @pl.when(a > 0)
        def _():
            self.moved(i, a, 7, self.left).start()

        if self.across[i] == 1:
            self.moved(i, a, 10, self.side).start()

    def along(self, i, k):
        links, a = self.links, self.links.a

        @pl.when(a - 1 - k >= 0)
        def _():
            links.arrived(self.part(i, a - 1 - k, links.b), self.flow(i, 4 + k), self.left)
            if k < LINE - 2:

                @pl.when(a < LINE - 1)
                def _():
                    self.moved(i, a - 1 - k, 5 + k, self.right).start()

            self.moved(i, a - 1 - k, 11 + k, self.side).start()

        @pl.when(a + 1 + k <= LINE - 1)
        def _():
            links.arrived(self.part(i, a + 1 + k, links.b), self.flow(i, 7 + k), self.right)
            if k < LINE - 2:

                @pl.when(a > 0)
                def _():
                    self.moved(i, a + 1 + k, 8 + k, self.left).start()

            self.moved(i, a + 1 + k, 13 - k, self.side).start()

    def side_part(self, i, k):
        links, a = self.links, self.links.a
        if k == 0:
            return self.part(i, a, 1 - links.b)
        piece = jnp.where(k <= a, a - k, a + LINE - k)
        return self.part(i, piece, 1 - links.b)

    def complete(self, i):
        links = self.links
        if self.across[i] == 2:
            links.arrived(self.side_part(i, 0), self.flow(i, 1), self.over)
        for k in range(self.across[i] - 1, LINE):
            links.arrived(self.side_part(i, k), self.flow(i, 10 + k), self.side)
        self.pass_copy(i).start()

    def finish(self, i):
        if self.stage is not None:
            self.beside_ready(i)
            self.far_ready(i)
            self.stage_out(i).wait()
        for k in range(self.across[i]):
            self.over_copy(i, k).wait_send()
        self.beside_copy(i).wait_send()
        self.spread_sent(i)

    def spread_sent(self, i):
        a = self.links.a
        self.pass_copy(i).wait_send()
        for k in range(LINE - 1):

            @pl.when((a < LINE - 1) & (a - k >= 0))
            def _():
                self.moved(i, a - k, 4 + k, self.right).wait_send()

            @pl.when((a > 0) & (a + k <= LINE - 1))
            def _():
                self.moved(i, a + k, 7 + k, self.left).wait_send()

        for k in range(self.across[i] - 1, LINE):
            piece = a if k == 0 else jnp.where(k <= a, a - k, a + LINE - k)
            self.moved(i, piece, 10 + k, self.side).wait_send()


class AdapterSpread(WeightGather):
    def __init__(self, links, base, full):
        super().__init__(links, base, [1], None, full, None, None)
        self.half = lax.rem(links.t, 2)

    def part(self, i, a, b):
        return self.full.at[self.half, b, a]

    def pass_copy(self, i):
        whole = self.full.at[self.half]
        return self.links.copy(whole, whole, self.flow(i, 3), self.sibling)

    def finish(self, i):
        self.links.arrived(self.full.at[1 - self.half], self.flow(i, 3), self.sibling)
        self.spread_sent(i)


class AdapterReduce:
    def __init__(self, links, base, levels, g, s1, h, xb, h2, zb, p3, yb, hb):
        self.links, self.base, self.levels = links, base, levels
        self.g, self.s1, self.h, self.xb, self.h2 = g, s1, h, xb, h2
        self.zb, self.p3, self.yb, self.hb = zb, p3, yb, hb
        self.half = lax.rem(links.t, 2)
        self.groups = [(links.row ^ (GROUP << level), links.t) for level in range(levels)]

    def beside(self):
        return self.links.copy(
            self.g.at[1 - self.half], self.s1, self.base, self.links.tp_peer(1)
        )

    def side(self):
        links = self.links
        return links.copy(self.h.at[1 - links.b], self.xb, self.base + 1, links.side_peer())

    def line(self, d):
        links = self.links
        return links.copy(
            self.h2.at[lax.rem(links.a + d, LINE)],
            self.zb.at[d - 1],
            self.base + 1 + d,
            links.line_peer(d),
        )

    def over(self):
        return self.links.copy(self.p3, self.yb, self.base + 1 + LINE, self.links.tp_peer(2))

    def group(self, level):
        return self.links.copy(
            self.hb.at[2 * level],
            self.hb.at[2 * level + 1],
            self.base + 2 + LINE + level,
            self.groups[level],
        )

    def start_beside(self):
        self.beside().start()

    def start_side(self):
        self.beside().wait()
        self.h[...] = (self.g[self.half].astype(f32) + self.s1[...].astype(f32)).astype(bf16)
        self.side().start()

    def sum_side(self):
        self.side().wait()
        self.h2[...] = (self.h[self.links.b].astype(f32) + self.xb[...].astype(f32)).astype(bf16)

    def start_line(self):
        for d in range(1, LINE):
            self.line(d).start()

    def start_over(self):
        for d in range(1, LINE):
            self.line(d).wait()
        total = self.h2[self.links.a].astype(f32)
        for d in range(1, LINE):
            total = total + self.zb[d - 1].astype(f32)
        self.p3[...] = total.astype(bf16)
        self.over().start()

    def result(self):
        self.over().wait()
        value = self.p3[...].astype(f32) + self.yb[...].astype(f32)
        for level in range(self.levels):
            self.hb[2 * level] = value.astype(bf16)
            self.group(level).start()
            self.group(level).wait()
            value = self.hb[2 * level].astype(f32) + self.hb[2 * level + 1].astype(f32)
        return value.astype(bf16)


class RowGather:
    FLOWS = 1 + 2 * 4

    def __init__(self, links, base, own, full):
        self.links, self.base, self.own, self.full = links, base, own, full
        self.far, self.last = links.t ^ 2, links.t ^ 3
        self.sibling, self.over = links.tp_peer(1), links.tp_peer(2)

    def at(self, c):
        rows = self.own.shape[0] // CHUNKS
        return pl.ds(c * rows, rows)

    def beside_copy(self):
        return self.links.copy(self.own, self.full.at[self.links.t], self.base, self.sibling)

    def over_copy(self, c):
        at = self.at(c)
        return self.links.copy(
            self.own.at[at], self.full.at[self.links.t, at], self.base + 1 + c, self.over
        )

    def pass_copy(self, c):
        part = self.full.at[self.far, self.at(c)]
        return self.links.copy(part, part, self.base + 1 + CHUNKS + c, self.sibling)

    def start_beside(self):
        self.beside_copy().start()

    def start_over(self):
        for c in range(CHUNKS):
            self.over_copy(c).start()

    def came_beside(self):
        self.links.arrived(self.full.at[self.links.t ^ 1], self.base, self.sibling)

    def came_over_chunk(self, c):
        self.links.arrived(self.full.at[self.far, self.at(c)], self.base + 1 + c, self.over)
        self.pass_copy(c).start()

    def came_over(self):
        for c in range(CHUNKS):
            self.came_over_chunk(c)

    def came_last(self):
        for c in range(CHUNKS):
            self.links.arrived(
                self.full.at[self.last, self.at(c)], self.base + 1 + CHUNKS + c, self.sibling
            )

    def sent(self):
        self.beside_copy().wait_send()
        for c in range(CHUNKS):
            self.over_copy(c).wait_send()
            self.pass_copy(c).wait_send()


class RowScatter:
    FLOWS = 2 + 4

    def __init__(self, links, base, part, near, near_far, mid, far):
        self.links, self.base, self.part = links, base, part
        self.near, self.near_far, self.mid, self.far = near, near_far, mid, far
        self.sibling, self.over = links.tp_peer(1), links.tp_peer(2)

    def at(self, c):
        rows = self.near.shape[0] // CHUNKS
        return pl.ds(c * rows, rows)

    def first_copy(self):
        return self.links.copy(
            self.part.at[self.links.t ^ 3], self.near_far, self.base, self.sibling
        )

    def second_copy(self):
        return self.links.copy(
            self.part.at[self.links.t ^ 1], self.near, self.base + 1, self.sibling
        )

    def over_copy(self, c):
        at = self.at(c)
        return self.links.copy(
            self.mid.at[at], self.far.at[at], self.base + 2 + c, self.over
        )

    def send_over(self):
        self.links.arrived(self.near_far, self.base, self.sibling)
        for c in range(CHUNKS):
            at = self.at(c)
            self.mid[at] = (
                self.part[self.links.t ^ 2, at].astype(f32) + self.near_far[at].astype(f32)
            ).astype(bf16)
            self.over_copy(c).start()

    def came_beside(self):
        self.links.arrived(self.near, self.base + 1, self.sibling)

    def came_over(self, c):
        at = self.at(c)
        self.links.arrived(self.far.at[at], self.base + 2 + c, self.over)
        return (
            self.part[self.links.t, at].astype(f32)
            + self.near[at].astype(f32)
            + self.far[at].astype(f32)
        )

    def sent(self):
        self.first_copy().wait_send()
        self.second_copy().wait_send()
        for c in range(CHUNKS):
            self.over_copy(c).wait_send()


def halves(own, full, stage):
    outs = ([], [], [])
    for one, whole, held in zip(own, full, stage):
        rows = one.shape[0] // 2
        for o in range(2):
            at = pl.ds(o * rows, rows)
            for out, view in zip(outs, (one.at[at], whole.at[:, at], held.at[at])):
                out.append(view)
    return outs


def cut(refs, *counts):
    out, at = [], 0
    for count in counts:
        out.append(refs[at : at + count])
        at += count
    return out


def forward_kernel(prefix_len, *refs):
    ins, self_outs, cross_outs, kept_outs, scratch = cut(refs, 18, 6, 6, 6, 26)
    x, pre_cross, wq, wk, wv, wo, pre, dec, src, gain, shift = ins[:11]
    memory, own_cross, own_ffn = ins[11], list(ins[12:16]), list(ins[16:18])
    q_out, k_out, v_out, a_out, l_out, resid = self_outs
    q2_out, k2_out, v2_out, a2_out, l2_out, resid2 = cross_outs
    cross_kept, ffn_full = list(kept_outs[:4]), list(kept_outs[4:])
    cross_full, held = list(scratch[:4]), list(scratch[4:6])
    (
        m_full, pre_full, x_full, part, kept, bias, near, near_far, mid, far, pre_stage, n1_low,
        send, recv, cross_local, ffn_local, m_local, keep_local, pre_local, spare,
    ) = scratch[6:]
    del spare
    block, lanes = x.shape[0], q_out.shape[1]
    links = Links(send, recv)
    t = links.t
    early = range(4)
    late = range(4)
    cross = WeightGather(links, 0, [1] * 4, own_cross, cross_full, None, cross_local)
    ffn = WeightGather(links, 4 * FLOWS, [2] * 4, *halves(own_ffn, ffn_full, held), ffn_local)
    at = 8 * FLOWS
    x_rows = RowGather(links, at, x, x_full)
    at += RowGather.FLOWS
    m_rows = RowGather(links, at, memory, m_full)
    at += RowGather.FLOWS
    sums = RowScatter(links, at, part, near, near_far, mid, far)
    at += RowScatter.FLOWS
    m_keep = pltpu.make_async_copy(memory, m_full.at[t], m_local.at[0])
    pre_keep = pltpu.make_async_copy(pre_stage, pre_full.at[t], pre_local.at[0])
    pre_sends = [
        links.copy(pre_stage, pre_full.at[t], at + m - 1, links.tp_peer(m)) for m in (1, 2, 3)
    ]
    cross_keeps = [
        pltpu.make_async_copy(cross_full[i], cross_kept[i], keep_local.at[i]) for i in range(4)
    ]

    greet(
        [links.tp_peer(m) for m in (1, 2, 3)]
        + [links.line_peer(d) for d in range(1, LINE)]
        + [links.side_peer()]
    )
    x_rows.start_over()
    x_rows.start_beside()
    kept[...] = jnp.zeros_like(kept)
    pre_stage[...] = jnp.zeros_like(pre_stage)
    for o in range(2):
        pre_stage[o * PRE_PACK : o * PRE_PACK + prefix_len] = pre_cross[:, o]
    pre_keep.start()
    for one in pre_sends:
        one.start()
    m_rows.start_beside()
    m_keep.start()
    for i in early:
        cross.start_beside(i)
    for i in late:
        ffn.start_beside(i)

    for target, o in ((k_out, 0), (v_out, 1)):
        target[0:PRE] = jnp.zeros((PRE, lanes), bf16)
        target[0:prefix_len] = pre[:, o]

    def project(rows, index):
        at = pl.multiple_of(index * block, block)
        q_out[pl.ds(at, block)] = (SCALE * nn(rows, wq[...])).astype(bf16)
        k_out[pl.ds(PRE + at, block)] = nn(rows, wk[...]).astype(bf16)
        v_out[pl.ds(PRE + at, block)] = nn(rows, wv[...]).astype(bf16)

    project(x[...], t)
    x_rows.came_beside()
    project(x_full[t ^ 1], t ^ 1)
    for c in range(CHUNKS):
        x_rows.came_over_chunk(c)
        if c == 1:
            for i in early:
                cross.start_over(i, 0)
    for i in range(2):
        ffn.start_over(i, 0)
    project(x_full[t ^ 2], t ^ 2)
    x_rows.came_last()
    project(x_full[t ^ 3], t ^ 3)

    @pl.loop(0, 4)
    def _(order):
        here = t ^ (3 - order)
        for i in range(4):
            keys = PRE + (i + 1) * block

            @pl.when(here == i)
            def _():
                bias[:, 0:PRE] = prefix_bias((block, PRE), 1, prefix_len)
                bias[:, PRE:keys] = mask_bias(
                    column(dec[:, i * block : (i + 1) * block]),
                    dec[:, 0 : keys - PRE],
                    (block, keys - PRE),
                    1,
                    i * block,
                )

                @pl.loop(0, lanes // PAIR)
                def _(j):
                    cols = pl.ds(pl.multiple_of(j * PAIR, PAIR), PAIR)
                    mixture, logs = pair_forward(
                        q_out[i * block : (i + 1) * block, cols],
                        k_out[0:keys, cols],
                        v_out[0:keys, cols],
                        bias[:, 0:keys],
                    )
                    a_out[i, :, cols] = mixture
                    keep_logs(kept, logs, j)

        l_out[here] = kept[...].T[0:8]
        part[here] = nn(a_out[here], wo[...]).astype(bf16)

        @pl.when(order == 0)
        def _():
            sums.first_copy().start()
            for i in early:
                cross.came_over(i)

        @pl.when(order == 1)
        def _():
            m_rows.start_over()
            sums.send_over()

        @pl.when(order == 2)
        def _():
            sums.second_copy().start()
            for i in early:
                cross.along(i, 0)

    for i in range(2):
        ffn.came_over(i)
    for i in late:
        ffn.keep_own(i)
    for i in early:
        cross.along(i, 1)
    for i in early:
        cross.along(i, 2)
    sums.came_beside()
    for c in range(CHUNKS):
        rows = sums.at(c)
        resid[rows] = x[rows].astype(f32) + sums.came_over(c)
    for i in range(2):
        ffn.start_over(i, 1)
    for k in range(2):
        for i in (2, 3):
            ffn.start_over(i, k)
    for i in range(2):
        ffn.along(i, 0)
    m_rows.came_over()

    n, _ = norm_parts(resid[...])
    normed = n * gain[0:1] + shift[0:1]
    resid2[...] = normed
    n1_low[...] = normed.astype(bf16)
    kept[...] = jnp.zeros_like(kept)
    own_queries = dec[:, pl.ds(pl.multiple_of(t * block, block), block)]
    keys = k2_out.shape[1]
    bias[:, 0:PRE] = prefix_bias((block, PRE), 1, prefix_len)
    bias[:, PRE:] = mask_bias(column(own_queries), src[...], (block, keys - PRE), 1, None)
    for i in early:
        cross.complete(i)
    m_rows.came_beside()
    m_rows.came_last()
    for m in (1, 2, 3):
        links.arrived(pre_full.at[t ^ m], at + m - 1, links.tp_peer(m))
    m_keep.wait()
    pre_keep.wait()
    for i in early:
        cross.own_ready(i)

    events = {
        0: [lambda: ffn.along(0, 1), lambda: ffn.along(1, 1)],
        2: [lambda: ffn.along(0, 2), lambda: ffn.came_over(2)],
        3: [lambda: ffn.along(1, 2), lambda: ffn.came_over(3)]
        + [functools.partial(cross.far_ready, i) for i in range(4)],
        4: [lambda: ffn.along(2, 0), lambda: ffn.complete(0)],
        5: [lambda: ffn.along(3, 0), lambda: ffn.along(2, 1), lambda: ffn.complete(1)],
        6: [lambda: ffn.along(3, 1), lambda: ffn.along(2, 2)],
        7: [lambda: ffn.along(3, 2)],
    }

    @pl.loop(0, 4)
    def _(order):
        s = t ^ order

        @pl.when(order == 1)
        def _():
            for i in early:
                cross.beside_ready(i)

        q2_out[s] = (SCALE * nn(n1_low[...], cross_full[0][s])).astype(bf16)
        for target, o in ((k2_out, 0), (v2_out, PRE_PACK)):
            target[s, 0:PRE_PACK] = pre_full[s, o : o + PRE_PACK]
            target[s, PRE_PACK:PRE] = jnp.zeros((PRE - PRE_PACK, lanes), bf16)

        @pl.loop(0, 4)
        def _(i):
            rows = m_full[i]
            to = pl.ds(pl.multiple_of(PRE + i * block, PRE), block)
            k2_out[s, to] = nn(rows, cross_full[1][s]).astype(bf16)
            v2_out[s, to] = nn(rows, cross_full[2][s]).astype(bf16)

        for j in range(lanes // PAIR):
            cols = slice(j * PAIR, (j + 1) * PAIR)
            mixture, logs = pair_forward(
                q2_out[s, :, cols], k2_out[s, :, cols], v2_out[s, :, cols], bias[...]
            )
            a2_out[s, :, cols] = mixture
            keep_logs(kept, logs, j)
            for step in range(4):

                @pl.when(order == step)
                def _():
                    for event in events.get(2 * step + j, []):
                        event()

        l2_out[s] = kept[...].T[0:8]
        resid2[...] += nn(a2_out[s], cross_full[3][s])

    for one in cross_keeps:
        one.start()
    for i in (2, 3):
        ffn.complete(i)
    for i in early:
        cross.finish(i)
    for i in late:
        ffn.finish(i)
    x_rows.sent()
    m_rows.sent()
    sums.sent()
    for one in pre_sends:
        one.wait_send()
    for one in cross_keeps:
        one.wait()


def forward(
    prefix_len, x, memory, prefixes, self_weights, cross_weights, ffn_weights, dec, src, gain, shift
):
    n = 4
    block, width = x.shape
    lanes = self_weights[0].shape[1]
    seq = n * block
    out = jax.ShapeDtypeStruct
    flows = 8 * FLOWS + 2 * RowGather.FLOWS + RowScatter.FLOWS + 3
    self_outs = (
        out((seq, lanes), bf16),
        out((PRE + seq, lanes), bf16),
        out((PRE + seq, lanes), bf16),
        out((n, block, lanes), bf16),
        out((n, 8, block), f32),
        out((block, width), f32),
    )
    cross_outs = (
        out((n, block, lanes), bf16),
        out((n, PRE + seq, lanes), bf16),
        out((n, PRE + seq, lanes), bf16),
        out((n, block, lanes), bf16),
        out((n, 8, block), f32),
        out((block, width), f32),
    )
    full = tuple(out((n,) + w.shape, w.dtype) for w in (*cross_weights, *ffn_weights))
    given = (x, prefixes[1], *self_weights, prefixes[0], dec, src, gain, shift)
    anywhere = pl.BlockSpec(memory_space=pltpu.HBM)
    rows = VMEM((block, width), bf16)
    all_rows = VMEM((n, block, width), bf16)
    dma = pltpu.SemaphoreType.DMA
    return pl.pallas_call(
        functools.partial(forward_kernel, prefix_len),
        grid=(1,),
        out_shape=self_outs + cross_outs + full,
        in_specs=[whole_spec(g.shape) for g in given] + [anywhere] * 7,
        out_specs=[whole_spec(o.shape) for o in self_outs + cross_outs] + [anywhere] * 6,
        scratch_shapes=[VMEM((n,) + w.shape, w.dtype) for w in cross_weights]
        + [VMEM(w.shape, w.dtype) for w in ffn_weights]
        + [
            all_rows,
            VMEM((n, 2 * PRE_PACK, lanes), bf16),
            all_rows,
            all_rows,
            VMEM((block, 128), f32),
            VMEM((block, PRE + seq), f32),
            rows,
            rows,
            rows,
            rows,
            VMEM((2 * PRE_PACK, lanes), bf16),
            rows,
            dma((flows,)),
            dma((flows,)),
            dma((8,)),
            dma((8,)),
            dma((1,)),
            dma((4,)),
            dma((1,)),
            dma((1,)),
        ],
        compiler_params=pltpu.CompilerParams(
            collective_id=0, has_side_effects=True, vmem_limit_bytes=VMEM_BYTES
        ),
        name="forward",
    )(*given, memory, *cross_weights, *ffn_weights)


def doublings(count):
    levels = 0
    while (1 << levels) < count:
        levels += 1
    return levels


class Doubling:
    def __init__(self, links, base, levels, outgo, income):
        self.links, self.base, self.levels = links, base, levels
        self.outgo, self.income = outgo, income

    def move(self, level):
        return self.links.copy(
            self.outgo.at[level],
            self.income.at[level],
            self.base + level,
            (self.links.row ^ (1 << level), self.links.t),
        )

    def begin(self, value):
        self.outgo[0] = value
        self.move(0).start()

    def value(self, level):
        self.move(level).wait()
        return self.outgo[level] + self.income[level]

    def step(self, level):
        value = self.value(level)
        self.outgo[level + 1] = value
        self.move(level + 1).start()


def backward_kernel(prefix_len, reduce_levels, levels, *refs):
    ins, later, outs, scratch = cut(refs, 16, 9, 5, 52)
    dr2, v1, q, k, v, a, logs, wq, wo, wk, wv, dec, src, gain, vecs_in, h2 = ins
    tokens_grad, memory_grad, adapter, self_pre, sums = outs
    (
        dr1, dr1_low, dr2_low, bias, da, dq, dk, dv, total, zb, p3, yb, hb,
        cross, vecs, dm, dr1_full, part, dq1, dk1, dv1,
        near, near_far, mid, far, m_near, m_near_far, m_mid, m_far,
        cross_beside, cross_mid, cross_over, vecs_beside, vecs_mid, vecs_over,
        outgo, income, pre_outgo, pre_income, send, recv, keep_sem, load_sem,
    ) = scratch[:-9]
    loaded = scratch[-9:]
    q1, k1, v1_heads, a1, logs1, wq1, wk1, wv1, wo1 = loaded
    step = pl.program_id(0)
    steps = pl.num_programs(0) - 1
    block, lanes = q.shape[1:]
    keys = k.shape[1]
    links = Links(send, recv)
    t = links.t
    at = 0
    rows = RowGather(links, at, dr1_low, dr1_full)
    at += RowGather.FLOWS
    reduce = AdapterReduce(links, at, reduce_levels, None, None, None, None, h2, zb, p3, yb, hb)
    at += 2 + LINE + reduce_levels
    spread = AdapterSpread(links, at, adapter)
    at += FLOWS
    m_sums = RowScatter(links, at, dm, m_near, m_near_far, m_mid, m_far)
    at += RowScatter.FLOWS
    x_sums = RowScatter(links, at, part, near, near_far, mid, far)
    at += RowScatter.FLOWS
    totals = Doubling(links, at, levels, outgo, income)
    at += levels
    pre_totals = Doubling(links, at, levels, pre_outgo, pre_income)
    at += levels
    keep = pltpu.make_async_copy(dr1_low, dr1_full.at[t], keep_sem.at[0])
    loads = [
        pltpu.make_async_copy(src_ref, dst_ref, load_sem.at[i])
        for i, (src_ref, dst_ref) in enumerate(zip(later, loaded))
    ]

    beside, over = links.tp_peer(1), links.tp_peer(2)
    to_beside = (
        links.copy(cross.at[t ^ 1], cross_beside.at[0], at, beside),
        links.copy(cross.at[t ^ 3], cross_beside.at[1], at + 1, beside),
        links.copy(vecs, vecs_beside, at + 2, beside),
    )
    to_over = (
        links.copy(cross_mid, cross_over, at + 3, over),
        links.copy(vecs_mid, vecs_over, at + 4, over),
    )

    @pl.when(step == 0)
    def _():
        greet(
            [links.tp_peer(m) for m in (1, 2, 3)]
            + [links.line_peer(d) for d in range(1, LINE)]
            + [links.side_peer()]
            + [(links.row ^ (1 << level), t) for level in range(doublings(GROUP), levels)]
        )
        reduce.start_line()
        dr2_low[...] = dr2[...].astype(bf16)
        total[...] = jnp.zeros_like(total)
        own_queries = dec[:, pl.ds(pl.multiple_of(t * block, block), block)]
        bias[0:PRE] = prefix_bias((PRE, block), 0, prefix_len)
        bias[PRE:] = mask_bias(own_queries, column(src[...]), (keys - PRE, block), 0, None)

    @pl.when(step < steps)
    def _():
        da[...] = nt(dr2_low[...], wo[0]).astype(bf16)

        @pl.when(step == 0)
        def _():
            for one in loads:
                one.start()

        @pl.loop(0, lanes // PAIR)
        def _(j):
            cols = pl.ds(pl.multiple_of(j * PAIR, PAIR), PAIR)
            dq_pair, dk_pair, dv_pair = pair_backward(
                q[0, :, cols],
                k[0, :, cols],
                v[0, :, cols],
                a[0, :, cols],
                da[:, cols],
                [logs[0, pl.ds(2 * j + i, 1)] for i in range(2)],
                bias[...],
            )
            dq[:, cols] = dq_pair
            cross[step, 0:PRE_PACK, cols] = dk_pair[0:PRE_PACK]
            cross[step, PRE_PACK : 2 * PRE_PACK, cols] = dv_pair[0:PRE_PACK]
            dk[step, :, cols] = dk_pair[PRE:].astype(bf16)
            dv[step, :, cols] = dv_pair[PRE:].astype(bf16)

            @pl.when((step == 2) & (j == 1))
            def _():
                reduce.start_over()

            @pl.when((step == 3) & (j == 1))
            def _():
                p3[...] = reduce.result()
                settle = pltpu.make_async_copy(
                    p3, adapter.at[spread.half, links.b, links.a], keep_sem.at[1]
                )
                settle.start()
                settle.wait()
                spread.spread(0)

        total[...] += nt(dq[...], wq[0])

    @pl.when(step == steps)
    def _():
        n, spread_one = norm_parts(v1[...])
        grad, gain_part, shift_part = norm_back(
            dr2[...] + SCALE * total[...], gain[0:1], n, spread_one
        )
        dr1_low[...] = grad.astype(bf16)
        rows.start_over()
        rows.start_beside()
        keep.start()
        dr1[...] = grad
        vecs[...] = vecs_in[...]
        vecs[0:1] = gain_part
        vecs[3:4] = shift_part
        for one in to_beside:
            one.start()
        dk1[...] = jnp.zeros_like(dk1)
        dv1[...] = jnp.zeros_like(dv1)

        @pl.loop(0, 4)
        def _(order):
            here = t ^ (3 - order)
            to = pl.ds(pl.multiple_of(here * block, block), block)
            value = None
            for shard in range(dk.shape[0]):
                term = nt(dk[shard, to], wk[shard]) + nt(dv[shard, to], wv[shard])
                value = term if value is None else value + term
            dm[here] = value.astype(bf16)

        m_sums.first_copy().start()
        m_sums.second_copy().start()
        for one in loads:
            one.wait()
        keep.wait()
        rows.came_beside()
        for one in to_beside:
            one.wait()
        cross_mid[...] = cross[t ^ 2] + cross_beside[1]
        vecs_mid[...] = vecs[...] + vecs_beside[...]
        for one in to_over:
            one.start()
        spread.along(0, 0)

        @pl.loop(0, 4)
        def _(order):
            here = t ^ order

            @pl.when(order == 2)
            def _():
                rows.came_over()
                m_sums.send_over()
                rows.came_last()

            da[...] = nt(dr1_full[here], wo1[...]).astype(bf16)
            for i in range(4):
                own = slice(i * block, (i + 1) * block)
                size = PRE + (i + 1) * block

                @pl.when(here == i)
                def _():
                    bias[0:PRE] = prefix_bias((PRE, block), 0, prefix_len)
                    bias[PRE:size] = mask_bias(
                        dec[:, own],
                        column(dec[:, 0 : size - PRE]),
                        (size - PRE, block),
                        0,
                        i * block,
                    )

                    @pl.loop(0, lanes // PAIR)
                    def _(j):
                        cols = pl.ds(pl.multiple_of(j * PAIR, PAIR), PAIR)
                        dq_pair, dk_pair, dv_pair = pair_backward(
                            q1[own, cols],
                            k1[0:size, cols],
                            v1_heads[0:size, cols],
                            a1[i, :, cols],
                            da[:, cols],
                            [logs1[i, pl.ds(2 * j + o, 1)] for o in range(2)],
                            bias[0:size],
                        )
                        dq1[i, :, cols] = dq_pair
                        dk1[0:size, cols] += dk_pair
                        dv1[0:size, cols] += dv_pair

            @pl.when(order < 2)
            def _():
                for k in range(2):

                    @pl.when(order == k)
                    def _():
                        spread.along(0, k + 1)

            @pl.when(order == 2)
            def _():
                for one in to_over:
                    one.wait()
                value = vecs_mid[...] + vecs_over[...]
                pieces = [cross[t] + cross_beside[0] + cross_over[...]] + [
                    value[:, o * lanes : (o + 1) * lanes] for o in range(vecs.shape[1] // lanes)
                ]
                totals.begin(jnp.concatenate(pieces, axis=0))
                spread.complete(0)

        pre_totals.begin(jnp.concatenate([dk1[0:PRE_PACK], dv1[0:PRE_PACK]], axis=0))
        for order in range(4):
            here = t ^ (3 - order)
            done = pl.ds(pl.multiple_of(PRE + here * block, PRE), block)
            part[here] = (
                SCALE * nt(dq1[here], wq1[...])
                + nt(dk1[done].astype(bf16), wk1[...])
                + nt(dv1[done].astype(bf16), wv1[...])
            ).astype(bf16)
            if order == 0:
                x_sums.first_copy().start()
                totals.step(0)
            if order == 1:
                x_sums.send_over()
                pre_totals.step(0)
            if order == 2:
                x_sums.second_copy().start()

        for level in range(1, levels - 1):
            totals.step(level)
            pre_totals.step(level)
        m_sums.came_beside()
        for c in range(CHUNKS):
            memory_grad[m_sums.at(c)] = m_sums.came_over(c).astype(bf16)
        sums[...] = totals.value(levels - 1)
        self_pre[...] = pre_totals.value(levels - 1)
        x_sums.came_beside()
        for c in range(CHUNKS):
            here = x_sums.at(c)
            tokens_grad[here] = (dr1[here] + x_sums.came_over(c)).astype(bf16)
        spread.finish(0)
        rows.sent()
        m_sums.sent()
        x_sums.sent()


def backward(
    prefix_len, row_count, dr2, resid_one, cross_saved, cross_weights, self_saved, self_weights,
    dec, src, gain, vecs, summed,
):
    q, k, v, a, logs = cross_saved
    wq, wk, wv, wo = cross_weights
    n, block, lanes = q.shape
    keys = k.shape[1]
    width = dr2.shape[1]
    reduce_levels = doublings(row_count // GROUP)
    levels = doublings(row_count)
    piece = summed.shape[1]
    half = (2, LINE, piece, width)
    packed = 2 * PRE_PACK
    height = packed + vecs.shape[0] * width // lanes
    out = jax.ShapeDtypeStruct
    outs = (
        out((block, width), bf16),
        out((block, width), bf16),
        out((2,) + half, bf16),
        out((packed, lanes), f32),
        out((height, lanes), f32),
    )
    flows = (
        RowGather.FLOWS + 2 + LINE + reduce_levels + FLOWS + 2 * RowScatter.FLOWS + 2 * levels + 5
    )
    later = (*self_saved, *self_weights)
    low, wide = VMEM((block, width), bf16), VMEM((block, width), f32)
    dma = pltpu.SemaphoreType.DMA
    bounded = lambda i: jnp.minimum(i, n - 1)

    def once(x):
        return pl.BlockSpec(x.shape, lambda i: (0,) * len(x.shape), pipeline_mode=pl.Buffered(1))

    return pl.pallas_call(
        functools.partial(backward_kernel, prefix_len, reduce_levels, levels),
        grid=(n + 1,),
        out_shape=outs,
        in_specs=[once(dr2), once(resid_one)]
        + [shard_spec(x.shape, bounded) for x in (q, k, v, a, logs, wq, wo)]
        + [once(x) for x in (wk, wv, dec, src, gain, vecs, summed)]
        + [pl.BlockSpec(memory_space=pltpu.HBM)] * len(later),
        out_specs=[whole_spec(o.shape) for o in outs[:2]]
        + [pl.BlockSpec(memory_space=pltpu.HBM)]
        + [whole_spec(o.shape) for o in outs[3:]],
        scratch_shapes=[
            wide,
            low,
            low,
            VMEM((keys, block), f32),
            VMEM((block, lanes), bf16),
            VMEM((block, lanes), bf16),
            VMEM((n, keys - PRE, lanes), bf16),
            VMEM((n, keys - PRE, lanes), bf16),
            wide,
            VMEM((LINE - 1, piece, width), bf16),
            VMEM((piece, width), bf16),
            VMEM((piece, width), bf16),
            VMEM((max(1, 2 * reduce_levels), piece, width), bf16),
            VMEM((n, packed, lanes), f32),
            VMEM(vecs.shape, f32),
            VMEM((n, block, width), bf16),
            VMEM((n, block, width), bf16),
            VMEM((n, block, width), bf16),
            VMEM((n, block, lanes), bf16),
            VMEM((keys, lanes), f32),
            VMEM((keys, lanes), f32),
        ]
        + [low] * 8
        + [
            VMEM((2, packed, lanes), f32),
            VMEM((packed, lanes), f32),
            VMEM((packed, lanes), f32),
            VMEM(vecs.shape, f32),
            VMEM(vecs.shape, f32),
            VMEM(vecs.shape, f32),
            VMEM((levels, height, lanes), f32),
            VMEM((levels, height, lanes), f32),
            VMEM((levels, packed, lanes), f32),
            VMEM((levels, packed, lanes), f32),
            dma((flows,)),
            dma((flows,)),
            dma((2,)),
            dma((len(later),)),
        ]
        + [VMEM(x.shape, x.dtype) for x in later],
        compiler_params=pltpu.CompilerParams(
            collective_id=1, has_side_effects=True, vmem_limit_bytes=VMEM_BYTES
        ),
        name="backward",
    )(dr2, resid_one, q, k, v, a, logs, wq, wo, wk, wv, dec, src, gain, vecs, summed, *later)


def finish_kernel(
    prefix_len, lanes, output_low, tokens_low, memory_low, adapter, self_pre, sums,
    output, tokens_grad, memory_grad, self_out, cross_out, gains, shifts, down, down_bias, up, up_bias,
):
    output[...] = output_low[...]
    tokens_grad[...] = tokens_low[...]
    memory_grad[...] = memory_low[...]
    up[...] = adapter[0].astype(f32)
    down[...] = adapter[1].astype(f32).T

    @pl.when(pl.program_id(0) == 0)
    def _():
        for o in range(2):
            rows = slice(o * PRE_PACK, o * PRE_PACK + prefix_len)
            self_out[:, o] = self_pre[rows]
            cross_out[:, o] = sums[rows]
        for i in range(gains.shape[1] // lanes):
            at = 2 * PRE_PACK + 8 * i
            cols = slice(i * lanes, (i + 1) * lanes)
            gains[:, cols] = sums[at : at + 3]
            shifts[:, cols] = sums[at + 3 : at + 6]
            up_bias[:, cols] = sums[at + 6 : at + 7]
            if (i + 1) * lanes <= down_bias.shape[1]:
                down_bias[:, cols] = sums[at + 7 : at + 8]


def finish(prefix_len, output_low, tokens_low, memory_low, adapter, self_pre, sums):
    steps = 4
    block, width = tokens_low.shape
    adapt = adapter.shape[1]
    lanes = sums.shape[1]
    out = jax.ShapeDtypeStruct
    outs = (
        out((block, width), bf16),
        out((block, width), bf16),
        out((block, width), bf16),
        out((prefix_len, 2, lanes), f32),
        out((prefix_len, 2, lanes), f32),
        out((3, width), f32),
        out((3, width), f32),
        out((width, adapt), f32),
        out((1, adapt), f32),
        out((adapt, width), f32),
        out((1, width), f32),
    )
    rows = pl.BlockSpec((block // steps, width), lambda i: (i, 0))
    specs = [whole_spec(o.shape) for o in outs]
    specs[0] = specs[1] = specs[2] = rows
    specs[7] = pl.BlockSpec((width, adapt // steps), lambda i: (0, i))
    specs[9] = pl.BlockSpec((adapt // steps, width), lambda i: (i, 0))
    return pl.pallas_call(
        functools.partial(finish_kernel, prefix_len, lanes),
        grid=(steps,),
        out_shape=outs,
        in_specs=[rows, rows, rows, pl.BlockSpec((2, adapt // steps, width), lambda i: (0, i, 0))]
        + [whole_spec(self_pre.shape), whole_spec(sums.shape)],
        out_specs=specs,
        compiler_params=pltpu.CompilerParams(vmem_limit_bytes=VMEM_BYTES),
        name="finish",
    )(output_low, tokens_low, memory_low, adapter, self_pre, sums)


def per_device(
    row_count,
    tokens, memory, out_grad, dec_segments, src_segments,
    self_query, self_key, self_value, self_out,
    cross_query, cross_key, cross_value, cross_out,
    ffn_in, ffn_out, adapt_down, adapt_down_bias, adapt_up, adapt_up_bias,
    self_prefix, cross_prefix, norm_gain, norm_shift,
):
    seq_local, _, width = tokens.shape
    prefix_len = self_prefix.shape[1]
    adapt = adapt_down.shape[1]
    x, mem, grad_in = (a.reshape(seq_local, width) for a in (tokens, memory, out_grad))
    self_weights = (self_query, self_key, self_value, self_out)

    (
        q1, k1, v1_heads, a1, logs1, resid_one, q2, k2, v2_heads, a2, logs2, resid_two, *gathered
    ) = forward(
        prefix_len, x, mem, [jnp.swapaxes(p, 0, 1) for p in (self_prefix, cross_prefix)], self_weights,
        (cross_query, cross_key, cross_value, cross_out), (ffn_in, ffn_out),
        dec_segments, src_segments, norm_gain, norm_shift,
    )
    cross_weights, (w_in, w_out) = gathered[:4], gathered[4:]
    output_low, dr2, summed, vecs = feed_forward(
        resid_two, grad_in, w_in, w_out,
        adapt_down, adapt_down_bias.reshape(1, adapt), adapt_up, adapt_up_bias.reshape(1, width),
        norm_gain, norm_shift,
    )
    tokens_low, memory_low, adapter, self_pre, sums = backward(
        prefix_len, row_count, dr2, resid_one, (q2, k2, v2_heads, a2, logs2), cross_weights,
        (q1, k1, v1_heads, a1, logs1), self_weights,
        dec_segments, src_segments, norm_gain, vecs, summed,
    )
    (
        output, tokens_grad, memory_grad, self_grad, cross_grad, gains, shifts,
        down, down_bias, up, up_bias,
    ) = finish(
        prefix_len, output_low, tokens_low, memory_low, adapter.reshape(2, adapt, width), self_pre, sums
    )
    local = tokens.shape
    return (
        output.reshape(local),
        tokens_grad.reshape(local),
        memory_grad.reshape(local),
        jnp.swapaxes(self_grad, 0, 1),
        jnp.swapaxes(cross_grad, 0, 1),
        gains,
        shifts,
        down,
        down_bias.reshape(adapt),
        up,
        up_bias.reshape(width),
    )


def solution(mesh):
    placed = (
        (P("tp", "rows", None),) * 3
        + (P("rows", None),) * 2
        + (P(None, "tp"),) * 3
        + (P("tp", None),)
        + (P(None, "tp"),) * 3
        + (P("tp", None),)
        + (P(None, "tp"), P("tp", None))
        + (P(),) * 4
        + (P(None, None, "tp"),) * 2
        + (P(),) * 2
    )
    return jax.shard_map(
        functools.partial(per_device, mesh.shape["rows"]),
        mesh=mesh,
        in_specs=placed,
        out_specs=(P("tp", "rows", None),) * 3 + (P(None, None, "tp"),) * 2 + (P(),) * 6,
        check_vma=False,
    )
```

```python
import functools

import jax
import jax.numpy as jnp
from jax import lax
from jax.experimental import pallas as pl
from jax.experimental.pallas import tpu as pltpu
from jax.sharding import PartitionSpec as P

HEAD = 64
PAIR = 2 * HEAD
PRE = 128
PRE_PACK = 32
GROUP = 8
LINE = 4
MASKED = -1000000000.0
EPSILON = 1e-05
VMEM_BYTES = 62 << 20
SCALE = HEAD**-0.5
f32 = jnp.float32
bf16 = jnp.bfloat16
MESH = pl.DeviceIdType.MESH
VMEM = pltpu.VMEM
ANY = pl.ANY


def nn(a, b):
    return lax.dot_general(a, b, (((1,), (0,)), ((), ())), preferred_element_type=f32)


def nt(a, b):
    return lax.dot_general(a, b, (((1,), (1,)), ((), ())), preferred_element_type=f32)


def tn(a, b):
    return lax.dot_general(a, b, (((0,), (0,)), ((), ())), preferred_element_type=f32)


def gelu_parts(v):
    phi = 0.5 + 0.5 * lax.erf(v * (0.5**0.5))
    slope = phi + v * (jnp.exp(-0.5 * v * v) * 0.3989422804014327)
    return v * phi, slope


def norm_parts(v):
    centered = v - jnp.mean(v, axis=-1, keepdims=True)
    spread = lax.rsqrt(jnp.mean(centered * centered, axis=-1, keepdims=True) + EPSILON)
    return centered * spread, spread


def norm_back(dy, gain, n, spread):
    dn = dy * gain
    dv = spread * (
        dn - jnp.mean(dn, axis=-1, keepdims=True) - n * jnp.mean(dn * n, axis=-1, keepdims=True)
    )
    return dv, jnp.sum(dy * n, axis=0, keepdims=True), jnp.sum(dy, axis=0, keepdims=True)


def lane_half(shape, h):
    return (lax.broadcasted_iota(jnp.int32, shape, 1) // HEAD) == h


def column(row):
    return jnp.broadcast_to(row, (8, row.shape[1])).T[:, 0:1]


def prefix_bias(shape, axis, prefix_len):
    return jnp.where(lax.broadcasted_iota(jnp.int32, shape, axis) < prefix_len, 0.0, MASKED)


def mask_bias(seg_q, seg_k, shape, key_axis, first_query):
    keep = seg_q == seg_k
    if first_query is not None:
        query = first_query + lax.broadcasted_iota(jnp.int32, shape, 1 - key_axis)
        keep = keep & (lax.broadcasted_iota(jnp.int32, shape, key_axis) <= query)
    return jnp.where(keep, 0.0, MASKED)


def pair_forward(q_pair, k_pair, v_pair, bias):
    outs, logs = [], []
    for h in range(2):
        half = lane_half(q_pair.shape, h)
        scores = nt(jnp.where(half, q_pair, jnp.zeros_like(q_pair)), k_pair) + bias
        top = jnp.max(scores, axis=1, keepdims=True)
        e = jnp.exp(scores - top)
        total = jnp.sum(e, axis=1, keepdims=True)
        outs.append(nn(e.astype(bf16), v_pair) * (1.0 / total))
        logs.append(top + jnp.log(total))
    return jnp.where(lane_half(outs[0].shape, 0), outs[0], outs[1]).astype(bf16), logs


def keep_logs(kept, logs, j):
    lane = lax.broadcasted_iota(jnp.int32, kept.shape, 1)
    for h in range(2):
        kept[...] = jnp.where(lane == 2 * j + h, logs[h], kept[...])


def pair_backward(q_pair, k_pair, v_pair, a_pair, da_pair, logs, bias_t):
    k_turned = k_pair.T
    prod = da_pair.astype(f32) * a_pair.astype(f32)
    prod_high = prod.astype(bf16)
    prod_low = (prod - prod_high.astype(f32)).astype(bf16)
    pick = (
        lax.broadcasted_iota(jnp.int32, (8, PAIR), 1) // HEAD
        == lax.broadcasted_iota(jnp.int32, (8, PAIR), 0)
    ).astype(bf16)
    delta = nt(pick, prod_high) + nt(pick, prod_low)
    dk = dv = None
    dq = []
    for h in range(2):
        half = lane_half(q_pair.shape, h)
        q = jnp.where(half, q_pair, jnp.zeros_like(q_pair))
        da = jnp.where(half, da_pair, jnp.zeros_like(da_pair))
        p = jnp.exp(nt(k_pair, q) + (bias_t - logs[h]))
        ds = (p * (nt(v_pair, da) - delta[h : h + 1])).astype(bf16)
        dv_h = nn(p.astype(bf16), da)
        dk_h = nn(ds, q)
        dk = dk_h if dk is None else dk + dk_h
        dv = dv_h if dv is None else dv + dv_h
        dq.append(nn(k_turned[h * HEAD : (h + 1) * HEAD], ds))
    return jnp.concatenate(dq, axis=0).T.astype(bf16), dk, dv


def whole_spec(shape):
    return pl.BlockSpec(shape, lambda i: (0,) * len(shape))


def shard_spec(shape, index=lambda i: i):
    return pl.BlockSpec((1,) + shape[1:], lambda i: (index(i), 0, 0))


def feed_forward_kernel(
    v2, out_grad, w_in, w_out, down, down_bias, up, up_bias, gain, shift,
    output, dr2, summed, rest, vecs,
    n2_low, n2_hat, total, e_low, slope, grad, g, s1, h, xb, send, recv,
):
    step = pl.program_id(0)
    half = pl.num_programs(0) // 2
    links = Links(send, recv)
    reduce = AdapterReduceFirst(links, g, s1, h, xb)

    @pl.when(step == 0)
    def _():
        greet([links.tp_peer(1), links.side_peer()])
        n, _ = norm_parts(v2[...])
        n2_hat[...] = n
        normed = n * gain[1:2] + shift[1:2]
        total[...] = normed
        n2_low[...] = normed.astype(bf16)

    @pl.when(step < half)
    def _():
        act, bend = gelu_parts(nn(n2_low[...], w_in[0]))
        slope[step] = bend
        total[...] += nn(act.astype(bf16), w_out[0])

    @pl.when(step == half - 1)
    def _():
        act, bend = gelu_parts(nn(n2_low[...], down[...]) + down_bias[...])
        act = act.astype(bf16)
        resid = total[...] + 4.0 * (nn(act, up[...]) + up_bias[...])
        n, spread = norm_parts(resid)
        output[...] = (n * gain[2:3] + shift[2:3]).astype(bf16)
        dz, gain_part, shift_part = norm_back(out_grad[...].astype(f32), gain[2:3], n, spread)
        e_low[...] = dz.astype(bf16)
        four = (4.0 * dz).astype(bf16)
        g[0] = tn(act, four).astype(bf16).reshape(g.shape[1:])
        da = (nt(four, up[...]) * bend).astype(bf16)
        g[1] = tn(da, n2_low[...]).astype(bf16).reshape(g.shape[1:])
        reduce.start_beside()
        grad[...] = dz + nt(da, down[...])
        vecs[...] = jnp.zeros_like(vecs)
        vecs[2:3] = gain_part
        vecs[5:6] = shift_part
        vecs[6:7] = jnp.sum(four.astype(f32), axis=0, keepdims=True)
        vecs[7:8, 0 : down.shape[1]] = jnp.sum(da.astype(f32), axis=0, keepdims=True)

    @pl.when(step >= half)
    def _():
        du = (nt(e_low[...], w_out[0]) * slope[2 * half - 1 - step]).astype(bf16)
        grad[...] += nt(du, w_in[0])

    @pl.when(step == half)
    def _():
        reduce.start_side()

    @pl.when(step == 2 * half - 1)
    def _():
        _, spread = norm_parts(v2[...])
        dv, gain_part, shift_part = norm_back(grad[...], gain[1:2], n2_hat[...], spread)
        dr2[...] = dv
        vecs[1:2] = gain_part
        vecs[4:5] = shift_part
        reduce.finish(summed, rest)


def feed_forward(v2, out_grad, w_in, w_out, down, down_bias, up, up_bias, gain, shift):
    n, width, inner = w_in.shape
    block = v2.shape[0]
    adapt = down.shape[1]
    out = jax.ShapeDtypeStruct
    outs = (
        out((block, width), bf16),
        out((block, width), f32),
        out((LINE, adapt // GROUP, width), bf16),
        out((LINE // 2, adapt // GROUP, width), bf16),
        out((8, width), f32),
    )
    parts = (2, LINE, adapt // GROUP, width)
    turn = lambda i: jnp.minimum(i, 2 * n - 1 - i)
    return pl.pallas_call(
        feed_forward_kernel,
        grid=(2 * n,),
        out_shape=outs,
        in_specs=[whole_spec(v2.shape), whole_spec(out_grad.shape)]
        + [shard_spec(w_in.shape, turn), shard_spec(w_out.shape, turn)]
        + [whole_spec(a.shape) for a in (down, down_bias, up, up_bias, gain, shift)],
        out_specs=[whole_spec(a.shape) for a in outs],
        scratch_shapes=[
            VMEM((block, width), bf16),
            VMEM((block, width), f32),
            VMEM((block, width), f32),
            VMEM((block, width), bf16),
            VMEM((n, block, inner), f32),
            VMEM((block, width), f32),
            VMEM((2,) + parts, bf16),
            VMEM(parts, bf16),
            VMEM(parts, bf16),
            VMEM((LINE // 2,) + parts[2:], bf16),
            pltpu.SemaphoreType.DMA((2,)),
            pltpu.SemaphoreType.DMA((2,)),
        ],
        compiler_params=pltpu.CompilerParams(
            collective_id=2, has_side_effects=True, vmem_limit_bytes=VMEM_BYTES
        ),
        name="feed_forward",
    )(v2, out_grad, w_in, w_out, down, down_bias, up, up_bias, gain, shift)


class Links:
    def __init__(self, send, recv):
        self.send, self.recv = send, recv
        self.row = lax.axis_index("rows")
        self.t = lax.axis_index("tp")
        self.flows = 0
        place = lax.rem(self.row, GROUP)
        self.base = self.row - place
        self.a = place // 2
        self.b = lax.rem(place, 2)
        self.place = place

    def flow(self):
        self.flows += 1
        return self.flows - 1

    def tp_peer(self, mask):
        return (self.row, self.t ^ mask)

    def line_peer(self, d):
        return (self.base + lax.rem(self.a + d, LINE) * 2 + self.b, self.t)

    def side_peer(self):
        return (self.base + self.a * 2 + (1 - self.b), self.t)

    def copy(self, src, dst, flow, peer):
        return pltpu.make_async_remote_copy(
            src_ref=src,
            dst_ref=dst,
            send_sem=self.send.at[flow],
            recv_sem=self.recv.at[flow],
            device_id=peer,
            device_id_type=MESH,
        )

    def start(self, src, dst, flow, peer):
        made = self.copy(src, dst, flow, peer)
        made.start()
        return made

    def arrived(self, dst, flow, peer):
        self.copy(dst, dst, flow, peer).wait_recv()


def greet(peers):
    barrier = pltpu.get_barrier_semaphore()
    for peer in peers:
        pl.semaphore_signal(barrier, inc=1, device_id=peer, device_id_type=MESH)
    pl.semaphore_wait(barrier, len(peers))


CHUNKS = 4


FLOWS = 14


class WeightGather:
    def __init__(self, links, base, across, own, full, stage, local):
        self.links, self.base, self.across = links, base, across
        self.own, self.full, self.stage, self.local = own, full, stage, local
        self.far, self.last = links.t ^ 2, links.t ^ 3
        a = links.a
        self.right = (links.base + jnp.minimum(a + 1, LINE - 1) * 2 + links.b, links.t)
        self.left = (links.base + jnp.maximum(a - 1, 0) * 2 + links.b, links.t)
        self.side = links.side_peer()
        self.sibling = links.tp_peer(1)
        self.over = links.tp_peer(2)

    def at(self, i, a, b):
        rows = self.own[i].shape[0] // GROUP
        return pl.ds(pl.multiple_of((a * 2 + b) * rows, rows), rows)

    def part(self, i, a, b):
        return self.full[i].at[self.far, self.at(i, a, b)]

    def flow(self, i, k):
        return self.base + i * FLOWS + k

    def over_copy(self, i, k):
        links = self.links
        b = links.b if k == 0 else 1 - links.b
        at = self.at(i, links.a, b)
        return links.copy(
            self.own[i].at[at], self.full[i].at[links.t, at], self.flow(i, k), self.over
        )

    def beside_copy(self, i):
        return self.links.copy(
            self.own[i], self.full[i].at[self.links.t], self.flow(i, 2), self.sibling
        )

    def pass_copy(self, i):
        whole = self.full[i].at[self.far]
        return self.links.copy(whole, whole, self.flow(i, 3), self.sibling)

    def moved(self, i, a, flow, peer):
        part = self.part(i, a, self.links.b)
        return self.links.copy(part, part, self.flow(i, flow), peer)

    def stage_in(self, i):
        stage = self.full[i].at[self.links.t] if self.stage is None else self.stage[i]
        return pltpu.make_async_copy(self.own[i], stage, self.local.at[2 * i])

    def stage_out(self, i):
        return pltpu.make_async_copy(
            self.stage[i], self.full[i].at[self.links.t], self.local.at[2 * i + 1]
        )

    def start_over(self, i, k):
        self.over_copy(i, k).start()

    def start_beside(self, i):
        self.beside_copy(i).start()
        self.stage_in(i).start()

    def own_ready(self, i):
        self.stage_in(i).wait()

    def beside_ready(self, i):
        self.links.arrived(self.full[i].at[self.links.t ^ 1], self.flow(i, 2), self.sibling)

    def far_ready(self, i):
        self.links.arrived(self.full[i].at[self.last], self.flow(i, 3), self.sibling)

    def keep_own(self, i):
        self.own_ready(i)
        self.stage_out(i).start()

    def came_over(self, i):
        mine = self.part(i, self.links.a, self.links.b)
        self.links.arrived(mine, self.flow(i, 0), self.over)
        self.spread(i)

    def spread(self, i):
        a = self.links.a

        @pl.when(a < LINE - 1)
        def _():
            self.moved(i, a, 4, self.right).start()

        @pl.when(a > 0)
        def _():
            self.moved(i, a, 7, self.left).start()

        if self.across[i] == 1:
            self.moved(i, a, 10, self.side).start()

    def along(self, i, k):
        links, a = self.links, self.links.a

        @pl.when(a - 1 - k >= 0)
        def _():
            links.arrived(self.part(i, a - 1 - k, links.b), self.flow(i, 4 + k), self.left)
            if k < LINE - 2:

                @pl.when(a < LINE - 1)
                def _():
                    self.moved(i, a - 1 - k, 5 + k, self.right).start()

            self.moved(i, a - 1 - k, 11 + k, self.side).start()

        @pl.when(a + 1 + k <= LINE - 1)
        def _():
            links.arrived(self.part(i, a + 1 + k, links.b), self.flow(i, 7 + k), self.right)
            if k < LINE - 2:

                @pl.when(a > 0)
                def _():
                    self.moved(i, a + 1 + k, 8 + k, self.left).start()

            self.moved(i, a + 1 + k, 13 - k, self.side).start()

    def side_part(self, i, k):
        links, a = self.links, self.links.a
        if k == 0:
            return self.part(i, a, 1 - links.b)
        piece = jnp.where(k <= a, a - k, a + LINE - k)
        return self.part(i, piece, 1 - links.b)

    def complete(self, i):
        links = self.links
        if self.across[i] == 2:
            links.arrived(self.side_part(i, 0), self.flow(i, 1), self.over)
        for k in range(self.across[i] - 1, LINE):
            links.arrived(self.side_part(i, k), self.flow(i, 10 + k), self.side)
        self.pass_copy(i).start()

    def finish(self, i):
        if self.stage is not None:
            self.beside_ready(i)
            self.far_ready(i)
            self.stage_out(i).wait()
        for k in range(self.across[i]):
            self.over_copy(i, k).wait_send()
        self.beside_copy(i).wait_send()
        self.spread_sent(i)

    def spread_sent(self, i):
        a = self.links.a
        self.pass_copy(i).wait_send()
        for k in range(LINE - 1):

            @pl.when((a < LINE - 1) & (a - k >= 0))
            def _():
                self.moved(i, a - k, 4 + k, self.right).wait_send()

            @pl.when((a > 0) & (a + k <= LINE - 1))
            def _():
                self.moved(i, a + k, 7 + k, self.left).wait_send()

        for k in range(self.across[i] - 1, LINE):
            piece = a if k == 0 else jnp.where(k <= a, a - k, a + LINE - k)
            self.moved(i, piece, 10 + k, self.side).wait_send()


class AdapterSpread(WeightGather):
    def __init__(self, links, base, full):
        super().__init__(links, base, [1], None, full, None, None)
        self.half = lax.rem(links.t, 2)

    def part(self, i, a, b):
        return self.full.at[self.half, b, a]

    def pass_copy(self, i):
        whole = self.full.at[self.half]
        return self.links.copy(whole, whole, self.flow(i, 3), self.sibling)

    def finish(self, i):
        self.links.arrived(self.full.at[1 - self.half], self.flow(i, 3), self.sibling)
        self.spread_sent(i)


class AdapterReduceFirst:
    def __init__(self, links, g, s1, h, xb):
        self.links, self.g, self.s1, self.h, self.xb = links, g, s1, h, xb
        self.half = lax.rem(links.t, 2)

    def beside(self):
        return self.links.copy(self.g.at[1 - self.half], self.s1, 0, self.links.tp_peer(1))

    def side(self):
        links = self.links
        return links.copy(
            self.h.at[1 - links.b, pl.ds(0, LINE // 2)], self.xb, 1, links.side_peer()
        )

    def start_beside(self):
        self.beside().start()

    def start_side(self):
        self.beside().wait()
        self.h[...] = (self.g[self.half].astype(f32) + self.s1[...].astype(f32)).astype(bf16)
        self.side().start()

    def finish(self, summed, rest):
        kept = LINE // 2
        mine = self.h[self.links.b]
        rest[...] = self.h[1 - self.links.b, kept:]
        summed[kept:] = mine[kept:]
        self.side().wait()
        summed[0:kept] = (mine[0:kept].astype(f32) + self.xb[...].astype(f32)).astype(bf16)


class AdapterReduce:
    def __init__(self, links, base, levels, summed, rest, xb, h2, zb, p3, yb, hb):
        self.links, self.base, self.levels = links, base, levels
        self.summed, self.rest, self.xb, self.h2 = summed, rest, xb, h2
        self.zb, self.p3, self.yb, self.hb = zb, p3, yb, hb
        self.half = lax.rem(links.t, 2)
        self.groups = [(links.row ^ (GROUP << level), links.t) for level in range(levels)]

    def side(self):
        return self.links.copy(self.rest, self.xb, self.base, self.links.side_peer())

    def piece(self, d):
        return lax.rem(self.links.a + d, LINE)

    def line(self, d):
        return self.links.copy(
            self.h2.at[self.piece(d)], self.zb.at[d - 1], self.base + d, self.links.line_peer(d)
        )

    def over(self):
        return self.links.copy(self.p3, self.yb, self.base + LINE, self.links.tp_peer(2))

    def group(self, level):
        return self.links.copy(
            self.hb.at[2 * level],
            self.hb.at[2 * level + 1],
            self.base + LINE + 1 + level,
            self.groups[level],
        )

    def start(self):
        kept = LINE // 2
        self.side().start()
        self.h2[0:kept] = self.summed[0:kept]
        for d in range(1, LINE):

            @pl.when(self.piece(d) < kept)
            def _():
                self.line(d).start()

    def start_line(self):
        kept = LINE // 2
        self.side().wait()
        self.h2[kept:] = (self.summed[kept:].astype(f32) + self.xb[...].astype(f32)).astype(bf16)
        for d in range(1, LINE):

            @pl.when(self.piece(d) >= kept)
            def _():
                self.line(d).start()

    def start_over(self):
        for d in range(1, LINE):
            self.line(d).wait()
        total = self.h2[self.links.a].astype(f32)
        for d in range(1, LINE):
            total = total + self.zb[d - 1].astype(f32)
        self.p3[...] = total.astype(bf16)
        self.over().start()

    def result(self):
        self.over().wait()
        value = self.p3[...].astype(f32) + self.yb[...].astype(f32)
        for level in range(self.levels):
            self.hb[2 * level] = value.astype(bf16)
            self.group(level).start()
            self.group(level).wait()
            value = self.hb[2 * level].astype(f32) + self.hb[2 * level + 1].astype(f32)
        return value.astype(bf16)


class RowGather:
    FLOWS = 1 + 2 * 4

    def __init__(self, links, base, own, full):
        self.links, self.base, self.own, self.full = links, base, own, full
        self.far, self.last = links.t ^ 2, links.t ^ 3
        self.sibling, self.over = links.tp_peer(1), links.tp_peer(2)

    def at(self, c):
        rows = self.own.shape[0] // CHUNKS
        return pl.ds(c * rows, rows)

    def beside_copy(self):
        return self.links.copy(self.own, self.full.at[self.links.t], self.base, self.sibling)

    def over_copy(self, c):
        at = self.at(c)
        return self.links.copy(
            self.own.at[at], self.full.at[self.links.t, at], self.base + 1 + c, self.over
        )

    def pass_copy(self, c):
        part = self.full.at[self.far, self.at(c)]
        return self.links.copy(part, part, self.base + 1 + CHUNKS + c, self.sibling)

    def start_beside(self):
        self.beside_copy().start()

    def start_over(self):
        for c in range(CHUNKS):
            self.over_copy(c).start()

    def came_beside(self):
        self.links.arrived(self.full.at[self.links.t ^ 1], self.base, self.sibling)

    def came_over_chunk(self, c):
        self.links.arrived(self.full.at[self.far, self.at(c)], self.base + 1 + c, self.over)
        self.pass_copy(c).start()

    def came_over(self):
        for c in range(CHUNKS):
            self.came_over_chunk(c)

    def came_last(self):
        for c in range(CHUNKS):
            self.links.arrived(
                self.full.at[self.last, self.at(c)], self.base + 1 + CHUNKS + c, self.sibling
            )

    def sent(self):
        self.beside_copy().wait_send()
        for c in range(CHUNKS):
            self.over_copy(c).wait_send()
            self.pass_copy(c).wait_send()


class RowScatter:
    FLOWS = 2 + 4

    def __init__(self, links, base, part, near, near_far, mid, far):
        self.links, self.base, self.part = links, base, part
        self.near, self.near_far, self.mid, self.far = near, near_far, mid, far
        self.sibling, self.over = links.tp_peer(1), links.tp_peer(2)

    def at(self, c):
        rows = self.near.shape[0] // CHUNKS
        return pl.ds(c * rows, rows)

    def first_copy(self):
        return self.links.copy(
            self.part.at[self.links.t ^ 3], self.near_far, self.base, self.sibling
        )

    def second_copy(self):
        return self.links.copy(
            self.part.at[self.links.t ^ 1], self.near, self.base + 1, self.sibling
        )

    def over_copy(self, c):
        at = self.at(c)
        return self.links.copy(
            self.mid.at[at], self.far.at[at], self.base + 2 + c, self.over
        )

    def send_over(self):
        self.links.arrived(self.near_far, self.base, self.sibling)
        for c in range(CHUNKS):
            at = self.at(c)
            self.mid[at] = (
                self.part[self.links.t ^ 2, at].astype(f32) + self.near_far[at].astype(f32)
            ).astype(bf16)
            self.over_copy(c).start()

    def came_beside(self):
        self.links.arrived(self.near, self.base + 1, self.sibling)

    def came_over(self, c):
        at = self.at(c)
        self.links.arrived(self.far.at[at], self.base + 2 + c, self.over)
        return (
            self.part[self.links.t, at].astype(f32)
            + self.near[at].astype(f32)
            + self.far[at].astype(f32)
        )

    def sent(self):
        self.first_copy().wait_send()
        self.second_copy().wait_send()
        for c in range(CHUNKS):
            self.over_copy(c).wait_send()


def halves(own, full, stage):
    outs = ([], [], [])
    for one, whole, held in zip(own, full, stage):
        rows = one.shape[0] // 2
        for o in range(2):
            at = pl.ds(o * rows, rows)
            for out, view in zip(outs, (one.at[at], whole.at[:, at], held.at[at])):
                out.append(view)
    return outs


def cut(refs, *counts):
    out, at = [], 0
    for count in counts:
        out.append(refs[at : at + count])
        at += count
    return out


def forward_kernel(prefix_len, *refs):
    ins, self_outs, cross_outs, kept_outs, scratch = cut(refs, 18, 6, 6, 6, 26)
    x, pre_cross, wq, wk, wv, wo, pre, dec, src, gain, shift = ins[:11]
    memory, own_cross, own_ffn = ins[11], list(ins[12:16]), list(ins[16:18])
    q_out, k_out, v_out, a_out, l_out, resid = self_outs
    q2_out, k2_out, v2_out, a2_out, l2_out, resid2 = cross_outs
    cross_kept, ffn_full = list(kept_outs[:4]), list(kept_outs[4:])
    cross_full, held = list(scratch[:4]), list(scratch[4:6])
    (
        m_full, pre_full, x_full, part, kept, bias, near, near_far, mid, far, pre_stage, n1_low,
        send, recv, cross_local, ffn_local, m_local, keep_local, pre_local, spare,
    ) = scratch[6:]
    del spare
    block, lanes = x.shape[0], q_out.shape[1]
    links = Links(send, recv)
    t = links.t
    early = range(4)
    late = range(4)
    cross = WeightGather(links, 0, [1] * 4, own_cross, cross_full, None, cross_local)
    ffn = WeightGather(links, 4 * FLOWS, [2] * 4, *halves(own_ffn, ffn_full, held), ffn_local)
    at = 8 * FLOWS
    x_rows = RowGather(links, at, x, x_full)
    at += RowGather.FLOWS
    m_rows = RowGather(links, at, memory, m_full)
    at += RowGather.FLOWS
    sums = RowScatter(links, at, part, near, near_far, mid, far)
    at += RowScatter.FLOWS
    m_keep = pltpu.make_async_copy(memory, m_full.at[t], m_local.at[0])
    pre_keep = pltpu.make_async_copy(pre_stage, pre_full.at[t], pre_local.at[0])
    pre_sends = [
        links.copy(pre_stage, pre_full.at[t], at + m - 1, links.tp_peer(m)) for m in (1, 2, 3)
    ]
    cross_keeps = [
        pltpu.make_async_copy(cross_full[i], cross_kept[i], keep_local.at[i]) for i in range(4)
    ]

    greet(
        [links.tp_peer(m) for m in (1, 2, 3)]
        + [links.line_peer(d) for d in range(1, LINE)]
        + [links.side_peer()]
    )
    x_rows.start_over()
    x_rows.start_beside()
    kept[...] = jnp.zeros_like(kept)
    pre_stage[...] = jnp.zeros_like(pre_stage)
    for o in range(2):
        pre_stage[o * PRE_PACK : o * PRE_PACK + prefix_len] = pre_cross[:, o]
    pre_keep.start()
    for one in pre_sends:
        one.start()
    m_keep.start()

    for target, o in ((k_out, 0), (v_out, 1)):
        target[0:PRE] = jnp.zeros((PRE, lanes), bf16)
        target[0:prefix_len] = pre[:, o]

    def project(rows, index):
        at = pl.multiple_of(index * block, block)
        q_out[pl.ds(at, block)] = (SCALE * nn(rows, wq[...])).astype(bf16)
        k_out[pl.ds(PRE + at, block)] = nn(rows, wk[...]).astype(bf16)
        v_out[pl.ds(PRE + at, block)] = nn(rows, wv[...]).astype(bf16)

    project(x[...], t)
    x_rows.came_beside()
    project(x_full[t ^ 1], t ^ 1)
    for c in range(CHUNKS):
        x_rows.came_over_chunk(c)
        if c == 3:
            for i in early:
                cross.start_over(i, 0)
    project(x_full[t ^ 2], t ^ 2)
    x_rows.came_last()
    for i in early:
        cross.start_beside(i)
    m_rows.start_beside()
    project(x_full[t ^ 3], t ^ 3)

    @pl.loop(0, 4)
    def _(order):
        here = t ^ (3 - order)
        for i in range(4):
            keys = PRE + (i + 1) * block

            @pl.when(here == i)
            def _():
                bias[:, 0:PRE] = prefix_bias((block, PRE), 1, prefix_len)
                bias[:, PRE:keys] = mask_bias(
                    column(dec[:, i * block : (i + 1) * block]),
                    dec[:, 0 : keys - PRE],
                    (block, keys - PRE),
                    1,
                    i * block,
                )

                @pl.loop(0, lanes // PAIR)
                def _(j):
                    cols = pl.ds(pl.multiple_of(j * PAIR, PAIR), PAIR)
                    mixture, logs = pair_forward(
                        q_out[i * block : (i + 1) * block, cols],
                        k_out[0:keys, cols],
                        v_out[0:keys, cols],
                        bias[:, 0:keys],
                    )
                    a_out[i, :, cols] = mixture
                    keep_logs(kept, logs, j)

        l_out[here] = kept[...].T[0:8]
        part[here] = nn(a_out[here], wo[...]).astype(bf16)

        @pl.when(order == 0)
        def _():
            sums.first_copy().start()
            for i in early:
                cross.came_over(i)
            for i in range(2):
                ffn.start_over(i, 0)

        @pl.when(order == 1)
        def _():
            sums.send_over()

        @pl.when(order == 2)
        def _():
            sums.second_copy().start()
            for i in early:
                cross.along(i, 0)

    for i in range(2):
        ffn.came_over(i)
    for i in late:
        ffn.start_beside(i)
    for i in early:
        cross.along(i, 1)
    for i in range(2):
        ffn.along(i, 0)
    sums.came_beside()
    for c in range(CHUNKS):
        rows = sums.at(c)
        resid[rows] = x[rows].astype(f32) + sums.came_over(c)
    m_rows.start_over()

    n, _ = norm_parts(resid[...])
    normed = n * gain[0:1] + shift[0:1]
    resid2[...] = normed
    n1_low[...] = normed.astype(bf16)
    kept[...] = jnp.zeros_like(kept)
    own_queries = dec[:, pl.ds(pl.multiple_of(t * block, block), block)]
    keys = k2_out.shape[1]
    bias[:, 0:PRE] = prefix_bias((block, PRE), 1, prefix_len)
    bias[:, PRE:] = mask_bias(column(own_queries), src[...], (block, keys - PRE), 1, None)
    for i in early:
        cross.along(i, 2)
    for i in range(2):
        ffn.along(i, 1)
    m_rows.came_over()
    for i in (2, 3):
        ffn.start_over(i, 0)
    m_rows.came_beside()
    m_rows.came_last()
    for m in (1, 2, 3):
        links.arrived(pre_full.at[t ^ m], at + m - 1, links.tp_peer(m))
    m_keep.wait()
    pre_keep.wait()
    for i in early:
        cross.own_ready(i)

    def each(method, indices, *more):
        def run():
            for i in indices:
                method(i, *more)

        return run

    events = {
        0: [each(ffn.keep_own, late), each(ffn.along, (0, 1), 2)],
        1: [each(ffn.came_over, (2,)), each(cross.complete, early)],
        2: [each(ffn.came_over, (3,)), each(ffn.start_over, late, 1)],
        3: [each(ffn.along, (2,), 0), each(cross.far_ready, early)],
        4: [each(ffn.along, (3,), 0), each(ffn.along, (2,), 1)],
        5: [each(ffn.along, (3,), 1)],
        6: [each(ffn.along, (2,), 2), each(ffn.complete, (0, 1))],
        7: [each(ffn.along, (3,), 2)],
    }

    @pl.loop(0, 4)
    def _(order):
        s = t ^ order

        @pl.when(order == 1)
        def _():
            for i in early:
                cross.beside_ready(i)

        q2_out[s] = (SCALE * nn(n1_low[...], cross_full[0][s])).astype(bf16)
        for target, o in ((k2_out, 0), (v2_out, PRE_PACK)):
            target[s, 0:PRE_PACK] = pre_full[s, o : o + PRE_PACK]
            target[s, PRE_PACK:PRE] = jnp.zeros((PRE - PRE_PACK, lanes), bf16)

        @pl.loop(0, 4)
        def _(i):
            rows = m_full[i]
            to = pl.ds(pl.multiple_of(PRE + i * block, PRE), block)
            k2_out[s, to] = nn(rows, cross_full[1][s]).astype(bf16)
            v2_out[s, to] = nn(rows, cross_full[2][s]).astype(bf16)

        for j in range(lanes // PAIR):
            cols = slice(j * PAIR, (j + 1) * PAIR)
            mixture, logs = pair_forward(
                q2_out[s, :, cols], k2_out[s, :, cols], v2_out[s, :, cols], bias[...]
            )
            a2_out[s, :, cols] = mixture
            keep_logs(kept, logs, j)
            for step in range(4):

                @pl.when(order == step)
                def _():
                    for event in events.get(2 * step + j, []):
                        event()

        l2_out[s] = kept[...].T[0:8]
        resid2[...] += nn(a2_out[s], cross_full[3][s])

    for one in cross_keeps:
        one.start()
    for i in (2, 3):
        ffn.complete(i)
    for i in early:
        cross.finish(i)
    for i in late:
        ffn.finish(i)
    x_rows.sent()
    m_rows.sent()
    sums.sent()
    for one in pre_sends:
        one.wait_send()
    for one in cross_keeps:
        one.wait()


def forward(
    prefix_len, x, memory, prefixes, self_weights, cross_weights, ffn_weights, dec, src, gain, shift
):
    n = 4
    block, width = x.shape
    lanes = self_weights[0].shape[1]
    seq = n * block
    out = jax.ShapeDtypeStruct
    flows = 8 * FLOWS + 2 * RowGather.FLOWS + RowScatter.FLOWS + 3
    self_outs = (
        out((seq, lanes), bf16),
        out((PRE + seq, lanes), bf16),
        out((PRE + seq, lanes), bf16),
        out((n, block, lanes), bf16),
        out((n, 8, block), f32),
        out((block, width), f32),
    )
    cross_outs = (
        out((n, block, lanes), bf16),
        out((n, PRE + seq, lanes), bf16),
        out((n, PRE + seq, lanes), bf16),
        out((n, block, lanes), bf16),
        out((n, 8, block), f32),
        out((block, width), f32),
    )
    full = tuple(out((n,) + w.shape, w.dtype) for w in (*cross_weights, *ffn_weights))
    given = (x, prefixes[1], *self_weights, prefixes[0], dec, src, gain, shift)
    anywhere = pl.BlockSpec(memory_space=pltpu.HBM)
    rows = VMEM((block, width), bf16)
    all_rows = VMEM((n, block, width), bf16)
    dma = pltpu.SemaphoreType.DMA
    return pl.pallas_call(
        functools.partial(forward_kernel, prefix_len),
        grid=(1,),
        out_shape=self_outs + cross_outs + full,
        in_specs=[whole_spec(g.shape) for g in given] + [anywhere] * 7,
        out_specs=[whole_spec(o.shape) for o in self_outs + cross_outs] + [anywhere] * 6,
        scratch_shapes=[VMEM((n,) + w.shape, w.dtype) for w in cross_weights]
        + [VMEM(w.shape, w.dtype) for w in ffn_weights]
        + [
            all_rows,
            VMEM((n, 2 * PRE_PACK, lanes), bf16),
            all_rows,
            all_rows,
            VMEM((block, 128), f32),
            VMEM((block, PRE + seq), f32),
            rows,
            rows,
            rows,
            rows,
            VMEM((2 * PRE_PACK, lanes), bf16),
            rows,
            dma((flows,)),
            dma((flows,)),
            dma((8,)),
            dma((8,)),
            dma((1,)),
            dma((4,)),
            dma((1,)),
            dma((1,)),
        ],
        compiler_params=pltpu.CompilerParams(
            collective_id=0, has_side_effects=True, vmem_limit_bytes=VMEM_BYTES
        ),
        name="forward",
    )(*given, memory, *cross_weights, *ffn_weights)


def doublings(count):
    levels = 0
    while (1 << levels) < count:
        levels += 1
    return levels


class Doubling:
    def __init__(self, links, base, levels, outgo, income):
        self.links, self.base, self.levels = links, base, levels
        self.outgo, self.income = outgo, income

    def move(self, level):
        return self.links.copy(
            self.outgo.at[level],
            self.income.at[level],
            self.base + level,
            (self.links.row ^ (1 << level), self.links.t),
        )

    def begin(self, value):
        self.outgo[0] = value
        self.move(0).start()

    def value(self, level):
        self.move(level).wait()
        return self.outgo[level] + self.income[level]

    def step(self, level):
        value = self.value(level)
        self.outgo[level + 1] = value
        self.move(level + 1).start()


def backward_kernel(prefix_len, reduce_levels, levels, *refs):
    ins, later, outs, scratch = cut(refs, 17, 9, 5, 54)
    dr2, v1, q, k, v, a, logs, wq, wo, wk, wv, dec, src, gain, vecs_in, summed, rest = ins
    tokens_grad, memory_grad, adapter, self_pre, sums = outs
    (
        dr1, dr1_low, dr2_low, bias, da, dq, dk, dv, total, xb, h2, zb, p3, yb, hb,
        cross, vecs, dm, dr1_full, part, dq1, dk1, dv1,
        near, near_far, mid, far, m_near, m_near_far, m_mid, m_far,
        cross_beside, cross_mid, cross_over, vecs_beside, vecs_mid, vecs_over,
        outgo, income, pre_outgo, pre_income, send, recv, keep_sem, load_sem,
    ) = scratch[:-9]
    loaded = scratch[-9:]
    q1, k1, v1_heads, a1, logs1, wq1, wk1, wv1, wo1 = loaded
    step = pl.program_id(0)
    steps = pl.num_programs(0) - 1
    block, lanes = q.shape[1:]
    keys = k.shape[1]
    links = Links(send, recv)
    t = links.t
    at = 0
    rows = RowGather(links, at, dr1_low, dr1_full)
    at += RowGather.FLOWS
    reduce = AdapterReduce(links, at, reduce_levels, summed, rest, xb, h2, zb, p3, yb, hb)
    at += 1 + LINE + reduce_levels
    spread = AdapterSpread(links, at, adapter)
    at += FLOWS
    m_sums = RowScatter(links, at, dm, m_near, m_near_far, m_mid, m_far)
    at += RowScatter.FLOWS
    x_sums = RowScatter(links, at, part, near, near_far, mid, far)
    at += RowScatter.FLOWS
    totals = Doubling(links, at, levels, outgo, income)
    at += levels
    pre_totals = Doubling(links, at, levels, pre_outgo, pre_income)
    at += levels
    keep = pltpu.make_async_copy(dr1_low, dr1_full.at[t], keep_sem.at[0])
    loads = [
        pltpu.make_async_copy(src_ref, dst_ref, load_sem.at[i])
        for i, (src_ref, dst_ref) in enumerate(zip(later, loaded))
    ]

    beside, over = links.tp_peer(1), links.tp_peer(2)
    to_beside = (
        links.copy(cross.at[t ^ 1], cross_beside.at[0], at, beside),
        links.copy(cross.at[t ^ 3], cross_beside.at[1], at + 1, beside),
        links.copy(vecs, vecs_beside, at + 2, beside),
    )
    to_over = (
        links.copy(cross_mid, cross_over, at + 3, over),
        links.copy(vecs_mid, vecs_over, at + 4, over),
    )

    @pl.when(step == 0)
    def _():
        greet(
            [links.tp_peer(m) for m in (1, 2, 3)]
            + [links.line_peer(d) for d in range(1, LINE)]
            + [links.side_peer()]
            + [(links.row ^ (1 << level), t) for level in range(doublings(GROUP), levels)]
        )
        reduce.start()
        dr2_low[...] = dr2[...].astype(bf16)
        total[...] = jnp.zeros_like(total)
        own_queries = dec[:, pl.ds(pl.multiple_of(t * block, block), block)]
        bias[0:PRE] = prefix_bias((PRE, block), 0, prefix_len)
        bias[PRE:] = mask_bias(own_queries, column(src[...]), (keys - PRE, block), 0, None)

    @pl.when(step < steps)
    def _():
        da[...] = nt(dr2_low[...], wo[0]).astype(bf16)

        @pl.when(step == 0)
        def _():
            for one in loads:
                one.start()

        @pl.loop(0, lanes // PAIR)
        def _(j):
            cols = pl.ds(pl.multiple_of(j * PAIR, PAIR), PAIR)
            dq_pair, dk_pair, dv_pair = pair_backward(
                q[0, :, cols],
                k[0, :, cols],
                v[0, :, cols],
                a[0, :, cols],
                da[:, cols],
                [logs[0, pl.ds(2 * j + i, 1)] for i in range(2)],
                bias[...],
            )
            dq[:, cols] = dq_pair
            cross[step, 0:PRE_PACK, cols] = dk_pair[0:PRE_PACK]
            cross[step, PRE_PACK : 2 * PRE_PACK, cols] = dv_pair[0:PRE_PACK]
            dk[step, :, cols] = dk_pair[PRE:].astype(bf16)
            dv[step, :, cols] = dv_pair[PRE:].astype(bf16)

            @pl.when((step == 1) & (j == 1))
            def _():
                reduce.start_line()

            @pl.when((step == 3) & (j == 1))
            def _():
                reduce.start_over()


        total[...] += nt(dq[...], wq[0])

    @pl.when(step == steps)
    def _():
        n, spread_one = norm_parts(v1[...])
        grad, gain_part, shift_part = norm_back(
            dr2[...] + SCALE * total[...], gain[0:1], n, spread_one
        )
        dr1_low[...] = grad.astype(bf16)
        rows.start_over()
        rows.start_beside()
        keep.start()
        dr1[...] = grad
        vecs[...] = vecs_in[...]
        vecs[0:1] = gain_part
        vecs[3:4] = shift_part
        for one in to_beside:
            one.start()
        dk1[...] = jnp.zeros_like(dk1)
        dv1[...] = jnp.zeros_like(dv1)

        @pl.loop(0, 4)
        def _(order):
            here = t ^ (3 - order)
            to = pl.ds(pl.multiple_of(here * block, block), block)
            value = None
            for shard in range(dk.shape[0]):
                term = nt(dk[shard, to], wk[shard]) + nt(dv[shard, to], wv[shard])
                value = term if value is None else value + term
            dm[here] = value.astype(bf16)

        m_sums.first_copy().start()
        m_sums.second_copy().start()
        for one in loads:
            one.wait()
        keep.wait()
        rows.came_beside()
        for one in to_beside:
            one.wait()
        cross_mid[...] = cross[t ^ 2] + cross_beside[1]
        vecs_mid[...] = vecs[...] + vecs_beside[...]
        for one in to_over:
            one.start()
        p3[...] = reduce.result()
        settle = pltpu.make_async_copy(
            p3, adapter.at[spread.half, links.b, links.a], keep_sem.at[1]
        )
        settle.start()
        settle.wait()
        spread.spread(0)

        @pl.loop(0, 4)
        def _(order):
            here = t ^ order

            @pl.when(order == 2)
            def _():
                rows.came_over()
                m_sums.send_over()
                rows.came_last()

            da[...] = nt(dr1_full[here], wo1[...]).astype(bf16)
            for i in range(4):
                own = slice(i * block, (i + 1) * block)
                size = PRE + (i + 1) * block

                @pl.when(here == i)
                def _():
                    bias[0:PRE] = prefix_bias((PRE, block), 0, prefix_len)
                    bias[PRE:size] = mask_bias(
                        dec[:, own],
                        column(dec[:, 0 : size - PRE]),
                        (size - PRE, block),
                        0,
                        i * block,
                    )

                    @pl.loop(0, lanes // PAIR)
                    def _(j):
                        cols = pl.ds(pl.multiple_of(j * PAIR, PAIR), PAIR)
                        dq_pair, dk_pair, dv_pair = pair_backward(
                            q1[own, cols],
                            k1[0:size, cols],
                            v1_heads[0:size, cols],
                            a1[i, :, cols],
                            da[:, cols],
                            [logs1[i, pl.ds(2 * j + o, 1)] for o in range(2)],
                            bias[0:size],
                        )
                        dq1[i, :, cols] = dq_pair
                        dk1[0:size, cols] += dk_pair
                        dv1[0:size, cols] += dv_pair

            for k in range(3):

                @pl.when(order == k)
                def _():
                    spread.along(0, k)

            @pl.when(order == 2)
            def _():
                for one in to_over:
                    one.wait()
                value = vecs_mid[...] + vecs_over[...]
                pieces = [cross[t] + cross_beside[0] + cross_over[...]] + [
                    value[:, o * lanes : (o + 1) * lanes] for o in range(vecs.shape[1] // lanes)
                ]
                totals.begin(jnp.concatenate(pieces, axis=0))

        pre_totals.begin(jnp.concatenate([dk1[0:PRE_PACK], dv1[0:PRE_PACK]], axis=0))
        for order in range(4):
            here = t ^ (3 - order)
            done = pl.ds(pl.multiple_of(PRE + here * block, PRE), block)
            part[here] = (
                SCALE * nt(dq1[here], wq1[...])
                + nt(dk1[done].astype(bf16), wk1[...])
                + nt(dv1[done].astype(bf16), wv1[...])
            ).astype(bf16)
            if order == 0:
                x_sums.first_copy().start()
                totals.step(0)
            if order == 1:
                x_sums.send_over()
                pre_totals.step(0)
            if order == 2:
                x_sums.second_copy().start()

        for level in range(1, levels - 1):
            totals.step(level)
            pre_totals.step(level)
        spread.complete(0)
        m_sums.came_beside()
        for c in range(CHUNKS):
            memory_grad[m_sums.at(c)] = m_sums.came_over(c).astype(bf16)
        sums[...] = totals.value(levels - 1)
        self_pre[...] = pre_totals.value(levels - 1)
        x_sums.came_beside()
        for c in range(CHUNKS):
            here = x_sums.at(c)
            tokens_grad[here] = (dr1[here] + x_sums.came_over(c)).astype(bf16)
        spread.finish(0)
        rows.sent()
        m_sums.sent()
        x_sums.sent()


def backward(
    prefix_len, row_count, dr2, resid_one, cross_saved, cross_weights, self_saved, self_weights,
    dec, src, gain, vecs, summed, rest,
):
    q, k, v, a, logs = cross_saved
    wq, wk, wv, wo = cross_weights
    n, block, lanes = q.shape
    keys = k.shape[1]
    width = dr2.shape[1]
    reduce_levels = doublings(row_count // GROUP)
    levels = doublings(row_count)
    piece = summed.shape[1]
    half = (2, LINE, piece, width)
    packed = 2 * PRE_PACK
    height = packed + vecs.shape[0] * width // lanes
    out = jax.ShapeDtypeStruct
    outs = (
        out((block, width), bf16),
        out((block, width), bf16),
        out((2,) + half, bf16),
        out((packed, lanes), f32),
        out((height, lanes), f32),
    )
    flows = (
        RowGather.FLOWS + 1 + LINE + reduce_levels + FLOWS + 2 * RowScatter.FLOWS + 2 * levels + 5
    )
    later = (*self_saved, *self_weights)
    low, wide = VMEM((block, width), bf16), VMEM((block, width), f32)
    dma = pltpu.SemaphoreType.DMA
    bounded = lambda i: jnp.minimum(i, n - 1)

    def once(x):
        return pl.BlockSpec(x.shape, lambda i: (0,) * len(x.shape), pipeline_mode=pl.Buffered(1))

    return pl.pallas_call(
        functools.partial(backward_kernel, prefix_len, reduce_levels, levels),
        grid=(n + 1,),
        out_shape=outs,
        in_specs=[once(dr2), once(resid_one)]
        + [shard_spec(x.shape, bounded) for x in (q, k, v, a, logs, wq, wo)]
        + [once(x) for x in (wk, wv, dec, src, gain, vecs, summed, rest)]
        + [pl.BlockSpec(memory_space=pltpu.HBM)] * len(later),
        out_specs=[whole_spec(o.shape) for o in outs[:2]]
        + [pl.BlockSpec(memory_space=pltpu.HBM)]
        + [whole_spec(o.shape) for o in outs[3:]],
        scratch_shapes=[
            wide,
            low,
            low,
            VMEM((keys, block), f32),
            VMEM((block, lanes), bf16),
            VMEM((block, lanes), bf16),
            VMEM((n, keys - PRE, lanes), bf16),
            VMEM((n, keys - PRE, lanes), bf16),
            wide,
            VMEM((LINE // 2, piece, width), bf16),
            VMEM((LINE, piece, width), bf16),
            VMEM((LINE - 1, piece, width), bf16),
            VMEM((piece, width), bf16),
            VMEM((piece, width), bf16),
            VMEM((max(1, 2 * reduce_levels), piece, width), bf16),
            VMEM((n, packed, lanes), f32),
            VMEM(vecs.shape, f32),
            VMEM((n, block, width), bf16),
            VMEM((n, block, width), bf16),
            VMEM((n, block, width), bf16),
            VMEM((n, block, lanes), bf16),
            VMEM((keys, lanes), f32),
            VMEM((keys, lanes), f32),
        ]
        + [low] * 8
        + [
            VMEM((2, packed, lanes), f32),
            VMEM((packed, lanes), f32),
            VMEM((packed, lanes), f32),
            VMEM(vecs.shape, f32),
            VMEM(vecs.shape, f32),
            VMEM(vecs.shape, f32),
            VMEM((levels, height, lanes), f32),
            VMEM((levels, height, lanes), f32),
            VMEM((levels, packed, lanes), f32),
            VMEM((levels, packed, lanes), f32),
            dma((flows,)),
            dma((flows,)),
            dma((2,)),
            dma((len(later),)),
        ]
        + [VMEM(x.shape, x.dtype) for x in later],
        compiler_params=pltpu.CompilerParams(
            collective_id=1, has_side_effects=True, vmem_limit_bytes=VMEM_BYTES
        ),
        name="backward",
    )(dr2, resid_one, q, k, v, a, logs, wq, wo, wk, wv, dec, src, gain, vecs, summed, rest, *later)


def finish_kernel(
    prefix_len, lanes, output_low, tokens_low, memory_low, up_low, down_low, self_pre, sums,
    output, tokens_grad, memory_grad, self_out, cross_out, gains, shifts, down, down_bias, up, up_bias,
):
    output[...] = output_low[...]
    tokens_grad[...] = tokens_low[...]
    memory_grad[...] = memory_low[...]
    up[...] = up_low[0].astype(f32)
    rows = down.shape[0]
    at = pl.multiple_of(pl.program_id(0) * rows, rows)
    down[...] = down_low[0, :, pl.ds(at, rows)].astype(f32).T

    @pl.when(pl.program_id(0) == 0)
    def _():
        for o in range(2):
            rows = slice(o * PRE_PACK, o * PRE_PACK + prefix_len)
            self_out[:, o] = self_pre[rows]
            cross_out[:, o] = sums[rows]
        for i in range(gains.shape[1] // lanes):
            at = 2 * PRE_PACK + 8 * i
            cols = slice(i * lanes, (i + 1) * lanes)
            gains[:, cols] = sums[at : at + 3]
            shifts[:, cols] = sums[at + 3 : at + 6]
            up_bias[:, cols] = sums[at + 6 : at + 7]
            if (i + 1) * lanes <= down_bias.shape[1]:
                down_bias[:, cols] = sums[at + 7 : at + 8]


def finish(prefix_len, output_low, tokens_low, memory_low, adapter, self_pre, sums):
    steps = 4
    block, width = tokens_low.shape
    adapt = adapter.shape[1]
    lanes = sums.shape[1]
    out = jax.ShapeDtypeStruct
    outs = (
        out((block, width), bf16),
        out((block, width), bf16),
        out((block, width), bf16),
        out((prefix_len, 2, lanes), f32),
        out((prefix_len, 2, lanes), f32),
        out((3, width), f32),
        out((3, width), f32),
        out((width, adapt), f32),
        out((1, adapt), f32),
        out((adapt, width), f32),
        out((1, width), f32),
    )
    rows = pl.BlockSpec((block // steps, width), lambda i: (i, 0))
    specs = [whole_spec(o.shape) for o in outs]
    specs[0] = specs[1] = specs[2] = rows
    specs[7] = pl.BlockSpec((width // steps, adapt), lambda i: (i, 0))
    specs[9] = pl.BlockSpec((adapt // steps, width), lambda i: (i, 0))
    return pl.pallas_call(
        functools.partial(finish_kernel, prefix_len, lanes),
        grid=(steps,),
        out_shape=outs,
        in_specs=[rows, rows, rows]
        + [pl.BlockSpec((1, adapt // steps, width), lambda i: (0, i, 0))]
        + [pl.BlockSpec((1, adapt, width), lambda i: (1, 0, 0))]
        + [whole_spec(self_pre.shape), whole_spec(sums.shape)],
        out_specs=specs,
        compiler_params=pltpu.CompilerParams(vmem_limit_bytes=VMEM_BYTES),
        name="finish",
    )(output_low, tokens_low, memory_low, adapter, adapter, self_pre, sums)


def per_device(
    row_count,
    tokens, memory, out_grad, dec_segments, src_segments,
    self_query, self_key, self_value, self_out,
    cross_query, cross_key, cross_value, cross_out,
    ffn_in, ffn_out, adapt_down, adapt_down_bias, adapt_up, adapt_up_bias,
    self_prefix, cross_prefix, norm_gain, norm_shift,
):
    seq_local, _, width = tokens.shape
    prefix_len = self_prefix.shape[1]
    adapt = adapt_down.shape[1]
    x, mem, grad_in = (a.reshape(seq_local, width) for a in (tokens, memory, out_grad))
    self_weights = (self_query, self_key, self_value, self_out)

    (
        q1, k1, v1_heads, a1, logs1, resid_one, q2, k2, v2_heads, a2, logs2, resid_two, *gathered
    ) = forward(
        prefix_len, x, mem, [jnp.swapaxes(p, 0, 1) for p in (self_prefix, cross_prefix)], self_weights,
        (cross_query, cross_key, cross_value, cross_out), (ffn_in, ffn_out),
        dec_segments, src_segments, norm_gain, norm_shift,
    )
    cross_weights, (w_in, w_out) = gathered[:4], gathered[4:]
    output_low, dr2, summed, rest, vecs = feed_forward(
        resid_two, grad_in, w_in, w_out,
        adapt_down, adapt_down_bias.reshape(1, adapt), adapt_up, adapt_up_bias.reshape(1, width),
        norm_gain, norm_shift,
    )
    tokens_low, memory_low, adapter, self_pre, sums = backward(
        prefix_len, row_count, dr2, resid_one, (q2, k2, v2_heads, a2, logs2), cross_weights,
        (q1, k1, v1_heads, a1, logs1), self_weights,
        dec_segments, src_segments, norm_gain, vecs, summed, rest,
    )
    (
        output, tokens_grad, memory_grad, self_grad, cross_grad, gains, shifts,
        down, down_bias, up, up_bias,
    ) = finish(
        prefix_len, output_low, tokens_low, memory_low, adapter.reshape(2, adapt, width), self_pre, sums
    )
    local = tokens.shape
    return (
        output.reshape(local),
        tokens_grad.reshape(local),
        memory_grad.reshape(local),
        jnp.swapaxes(self_grad, 0, 1),
        jnp.swapaxes(cross_grad, 0, 1),
        gains,
        shifts,
        down,
        down_bias.reshape(adapt),
        up,
        up_bias.reshape(width),
    )


def solution(mesh):
    placed = (
        (P("tp", "rows", None),) * 3
        + (P("rows", None),) * 2
        + (P(None, "tp"),) * 3
        + (P("tp", None),)
        + (P(None, "tp"),) * 3
        + (P("tp", None),)
        + (P(None, "tp"), P("tp", None))
        + (P(),) * 4
        + (P(None, None, "tp"),) * 2
        + (P(),) * 2
    )
    return jax.shard_map(
        functools.partial(per_device, mesh.shape["rows"]),
        mesh=mesh,
        in_specs=placed,
        out_specs=(P("tp", "rows", None),) * 3 + (P(None, None, "tp"),) * 2 + (P(),) * 6,
        check_vma=False,
    )
```

```python
import functools

import jax
import jax.numpy as jnp
from jax import lax
from jax.experimental import pallas as pl
from jax.experimental.pallas import tpu as pltpu
from jax.sharding import PartitionSpec as P

HEAD = 64
PAIR = 2 * HEAD
PRE = 128
PRE_PACK = 32
GROUP = 8
LINE = 4
MASKED = -1000000000.0
EPSILON = 1e-05
VMEM_BYTES = 62 << 20
SCALE = HEAD**-0.5
f32 = jnp.float32
bf16 = jnp.bfloat16
MESH = pl.DeviceIdType.MESH
VMEM = pltpu.VMEM
ANY = pl.ANY


def nn(a, b):
    return lax.dot_general(a, b, (((1,), (0,)), ((), ())), preferred_element_type=f32)


def nt(a, b):
    return lax.dot_general(a, b, (((1,), (1,)), ((), ())), preferred_element_type=f32)


def tn(a, b):
    return lax.dot_general(a, b, (((0,), (0,)), ((), ())), preferred_element_type=f32)


def gelu_parts(v):
    phi = 0.5 + 0.5 * lax.erf(v * (0.5**0.5))
    slope = phi + v * (jnp.exp(-0.5 * v * v) * 0.3989422804014327)
    return v * phi, slope


def norm_parts(v):
    centered = v - jnp.mean(v, axis=-1, keepdims=True)
    spread = lax.rsqrt(jnp.mean(centered * centered, axis=-1, keepdims=True) + EPSILON)
    return centered * spread, spread


def norm_back(dy, gain, n, spread):
    dn = dy * gain
    dv = spread * (
        dn - jnp.mean(dn, axis=-1, keepdims=True) - n * jnp.mean(dn * n, axis=-1, keepdims=True)
    )
    return dv, jnp.sum(dy * n, axis=0, keepdims=True), jnp.sum(dy, axis=0, keepdims=True)


def lane_half(shape, h):
    return (lax.broadcasted_iota(jnp.int32, shape, 1) // HEAD) == h


def column(row):
    return jnp.broadcast_to(row, (8, row.shape[1])).T[:, 0:1]


def prefix_bias(shape, axis, prefix_len):
    return jnp.where(lax.broadcasted_iota(jnp.int32, shape, axis) < prefix_len, 0.0, MASKED)


def mask_bias(seg_q, seg_k, shape, key_axis, first_query):
    keep = seg_q == seg_k
    if first_query is not None:
        query = first_query + lax.broadcasted_iota(jnp.int32, shape, 1 - key_axis)
        keep = keep & (lax.broadcasted_iota(jnp.int32, shape, key_axis) <= query)
    return jnp.where(keep, 0.0, MASKED)


def pair_forward(q_pair, k_pair, v_pair, bias):
    outs, logs = [], []
    for h in range(2):
        half = lane_half(q_pair.shape, h)
        scores = nt(jnp.where(half, q_pair, jnp.zeros_like(q_pair)), k_pair) + bias
        top = jnp.max(scores, axis=1, keepdims=True)
        e = jnp.exp(scores - top)
        total = jnp.sum(e, axis=1, keepdims=True)
        outs.append(nn(e.astype(bf16), v_pair) * (1.0 / total))
        logs.append(top + jnp.log(total))
    return jnp.where(lane_half(outs[0].shape, 0), outs[0], outs[1]).astype(bf16), logs


def keep_logs(kept, logs, j):
    lane = lax.broadcasted_iota(jnp.int32, kept.shape, 1)
    for h in range(2):
        kept[...] = jnp.where(lane == 2 * j + h, logs[h], kept[...])


def pair_backward(q_pair, k_pair, v_pair, a_pair, da_pair, logs, bias_t):
    k_turned = k_pair.T
    prod = da_pair.astype(f32) * a_pair.astype(f32)
    prod_high = prod.astype(bf16)
    prod_low = (prod - prod_high.astype(f32)).astype(bf16)
    pick = (
        lax.broadcasted_iota(jnp.int32, (8, PAIR), 1) // HEAD
        == lax.broadcasted_iota(jnp.int32, (8, PAIR), 0)
    ).astype(bf16)
    delta = nt(pick, prod_high) + nt(pick, prod_low)
    dk = dv = None
    dq = []
    for h in range(2):
        half = lane_half(q_pair.shape, h)
        q = jnp.where(half, q_pair, jnp.zeros_like(q_pair))
        da = jnp.where(half, da_pair, jnp.zeros_like(da_pair))
        p = jnp.exp(nt(k_pair, q) + (bias_t - logs[h]))
        ds = (p * (nt(v_pair, da) - delta[h : h + 1])).astype(bf16)
        dv_h = nn(p.astype(bf16), da)
        dk_h = nn(ds, q)
        dk = dk_h if dk is None else dk + dk_h
        dv = dv_h if dv is None else dv + dv_h
        dq.append(nn(k_turned[h * HEAD : (h + 1) * HEAD], ds))
    return jnp.concatenate(dq, axis=0).T.astype(bf16), dk, dv


def whole_spec(shape):
    return pl.BlockSpec(shape, lambda i: (0,) * len(shape))


def shard_spec(shape, index=lambda i: i):
    return pl.BlockSpec((1,) + shape[1:], lambda i: (index(i), 0, 0))


def feed_forward_kernel(
    v2, out_grad, w_in, w_out, down, down_bias, up, up_bias, gain, shift,
    output, dr2, summed, rest, vecs,
    n2_low, n2_hat, total, e_low, slope, grad, g, s1, h, xb, send, recv,
):
    step = pl.program_id(0)
    half = pl.num_programs(0) // 2
    links = Links(send, recv)
    reduce = AdapterReduceFirst(links, g, s1, h, xb)

    @pl.when(step == 0)
    def _():
        greet([links.tp_peer(1), links.side_peer()])
        n, _ = norm_parts(v2[...])
        n2_hat[...] = n
        normed = n * gain[1:2] + shift[1:2]
        total[...] = normed
        n2_low[...] = normed.astype(bf16)

    @pl.when(step < half)
    def _():
        act, bend = gelu_parts(nn(n2_low[...], w_in[0]))
        slope[step] = bend
        total[...] += nn(act.astype(bf16), w_out[0])

    @pl.when(step == half - 1)
    def _():
        act, bend = gelu_parts(nn(n2_low[...], down[...]) + down_bias[...])
        act = act.astype(bf16)
        resid = total[...] + 4.0 * (nn(act, up[...]) + up_bias[...])
        n, spread = norm_parts(resid)
        output[...] = (n * gain[2:3] + shift[2:3]).astype(bf16)
        dz, gain_part, shift_part = norm_back(out_grad[...].astype(f32), gain[2:3], n, spread)
        e_low[...] = dz.astype(bf16)
        four = (4.0 * dz).astype(bf16)
        g[0] = tn(act, four).astype(bf16).reshape(g.shape[1:])
        da = (nt(four, up[...]) * bend).astype(bf16)
        g[1] = tn(da, n2_low[...]).astype(bf16).reshape(g.shape[1:])
        reduce.start_beside()
        grad[...] = dz + nt(da, down[...])
        vecs[...] = jnp.zeros_like(vecs)
        vecs[2:3] = gain_part
        vecs[5:6] = shift_part
        vecs[6:7] = jnp.sum(four.astype(f32), axis=0, keepdims=True)
        vecs[7:8, 0 : down.shape[1]] = jnp.sum(da.astype(f32), axis=0, keepdims=True)

    @pl.when(step >= half)
    def _():
        du = (nt(e_low[...], w_out[0]) * slope[2 * half - 1 - step]).astype(bf16)
        grad[...] += nt(du, w_in[0])

    @pl.when(step == half)
    def _():
        reduce.start_side()

    @pl.when(step == 2 * half - 1)
    def _():
        _, spread = norm_parts(v2[...])
        dv, gain_part, shift_part = norm_back(grad[...], gain[1:2], n2_hat[...], spread)
        dr2[...] = dv
        vecs[1:2] = gain_part
        vecs[4:5] = shift_part
        reduce.finish(summed, rest)


def feed_forward(v2, out_grad, w_in, w_out, down, down_bias, up, up_bias, gain, shift):
    n, width, inner = w_in.shape
    block = v2.shape[0]
    adapt = down.shape[1]
    out = jax.ShapeDtypeStruct
    outs = (
        out((block, width), bf16),
        out((block, width), f32),
        out((LINE, adapt // GROUP, width), bf16),
        out((LINE // 2, adapt // GROUP, width), bf16),
        out((8, width), f32),
    )
    parts = (2, LINE, adapt // GROUP, width)
    turn = lambda i: jnp.minimum(i, 2 * n - 1 - i)
    return pl.pallas_call(
        feed_forward_kernel,
        grid=(2 * n,),
        out_shape=outs,
        in_specs=[whole_spec(v2.shape), whole_spec(out_grad.shape)]
        + [shard_spec(w_in.shape, turn), shard_spec(w_out.shape, turn)]
        + [whole_spec(a.shape) for a in (down, down_bias, up, up_bias, gain, shift)],
        out_specs=[whole_spec(a.shape) for a in outs],
        scratch_shapes=[
            VMEM((block, width), bf16),
            VMEM((block, width), f32),
            VMEM((block, width), f32),
            VMEM((block, width), bf16),
            VMEM((n, block, inner), f32),
            VMEM((block, width), f32),
            VMEM((2,) + parts, bf16),
            VMEM(parts, bf16),
            VMEM(parts, bf16),
            VMEM((LINE // 2,) + parts[2:], bf16),
            pltpu.SemaphoreType.DMA((2,)),
            pltpu.SemaphoreType.DMA((2,)),
        ],
        compiler_params=pltpu.CompilerParams(
            collective_id=2, has_side_effects=True, vmem_limit_bytes=VMEM_BYTES
        ),
        name="feed_forward",
    )(v2, out_grad, w_in, w_out, down, down_bias, up, up_bias, gain, shift)


class Links:
    def __init__(self, send, recv):
        self.send, self.recv = send, recv
        self.row = lax.axis_index("rows")
        self.t = lax.axis_index("tp")
        self.flows = 0
        place = lax.rem(self.row, GROUP)
        self.base = self.row - place
        self.a = place // 2
        self.b = lax.rem(place, 2)
        self.place = place

    def flow(self):
        self.flows += 1
        return self.flows - 1

    def tp_peer(self, mask):
        return (self.row, self.t ^ mask)

    def line_peer(self, d):
        return (self.base + lax.rem(self.a + d, LINE) * 2 + self.b, self.t)

    def side_peer(self):
        return (self.base + self.a * 2 + (1 - self.b), self.t)

    def copy(self, src, dst, flow, peer):
        return pltpu.make_async_remote_copy(
            src_ref=src,
            dst_ref=dst,
            send_sem=self.send.at[flow],
            recv_sem=self.recv.at[flow],
            device_id=peer,
            device_id_type=MESH,
        )

    def start(self, src, dst, flow, peer):
        made = self.copy(src, dst, flow, peer)
        made.start()
        return made

    def arrived(self, dst, flow, peer):
        self.copy(dst, dst, flow, peer).wait_recv()


def greet(peers):
    barrier = pltpu.get_barrier_semaphore()
    for peer in peers:
        pl.semaphore_signal(barrier, inc=1, device_id=peer, device_id_type=MESH)
    pl.semaphore_wait(barrier, len(peers))


CHUNKS = 4


FLOWS = 14


class WeightGather:
    def __init__(self, links, base, across, own, full, stage, local):
        self.links, self.base, self.across = links, base, across
        self.own, self.full, self.stage, self.local = own, full, stage, local
        self.far, self.last = links.t ^ 2, links.t ^ 3
        a = links.a
        self.right = (links.base + jnp.minimum(a + 1, LINE - 1) * 2 + links.b, links.t)
        self.left = (links.base + jnp.maximum(a - 1, 0) * 2 + links.b, links.t)
        self.side = links.side_peer()
        self.sibling = links.tp_peer(1)
        self.over = links.tp_peer(2)

    def at(self, i, a, b):
        rows = self.own[i].shape[0] // GROUP
        return pl.ds(pl.multiple_of((a * 2 + b) * rows, rows), rows)

    def part(self, i, a, b):
        return self.full[i].at[self.far, self.at(i, a, b)]

    def flow(self, i, k):
        return self.base + i * FLOWS + k

    def over_copy(self, i, k):
        links = self.links
        b = links.b if k == 0 else 1 - links.b
        at = self.at(i, links.a, b)
        return links.copy(
            self.own[i].at[at], self.full[i].at[links.t, at], self.flow(i, k), self.over
        )

    def beside_copy(self, i):
        return self.links.copy(
            self.own[i], self.full[i].at[self.links.t], self.flow(i, 2), self.sibling
        )

    def pass_copy(self, i):
        whole = self.full[i].at[self.far]
        return self.links.copy(whole, whole, self.flow(i, 3), self.sibling)

    def moved(self, i, a, flow, peer):
        part = self.part(i, a, self.links.b)
        return self.links.copy(part, part, self.flow(i, flow), peer)

    def stage_in(self, i):
        stage = self.full[i].at[self.links.t] if self.stage is None else self.stage[i]
        return pltpu.make_async_copy(self.own[i], stage, self.local.at[2 * i])

    def stage_out(self, i):
        return pltpu.make_async_copy(
            self.stage[i], self.full[i].at[self.links.t], self.local.at[2 * i + 1]
        )

    def start_over(self, i, k):
        self.over_copy(i, k).start()

    def start_beside(self, i):
        self.beside_copy(i).start()
        self.stage_in(i).start()

    def own_ready(self, i):
        self.stage_in(i).wait()

    def beside_ready(self, i):
        self.links.arrived(self.full[i].at[self.links.t ^ 1], self.flow(i, 2), self.sibling)

    def far_ready(self, i):
        self.links.arrived(self.full[i].at[self.last], self.flow(i, 3), self.sibling)

    def keep_own(self, i):
        self.own_ready(i)
        self.stage_out(i).start()

    def came_over(self, i):
        mine = self.part(i, self.links.a, self.links.b)
        self.links.arrived(mine, self.flow(i, 0), self.over)
        self.spread(i)

    def spread(self, i):
        a = self.links.a

        @pl.when(a < LINE - 1)
        def _():
            self.moved(i, a, 4, self.right).start()

        @pl.when(a > 0)
        def _():
            self.moved(i, a, 7, self.left).start()

        if self.across[i] == 1:
            self.moved(i, a, 10, self.side).start()

    def along(self, i, k):
        links, a = self.links, self.links.a

        @pl.when(a - 1 - k >= 0)
        def _():
            links.arrived(self.part(i, a - 1 - k, links.b), self.flow(i, 4 + k), self.left)
            if k < LINE - 2:

                @pl.when(a < LINE - 1)
                def _():
                    self.moved(i, a - 1 - k, 5 + k, self.right).start()

            self.moved(i, a - 1 - k, 11 + k, self.side).start()

        @pl.when(a + 1 + k <= LINE - 1)
        def _():
            links.arrived(self.part(i, a + 1 + k, links.b), self.flow(i, 7 + k), self.right)
            if k < LINE - 2:

                @pl.when(a > 0)
                def _():
                    self.moved(i, a + 1 + k, 8 + k, self.left).start()

            self.moved(i, a + 1 + k, 13 - k, self.side).start()

    def side_part(self, i, k):
        links, a = self.links, self.links.a
        if k == 0:
            return self.part(i, a, 1 - links.b)
        piece = jnp.where(k <= a, a - k, a + LINE - k)
        return self.part(i, piece, 1 - links.b)

    def complete(self, i):
        links = self.links
        if self.across[i] == 2:
            links.arrived(self.side_part(i, 0), self.flow(i, 1), self.over)
        for k in range(self.across[i] - 1, LINE):
            links.arrived(self.side_part(i, k), self.flow(i, 10 + k), self.side)
        self.pass_copy(i).start()

    def finish(self, i):
        if self.stage is not None:
            self.beside_ready(i)
            self.far_ready(i)
            self.stage_out(i).wait()
        for k in range(self.across[i]):
            self.over_copy(i, k).wait_send()
        self.beside_copy(i).wait_send()
        self.spread_sent(i)

    def spread_sent(self, i):
        a = self.links.a
        self.pass_copy(i).wait_send()
        for k in range(LINE - 1):

            @pl.when((a < LINE - 1) & (a - k >= 0))
            def _():
                self.moved(i, a - k, 4 + k, self.right).wait_send()

            @pl.when((a > 0) & (a + k <= LINE - 1))
            def _():
                self.moved(i, a + k, 7 + k, self.left).wait_send()

        for k in range(self.across[i] - 1, LINE):
            piece = a if k == 0 else jnp.where(k <= a, a - k, a + LINE - k)
            self.moved(i, piece, 10 + k, self.side).wait_send()


class AdapterSpread(WeightGather):
    def __init__(self, links, base, full):
        super().__init__(links, base, [1], None, full, None, None)
        self.half = lax.rem(links.t, 2)

    def part(self, i, a, b):
        return self.full.at[self.half, b, a]

    def pass_copy(self, i):
        whole = self.full.at[self.half]
        return self.links.copy(whole, whole, self.flow(i, 3), self.sibling)

    def finish(self, i):
        self.links.arrived(self.full.at[1 - self.half], self.flow(i, 3), self.sibling)
        self.spread_sent(i)


class AdapterReduceFirst:
    def __init__(self, links, g, s1, h, xb):
        self.links, self.g, self.s1, self.h, self.xb = links, g, s1, h, xb
        self.half = lax.rem(links.t, 2)

    def beside(self):
        return self.links.copy(self.g.at[1 - self.half], self.s1, 0, self.links.tp_peer(1))

    def side(self):
        links = self.links
        return links.copy(
            self.h.at[1 - links.b, pl.ds(0, LINE // 2)], self.xb, 1, links.side_peer()
        )

    def start_beside(self):
        self.beside().start()

    def start_side(self):
        self.beside().wait()
        self.h[...] = (self.g[self.half].astype(f32) + self.s1[...].astype(f32)).astype(bf16)
        self.side().start()

    def finish(self, summed, rest):
        kept = LINE // 2
        mine = self.h[self.links.b]
        rest[...] = self.h[1 - self.links.b, kept:]
        summed[kept:] = mine[kept:]
        self.side().wait()
        summed[0:kept] = (mine[0:kept].astype(f32) + self.xb[...].astype(f32)).astype(bf16)


class AdapterReduce:
    def __init__(self, links, base, levels, summed, rest, xb, h2, zb, p3, yb, hb):
        self.links, self.base, self.levels = links, base, levels
        self.summed, self.rest, self.xb, self.h2 = summed, rest, xb, h2
        self.zb, self.p3, self.yb, self.hb = zb, p3, yb, hb
        self.half = lax.rem(links.t, 2)
        self.groups = [(links.row ^ (GROUP << level), links.t) for level in range(levels)]

    def side(self):
        return self.links.copy(self.rest, self.xb, self.base, self.links.side_peer())

    def piece(self, d):
        return lax.rem(self.links.a + d, LINE)

    def line(self, d):
        return self.links.copy(
            self.h2.at[self.piece(d)], self.zb.at[d - 1], self.base + d, self.links.line_peer(d)
        )

    def over(self):
        return self.links.copy(self.p3, self.yb, self.base + LINE, self.links.tp_peer(2))

    def group(self, level):
        return self.links.copy(
            self.hb.at[2 * level],
            self.hb.at[2 * level + 1],
            self.base + LINE + 1 + level,
            self.groups[level],
        )

    def start(self):
        kept = LINE // 2
        self.side().start()
        self.h2[0:kept] = self.summed[0:kept]
        for d in range(1, LINE):

            @pl.when(self.piece(d) < kept)
            def _():
                self.line(d).start()

    def start_line(self):
        kept = LINE // 2
        self.side().wait()
        self.h2[kept:] = (self.summed[kept:].astype(f32) + self.xb[...].astype(f32)).astype(bf16)
        for d in range(1, LINE):

            @pl.when(self.piece(d) >= kept)
            def _():
                self.line(d).start()

    def start_over(self):
        for d in range(1, LINE):
            self.line(d).wait()
        total = self.h2[self.links.a].astype(f32)
        for d in range(1, LINE):
            total = total + self.zb[d - 1].astype(f32)
        self.p3[...] = total.astype(bf16)
        self.over().start()

    def result(self):
        self.over().wait()
        value = self.p3[...].astype(f32) + self.yb[...].astype(f32)
        for level in range(self.levels):
            self.hb[2 * level] = value.astype(bf16)
            self.group(level).start()
            self.group(level).wait()
            value = self.hb[2 * level].astype(f32) + self.hb[2 * level + 1].astype(f32)
        return value.astype(bf16)


class RowGather:
    FLOWS = 1 + 2 * 4

    def __init__(self, links, base, own, full):
        self.links, self.base, self.own, self.full = links, base, own, full
        self.far, self.last = links.t ^ 2, links.t ^ 3
        self.sibling, self.over = links.tp_peer(1), links.tp_peer(2)

    def at(self, c):
        rows = self.own.shape[0] // CHUNKS
        return pl.ds(c * rows, rows)

    def beside_copy(self):
        return self.links.copy(self.own, self.full.at[self.links.t], self.base, self.sibling)

    def over_copy(self, c):
        at = self.at(c)
        return self.links.copy(
            self.own.at[at], self.full.at[self.links.t, at], self.base + 1 + c, self.over
        )

    def pass_copy(self, c):
        part = self.full.at[self.far, self.at(c)]
        return self.links.copy(part, part, self.base + 1 + CHUNKS + c, self.sibling)

    def start_beside(self):
        self.beside_copy().start()

    def start_over(self):
        for c in range(CHUNKS):
            self.over_copy(c).start()

    def came_beside(self):
        self.links.arrived(self.full.at[self.links.t ^ 1], self.base, self.sibling)

    def came_over_chunk(self, c):
        self.links.arrived(self.full.at[self.far, self.at(c)], self.base + 1 + c, self.over)
        self.pass_copy(c).start()

    def came_over(self):
        for c in range(CHUNKS):
            self.came_over_chunk(c)

    def came_last(self):
        for c in range(CHUNKS):
            self.links.arrived(
                self.full.at[self.last, self.at(c)], self.base + 1 + CHUNKS + c, self.sibling
            )

    def sent(self):
        self.beside_copy().wait_send()
        for c in range(CHUNKS):
            self.over_copy(c).wait_send()
            self.pass_copy(c).wait_send()


class RowScatter:
    FLOWS = 2 + 4

    def __init__(self, links, base, part, near, near_far, mid, far):
        self.links, self.base, self.part = links, base, part
        self.near, self.near_far, self.mid, self.far = near, near_far, mid, far
        self.sibling, self.over = links.tp_peer(1), links.tp_peer(2)

    def at(self, c):
        rows = self.near.shape[0] // CHUNKS
        return pl.ds(c * rows, rows)

    def first_copy(self):
        return self.links.copy(
            self.part.at[self.links.t ^ 3], self.near_far, self.base, self.sibling
        )

    def second_copy(self):
        return self.links.copy(
            self.part.at[self.links.t ^ 1], self.near, self.base + 1, self.sibling
        )

    def over_copy(self, c):
        at = self.at(c)
        return self.links.copy(
            self.mid.at[at], self.far.at[at], self.base + 2 + c, self.over
        )

    def send_over(self):
        self.links.arrived(self.near_far, self.base, self.sibling)
        for c in range(CHUNKS):
            at = self.at(c)
            self.mid[at] = (
                self.part[self.links.t ^ 2, at].astype(f32) + self.near_far[at].astype(f32)
            ).astype(bf16)
            self.over_copy(c).start()

    def came_beside(self):
        self.links.arrived(self.near, self.base + 1, self.sibling)

    def came_over(self, c):
        at = self.at(c)
        self.links.arrived(self.far.at[at], self.base + 2 + c, self.over)
        return (
            self.part[self.links.t, at].astype(f32)
            + self.near[at].astype(f32)
            + self.far[at].astype(f32)
        )

    def sent(self):
        self.first_copy().wait_send()
        self.second_copy().wait_send()
        for c in range(CHUNKS):
            self.over_copy(c).wait_send()


def halves(own, full, stage):
    outs = ([], [], [])
    for one, whole, held in zip(own, full, stage):
        rows = one.shape[0] // 2
        for o in range(2):
            at = pl.ds(o * rows, rows)
            for out, view in zip(outs, (one.at[at], whole.at[:, at], held.at[at])):
                out.append(view)
    return outs


def cut(refs, *counts):
    out, at = [], 0
    for count in counts:
        out.append(refs[at : at + count])
        at += count
    return out


def forward_kernel(prefix_len, *refs):
    ins, self_outs, cross_outs, kept_outs, scratch = cut(refs, 18, 6, 6, 6, 26)
    x, pre_cross, wq, wk, wv, wo, pre, dec, src, gain, shift = ins[:11]
    memory, own_cross, own_ffn = ins[11], list(ins[12:16]), list(ins[16:18])
    q_out, k_out, v_out, a_out, l_out, resid = self_outs
    q2_out, k2_out, v2_out, a2_out, l2_out, resid2 = cross_outs
    cross_kept, ffn_full = list(kept_outs[:4]), list(kept_outs[4:])
    cross_full, held = list(scratch[:4]), list(scratch[4:6])
    (
        m_full, pre_full, x_full, part, kept, bias, near, near_far, mid, far, pre_stage, n1_low,
        send, recv, cross_local, ffn_local, m_local, keep_local, pre_local, spare,
    ) = scratch[6:]
    del spare
    block, lanes = x.shape[0], q_out.shape[1]
    links = Links(send, recv)
    t = links.t
    early = range(4)
    late = range(4)
    cross = WeightGather(links, 0, [1] * 4, own_cross, cross_full, None, cross_local)
    ffn = WeightGather(links, 4 * FLOWS, [2] * 4, *halves(own_ffn, ffn_full, held), ffn_local)
    at = 8 * FLOWS
    x_rows = RowGather(links, at, x, x_full)
    at += RowGather.FLOWS
    m_rows = RowGather(links, at, memory, m_full)
    at += RowGather.FLOWS
    sums = RowScatter(links, at, part, near, near_far, mid, far)
    at += RowScatter.FLOWS
    m_keep = pltpu.make_async_copy(memory, m_full.at[t], m_local.at[0])
    pre_keep = pltpu.make_async_copy(pre_stage, pre_full.at[t], pre_local.at[0])
    pre_sends = [
        links.copy(pre_stage, pre_full.at[t], at + m - 1, links.tp_peer(m)) for m in (1, 2, 3)
    ]
    cross_keeps = [
        pltpu.make_async_copy(cross_full[i], cross_kept[i], keep_local.at[i]) for i in range(4)
    ]

    greet(
        [links.tp_peer(m) for m in (1, 2, 3)]
        + [links.line_peer(d) for d in range(1, LINE)]
        + [links.side_peer()]
    )
    x_rows.start_over()
    x_rows.start_beside()
    kept[...] = jnp.zeros_like(kept)
    pre_stage[...] = jnp.zeros_like(pre_stage)
    for o in range(2):
        pre_stage[o * PRE_PACK : o * PRE_PACK + prefix_len] = pre_cross[:, o]
    pre_keep.start()
    for one in pre_sends:
        one.start()
    m_keep.start()

    for target, o in ((k_out, 0), (v_out, 1)):
        target[0:PRE] = jnp.zeros((PRE, lanes), bf16)
        target[0:prefix_len] = pre[:, o]

    def project(rows, index):
        at = pl.multiple_of(index * block, block)
        q_out[pl.ds(at, block)] = (SCALE * nn(rows, wq[...])).astype(bf16)
        k_out[pl.ds(PRE + at, block)] = nn(rows, wk[...]).astype(bf16)
        v_out[pl.ds(PRE + at, block)] = nn(rows, wv[...]).astype(bf16)

    project(x[...], t)
    x_rows.came_beside()
    project(x_full[t ^ 1], t ^ 1)
    for c in range(CHUNKS):
        x_rows.came_over_chunk(c)
        if c == 3:
            for i in early:
                cross.start_over(i, 0)
    project(x_full[t ^ 2], t ^ 2)
    x_rows.came_last()
    for i in early:
        cross.start_beside(i)
    m_rows.start_beside()
    project(x_full[t ^ 3], t ^ 3)

    @pl.loop(0, 4)
    def _(order):
        here = t ^ (3 - order)
        for i in range(4):
            keys = PRE + (i + 1) * block

            @pl.when(here == i)
            def _():
                bias[:, 0:PRE] = prefix_bias((block, PRE), 1, prefix_len)
                bias[:, PRE:keys] = mask_bias(
                    column(dec[:, i * block : (i + 1) * block]),
                    dec[:, 0 : keys - PRE],
                    (block, keys - PRE),
                    1,
                    i * block,
                )

                @pl.loop(0, lanes // PAIR)
                def _(j):
                    cols = pl.ds(pl.multiple_of(j * PAIR, PAIR), PAIR)
                    mixture, logs = pair_forward(
                        q_out[i * block : (i + 1) * block, cols],
                        k_out[0:keys, cols],
                        v_out[0:keys, cols],
                        bias[:, 0:keys],
                    )
                    a_out[i, :, cols] = mixture
                    keep_logs(kept, logs, j)

        l_out[here] = kept[...].T[0:8]
        part[here] = nn(a_out[here], wo[...]).astype(bf16)

        @pl.when(order == 0)
        def _():
            sums.first_copy().start()
            for i in early:
                cross.came_over(i)
            for i in range(2):
                ffn.start_over(i, 0)

        @pl.when(order == 1)
        def _():
            sums.send_over()

        @pl.when(order == 2)
        def _():
            sums.second_copy().start()
            m_rows.start_over()
            for i in early:
                cross.along(i, 0)

    for i in range(2):
        ffn.came_over(i)
    for i in late:
        ffn.start_beside(i)
    for i in early:
        cross.along(i, 1)
    for i in range(2):
        ffn.along(i, 0)
    sums.came_beside()
    for c in range(CHUNKS):
        rows = sums.at(c)
        resid[rows] = x[rows].astype(f32) + sums.came_over(c)
    n, _ = norm_parts(resid[...])
    normed = n * gain[0:1] + shift[0:1]
    resid2[...] = normed
    n1_low[...] = normed.astype(bf16)
    kept[...] = jnp.zeros_like(kept)
    own_queries = dec[:, pl.ds(pl.multiple_of(t * block, block), block)]
    keys = k2_out.shape[1]
    bias[:, 0:PRE] = prefix_bias((block, PRE), 1, prefix_len)
    bias[:, PRE:] = mask_bias(column(own_queries), src[...], (block, keys - PRE), 1, None)
    for i in early:
        cross.along(i, 2)
    for i in range(2):
        ffn.along(i, 1)
    m_rows.came_over()
    for i in (2, 3):
        ffn.start_over(i, 0)
    m_rows.came_beside()
    m_rows.came_last()
    for m in (1, 2, 3):
        links.arrived(pre_full.at[t ^ m], at + m - 1, links.tp_peer(m))
    m_keep.wait()
    pre_keep.wait()
    for i in early:
        cross.own_ready(i)

    def each(method, indices, *more):
        def run():
            for i in indices:
                method(i, *more)

        return run

    events = {
        0: [each(ffn.keep_own, late), each(ffn.along, (0, 1), 2)],
        1: [each(ffn.came_over, (2,)), each(cross.complete, early)],
        2: [each(ffn.came_over, (3,)), each(ffn.start_over, late, 1)],
        3: [each(ffn.along, (2,), 0), each(cross.far_ready, early)],
        4: [each(ffn.along, (3,), 0), each(ffn.along, (2,), 1)],
        5: [each(ffn.along, (3,), 1)],
        6: [each(ffn.along, (2,), 2), each(ffn.complete, (0, 1))],
        7: [each(ffn.along, (3,), 2)],
    }

    @pl.loop(0, 4)
    def _(order):
        s = t ^ order

        @pl.when(order == 1)
        def _():
            for i in early:
                cross.beside_ready(i)

        q2_out[s] = (SCALE * nn(n1_low[...], cross_full[0][s])).astype(bf16)
        for target, o in ((k2_out, 0), (v2_out, PRE_PACK)):
            target[s, 0:PRE_PACK] = pre_full[s, o : o + PRE_PACK]
            target[s, PRE_PACK:PRE] = jnp.zeros((PRE - PRE_PACK, lanes), bf16)

        @pl.loop(0, 4)
        def _(i):
            rows = m_full[i]
            to = pl.ds(pl.multiple_of(PRE + i * block, PRE), block)
            k2_out[s, to] = nn(rows, cross_full[1][s]).astype(bf16)
            v2_out[s, to] = nn(rows, cross_full[2][s]).astype(bf16)

        for j in range(lanes // PAIR):
            cols = slice(j * PAIR, (j + 1) * PAIR)
            mixture, logs = pair_forward(
                q2_out[s, :, cols], k2_out[s, :, cols], v2_out[s, :, cols], bias[...]
            )
            a2_out[s, :, cols] = mixture
            keep_logs(kept, logs, j)
            for step in range(4):

                @pl.when(order == step)
                def _():
                    for event in events.get(2 * step + j, []):
                        event()

        l2_out[s] = kept[...].T[0:8]
        resid2[...] += nn(a2_out[s], cross_full[3][s])

    for one in cross_keeps:
        one.start()
    for i in (2, 3):
        ffn.complete(i)
    for i in early:
        cross.finish(i)
    for i in late:
        ffn.finish(i)
    x_rows.sent()
    m_rows.sent()
    sums.sent()
    for one in pre_sends:
        one.wait_send()
    for one in cross_keeps:
        one.wait()


def forward(
    prefix_len, x, memory, prefixes, self_weights, cross_weights, ffn_weights, dec, src, gain, shift
):
    n = 4
    block, width = x.shape
    lanes = self_weights[0].shape[1]
    seq = n * block
    out = jax.ShapeDtypeStruct
    flows = 8 * FLOWS + 2 * RowGather.FLOWS + RowScatter.FLOWS + 3
    self_outs = (
        out((seq, lanes), bf16),
        out((PRE + seq, lanes), bf16),
        out((PRE + seq, lanes), bf16),
        out((n, block, lanes), bf16),
        out((n, 8, block), f32),
        out((block, width), f32),
    )
    cross_outs = (
        out((n, block, lanes), bf16),
        out((n, PRE + seq, lanes), bf16),
        out((n, PRE + seq, lanes), bf16),
        out((n, block, lanes), bf16),
        out((n, 8, block), f32),
        out((block, width), f32),
    )
    full = tuple(out((n,) + w.shape, w.dtype) for w in (*cross_weights, *ffn_weights))
    given = (x, prefixes[1], *self_weights, prefixes[0], dec, src, gain, shift)
    anywhere = pl.BlockSpec(memory_space=pltpu.HBM)
    rows = VMEM((block, width), bf16)
    all_rows = VMEM((n, block, width), bf16)
    dma = pltpu.SemaphoreType.DMA
    return pl.pallas_call(
        functools.partial(forward_kernel, prefix_len),
        grid=(1,),
        out_shape=self_outs + cross_outs + full,
        in_specs=[whole_spec(g.shape) for g in given] + [anywhere] * 7,
        out_specs=[whole_spec(o.shape) for o in self_outs + cross_outs] + [anywhere] * 6,
        scratch_shapes=[VMEM((n,) + w.shape, w.dtype) for w in cross_weights]
        + [VMEM(w.shape, w.dtype) for w in ffn_weights]
        + [
            all_rows,
            VMEM((n, 2 * PRE_PACK, lanes), bf16),
            all_rows,
            all_rows,
            VMEM((block, 128), f32),
            VMEM((block, PRE + seq), f32),
            rows,
            rows,
            rows,
            rows,
            VMEM((2 * PRE_PACK, lanes), bf16),
            rows,
            dma((flows,)),
            dma((flows,)),
            dma((8,)),
            dma((8,)),
            dma((1,)),
            dma((4,)),
            dma((1,)),
            dma((1,)),
        ],
        compiler_params=pltpu.CompilerParams(
            collective_id=0, has_side_effects=True, vmem_limit_bytes=VMEM_BYTES
        ),
        name="forward",
    )(*given, memory, *cross_weights, *ffn_weights)


def doublings(count):
    levels = 0
    while (1 << levels) < count:
        levels += 1
    return levels


class Doubling:
    def __init__(self, links, base, levels, outgo, income):
        self.links, self.base, self.levels = links, base, levels
        self.outgo, self.income = outgo, income

    def move(self, level):
        return self.links.copy(
            self.outgo.at[level],
            self.income.at[level],
            self.base + level,
            (self.links.row ^ (1 << level), self.links.t),
        )

    def begin(self, value):
        self.outgo[0] = value
        self.move(0).start()

    def value(self, level):
        self.move(level).wait()
        return self.outgo[level] + self.income[level]

    def step(self, level):
        value = self.value(level)
        self.outgo[level + 1] = value
        self.move(level + 1).start()


def backward_kernel(prefix_len, reduce_levels, levels, *refs):
    ins, later, outs, scratch = cut(refs, 17, 9, 5, 54)
    dr2, v1, q, k, v, a, logs, wq, wo, wk, wv, dec, src, gain, vecs_in, summed, rest = ins
    tokens_grad, memory_grad, adapter, self_pre, sums = outs
    (
        dr1, dr1_low, dr2_low, bias, da, dq, dk, dv, total, xb, h2, zb, p3, yb, hb,
        cross, vecs, dm, dr1_full, part, dq1, dk1, dv1,
        near, near_far, mid, far, m_near, m_near_far, m_mid, m_far,
        cross_beside, cross_mid, cross_over, vecs_beside, vecs_mid, vecs_over,
        outgo, income, pre_outgo, pre_income, send, recv, keep_sem, load_sem,
    ) = scratch[:-9]
    loaded = scratch[-9:]
    q1, k1, v1_heads, a1, logs1, wq1, wk1, wv1, wo1 = loaded
    step = pl.program_id(0)
    steps = pl.num_programs(0) - 1
    block, lanes = q.shape[1:]
    keys = k.shape[1]
    links = Links(send, recv)
    t = links.t
    at = 0
    rows = RowGather(links, at, dr1_low, dr1_full)
    at += RowGather.FLOWS
    reduce = AdapterReduce(links, at, reduce_levels, summed, rest, xb, h2, zb, p3, yb, hb)
    at += 1 + LINE + reduce_levels
    spread = AdapterSpread(links, at, adapter)
    at += FLOWS
    m_sums = RowScatter(links, at, dm, m_near, m_near_far, m_mid, m_far)
    at += RowScatter.FLOWS
    x_sums = RowScatter(links, at, part, near, near_far, mid, far)
    at += RowScatter.FLOWS
    totals = Doubling(links, at, levels, outgo, income)
    at += levels
    pre_totals = Doubling(links, at, levels, pre_outgo, pre_income)
    at += levels
    keep = pltpu.make_async_copy(dr1_low, dr1_full.at[t], keep_sem.at[0])
    loads = [
        pltpu.make_async_copy(src_ref, dst_ref, load_sem.at[i])
        for i, (src_ref, dst_ref) in enumerate(zip(later, loaded))
    ]

    beside, over = links.tp_peer(1), links.tp_peer(2)
    to_beside = (
        links.copy(cross.at[t ^ 1], cross_beside.at[0], at, beside),
        links.copy(cross.at[t ^ 3], cross_beside.at[1], at + 1, beside),
        links.copy(vecs, vecs_beside, at + 2, beside),
    )
    to_over = (
        links.copy(cross_mid, cross_over, at + 3, over),
        links.copy(vecs_mid, vecs_over, at + 4, over),
    )

    @pl.when(step == 0)
    def _():
        greet(
            [links.tp_peer(m) for m in (1, 2, 3)]
            + [links.line_peer(d) for d in range(1, LINE)]
            + [links.side_peer()]
            + [(links.row ^ (1 << level), t) for level in range(doublings(GROUP), levels)]
        )
        reduce.start()
        dr2_low[...] = dr2[...].astype(bf16)
        total[...] = jnp.zeros_like(total)
        own_queries = dec[:, pl.ds(pl.multiple_of(t * block, block), block)]
        bias[0:PRE] = prefix_bias((PRE, block), 0, prefix_len)
        bias[PRE:] = mask_bias(own_queries, column(src[...]), (keys - PRE, block), 0, None)

    @pl.when(step < steps)
    def _():
        da[...] = nt(dr2_low[...], wo[0]).astype(bf16)

        @pl.when(step == 0)
        def _():
            for one in loads:
                one.start()

        @pl.loop(0, lanes // PAIR)
        def _(j):
            cols = pl.ds(pl.multiple_of(j * PAIR, PAIR), PAIR)
            dq_pair, dk_pair, dv_pair = pair_backward(
                q[0, :, cols],
                k[0, :, cols],
                v[0, :, cols],
                a[0, :, cols],
                da[:, cols],
                [logs[0, pl.ds(2 * j + i, 1)] for i in range(2)],
                bias[...],
            )
            dq[:, cols] = dq_pair
            cross[step, 0:PRE_PACK, cols] = dk_pair[0:PRE_PACK]
            cross[step, PRE_PACK : 2 * PRE_PACK, cols] = dv_pair[0:PRE_PACK]
            dk[step, :, cols] = dk_pair[PRE:].astype(bf16)
            dv[step, :, cols] = dv_pair[PRE:].astype(bf16)

            @pl.when((step == 1) & (j == 1))
            def _():
                reduce.start_line()

            @pl.when((step == 3) & (j == 1))
            def _():
                reduce.start_over()


        total[...] += nt(dq[...], wq[0])

    @pl.when(step == steps)
    def _():
        n, spread_one = norm_parts(v1[...])
        grad, gain_part, shift_part = norm_back(
            dr2[...] + SCALE * total[...], gain[0:1], n, spread_one
        )
        dr1_low[...] = grad.astype(bf16)
        rows.start_over()
        rows.start_beside()
        keep.start()
        dr1[...] = grad
        vecs[...] = vecs_in[...]
        vecs[0:1] = gain_part
        vecs[3:4] = shift_part
        for one in to_beside:
            one.start()
        dk1[...] = jnp.zeros_like(dk1)
        dv1[...] = jnp.zeros_like(dv1)

        @pl.loop(0, 4)
        def _(order):
            here = t ^ (3 - order)
            to = pl.ds(pl.multiple_of(here * block, block), block)
            value = None
            for shard in range(dk.shape[0]):
                term = nt(dk[shard, to], wk[shard]) + nt(dv[shard, to], wv[shard])
                value = term if value is None else value + term
            dm[here] = value.astype(bf16)

        m_sums.first_copy().start()
        m_sums.second_copy().start()
        for one in loads:
            one.wait()
        keep.wait()
        rows.came_beside()
        for one in to_beside:
            one.wait()
        cross_mid[...] = cross[t ^ 2] + cross_beside[1]
        vecs_mid[...] = vecs[...] + vecs_beside[...]
        for one in to_over:
            one.start()
        p3[...] = reduce.result()
        settle = pltpu.make_async_copy(
            p3, adapter.at[spread.half, links.b, links.a], keep_sem.at[1]
        )
        settle.start()
        settle.wait()
        spread.spread(0)

        @pl.loop(0, 4)
        def _(order):
            here = t ^ order

            @pl.when(order == 2)
            def _():
                rows.came_over()
                m_sums.send_over()
                rows.came_last()

            da[...] = nt(dr1_full[here], wo1[...]).astype(bf16)
            for i in range(4):
                own = slice(i * block, (i + 1) * block)
                size = PRE + (i + 1) * block

                @pl.when(here == i)
                def _():
                    bias[0:PRE] = prefix_bias((PRE, block), 0, prefix_len)
                    bias[PRE:size] = mask_bias(
                        dec[:, own],
                        column(dec[:, 0 : size - PRE]),
                        (size - PRE, block),
                        0,
                        i * block,
                    )

                    @pl.loop(0, lanes // PAIR)
                    def _(j):
                        cols = pl.ds(pl.multiple_of(j * PAIR, PAIR), PAIR)
                        dq_pair, dk_pair, dv_pair = pair_backward(
                            q1[own, cols],
                            k1[0:size, cols],
                            v1_heads[0:size, cols],
                            a1[i, :, cols],
                            da[:, cols],
                            [logs1[i, pl.ds(2 * j + o, 1)] for o in range(2)],
                            bias[0:size],
                        )
                        dq1[i, :, cols] = dq_pair
                        dk1[0:size, cols] += dk_pair
                        dv1[0:size, cols] += dv_pair

            for k in range(3):

                @pl.when(order == k)
                def _():
                    spread.along(0, k)

            @pl.when(order == 2)
            def _():
                for one in to_over:
                    one.wait()
                value = vecs_mid[...] + vecs_over[...]
                pieces = [cross[t] + cross_beside[0] + cross_over[...]] + [
                    value[:, o * lanes : (o + 1) * lanes] for o in range(vecs.shape[1] // lanes)
                ]
                totals.begin(jnp.concatenate(pieces, axis=0))

        pre_totals.begin(jnp.concatenate([dk1[0:PRE_PACK], dv1[0:PRE_PACK]], axis=0))
        for order in range(4):
            here = t ^ (3 - order)
            done = pl.ds(pl.multiple_of(PRE + here * block, PRE), block)
            part[here] = (
                SCALE * nt(dq1[here], wq1[...])
                + nt(dk1[done].astype(bf16), wk1[...])
                + nt(dv1[done].astype(bf16), wv1[...])
            ).astype(bf16)
            if order == 0:
                x_sums.first_copy().start()
                totals.step(0)
            if order == 1:
                x_sums.send_over()
                pre_totals.step(0)
            if order == 2:
                x_sums.second_copy().start()

        for level in range(1, levels - 1):
            totals.step(level)
            pre_totals.step(level)
        spread.complete(0)
        m_sums.came_beside()
        for c in range(CHUNKS):
            memory_grad[m_sums.at(c)] = m_sums.came_over(c).astype(bf16)
        sums[...] = totals.value(levels - 1)
        self_pre[...] = pre_totals.value(levels - 1)
        x_sums.came_beside()
        for c in range(CHUNKS):
            here = x_sums.at(c)
            tokens_grad[here] = (dr1[here] + x_sums.came_over(c)).astype(bf16)
        spread.finish(0)
        rows.sent()
        m_sums.sent()
        x_sums.sent()


def backward(
    prefix_len, row_count, dr2, resid_one, cross_saved, cross_weights, self_saved, self_weights,
    dec, src, gain, vecs, summed, rest,
):
    q, k, v, a, logs = cross_saved
    wq, wk, wv, wo = cross_weights
    n, block, lanes = q.shape
    keys = k.shape[1]
    width = dr2.shape[1]
    reduce_levels = doublings(row_count // GROUP)
    levels = doublings(row_count)
    piece = summed.shape[1]
    half = (2, LINE, piece, width)
    packed = 2 * PRE_PACK
    height = packed + vecs.shape[0] * width // lanes
    out = jax.ShapeDtypeStruct
    outs = (
        out((block, width), bf16),
        out((block, width), bf16),
        out((2,) + half, bf16),
        out((packed, lanes), f32),
        out((height, lanes), f32),
    )
    flows = (
        RowGather.FLOWS + 1 + LINE + reduce_levels + FLOWS + 2 * RowScatter.FLOWS + 2 * levels + 5
    )
    later = (*self_saved, *self_weights)
    low, wide = VMEM((block, width), bf16), VMEM((block, width), f32)
    dma = pltpu.SemaphoreType.DMA
    bounded = lambda i: jnp.minimum(i, n - 1)

    def once(x):
        return pl.BlockSpec(x.shape, lambda i: (0,) * len(x.shape), pipeline_mode=pl.Buffered(1))

    return pl.pallas_call(
        functools.partial(backward_kernel, prefix_len, reduce_levels, levels),
        grid=(n + 1,),
        out_shape=outs,
        in_specs=[once(dr2), once(resid_one)]
        + [shard_spec(x.shape, bounded) for x in (q, k, v, a, logs, wq, wo)]
        + [once(x) for x in (wk, wv, dec, src, gain, vecs, summed, rest)]
        + [pl.BlockSpec(memory_space=pltpu.HBM)] * len(later),
        out_specs=[whole_spec(o.shape) for o in outs[:2]]
        + [pl.BlockSpec(memory_space=pltpu.HBM)]
        + [whole_spec(o.shape) for o in outs[3:]],
        scratch_shapes=[
            wide,
            low,
            low,
            VMEM((keys, block), f32),
            VMEM((block, lanes), bf16),
            VMEM((block, lanes), bf16),
            VMEM((n, keys - PRE, lanes), bf16),
            VMEM((n, keys - PRE, lanes), bf16),
            wide,
            VMEM((LINE // 2, piece, width), bf16),
            VMEM((LINE, piece, width), bf16),
            VMEM((LINE - 1, piece, width), bf16),
            VMEM((piece, width), bf16),
            VMEM((piece, width), bf16),
            VMEM((max(1, 2 * reduce_levels), piece, width), bf16),
            VMEM((n, packed, lanes), f32),
            VMEM(vecs.shape, f32),
            VMEM((n, block, width), bf16),
            VMEM((n, block, width), bf16),
            VMEM((n, block, width), bf16),
            VMEM((n, block, lanes), bf16),
            VMEM((keys, lanes), f32),
            VMEM((keys, lanes), f32),
        ]
        + [low] * 8
        + [
            VMEM((2, packed, lanes), f32),
            VMEM((packed, lanes), f32),
            VMEM((packed, lanes), f32),
            VMEM(vecs.shape, f32),
            VMEM(vecs.shape, f32),
            VMEM(vecs.shape, f32),
            VMEM((levels, height, lanes), f32),
            VMEM((levels, height, lanes), f32),
            VMEM((levels, packed, lanes), f32),
            VMEM((levels, packed, lanes), f32),
            dma((flows,)),
            dma((flows,)),
            dma((2,)),
            dma((len(later),)),
        ]
        + [VMEM(x.shape, x.dtype) for x in later],
        compiler_params=pltpu.CompilerParams(
            collective_id=1, has_side_effects=True, vmem_limit_bytes=VMEM_BYTES
        ),
        name="backward",
    )(dr2, resid_one, q, k, v, a, logs, wq, wo, wk, wv, dec, src, gain, vecs, summed, rest, *later)


def finish_kernel(
    prefix_len, lanes, output_low, tokens_low, memory_low, up_low, down_low, self_pre, sums,
    output, tokens_grad, memory_grad, self_out, cross_out, gains, shifts, down, down_bias, up, up_bias,
):
    output[...] = output_low[...]
    tokens_grad[...] = tokens_low[...]
    memory_grad[...] = memory_low[...]
    up[...] = up_low[0].astype(f32)
    rows = down.shape[0]
    at = pl.multiple_of(pl.program_id(0) * rows, rows)
    down[...] = down_low[0, :, pl.ds(at, rows)].astype(f32).T

    @pl.when(pl.program_id(0) == 0)
    def _():
        for o in range(2):
            rows = slice(o * PRE_PACK, o * PRE_PACK + prefix_len)
            self_out[:, o] = self_pre[rows]
            cross_out[:, o] = sums[rows]
        for i in range(gains.shape[1] // lanes):
            at = 2 * PRE_PACK + 8 * i
            cols = slice(i * lanes, (i + 1) * lanes)
            gains[:, cols] = sums[at : at + 3]
            shifts[:, cols] = sums[at + 3 : at + 6]
            up_bias[:, cols] = sums[at + 6 : at + 7]
            if (i + 1) * lanes <= down_bias.shape[1]:
                down_bias[:, cols] = sums[at + 7 : at + 8]


def finish(prefix_len, output_low, tokens_low, memory_low, adapter, self_pre, sums):
    steps = 2
    block, width = tokens_low.shape
    adapt = adapter.shape[1]
    lanes = sums.shape[1]
    out = jax.ShapeDtypeStruct
    outs = (
        out((block, width), bf16),
        out((block, width), bf16),
        out((block, width), bf16),
        out((prefix_len, 2, lanes), f32),
        out((prefix_len, 2, lanes), f32),
        out((3, width), f32),
        out((3, width), f32),
        out((width, adapt), f32),
        out((1, adapt), f32),
        out((adapt, width), f32),
        out((1, width), f32),
    )
    rows = pl.BlockSpec((block // steps, width), lambda i: (i, 0))
    specs = [whole_spec(o.shape) for o in outs]
    specs[0] = specs[1] = specs[2] = rows
    specs[7] = pl.BlockSpec((width // steps, adapt), lambda i: (i, 0))
    specs[9] = pl.BlockSpec((adapt // steps, width), lambda i: (i, 0))
    return pl.pallas_call(
        functools.partial(finish_kernel, prefix_len, lanes),
        grid=(steps,),
        out_shape=outs,
        in_specs=[rows, rows, rows]
        + [pl.BlockSpec((1, adapt // steps, width), lambda i: (0, i, 0))]
        + [pl.BlockSpec((1, adapt, width), lambda i: (1, 0, 0))]
        + [whole_spec(self_pre.shape), whole_spec(sums.shape)],
        out_specs=specs,
        compiler_params=pltpu.CompilerParams(vmem_limit_bytes=VMEM_BYTES),
        name="finish",
    )(output_low, tokens_low, memory_low, adapter, adapter, self_pre, sums)


def per_device(
    row_count,
    tokens, memory, out_grad, dec_segments, src_segments,
    self_query, self_key, self_value, self_out,
    cross_query, cross_key, cross_value, cross_out,
    ffn_in, ffn_out, adapt_down, adapt_down_bias, adapt_up, adapt_up_bias,
    self_prefix, cross_prefix, norm_gain, norm_shift,
):
    seq_local, _, width = tokens.shape
    prefix_len = self_prefix.shape[1]
    adapt = adapt_down.shape[1]
    x, mem, grad_in = (a.reshape(seq_local, width) for a in (tokens, memory, out_grad))
    self_weights = (self_query, self_key, self_value, self_out)

    (
        q1, k1, v1_heads, a1, logs1, resid_one, q2, k2, v2_heads, a2, logs2, resid_two, *gathered
    ) = forward(
        prefix_len, x, mem, [jnp.swapaxes(p, 0, 1) for p in (self_prefix, cross_prefix)], self_weights,
        (cross_query, cross_key, cross_value, cross_out), (ffn_in, ffn_out),
        dec_segments, src_segments, norm_gain, norm_shift,
    )
    cross_weights, (w_in, w_out) = gathered[:4], gathered[4:]
    output_low, dr2, summed, rest, vecs = feed_forward(
        resid_two, grad_in, w_in, w_out,
        adapt_down, adapt_down_bias.reshape(1, adapt), adapt_up, adapt_up_bias.reshape(1, width),
        norm_gain, norm_shift,
    )
    tokens_low, memory_low, adapter, self_pre, sums = backward(
        prefix_len, row_count, dr2, resid_one, (q2, k2, v2_heads, a2, logs2), cross_weights,
        (q1, k1, v1_heads, a1, logs1), self_weights,
        dec_segments, src_segments, norm_gain, vecs, summed, rest,
    )
    (
        output, tokens_grad, memory_grad, self_grad, cross_grad, gains, shifts,
        down, down_bias, up, up_bias,
    ) = finish(
        prefix_len, output_low, tokens_low, memory_low, adapter.reshape(2, adapt, width), self_pre, sums
    )
    local = tokens.shape
    return (
        output.reshape(local),
        tokens_grad.reshape(local),
        memory_grad.reshape(local),
        jnp.swapaxes(self_grad, 0, 1),
        jnp.swapaxes(cross_grad, 0, 1),
        gains,
        shifts,
        down,
        down_bias.reshape(adapt),
        up,
        up_bias.reshape(width),
    )


def solution(mesh):
    placed = (
        (P("tp", "rows", None),) * 3
        + (P("rows", None),) * 2
        + (P(None, "tp"),) * 3
        + (P("tp", None),)
        + (P(None, "tp"),) * 3
        + (P("tp", None),)
        + (P(None, "tp"), P("tp", None))
        + (P(),) * 4
        + (P(None, None, "tp"),) * 2
        + (P(),) * 2
    )
    return jax.shard_map(
        functools.partial(per_device, mesh.shape["rows"]),
        mesh=mesh,
        in_specs=placed,
        out_specs=(P("tp", "rows", None),) * 3 + (P(None, None, "tp"),) * 2 + (P(),) * 6,
        check_vma=False,
    )
```

```python
import functools

import jax
import jax.numpy as jnp
from jax import lax
from jax.experimental import pallas as pl
from jax.experimental.pallas import tpu as pltpu
from jax.sharding import PartitionSpec as P

HEAD = 64
PAIR = 2 * HEAD
PRE = 128
PRE_PACK = 32
GROUP = 8
LINE = 4
MASKED = -1000000000.0
EPSILON = 1e-05
VMEM_BYTES = 62 << 20
SCALE = HEAD**-0.5
f32 = jnp.float32
bf16 = jnp.bfloat16
MESH = pl.DeviceIdType.MESH
VMEM = pltpu.VMEM
ANY = pl.ANY


def nn(a, b):
    return lax.dot_general(a, b, (((1,), (0,)), ((), ())), preferred_element_type=f32)


def nt(a, b):
    return lax.dot_general(a, b, (((1,), (1,)), ((), ())), preferred_element_type=f32)


def tn(a, b):
    return lax.dot_general(a, b, (((0,), (0,)), ((), ())), preferred_element_type=f32)


def gelu_parts(v):
    phi = 0.5 + 0.5 * lax.erf(v * (0.5**0.5))
    slope = phi + v * (jnp.exp(-0.5 * v * v) * 0.3989422804014327)
    return v * phi, slope


def norm_parts(v):
    centered = v - jnp.mean(v, axis=-1, keepdims=True)
    spread = lax.rsqrt(jnp.mean(centered * centered, axis=-1, keepdims=True) + EPSILON)
    return centered * spread, spread


def norm_back(dy, gain, n, spread):
    dn = dy * gain
    dv = spread * (
        dn - jnp.mean(dn, axis=-1, keepdims=True) - n * jnp.mean(dn * n, axis=-1, keepdims=True)
    )
    return dv, jnp.sum(dy * n, axis=0, keepdims=True), jnp.sum(dy, axis=0, keepdims=True)


def lane_half(shape, h):
    return (lax.broadcasted_iota(jnp.int32, shape, 1) // HEAD) == h


def column(row):
    return jnp.broadcast_to(row, (8, row.shape[1])).T[:, 0:1]


def prefix_bias(shape, axis, prefix_len):
    return jnp.where(lax.broadcasted_iota(jnp.int32, shape, axis) < prefix_len, 0.0, MASKED)


def mask_bias(seg_q, seg_k, shape, key_axis, first_query):
    keep = seg_q == seg_k
    if first_query is not None:
        query = first_query + lax.broadcasted_iota(jnp.int32, shape, 1 - key_axis)
        keep = keep & (lax.broadcasted_iota(jnp.int32, shape, key_axis) <= query)
    return jnp.where(keep, 0.0, MASKED)


def pair_forward(q_pair, k_pair, v_pair, bias):
    outs, logs = [], []
    for h in range(2):
        half = lane_half(q_pair.shape, h)
        scores = nt(jnp.where(half, q_pair, jnp.zeros_like(q_pair)), k_pair) + bias
        top = jnp.max(scores, axis=1, keepdims=True)
        e = jnp.exp(scores - top)
        total = jnp.sum(e, axis=1, keepdims=True)
        outs.append(nn(e.astype(bf16), v_pair) * (1.0 / total))
        logs.append(top + jnp.log(total))
    return jnp.where(lane_half(outs[0].shape, 0), outs[0], outs[1]).astype(bf16), logs


def keep_logs(kept, logs, j):
    lane = lax.broadcasted_iota(jnp.int32, kept.shape, 1)
    for h in range(2):
        kept[...] = jnp.where(lane == 2 * j + h, logs[h], kept[...])


def pair_backward(q_pair, k_pair, v_pair, a_pair, da_pair, logs, bias_t):
    k_turned = k_pair.T
    prod = da_pair.astype(f32) * a_pair.astype(f32)
    prod_high = prod.astype(bf16)
    prod_low = (prod - prod_high.astype(f32)).astype(bf16)
    pick = (
        lax.broadcasted_iota(jnp.int32, (8, PAIR), 1) // HEAD
        == lax.broadcasted_iota(jnp.int32, (8, PAIR), 0)
    ).astype(bf16)
    delta = nt(pick, prod_high) + nt(pick, prod_low)
    dk = dv = None
    dq = []
    for h in range(2):
        half = lane_half(q_pair.shape, h)
        q = jnp.where(half, q_pair, jnp.zeros_like(q_pair))
        da = jnp.where(half, da_pair, jnp.zeros_like(da_pair))
        p = jnp.exp(nt(k_pair, q) + (bias_t - logs[h]))
        ds = (p * (nt(v_pair, da) - delta[h : h + 1])).astype(bf16)
        dv_h = nn(p.astype(bf16), da)
        dk_h = nn(ds, q)
        dk = dk_h if dk is None else dk + dk_h
        dv = dv_h if dv is None else dv + dv_h
        dq.append(nn(k_turned[h * HEAD : (h + 1) * HEAD], ds))
    return jnp.concatenate(dq, axis=0).T.astype(bf16), dk, dv


def whole_spec(shape):
    return pl.BlockSpec(shape, lambda i: (0,) * len(shape))


def shard_spec(shape, index=lambda i: i):
    return pl.BlockSpec((1,) + shape[1:], lambda i: (index(i), 0, 0))


def feed_forward_kernel(
    v2, out_grad, w_in, w_out, down, down_bias, up, up_bias, gain, shift,
    output, dr2, summed, rest, vecs,
    n2_low, n2_hat, total, e_low, slope, grad, g, s1, h, xb, send, recv,
):
    step = pl.program_id(0)
    half = pl.num_programs(0) // 2
    links = Links(send, recv)
    reduce = AdapterReduceFirst(links, g, s1, h, xb)

    @pl.when(step == 0)
    def _():
        greet([links.tp_peer(1), links.side_peer()])
        n, _ = norm_parts(v2[...])
        n2_hat[...] = n
        normed = n * gain[1:2] + shift[1:2]
        total[...] = normed
        n2_low[...] = normed.astype(bf16)

    @pl.when(step < half)
    def _():
        act, bend = gelu_parts(nn(n2_low[...], w_in[0]))
        slope[step] = bend
        total[...] += nn(act.astype(bf16), w_out[0])

    @pl.when(step == half - 1)
    def _():
        act, bend = gelu_parts(nn(n2_low[...], down[...]) + down_bias[...])
        act = act.astype(bf16)
        resid = total[...] + 4.0 * (nn(act, up[...]) + up_bias[...])
        n, spread = norm_parts(resid)
        output[...] = (n * gain[2:3] + shift[2:3]).astype(bf16)
        dz, gain_part, shift_part = norm_back(out_grad[...].astype(f32), gain[2:3], n, spread)
        e_low[...] = dz.astype(bf16)
        four = (4.0 * dz).astype(bf16)
        g[0] = tn(act, four).astype(bf16).reshape(g.shape[1:])
        da = (nt(four, up[...]) * bend).astype(bf16)
        g[1] = tn(da, n2_low[...]).astype(bf16).reshape(g.shape[1:])
        reduce.start_beside()
        grad[...] = dz + nt(da, down[...])
        vecs[...] = jnp.zeros_like(vecs)
        vecs[2:3] = gain_part
        vecs[5:6] = shift_part
        vecs[6:7] = jnp.sum(four.astype(f32), axis=0, keepdims=True)
        vecs[7:8, 0 : down.shape[1]] = jnp.sum(da.astype(f32), axis=0, keepdims=True)

    @pl.when(step >= half)
    def _():
        du = (nt(e_low[...], w_out[0]) * slope[2 * half - 1 - step]).astype(bf16)
        grad[...] += nt(du, w_in[0])

    @pl.when(step == half)
    def _():
        reduce.start_side()

    @pl.when(step == 2 * half - 1)
    def _():
        _, spread = norm_parts(v2[...])
        dv, gain_part, shift_part = norm_back(grad[...], gain[1:2], n2_hat[...], spread)
        dr2[...] = dv
        vecs[1:2] = gain_part
        vecs[4:5] = shift_part
        reduce.finish(summed, rest)


def feed_forward(v2, out_grad, w_in, w_out, down, down_bias, up, up_bias, gain, shift):
    n, width, inner = w_in.shape
    block = v2.shape[0]
    adapt = down.shape[1]
    out = jax.ShapeDtypeStruct
    outs = (
        out((block, width), bf16),
        out((block, width), f32),
        out((LINE, adapt // GROUP, width), bf16),
        out((LINE // 2, adapt // GROUP, width), bf16),
        out((8, width), f32),
    )
    parts = (2, LINE, adapt // GROUP, width)
    turn = lambda i: jnp.minimum(i, 2 * n - 1 - i)
    return pl.pallas_call(
        feed_forward_kernel,
        grid=(2 * n,),
        out_shape=outs,
        in_specs=[whole_spec(v2.shape), whole_spec(out_grad.shape)]
        + [shard_spec(w_in.shape, turn), shard_spec(w_out.shape, turn)]
        + [whole_spec(a.shape) for a in (down, down_bias, up, up_bias, gain, shift)],
        out_specs=[whole_spec(a.shape) for a in outs],
        scratch_shapes=[
            VMEM((block, width), bf16),
            VMEM((block, width), f32),
            VMEM((block, width), f32),
            VMEM((block, width), bf16),
            VMEM((n, block, inner), f32),
            VMEM((block, width), f32),
            VMEM((2,) + parts, bf16),
            VMEM(parts, bf16),
            VMEM(parts, bf16),
            VMEM((LINE // 2,) + parts[2:], bf16),
            pltpu.SemaphoreType.DMA((2,)),
            pltpu.SemaphoreType.DMA((2,)),
        ],
        compiler_params=pltpu.CompilerParams(
            collective_id=2, has_side_effects=True, vmem_limit_bytes=VMEM_BYTES
        ),
        name="feed_forward",
    )(v2, out_grad, w_in, w_out, down, down_bias, up, up_bias, gain, shift)


class Links:
    def __init__(self, send, recv):
        self.send, self.recv = send, recv
        self.row = lax.axis_index("rows")
        self.t = lax.axis_index("tp")
        self.flows = 0
        place = lax.rem(self.row, GROUP)
        self.base = self.row - place
        self.a = place // 2
        self.b = lax.rem(place, 2)
        self.place = place

    def flow(self):
        self.flows += 1
        return self.flows - 1

    def tp_peer(self, mask):
        return (self.row, self.t ^ mask)

    def line_peer(self, d):
        return (self.base + lax.rem(self.a + d, LINE) * 2 + self.b, self.t)

    def side_peer(self):
        return (self.base + self.a * 2 + (1 - self.b), self.t)

    def copy(self, src, dst, flow, peer):
        return pltpu.make_async_remote_copy(
            src_ref=src,
            dst_ref=dst,
            send_sem=self.send.at[flow],
            recv_sem=self.recv.at[flow],
            device_id=peer,
            device_id_type=MESH,
        )

    def start(self, src, dst, flow, peer):
        made = self.copy(src, dst, flow, peer)
        made.start()
        return made

    def arrived(self, dst, flow, peer):
        self.copy(dst, dst, flow, peer).wait_recv()


def greet(peers):
    barrier = pltpu.get_barrier_semaphore()
    for peer in peers:
        pl.semaphore_signal(barrier, inc=1, device_id=peer, device_id_type=MESH)
    pl.semaphore_wait(barrier, len(peers))


CHUNKS = 4


FLOWS = 14


class WeightGather:
    def __init__(self, links, base, across, own, full, stage, local):
        self.links, self.base, self.across = links, base, across
        self.own, self.full, self.stage, self.local = own, full, stage, local
        self.far, self.last = links.t ^ 2, links.t ^ 3
        a = links.a
        self.right = (links.base + jnp.minimum(a + 1, LINE - 1) * 2 + links.b, links.t)
        self.left = (links.base + jnp.maximum(a - 1, 0) * 2 + links.b, links.t)
        self.side = links.side_peer()
        self.sibling = links.tp_peer(1)
        self.over = links.tp_peer(2)

    def at(self, i, a, b):
        rows = self.own[i].shape[0] // GROUP
        return pl.ds(pl.multiple_of((a * 2 + b) * rows, rows), rows)

    def part(self, i, a, b):
        return self.full[i].at[self.far, self.at(i, a, b)]

    def flow(self, i, k):
        return self.base + i * FLOWS + k

    def over_copy(self, i, k):
        links = self.links
        b = links.b if k == 0 else 1 - links.b
        at = self.at(i, links.a, b)
        return links.copy(
            self.own[i].at[at], self.full[i].at[links.t, at], self.flow(i, k), self.over
        )

    def beside_copy(self, i):
        return self.links.copy(
            self.own[i], self.full[i].at[self.links.t], self.flow(i, 2), self.sibling
        )

    def pass_copy(self, i):
        whole = self.full[i].at[self.far]
        return self.links.copy(whole, whole, self.flow(i, 3), self.sibling)

    def moved(self, i, a, flow, peer):
        part = self.part(i, a, self.links.b)
        return self.links.copy(part, part, self.flow(i, flow), peer)

    def stage_in(self, i):
        stage = self.full[i].at[self.links.t] if self.stage is None else self.stage[i]
        return pltpu.make_async_copy(self.own[i], stage, self.local.at[2 * i])

    def stage_out(self, i):
        return pltpu.make_async_copy(
            self.stage[i], self.full[i].at[self.links.t], self.local.at[2 * i + 1]
        )

    def start_over(self, i, k):
        self.over_copy(i, k).start()

    def start_beside(self, i):
        self.beside_copy(i).start()
        self.stage_in(i).start()

    def own_ready(self, i):
        self.stage_in(i).wait()

    def beside_ready(self, i):
        self.links.arrived(self.full[i].at[self.links.t ^ 1], self.flow(i, 2), self.sibling)

    def far_ready(self, i):
        self.links.arrived(self.full[i].at[self.last], self.flow(i, 3), self.sibling)

    def keep_own(self, i):
        self.own_ready(i)
        self.stage_out(i).start()

    def came_over(self, i):
        mine = self.part(i, self.links.a, self.links.b)
        self.links.arrived(mine, self.flow(i, 0), self.over)
        self.spread(i)

    def spread(self, i):
        a = self.links.a

        @pl.when(a < LINE - 1)
        def _():
            self.moved(i, a, 4, self.right).start()

        @pl.when(a > 0)
        def _():
            self.moved(i, a, 7, self.left).start()

        if self.across[i] == 1:
            self.moved(i, a, 10, self.side).start()

    def along(self, i, k):
        links, a = self.links, self.links.a

        @pl.when(a - 1 - k >= 0)
        def _():
            links.arrived(self.part(i, a - 1 - k, links.b), self.flow(i, 4 + k), self.left)
            if k < LINE - 2:

                @pl.when(a < LINE - 1)
                def _():
                    self.moved(i, a - 1 - k, 5 + k, self.right).start()

            self.moved(i, a - 1 - k, 11 + k, self.side).start()

        @pl.when(a + 1 + k <= LINE - 1)
        def _():
            links.arrived(self.part(i, a + 1 + k, links.b), self.flow(i, 7 + k), self.right)
            if k < LINE - 2:

                @pl.when(a > 0)
                def _():
                    self.moved(i, a + 1 + k, 8 + k, self.left).start()

            self.moved(i, a + 1 + k, 13 - k, self.side).start()

    def side_part(self, i, k):
        links, a = self.links, self.links.a
        if k == 0:
            return self.part(i, a, 1 - links.b)
        piece = jnp.where(k <= a, a - k, a + LINE - k)
        return self.part(i, piece, 1 - links.b)

    def complete(self, i):
        links = self.links
        if self.across[i] == 2:
            links.arrived(self.side_part(i, 0), self.flow(i, 1), self.over)
        for k in range(self.across[i] - 1, LINE):
            links.arrived(self.side_part(i, k), self.flow(i, 10 + k), self.side)
        self.pass_copy(i).start()

    def finish(self, i):
        if self.stage is not None:
            self.beside_ready(i)
            self.far_ready(i)
            self.stage_out(i).wait()
        for k in range(self.across[i]):
            self.over_copy(i, k).wait_send()
        self.beside_copy(i).wait_send()
        self.spread_sent(i)

    def spread_sent(self, i):
        a = self.links.a
        self.pass_copy(i).wait_send()
        for k in range(LINE - 1):

            @pl.when((a < LINE - 1) & (a - k >= 0))
            def _():
                self.moved(i, a - k, 4 + k, self.right).wait_send()

            @pl.when((a > 0) & (a + k <= LINE - 1))
            def _():
                self.moved(i, a + k, 7 + k, self.left).wait_send()

        for k in range(self.across[i] - 1, LINE):
            piece = a if k == 0 else jnp.where(k <= a, a - k, a + LINE - k)
            self.moved(i, piece, 10 + k, self.side).wait_send()


class AdapterSpread(WeightGather):
    def __init__(self, links, base, full):
        super().__init__(links, base, [1], None, full, None, None)
        self.half = lax.rem(links.t, 2)

    def part(self, i, a, b):
        return self.full.at[self.half, b, a]

    def pass_copy(self, i):
        whole = self.full.at[self.half]
        return self.links.copy(whole, whole, self.flow(i, 3), self.sibling)

    def finish(self, i):
        self.links.arrived(self.full.at[1 - self.half], self.flow(i, 3), self.sibling)
        self.spread_sent(i)


class AdapterReduceFirst:
    def __init__(self, links, g, s1, h, xb):
        self.links, self.g, self.s1, self.h, self.xb = links, g, s1, h, xb
        self.half = lax.rem(links.t, 2)

    def beside(self):
        return self.links.copy(self.g.at[1 - self.half], self.s1, 0, self.links.tp_peer(1))

    def side(self):
        links = self.links
        return links.copy(
            self.h.at[1 - links.b, pl.ds(0, LINE // 2)], self.xb, 1, links.side_peer()
        )

    def start_beside(self):
        self.beside().start()

    def start_side(self):
        self.beside().wait()
        self.h[...] = (self.g[self.half].astype(f32) + self.s1[...].astype(f32)).astype(bf16)
        self.side().start()

    def finish(self, summed, rest):
        kept = LINE // 2
        mine = self.h[self.links.b]
        rest[...] = self.h[1 - self.links.b, kept:]
        summed[kept:] = mine[kept:]
        self.side().wait()
        summed[0:kept] = (mine[0:kept].astype(f32) + self.xb[...].astype(f32)).astype(bf16)


class AdapterReduce:
    def __init__(self, links, base, levels, summed, rest, xb, h2, zb, p3, yb, hb):
        self.links, self.base, self.levels = links, base, levels
        self.summed, self.rest, self.xb, self.h2 = summed, rest, xb, h2
        self.zb, self.p3, self.yb, self.hb = zb, p3, yb, hb
        self.half = lax.rem(links.t, 2)
        self.groups = [(links.row ^ (GROUP << level), links.t) for level in range(levels)]

    def side(self):
        return self.links.copy(self.rest, self.xb, self.base, self.links.side_peer())

    def piece(self, d):
        return lax.rem(self.links.a + d, LINE)

    def line(self, d):
        return self.links.copy(
            self.h2.at[self.piece(d)], self.zb.at[d - 1], self.base + d, self.links.line_peer(d)
        )

    def over(self):
        return self.links.copy(self.p3, self.yb, self.base + LINE, self.links.tp_peer(2))

    def group(self, level):
        return self.links.copy(
            self.hb.at[2 * level],
            self.hb.at[2 * level + 1],
            self.base + LINE + 1 + level,
            self.groups[level],
        )

    def start(self):
        kept = LINE // 2
        self.side().start()
        self.h2[0:kept] = self.summed[0:kept]
        for d in range(1, LINE):

            @pl.when(self.piece(d) < kept)
            def _():
                self.line(d).start()

    def start_line(self):
        kept = LINE // 2
        self.side().wait()
        self.h2[kept:] = (self.summed[kept:].astype(f32) + self.xb[...].astype(f32)).astype(bf16)
        for d in range(1, LINE):

            @pl.when(self.piece(d) >= kept)
            def _():
                self.line(d).start()

    def start_over(self):
        for d in range(1, LINE):
            self.line(d).wait()
        total = self.h2[self.links.a].astype(f32)
        for d in range(1, LINE):
            total = total + self.zb[d - 1].astype(f32)
        self.p3[...] = total.astype(bf16)
        self.over().start()

    def result(self):
        self.over().wait()
        value = self.p3[...].astype(f32) + self.yb[...].astype(f32)
        for level in range(self.levels):
            self.hb[2 * level] = value.astype(bf16)
            self.group(level).start()
            self.group(level).wait()
            value = self.hb[2 * level].astype(f32) + self.hb[2 * level + 1].astype(f32)
        return value.astype(bf16)


class RowGather:
    FLOWS = 1 + 2 * 4

    def __init__(self, links, base, own, full):
        self.links, self.base, self.own, self.full = links, base, own, full
        self.far, self.last = links.t ^ 2, links.t ^ 3
        self.sibling, self.over = links.tp_peer(1), links.tp_peer(2)

    def at(self, c):
        rows = self.own.shape[0] // CHUNKS
        return pl.ds(c * rows, rows)

    def beside_copy(self):
        return self.links.copy(self.own, self.full.at[self.links.t], self.base, self.sibling)

    def over_copy(self, c):
        at = self.at(c)
        return self.links.copy(
            self.own.at[at], self.full.at[self.links.t, at], self.base + 1 + c, self.over
        )

    def pass_copy(self, c):
        part = self.full.at[self.far, self.at(c)]
        return self.links.copy(part, part, self.base + 1 + CHUNKS + c, self.sibling)

    def start_beside(self):
        self.beside_copy().start()

    def start_over(self):
        for c in range(CHUNKS):
            self.over_copy(c).start()

    def came_beside(self):
        self.links.arrived(self.full.at[self.links.t ^ 1], self.base, self.sibling)

    def came_over_chunk(self, c):
        self.links.arrived(self.full.at[self.far, self.at(c)], self.base + 1 + c, self.over)
        self.pass_copy(c).start()

    def came_over(self):
        for c in range(CHUNKS):
            self.came_over_chunk(c)

    def came_last(self):
        for c in range(CHUNKS):
            self.links.arrived(
                self.full.at[self.last, self.at(c)], self.base + 1 + CHUNKS + c, self.sibling
            )

    def sent(self):
        self.beside_copy().wait_send()
        for c in range(CHUNKS):
            self.over_copy(c).wait_send()
            self.pass_copy(c).wait_send()


class RowScatter:
    FLOWS = 2 + 4

    def __init__(self, links, base, part, near, near_far, mid, far):
        self.links, self.base, self.part = links, base, part
        self.near, self.near_far, self.mid, self.far = near, near_far, mid, far
        self.sibling, self.over = links.tp_peer(1), links.tp_peer(2)

    def at(self, c):
        rows = self.near.shape[0] // CHUNKS
        return pl.ds(c * rows, rows)

    def first_copy(self):
        return self.links.copy(
            self.part.at[self.links.t ^ 3], self.near_far, self.base, self.sibling
        )

    def second_copy(self):
        return self.links.copy(
            self.part.at[self.links.t ^ 1], self.near, self.base + 1, self.sibling
        )

    def over_copy(self, c):
        at = self.at(c)
        return self.links.copy(
            self.mid.at[at], self.far.at[at], self.base + 2 + c, self.over
        )

    def send_over(self):
        self.links.arrived(self.near_far, self.base, self.sibling)
        for c in range(CHUNKS):
            at = self.at(c)
            self.mid[at] = (
                self.part[self.links.t ^ 2, at].astype(f32) + self.near_far[at].astype(f32)
            ).astype(bf16)
            self.over_copy(c).start()

    def came_beside(self):
        self.links.arrived(self.near, self.base + 1, self.sibling)

    def came_over(self, c):
        at = self.at(c)
        self.links.arrived(self.far.at[at], self.base + 2 + c, self.over)
        return (
            self.part[self.links.t, at].astype(f32)
            + self.near[at].astype(f32)
            + self.far[at].astype(f32)
        )

    def sent(self):
        self.first_copy().wait_send()
        self.second_copy().wait_send()
        for c in range(CHUNKS):
            self.over_copy(c).wait_send()


def halves(own, full, stage):
    outs = ([], [], [])
    for one, whole, held in zip(own, full, stage):
        rows = one.shape[0] // 2
        for o in range(2):
            at = pl.ds(o * rows, rows)
            for out, view in zip(outs, (one.at[at], whole.at[:, at], held.at[at])):
                out.append(view)
    return outs


def cut(refs, *counts):
    out, at = [], 0
    for count in counts:
        out.append(refs[at : at + count])
        at += count
    return out


def forward_kernel(prefix_len, *refs):
    ins, self_outs, cross_outs, kept_outs, scratch = cut(refs, 18, 6, 6, 6, 26)
    x, pre_cross, wq, wk, wv, wo, pre, dec, src, gain, shift = ins[:11]
    memory, own_cross, own_ffn = ins[11], list(ins[12:16]), list(ins[16:18])
    q_out, k_out, v_out, a_out, l_out, resid = self_outs
    q2_out, k2_out, v2_out, a2_out, l2_out, resid2 = cross_outs
    cross_kept, ffn_full = list(kept_outs[:4]), list(kept_outs[4:])
    cross_full, held = list(scratch[:4]), list(scratch[4:6])
    (
        m_full, pre_full, x_full, part, kept, bias, near, near_far, mid, far, pre_stage, n1_low,
        send, recv, cross_local, ffn_local, m_local, keep_local, pre_local, spare,
    ) = scratch[6:]
    del spare
    block, lanes = x.shape[0], q_out.shape[1]
    links = Links(send, recv)
    t = links.t
    early = range(4)
    late = range(4)
    cross = WeightGather(links, 0, [1] * 4, own_cross, cross_full, None, cross_local)
    ffn = WeightGather(links, 4 * FLOWS, [2] * 4, *halves(own_ffn, ffn_full, held), ffn_local)
    at = 8 * FLOWS
    x_rows = RowGather(links, at, x, x_full)
    at += RowGather.FLOWS
    m_rows = RowGather(links, at, memory, m_full)
    at += RowGather.FLOWS
    sums = RowScatter(links, at, part, near, near_far, mid, far)
    at += RowScatter.FLOWS
    m_keep = pltpu.make_async_copy(memory, m_full.at[t], m_local.at[0])
    pre_keep = pltpu.make_async_copy(pre_stage, pre_full.at[t], pre_local.at[0])
    pre_sends = [
        links.copy(pre_stage, pre_full.at[t], at + m - 1, links.tp_peer(m)) for m in (1, 2, 3)
    ]
    cross_keeps = [
        pltpu.make_async_copy(cross_full[i], cross_kept[i], keep_local.at[i]) for i in range(4)
    ]

    greet(
        [links.tp_peer(m) for m in (1, 2, 3)]
        + [links.line_peer(d) for d in range(1, LINE)]
        + [links.side_peer()]
    )
    x_rows.start_over()
    x_rows.start_beside()
    kept[...] = jnp.zeros_like(kept)
    pre_stage[...] = jnp.zeros_like(pre_stage)
    for o in range(2):
        pre_stage[o * PRE_PACK : o * PRE_PACK + prefix_len] = pre_cross[:, o]
    pre_keep.start()
    for one in pre_sends:
        one.start()
    m_keep.start()

    for target, o in ((k_out, 0), (v_out, 1)):
        target[0:PRE] = jnp.zeros((PRE, lanes), bf16)
        target[0:prefix_len] = pre[:, o]

    def project(rows, index):
        at = pl.multiple_of(index * block, block)
        q_out[pl.ds(at, block)] = (SCALE * nn(rows, wq[...])).astype(bf16)
        k_out[pl.ds(PRE + at, block)] = nn(rows, wk[...]).astype(bf16)
        v_out[pl.ds(PRE + at, block)] = nn(rows, wv[...]).astype(bf16)

    project(x[...], t)
    x_rows.came_beside()
    project(x_full[t ^ 1], t ^ 1)
    for c in range(CHUNKS):
        x_rows.came_over_chunk(c)
        if c == 3:
            for i in early:
                cross.start_over(i, 0)
    project(x_full[t ^ 2], t ^ 2)
    x_rows.came_last()
    for i in early:
        cross.start_beside(i)
    m_rows.start_beside()
    project(x_full[t ^ 3], t ^ 3)

    @pl.loop(0, 4)
    def _(order):
        here = t ^ (3 - order)
        for i in range(4):
            keys = PRE + (i + 1) * block

            @pl.when(here == i)
            def _():
                bias[:, 0:PRE] = prefix_bias((block, PRE), 1, prefix_len)
                bias[:, PRE:keys] = mask_bias(
                    column(dec[:, i * block : (i + 1) * block]),
                    dec[:, 0 : keys - PRE],
                    (block, keys - PRE),
                    1,
                    i * block,
                )

                @pl.loop(0, lanes // PAIR)
                def _(j):
                    cols = pl.ds(pl.multiple_of(j * PAIR, PAIR), PAIR)
                    mixture, logs = pair_forward(
                        q_out[i * block : (i + 1) * block, cols],
                        k_out[0:keys, cols],
                        v_out[0:keys, cols],
                        bias[:, 0:keys],
                    )
                    a_out[i, :, cols] = mixture
                    keep_logs(kept, logs, j)

        l_out[here] = kept[...].T[0:8]
        part[here] = nn(a_out[here], wo[...]).astype(bf16)

        @pl.when(order == 0)
        def _():
            sums.first_copy().start()
            for i in early:
                cross.came_over(i)
            for i in range(2):
                ffn.start_over(i, 0)

        @pl.when(order == 1)
        def _():
            sums.send_over()

        @pl.when(order == 2)
        def _():
            sums.second_copy().start()
            m_rows.start_over()
            for i in early:
                cross.along(i, 0)

    for i in range(2):
        ffn.came_over(i)
    for i in late:
        ffn.start_beside(i)
    for i in early:
        cross.along(i, 1)
    for i in range(2):
        ffn.along(i, 0)
    sums.came_beside()
    for c in range(CHUNKS):
        rows = sums.at(c)
        resid[rows] = x[rows].astype(f32) + sums.came_over(c)
    n, _ = norm_parts(resid[...])
    normed = n * gain[0:1] + shift[0:1]
    resid2[...] = normed
    n1_low[...] = normed.astype(bf16)
    kept[...] = jnp.zeros_like(kept)
    own_queries = dec[:, pl.ds(pl.multiple_of(t * block, block), block)]
    keys = k2_out.shape[1]
    bias[:, 0:PRE] = prefix_bias((block, PRE), 1, prefix_len)
    bias[:, PRE:] = mask_bias(column(own_queries), src[...], (block, keys - PRE), 1, None)
    for i in early:
        cross.along(i, 2)
    for i in range(2):
        ffn.along(i, 1)
    m_rows.came_over()
    for i in (2, 3):
        ffn.start_over(i, 0)
    m_rows.came_beside()
    m_rows.came_last()
    for m in (1, 2, 3):
        links.arrived(pre_full.at[t ^ m], at + m - 1, links.tp_peer(m))
    m_keep.wait()
    pre_keep.wait()
    for i in early:
        cross.own_ready(i)

    def each(method, indices, *more):
        def run():
            for i in indices:
                method(i, *more)

        return run

    events = {
        0: [each(ffn.keep_own, late), each(ffn.along, (0, 1), 2)],
        1: [each(ffn.came_over, (2, 3)), each(cross.complete, early), each(ffn.start_over, late, 1)],
        3: [each(ffn.along, (2,), 0), each(cross.far_ready, early)],
        4: [each(ffn.along, (3,), 0), each(ffn.along, (2,), 1)],
        5: [each(ffn.along, (3,), 1)],
        6: [each(ffn.along, (2,), 2), each(ffn.complete, (0, 1))],
        7: [each(ffn.along, (3,), 2)],
    }

    @pl.loop(0, 4)
    def _(order):
        s = t ^ order

        @pl.when(order == 1)
        def _():
            for i in early:
                cross.beside_ready(i)

        q2_out[s] = (SCALE * nn(n1_low[...], cross_full[0][s])).astype(bf16)
        for target, o in ((k2_out, 0), (v2_out, PRE_PACK)):
            target[s, 0:PRE_PACK] = pre_full[s, o : o + PRE_PACK]
            target[s, PRE_PACK:PRE] = jnp.zeros((PRE - PRE_PACK, lanes), bf16)

        @pl.loop(0, 4)
        def _(i):
            rows = m_full[i]
            to = pl.ds(pl.multiple_of(PRE + i * block, PRE), block)
            k2_out[s, to] = nn(rows, cross_full[1][s]).astype(bf16)
            v2_out[s, to] = nn(rows, cross_full[2][s]).astype(bf16)

        for j in range(lanes // PAIR):
            cols = slice(j * PAIR, (j + 1) * PAIR)
            mixture, logs = pair_forward(
                q2_out[s, :, cols], k2_out[s, :, cols], v2_out[s, :, cols], bias[...]
            )
            a2_out[s, :, cols] = mixture
            keep_logs(kept, logs, j)
            for step in range(4):

                @pl.when(order == step)
                def _():
                    for event in events.get(2 * step + j, []):
                        event()

        l2_out[s] = kept[...].T[0:8]
        resid2[...] += nn(a2_out[s], cross_full[3][s])

    for one in cross_keeps:
        one.start()
    for i in (2, 3):
        ffn.complete(i)
    for i in early:
        cross.finish(i)
    for i in late:
        ffn.finish(i)
    x_rows.sent()
    m_rows.sent()
    sums.sent()
    for one in pre_sends:
        one.wait_send()
    for one in cross_keeps:
        one.wait()


def forward(
    prefix_len, x, memory, prefixes, self_weights, cross_weights, ffn_weights, dec, src, gain, shift
):
    n = 4
    block, width = x.shape
    lanes = self_weights[0].shape[1]
    seq = n * block
    out = jax.ShapeDtypeStruct
    flows = 8 * FLOWS + 2 * RowGather.FLOWS + RowScatter.FLOWS + 3
    self_outs = (
        out((seq, lanes), bf16),
        out((PRE + seq, lanes), bf16),
        out((PRE + seq, lanes), bf16),
        out((n, block, lanes), bf16),
        out((n, 8, block), f32),
        out((block, width), f32),
    )
    cross_outs = (
        out((n, block, lanes), bf16),
        out((n, PRE + seq, lanes), bf16),
        out((n, PRE + seq, lanes), bf16),
        out((n, block, lanes), bf16),
        out((n, 8, block), f32),
        out((block, width), f32),
    )
    full = tuple(out((n,) + w.shape, w.dtype) for w in (*cross_weights, *ffn_weights))
    given = (x, prefixes[1], *self_weights, prefixes[0], dec, src, gain, shift)
    anywhere = pl.BlockSpec(memory_space=pltpu.HBM)
    rows = VMEM((block, width), bf16)
    all_rows = VMEM((n, block, width), bf16)
    dma = pltpu.SemaphoreType.DMA
    return pl.pallas_call(
        functools.partial(forward_kernel, prefix_len),
        grid=(1,),
        out_shape=self_outs + cross_outs + full,
        in_specs=[whole_spec(g.shape) for g in given] + [anywhere] * 7,
        out_specs=[whole_spec(o.shape) for o in self_outs + cross_outs] + [anywhere] * 6,
        scratch_shapes=[VMEM((n,) + w.shape, w.dtype) for w in cross_weights]
        + [VMEM(w.shape, w.dtype) for w in ffn_weights]
        + [
            all_rows,
            VMEM((n, 2 * PRE_PACK, lanes), bf16),
            all_rows,
            all_rows,
            VMEM((block, 128), f32),
            VMEM((block, PRE + seq), f32),
            rows,
            rows,
            rows,
            rows,
            VMEM((2 * PRE_PACK, lanes), bf16),
            rows,
            dma((flows,)),
            dma((flows,)),
            dma((8,)),
            dma((8,)),
            dma((1,)),
            dma((4,)),
            dma((1,)),
            dma((1,)),
        ],
        compiler_params=pltpu.CompilerParams(
            collective_id=0, has_side_effects=True, vmem_limit_bytes=VMEM_BYTES
        ),
        name="forward",
    )(*given, memory, *cross_weights, *ffn_weights)


def doublings(count):
    levels = 0
    while (1 << levels) < count:
        levels += 1
    return levels


class Doubling:
    def __init__(self, links, base, levels, outgo, income):
        self.links, self.base, self.levels = links, base, levels
        self.outgo, self.income = outgo, income

    def move(self, level):
        return self.links.copy(
            self.outgo.at[level],
            self.income.at[level],
            self.base + level,
            (self.links.row ^ (1 << level), self.links.t),
        )

    def begin(self, value):
        self.outgo[0] = value
        self.move(0).start()

    def value(self, level):
        self.move(level).wait()
        return self.outgo[level] + self.income[level]

    def step(self, level):
        value = self.value(level)
        self.outgo[level + 1] = value
        self.move(level + 1).start()


def backward_kernel(prefix_len, reduce_levels, levels, *refs):
    ins, later, outs, scratch = cut(refs, 17, 9, 5, 54)
    dr2, v1, q, k, v, a, logs, wq, wo, wk, wv, dec, src, gain, vecs_in, summed, rest = ins
    tokens_grad, memory_grad, adapter, self_pre, sums = outs
    (
        dr1, dr1_low, dr2_low, bias, da, dq, dk, dv, total, xb, h2, zb, p3, yb, hb,
        cross, vecs, dm, dr1_full, part, dq1, dk1, dv1,
        near, near_far, mid, far, m_near, m_near_far, m_mid, m_far,
        cross_beside, cross_mid, cross_over, vecs_beside, vecs_mid, vecs_over,
        outgo, income, pre_outgo, pre_income, send, recv, keep_sem, load_sem,
    ) = scratch[:-9]
    loaded = scratch[-9:]
    q1, k1, v1_heads, a1, logs1, wq1, wk1, wv1, wo1 = loaded
    step = pl.program_id(0)
    steps = pl.num_programs(0) - 1
    block, lanes = q.shape[1:]
    keys = k.shape[1]
    links = Links(send, recv)
    t = links.t
    at = 0
    rows = RowGather(links, at, dr1_low, dr1_full)
    at += RowGather.FLOWS
    reduce = AdapterReduce(links, at, reduce_levels, summed, rest, xb, h2, zb, p3, yb, hb)
    at += 1 + LINE + reduce_levels
    spread = AdapterSpread(links, at, adapter)
    at += FLOWS
    m_sums = RowScatter(links, at, dm, m_near, m_near_far, m_mid, m_far)
    at += RowScatter.FLOWS
    x_sums = RowScatter(links, at, part, near, near_far, mid, far)
    at += RowScatter.FLOWS
    totals = Doubling(links, at, levels, outgo, income)
    at += levels
    pre_totals = Doubling(links, at, levels, pre_outgo, pre_income)
    at += levels
    keep = pltpu.make_async_copy(dr1_low, dr1_full.at[t], keep_sem.at[0])
    loads = [
        pltpu.make_async_copy(src_ref, dst_ref, load_sem.at[i])
        for i, (src_ref, dst_ref) in enumerate(zip(later, loaded))
    ]

    beside, over = links.tp_peer(1), links.tp_peer(2)
    to_beside = (
        links.copy(cross.at[t ^ 1], cross_beside.at[0], at, beside),
        links.copy(cross.at[t ^ 3], cross_beside.at[1], at + 1, beside),
        links.copy(vecs, vecs_beside, at + 2, beside),
    )
    to_over = (
        links.copy(cross_mid, cross_over, at + 3, over),
        links.copy(vecs_mid, vecs_over, at + 4, over),
    )

    @pl.when(step == 0)
    def _():
        greet(
            [links.tp_peer(m) for m in (1, 2, 3)]
            + [links.line_peer(d) for d in range(1, LINE)]
            + [links.side_peer()]
            + [(links.row ^ (1 << level), t) for level in range(doublings(GROUP), levels)]
        )
        reduce.start()
        dr2_low[...] = dr2[...].astype(bf16)
        total[...] = jnp.zeros_like(total)
        own_queries = dec[:, pl.ds(pl.multiple_of(t * block, block), block)]
        bias[0:PRE] = prefix_bias((PRE, block), 0, prefix_len)
        bias[PRE:] = mask_bias(own_queries, column(src[...]), (keys - PRE, block), 0, None)

    @pl.when(step < steps)
    def _():
        da[...] = nt(dr2_low[...], wo[0]).astype(bf16)

        @pl.when(step == 0)
        def _():
            for one in loads:
                one.start()

        @pl.loop(0, lanes // PAIR)
        def _(j):
            cols = pl.ds(pl.multiple_of(j * PAIR, PAIR), PAIR)
            dq_pair, dk_pair, dv_pair = pair_backward(
                q[0, :, cols],
                k[0, :, cols],
                v[0, :, cols],
                a[0, :, cols],
                da[:, cols],
                [logs[0, pl.ds(2 * j + i, 1)] for i in range(2)],
                bias[...],
            )
            dq[:, cols] = dq_pair
            cross[step, 0:PRE_PACK, cols] = dk_pair[0:PRE_PACK]
            cross[step, PRE_PACK : 2 * PRE_PACK, cols] = dv_pair[0:PRE_PACK]
            dk[step, :, cols] = dk_pair[PRE:].astype(bf16)
            dv[step, :, cols] = dv_pair[PRE:].astype(bf16)

            @pl.when((step == 1) & (j == 0))
            def _():
                reduce.start_line()

            @pl.when((step == 3) & (j == 1))
            def _():
                reduce.start_over()


        total[...] += nt(dq[...], wq[0])

    @pl.when(step == steps)
    def _():
        n, spread_one = norm_parts(v1[...])
        grad, gain_part, shift_part = norm_back(
            dr2[...] + SCALE * total[...], gain[0:1], n, spread_one
        )
        dr1_low[...] = grad.astype(bf16)
        rows.start_over()
        rows.start_beside()
        keep.start()
        dr1[...] = grad
        vecs[...] = vecs_in[...]
        vecs[0:1] = gain_part
        vecs[3:4] = shift_part
        for one in to_beside:
            one.start()
        dk1[...] = jnp.zeros_like(dk1)
        dv1[...] = jnp.zeros_like(dv1)

        @pl.loop(0, 4)
        def _(order):
            here = t ^ (3 - order)
            to = pl.ds(pl.multiple_of(here * block, block), block)
            value = None
            for shard in range(dk.shape[0]):
                term = nt(dk[shard, to], wk[shard]) + nt(dv[shard, to], wv[shard])
                value = term if value is None else value + term
            dm[here] = value.astype(bf16)

        m_sums.first_copy().start()
        m_sums.second_copy().start()
        for one in loads:
            one.wait()
        keep.wait()
        rows.came_beside()
        for one in to_beside:
            one.wait()
        cross_mid[...] = cross[t ^ 2] + cross_beside[1]
        vecs_mid[...] = vecs[...] + vecs_beside[...]
        for one in to_over:
            one.start()
        p3[...] = reduce.result()
        settle = pltpu.make_async_copy(
            p3, adapter.at[spread.half, links.b, links.a], keep_sem.at[1]
        )
        settle.start()
        settle.wait()
        spread.spread(0)

        @pl.loop(0, 4)
        def _(order):
            here = t ^ order

            @pl.when(order == 2)
            def _():
                rows.came_over()
                m_sums.send_over()
                rows.came_last()

            da[...] = nt(dr1_full[here], wo1[...]).astype(bf16)
            for i in range(4):
                own = slice(i * block, (i + 1) * block)
                size = PRE + (i + 1) * block

                @pl.when(here == i)
                def _():
                    bias[0:PRE] = prefix_bias((PRE, block), 0, prefix_len)
                    bias[PRE:size] = mask_bias(
                        dec[:, own],
                        column(dec[:, 0 : size - PRE]),
                        (size - PRE, block),
                        0,
                        i * block,
                    )

                    @pl.loop(0, lanes // PAIR)
                    def _(j):
                        cols = pl.ds(pl.multiple_of(j * PAIR, PAIR), PAIR)
                        dq_pair, dk_pair, dv_pair = pair_backward(
                            q1[own, cols],
                            k1[0:size, cols],
                            v1_heads[0:size, cols],
                            a1[i, :, cols],
                            da[:, cols],
                            [logs1[i, pl.ds(2 * j + o, 1)] for o in range(2)],
                            bias[0:size],
                        )
                        dq1[i, :, cols] = dq_pair
                        dk1[0:size, cols] += dk_pair
                        dv1[0:size, cols] += dv_pair

            for k in range(3):

                @pl.when(order == k)
                def _():
                    spread.along(0, k)

            @pl.when(order == 2)
            def _():
                for one in to_over:
                    one.wait()
                value = vecs_mid[...] + vecs_over[...]
                pieces = [cross[t] + cross_beside[0] + cross_over[...]] + [
                    value[:, o * lanes : (o + 1) * lanes] for o in range(vecs.shape[1] // lanes)
                ]
                totals.begin(jnp.concatenate(pieces, axis=0))

        pre_totals.begin(jnp.concatenate([dk1[0:PRE_PACK], dv1[0:PRE_PACK]], axis=0))
        for order in range(4):
            here = t ^ (3 - order)
            done = pl.ds(pl.multiple_of(PRE + here * block, PRE), block)
            part[here] = (
                SCALE * nt(dq1[here], wq1[...])
                + nt(dk1[done].astype(bf16), wk1[...])
                + nt(dv1[done].astype(bf16), wv1[...])
            ).astype(bf16)
            if order == 0:
                x_sums.first_copy().start()
                totals.step(0)
            if order == 1:
                x_sums.send_over()
                pre_totals.step(0)
            if order == 2:
                x_sums.second_copy().start()

        for level in range(1, levels - 1):
            totals.step(level)
            pre_totals.step(level)
        spread.complete(0)
        m_sums.came_beside()
        for c in range(CHUNKS):
            memory_grad[m_sums.at(c)] = m_sums.came_over(c).astype(bf16)
        sums[...] = totals.value(levels - 1)
        self_pre[...] = pre_totals.value(levels - 1)
        x_sums.came_beside()
        for c in range(CHUNKS):
            here = x_sums.at(c)
            tokens_grad[here] = (dr1[here] + x_sums.came_over(c)).astype(bf16)
        spread.finish(0)
        rows.sent()
        m_sums.sent()
        x_sums.sent()


def backward(
    prefix_len, row_count, dr2, resid_one, cross_saved, cross_weights, self_saved, self_weights,
    dec, src, gain, vecs, summed, rest,
):
    q, k, v, a, logs = cross_saved
    wq, wk, wv, wo = cross_weights
    n, block, lanes = q.shape
    keys = k.shape[1]
    width = dr2.shape[1]
    reduce_levels = doublings(row_count // GROUP)
    levels = doublings(row_count)
    piece = summed.shape[1]
    half = (2, LINE, piece, width)
    packed = 2 * PRE_PACK
    height = packed + vecs.shape[0] * width // lanes
    out = jax.ShapeDtypeStruct
    outs = (
        out((block, width), bf16),
        out((block, width), bf16),
        out((2,) + half, bf16),
        out((packed, lanes), f32),
        out((height, lanes), f32),
    )
    flows = (
        RowGather.FLOWS + 1 + LINE + reduce_levels + FLOWS + 2 * RowScatter.FLOWS + 2 * levels + 5
    )
    later = (*self_saved, *self_weights)
    low, wide = VMEM((block, width), bf16), VMEM((block, width), f32)
    dma = pltpu.SemaphoreType.DMA
    bounded = lambda i: jnp.minimum(i, n - 1)

    def once(x):
        return pl.BlockSpec(x.shape, lambda i: (0,) * len(x.shape), pipeline_mode=pl.Buffered(1))

    return pl.pallas_call(
        functools.partial(backward_kernel, prefix_len, reduce_levels, levels),
        grid=(n + 1,),
        out_shape=outs,
        in_specs=[once(dr2), once(resid_one)]
        + [shard_spec(x.shape, bounded) for x in (q, k, v, a, logs, wq, wo)]
        + [once(x) for x in (wk, wv, dec, src, gain, vecs, summed, rest)]
        + [pl.BlockSpec(memory_space=pltpu.HBM)] * len(later),
        out_specs=[whole_spec(o.shape) for o in outs[:2]]
        + [pl.BlockSpec(memory_space=pltpu.HBM)]
        + [whole_spec(o.shape) for o in outs[3:]],
        scratch_shapes=[
            wide,
            low,
            low,
            VMEM((keys, block), f32),
            VMEM((block, lanes), bf16),
            VMEM((block, lanes), bf16),
            VMEM((n, keys - PRE, lanes), bf16),
            VMEM((n, keys - PRE, lanes), bf16),
            wide,
            VMEM((LINE // 2, piece, width), bf16),
            VMEM((LINE, piece, width), bf16),
            VMEM((LINE - 1, piece, width), bf16),
            VMEM((piece, width), bf16),
            VMEM((piece, width), bf16),
            VMEM((max(1, 2 * reduce_levels), piece, width), bf16),
            VMEM((n, packed, lanes), f32),
            VMEM(vecs.shape, f32),
            VMEM((n, block, width), bf16),
            VMEM((n, block, width), bf16),
            VMEM((n, block, width), bf16),
            VMEM((n, block, lanes), bf16),
            VMEM((keys, lanes), f32),
            VMEM((keys, lanes), f32),
        ]
        + [low] * 8
        + [
            VMEM((2, packed, lanes), f32),
            VMEM((packed, lanes), f32),
            VMEM((packed, lanes), f32),
            VMEM(vecs.shape, f32),
            VMEM(vecs.shape, f32),
            VMEM(vecs.shape, f32),
            VMEM((levels, height, lanes), f32),
            VMEM((levels, height, lanes), f32),
            VMEM((levels, packed, lanes), f32),
            VMEM((levels, packed, lanes), f32),
            dma((flows,)),
            dma((flows,)),
            dma((2,)),
            dma((len(later),)),
        ]
        + [VMEM(x.shape, x.dtype) for x in later],
        compiler_params=pltpu.CompilerParams(
            collective_id=1, has_side_effects=True, vmem_limit_bytes=VMEM_BYTES
        ),
        name="backward",
    )(dr2, resid_one, q, k, v, a, logs, wq, wo, wk, wv, dec, src, gain, vecs, summed, rest, *later)


def finish_kernel(
    prefix_len, lanes, output_low, tokens_low, memory_low, up_low, down_low, self_pre, sums,
    output, tokens_grad, memory_grad, self_out, cross_out, gains, shifts, down, down_bias, up, up_bias,
):
    output[...] = output_low[...]
    tokens_grad[...] = tokens_low[...]
    memory_grad[...] = memory_low[...]
    up[...] = up_low[0].astype(f32)
    rows = down.shape[0]
    at = pl.multiple_of(pl.program_id(0) * rows, rows)
    down[...] = down_low[0, :, pl.ds(at, rows)].astype(f32).T

    @pl.when(pl.program_id(0) == 0)
    def _():
        for o in range(2):
            rows = slice(o * PRE_PACK, o * PRE_PACK + prefix_len)
            self_out[:, o] = self_pre[rows]
            cross_out[:, o] = sums[rows]
        for i in range(gains.shape[1] // lanes):
            at = 2 * PRE_PACK + 8 * i
            cols = slice(i * lanes, (i + 1) * lanes)
            gains[:, cols] = sums[at : at + 3]
            shifts[:, cols] = sums[at + 3 : at + 6]
            up_bias[:, cols] = sums[at + 6 : at + 7]
            if (i + 1) * lanes <= down_bias.shape[1]:
                down_bias[:, cols] = sums[at + 7 : at + 8]


def finish(prefix_len, output_low, tokens_low, memory_low, adapter, self_pre, sums):
    steps = 2
    block, width = tokens_low.shape
    adapt = adapter.shape[1]
    lanes = sums.shape[1]
    out = jax.ShapeDtypeStruct
    outs = (
        out((block, width), bf16),
        out((block, width), bf16),
        out((block, width), bf16),
        out((prefix_len, 2, lanes), f32),
        out((prefix_len, 2, lanes), f32),
        out((3, width), f32),
        out((3, width), f32),
        out((width, adapt), f32),
        out((1, adapt), f32),
        out((adapt, width), f32),
        out((1, width), f32),
    )
    rows = pl.BlockSpec((block // steps, width), lambda i: (i, 0))
    specs = [whole_spec(o.shape) for o in outs]
    specs[0] = specs[1] = specs[2] = rows
    specs[7] = pl.BlockSpec((width // steps, adapt), lambda i: (i, 0))
    specs[9] = pl.BlockSpec((adapt // steps, width), lambda i: (i, 0))
    return pl.pallas_call(
        functools.partial(finish_kernel, prefix_len, lanes),
        grid=(steps,),
        out_shape=outs,
        in_specs=[rows, rows, rows]
        + [pl.BlockSpec((1, adapt // steps, width), lambda i: (0, i, 0))]
        + [pl.BlockSpec((1, adapt, width), lambda i: (1, 0, 0))]
        + [whole_spec(self_pre.shape), whole_spec(sums.shape)],
        out_specs=specs,
        compiler_params=pltpu.CompilerParams(vmem_limit_bytes=VMEM_BYTES),
        name="finish",
    )(output_low, tokens_low, memory_low, adapter, adapter, self_pre, sums)


def per_device(
    row_count,
    tokens, memory, out_grad, dec_segments, src_segments,
    self_query, self_key, self_value, self_out,
    cross_query, cross_key, cross_value, cross_out,
    ffn_in, ffn_out, adapt_down, adapt_down_bias, adapt_up, adapt_up_bias,
    self_prefix, cross_prefix, norm_gain, norm_shift,
):
    seq_local, _, width = tokens.shape
    prefix_len = self_prefix.shape[1]
    adapt = adapt_down.shape[1]
    x, mem, grad_in = (a.reshape(seq_local, width) for a in (tokens, memory, out_grad))
    self_weights = (self_query, self_key, self_value, self_out)

    (
        q1, k1, v1_heads, a1, logs1, resid_one, q2, k2, v2_heads, a2, logs2, resid_two, *gathered
    ) = forward(
        prefix_len, x, mem, [jnp.swapaxes(p, 0, 1) for p in (self_prefix, cross_prefix)], self_weights,
        (cross_query, cross_key, cross_value, cross_out), (ffn_in, ffn_out),
        dec_segments, src_segments, norm_gain, norm_shift,
    )
    cross_weights, (w_in, w_out) = gathered[:4], gathered[4:]
    output_low, dr2, summed, rest, vecs = feed_forward(
        resid_two, grad_in, w_in, w_out,
        adapt_down, adapt_down_bias.reshape(1, adapt), adapt_up, adapt_up_bias.reshape(1, width),
        norm_gain, norm_shift,
    )
    tokens_low, memory_low, adapter, self_pre, sums = backward(
        prefix_len, row_count, dr2, resid_one, (q2, k2, v2_heads, a2, logs2), cross_weights,
        (q1, k1, v1_heads, a1, logs1), self_weights,
        dec_segments, src_segments, norm_gain, vecs, summed, rest,
    )
    (
        output, tokens_grad, memory_grad, self_grad, cross_grad, gains, shifts,
        down, down_bias, up, up_bias,
    ) = finish(
        prefix_len, output_low, tokens_low, memory_low, adapter.reshape(2, adapt, width), self_pre, sums
    )
    local = tokens.shape
    return (
        output.reshape(local),
        tokens_grad.reshape(local),
        memory_grad.reshape(local),
        jnp.swapaxes(self_grad, 0, 1),
        jnp.swapaxes(cross_grad, 0, 1),
        gains,
        shifts,
        down,
        down_bias.reshape(adapt),
        up,
        up_bias.reshape(width),
    )


def solution(mesh):
    placed = (
        (P("tp", "rows", None),) * 3
        + (P("rows", None),) * 2
        + (P(None, "tp"),) * 3
        + (P("tp", None),)
        + (P(None, "tp"),) * 3
        + (P("tp", None),)
        + (P(None, "tp"), P("tp", None))
        + (P(),) * 4
        + (P(None, None, "tp"),) * 2
        + (P(),) * 2
    )
    return jax.shard_map(
        functools.partial(per_device, mesh.shape["rows"]),
        mesh=mesh,
        in_specs=placed,
        out_specs=(P("tp", "rows", None),) * 3 + (P(None, None, "tp"),) * 2 + (P(),) * 6,
        check_vma=False,
    )
```
